32 devices in a mesh: dp: 8 (over y, x, core), tensor: 4 (over z).
Axes of the slice: x: 2, y: 2, z: 4, core: 2. Of those that a mesh axis runs over, the one named last changes fastest.
Arguments:
- tokens: bfloat16 [8192, 2048], P(('dp', 'tensor')), may hold values from -6 to 6
- attn_gain: bfloat16 [2048], P(('dp', 'tensor')), may hold values from 0.25 to 1.75
- w_query: bfloat16 [2048, 2048], P('dp', 'tensor'), may hold values from -0.125 to 0.125
- w_key: bfloat16 [2048, 256], P(('dp', 'tensor')), may hold values from -0.125 to 0.125
- w_value: bfloat16 [2048, 256], P(('dp', 'tensor')), may hold values from -0.125 to 0.125
- w_out: bfloat16 [2048, 2048], P('tensor', 'dp'), may hold values from -0.5 to 0.5
- mlp_gain: bfloat16 [2048], P(('dp', 'tensor')), may hold values from 0.25 to 1.75
- w_gate: bfloat16 [2048, 5632], P('dp', 'tensor'), may hold values from -0.125 to 0.125
- w_up: bfloat16 [2048, 5632], P('dp', 'tensor'), may hold values from -0.125 to 0.125
- w_down: bfloat16 [5632, 2048], P('tensor', 'dp'), may hold values from -0.15625 to 0.15625
- cotangent: bfloat16 [8192, 2048], P(('dp', 'tensor')), may hold values from -6 to 6
Outputs:
- output: bfloat16 [8192, 2048], P(('dp', 'tensor'))
- grad_tokens: float32 [8192, 2048], P(('dp', 'tensor'))
- grad_attn_gain: float32 [2048], P(('dp', 'tensor'))
- grad_query: float32 [2048, 2048], P('dp', 'tensor')
- grad_key: float32 [2048, 256], P(('dp', 'tensor'))
- grad_value: float32 [2048, 256], P(('dp', 'tensor'))
- grad_out: float32 [2048, 2048], P('tensor', 'dp')
- grad_mlp_gain: float32 [2048], P(('dp', 'tensor'))
- grad_gate: float32 [2048, 5632], P('dp', 'tensor')
- grad_up: float32 [2048, 5632], P('dp', 'tensor')
- grad_down: float32 [5632, 2048], P('tensor', 'dp')
The draws below stay inside these ranges and needn't reach their ends.
All inputs are finite; a program needn't handle non-finite values.
Results may differ from the reference program's by a relative error of at most 0.019.
Values may be sent and summed in bfloat16 or wider, within the bound.
A program may use at most 320 MiB of HBM per device.

```python
import jax
import jax.numpy as jnp
from jax import lax

D = 2048
HEADS = 32
KV_HEADS = 4
HEAD_DIM = 64
FF = 5632
SEQLEN = 1024
SEQS = 1
TOKENS = 8192


def levels(rng, extent, shards, smallest, largest):
    def one(axis_at, shards_of):
        heights = jax.random.uniform(jax.random.fold_in(jax.random.fold_in(rng, 6), axis_at), (shards_of,), jnp.float32, smallest / len(shards), largest / len(shards))
        return jnp.repeat(jnp.exp(heights), extent[axis_at] // shards_of).reshape((-1,) + (1,) * (len(extent) - axis_at - 1))

    level = one(*shards[0])
    for cut in shards[1:]:
        level = level * one(*cut)
    return level


def gaussian(rng, extent, deviation, limit, split=(), kind=jnp.bfloat16):
    drawn = deviation * jax.random.normal(rng, extent, jnp.float32)
    if split:
        drawn = drawn * levels(rng, extent, split, -0.22, 0.18)
    return jnp.clip(drawn, -limit, limit).astype(kind)


def setup_inputs(seed: int = 0) -> dict:
    splits = jax.random.split(jax.random.key(seed), 12)
    return {
        "tokens": gaussian(splits[0], (TOKENS, D), 1.0, 6.0, ((0, 32),)),
        "attn_gain": jnp.clip(1.0 + 0.15 * jax.random.normal(splits[1], (D,), jnp.float32), 0.25, 1.75).astype(jnp.bfloat16),
        "w_query": gaussian(splits[2], (D, HEADS * HEAD_DIM), D ** -0.5, 0.125, ((0, 8), (1, 4))),
        "w_key": gaussian(splits[3], (D, KV_HEADS * HEAD_DIM), D ** -0.5, 0.125, ((0, 32),)),
        "w_value": gaussian(splits[4], (D, KV_HEADS * HEAD_DIM), D ** -0.5, 0.125, ((0, 32),)),
        "w_out": gaussian(splits[5], (HEADS * HEAD_DIM, D), (HEADS * HEAD_DIM // 16) ** -0.5, 0.5, ((0, 4), (1, 8))),
        "mlp_gain": jnp.clip(1.0 + 0.15 * jax.random.normal(splits[6], (D,), jnp.float32), 0.25, 1.75).astype(jnp.bfloat16),
        "w_gate": gaussian(splits[7], (D, FF), D ** -0.5, 0.125, ((0, 8), (1, 4))),
        "w_up": gaussian(splits[8], (D, FF), D ** -0.5, 0.125, ((0, 8), (1, 4))),
        "w_down": gaussian(splits[9], (FF, D), (FF // 4) ** -0.5, 0.15625, ((0, 4), (1, 8))),
        "cotangent": gaussian(splits[10], (TOKENS, D), 1.0, 6.0, ((0, 32),)),
    }


@jax.custom_vjp
def low(v):
    return lax.optimization_barrier(v.astype(jnp.bfloat16)).astype(jnp.float32)

@jax.custom_vjp
def low_back(v):
    return v

def low_keep(v):
    return (low(v), None)

def low_pass(kept, grad):
    return (grad,)

def back_keep(v):
    return (v, None)

def back_low(kept, grad):
    return (low(grad),)
low.defvjp(low_keep, low_pass)
low_back.defvjp(back_keep, back_low)
epsilon = 1e-05
theta_base = 10000.0
highest = lax.Precision.HIGHEST

def rope_tables(length, head_width):
    halved = head_width // 2
    freqs = theta_base ** (-2.0 * jnp.arange(halved, dtype=jnp.float32) / head_width)
    angles = jnp.arange(length, dtype=jnp.float32)[:, None] * freqs[None, :]
    return (jnp.cos(angles), jnp.sin(angles))

def rotate(values, cosines, sines):
    halved = values.shape[-1] // 2
    first_half = values[..., :halved]
    second_half = values[..., halved:]
    return jnp.concatenate([first_half * cosines - second_half * sines, second_half * cosines + first_half * sines], axis=-1)

def matmul(left, right):
    return jnp.dot(left, right, precision=highest)

def rms_norm(hidden, gain):
    scaled = lax.rsqrt(lax.optimization_barrier(jnp.mean(hidden * hidden, axis=-1, keepdims=True)) + epsilon)
    return low(hidden * scaled * gain)

def attend(pieces):
    queries, key_heads, values = pieces
    length = queries.shape[1]
    causal = jnp.arange(length)[:, None] >= jnp.arange(length)[None, :]
    scores = low_back(jnp.einsum('hqd,hkd->hqk', queries, key_heads, precision=highest) * HEAD_DIM ** (-0.5))
    scores = jnp.where(causal[None], scores, -jnp.inf)
    row_max = lax.optimization_barrier(jnp.max(scores, axis=-1, keepdims=True))
    exponent = jnp.exp(scores - row_max)
    softmaxed = exponent / lax.optimization_barrier(jnp.sum(exponent, axis=-1, keepdims=True))
    return jnp.einsum('hqk,hkd->hqd', low(softmaxed), values, precision=highest)

def layer(tokens, attn_gain, w_query, w_key, w_value, w_out, mlp_gain, w_gate, w_up, w_down):
    seq_count = tokens.shape[0] // SEQLEN
    group_size = HEADS // KV_HEADS
    cosines, sines = rope_tables(SEQLEN, HEAD_DIM)
    normed = rms_norm(tokens, attn_gain)
    queries = low_back(matmul(normed, w_query)).reshape(seq_count, SEQLEN, HEADS, HEAD_DIM).transpose(0, 2, 1, 3)
    key_heads = matmul(normed, w_key).reshape(seq_count, SEQLEN, KV_HEADS, HEAD_DIM).transpose(0, 2, 1, 3)
    values = matmul(normed, w_value).reshape(seq_count, SEQLEN, KV_HEADS, HEAD_DIM).transpose(0, 2, 1, 3)
    key_heads = low(rotate(low_back(jnp.repeat(key_heads, group_size, axis=1)), cosines, sines))
    values = low(low_back(jnp.repeat(values, group_size, axis=1)))
    queries = low(rotate(queries, cosines, sines))
    context = lax.map(jax.checkpoint(attend), (queries, key_heads, values))
    context = low(low_back(context.transpose(0, 2, 1, 3).reshape(tokens.shape[0], HEADS * HEAD_DIM)))
    middle = tokens + low_back(matmul(context, w_out))
    normed_two = rms_norm(middle, mlp_gain)
    gate_pre = low_back(matmul(normed_two, w_gate))
    upward = low_back(matmul(normed_two, w_up))
    hidden = low(jax.nn.silu(gate_pre) * upward)
    return middle + low_back(matmul(hidden, w_down))

def reference(tokens, attn_gain, w_query, w_key, w_value, w_out, mlp_gain, w_gate, w_up, w_down, cotangent):
    weights = tuple((array_in.astype(jnp.float32) for array_in in (attn_gain, w_query, w_key, w_value, w_out, mlp_gain, w_gate, w_up, w_down)))
    block_rows = SEQS * SEQLEN
    inputs = tokens.astype(jnp.float32).reshape(-1, block_rows, D)
    cotangents = cotangent.astype(jnp.float32).reshape(-1, block_rows, D)

    def scan_step(running, pieces):
        block_in, block_cot = pieces
        result, pullback = jax.vjp(layer, block_in, *weights)
        gradients = pullback(block_cot)
        running = tuple((summed + fresh for summed, fresh in zip(running, gradients[1:])))
        return (running, (result, gradients[0]))
    zero_sums = tuple((jnp.zeros(array_in.shape, jnp.float32) for array_in in weights))
    running, (results, grad_inputs) = lax.scan(scan_step, zero_sums, (inputs, cotangents))
    return (results.reshape(-1, D).astype(jnp.bfloat16), grad_inputs.reshape(-1, D), running[0], running[1], running[2], running[3], running[4], running[5], running[6], running[7], running[8])
```

```python
import functools

import jax
import jax.numpy as jnp
from jax import lax
from jax.experimental import pallas as pl
from jax.experimental.pallas import tpu as pltpu
from jax.sharding import PartitionSpec as P

HEAD_DIM = 64
SEQLEN = 1024
MESH = pl.DeviceIdType.MESH
ANY = pl.BlockSpec(memory_space=pl.ANY)
VMEM = pl.BlockSpec(memory_space=pltpu.VMEM)
VMEM_LIMIT = 56 * 2**20

epsilon = 1e-05
theta_base = 10000.0


def product(left, right):
    return jnp.dot(left, right, preferred_element_type=jnp.float32)


def product_left(left, right):
    return lax.dot_general(
        left, right, (((0,), (0,)), ((), ())), preferred_element_type=jnp.float32
    )


def product_right(left, right):
    return lax.dot_general(
        left, right, (((1,), (1,)), ((), ())), preferred_element_type=jnp.float32
    )


def norm_back(grad_normed, unit_rows, scale_rows, gain):
    scaled_grad = grad_normed * gain
    return scale_rows * (
        scaled_grad - unit_rows * jnp.mean(scaled_grad * unit_rows, axis=-1, keepdims=True)
    )


def flip(index, bit):
    size = 1 << bit
    return index + size * (1 - 2 * lax.rem(lax.div(index, size), 2))


def masked(index, bits, rank):
    for place, bit in enumerate(bits):
        if rank >> place & 1:
            index = flip(index, bit)
    return index


def orders(bit_count, core_last):
    up = list(range(1, bit_count))
    down = up[::-1]
    return [up + [0], down + [0]] if core_last else [[0] + up, [0] + down]


def greet(spots, near, all_tensor, dp_bits):
    dp, tensor, tensor_size = spots
    barrier = pltpu.get_barrier_semaphore()

    def signal(where):
        pl.semaphore_signal(barrier, inc=1, device_id=where, device_id_type=MESH)

    peers = dp_bits
    for bit in range(dp_bits):
        signal((flip(dp, bit), tensor))
    if all_tensor:
        peers += tensor_size - 1
        for other in range(tensor_size):
            pl.when(other != tensor)(functools.partial(signal, (dp, other)))
    elif near:
        below, above = tensor > 0, tensor + 1 < tensor_size
        pl.when(below)(functools.partial(signal, (dp, tensor - 1)))
        pl.when(above)(functools.partial(signal, (dp, tensor + 1)))
        peers = peers + below.astype(jnp.int32) + above.astype(jnp.int32)
    pl.semaphore_wait(barrier, peers)


class Gather:
    def __init__(self, shape, slot, half=None):
        self.shape, self.slot, self.half = shape, slot, half


def gather_kernel(specs, dp_size, tensor_size, *refs):
    count = len(specs)
    sources, outs = refs[:count], refs[count : 2 * count]
    own_sem, z_send, z_recv, h_send, h_recv = refs[2 * count :]
    dp, tensor = lax.axis_index("dp"), lax.axis_index("tensor")
    dp_bits = dp_size.bit_length() - 1
    hyper = [i for i in range(count) if specs[i].half is not None]
    greet((dp, tensor, tensor_size), True, False, dp_bits if hyper else 0)

    def z_copy(i, block, way, source=None):
        slot = specs[i].slot(outs[i], dp, block)
        return pltpu.make_async_remote_copy(
            src_ref=slot if source is None else source,
            dst_ref=slot,
            send_sem=z_send.at[i, way, block],
            recv_sem=z_recv.at[i, block],
            device_id=(dp, tensor + 1 if way == 0 else tensor - 1),
            device_id_type=MESH,
        )

    can = [tensor + 1 < tensor_size, tensor > 0]
    for i in range(count):
        for way in (0, 1):

            @pl.when(can[way])
            def _():
                z_copy(i, tensor, way, sources[i]).start()

    owns = [
        pltpu.make_async_copy(sources[i], specs[i].slot(outs[i], dp, tensor), own_sem.at[i])
        for i in range(count)
    ]
    for own in owns:
        own.start()
    for step in range(1, tensor_size):
        for i in range(count):
            for way, block in ((0, tensor - step), (1, tensor + step)):

                @pl.when((block >= 0) & (block < tensor_size))
                def _():
                    z_copy(i, block, way).wait_recv()

                    @pl.when(can[way])
                    def _():
                        z_copy(i, block, way).start()

    for own in owns:
        own.wait()

    order = orders(dp_bits, True)

    def h_copy(n, half, rank, place):
        spec, out = specs[hyper[n]], outs[hyper[n]]
        bits = order[half]
        part = spec.half(out, masked(dp, bits, rank), half)
        return pltpu.make_async_remote_copy(
            src_ref=part,
            dst_ref=part,
            send_sem=h_send.at[n, half, rank, place],
            recv_sem=h_recv.at[n, half, rank | 1 << place],
            device_id=(flip(dp, bits[place]), tensor),
            device_id_type=MESH,
        )

    if hyper:
        for rank in range(1 << dp_bits):
            top = rank.bit_length()
            for n in range(len(hyper)):
                for half in (0, 1):
                    if rank:
                        wait_part(
                            specs[hyper[n]].half(
                                outs[hyper[n]], masked(dp, order[half], rank), half
                            ),
                            h_recv.at[n, half, rank],
                            h_send.at[n, half, 0, 0],
                            (flip(dp, 0), tensor),
                        )
                    for place in range(top, dp_bits):
                        h_copy(n, half, rank, place).start()
        for rank in range(1 << dp_bits):
            for n in range(len(hyper)):
                for half in (0, 1):
                    for place in range(rank.bit_length(), dp_bits):
                        h_copy(n, half, rank, place).wait_send()
    for i in range(count):
        for block in range(tensor_size):
            for way in (0, 1):
                sent = can[way] & ((block <= tensor) if way == 0 else (block >= tensor))

                @pl.when(sent)
                def _():
                    z_copy(i, block, way).wait_send()


def wait_part(part, recv_sem, send_sem, device):
    pltpu.make_async_remote_copy(
        src_ref=part,
        dst_ref=part,
        send_sem=send_sem,
        recv_sem=recv_sem,
        device_id=device,
        device_id_type=MESH,
    ).wait_recv()


def gather(specs, arrays, dp_size, tensor_size, collective_id):
    count = len(specs)
    hyper = max(1, sum(spec.half is not None for spec in specs))
    dp_bits = dp_size.bit_length() - 1
    return pl.pallas_call(
        functools.partial(gather_kernel, specs, dp_size, tensor_size),
        out_shape=[
            jax.ShapeDtypeStruct(spec.shape, array.dtype) for spec, array in zip(specs, arrays)
        ],
        in_specs=[ANY] * count,
        out_specs=[ANY] * count,
        scratch_shapes=[
            pltpu.SemaphoreType.DMA((count,)),
            pltpu.SemaphoreType.DMA((count, 2, tensor_size)),
            pltpu.SemaphoreType.DMA((count, tensor_size)),
            pltpu.SemaphoreType.DMA((hyper, 2, dp_size, max(dp_bits, 1))),
            pltpu.SemaphoreType.DMA((hyper, 2, dp_size)),
        ],
        compiler_params=pltpu.CompilerParams(
            collective_id=collective_id, has_side_effects=True
        ),
    )(*arrays)


def exchange_kernel(tensor_size, source, out, own_sem, send, recv):
    dp, tensor = lax.axis_index("dp"), lax.axis_index("tensor")
    greet((dp, tensor, tensor_size), False, True, 0)
    own = pltpu.make_async_copy(source.at[tensor], out.at[tensor], own_sem)

    def copy(other, slot):
        return pltpu.make_async_remote_copy(
            src_ref=source.at[other],
            dst_ref=out.at[slot],
            send_sem=send.at[other],
            recv_sem=recv.at[slot],
            device_id=(dp, other),
            device_id_type=MESH,
        )

    for other in range(tensor_size):

        @pl.when(other != tensor)
        def _():
            copy(other, tensor).start()

    own.start()
    own.wait()
    for other in range(tensor_size):

        @pl.when(other != tensor)
        def _():
            copy(other, tensor).wait_send()
            copy(other, other).wait_recv()


def exchange(blocks, tensor_size, collective_id):
    return pl.pallas_call(
        functools.partial(exchange_kernel, tensor_size),
        out_shape=jax.ShapeDtypeStruct(blocks.shape, blocks.dtype),
        in_specs=[ANY],
        out_specs=ANY,
        scratch_shapes=[
            pltpu.SemaphoreType.DMA,
            pltpu.SemaphoreType.DMA((tensor_size,)),
            pltpu.SemaphoreType.DMA((tensor_size,)),
        ],
        compiler_params=pltpu.CompilerParams(
            collective_id=collective_id, has_side_effects=True
        ),
    )(blocks)


class Scatter:
    def __init__(self, shape, part, part_shape, place, cut=None, cut_shape=None):
        self.shape, self.part, self.part_shape, self.place = shape, part, part_shape, place
        self.cut, self.cut_shape = cut, cut_shape


def add_into(total, extra):
    shape = total.shape
    rows = shape[-2]
    slab = min(16, rows)
    if len(shape) == 2:

        def body(step, carry):
            at = pl.ds(pl.multiple_of(step * slab, slab), slab)
            total[at, :] = (
                total[at, :].astype(jnp.float32) + extra[at, :].astype(jnp.float32)
            ).astype(total.dtype)
            return carry

        lax.fori_loop(0, rows // slab, body, 0, unroll=2 if (rows // slab) % 2 == 0 else 1)
    else:
        for lead in range(shape[0]):
            add_into(total.at[lead], extra.at[lead])


def scatter_kernel(specs, dp_size, tensor_size, *refs):
    count = len(specs)
    refs = list(refs)
    sources = [refs.pop(0) for _ in specs]
    outs = [refs.pop(0) for _ in specs]
    dp_bits = dp_size.bit_length() - 1
    total = [refs.pop(0) for _ in specs]
    landing = [[refs.pop(0) for _ in range(dp_bits)] for _ in specs]
    shares = [refs.pop(0) if spec.cut is not None else None for spec in specs]
    own_sem, send, recv, z_send, z_recv = refs
    dp, tensor = lax.axis_index("dp"), lax.axis_index("tensor")
    cuts = any(spec.cut is not None for spec in specs)
    greet((dp, tensor, tensor_size), False, cuts, dp_bits)
    order = orders(dp_bits, False)

    def own_copy(i, half, slot):
        return pltpu.make_async_copy(
            specs[i].part(sources[i], masked(dp, order[half], 2 * slot), half),
            total[i].at[half, slot],
            own_sem.at[i, half, slot],
        )

    def copy(i, half, stage, slot):
        if stage == 0:
            source = specs[i].part(sources[i], masked(dp, order[half], 2 * slot + 1), half)
        else:
            source = total[i].at[half, (2 * slot + 1) << (stage - 1)]
        return pltpu.make_async_remote_copy(
            src_ref=source,
            dst_ref=landing[i][stage].at[half, slot],
            send_sem=send.at[i, half, stage, slot],
            recv_sem=recv.at[i, half, stage, slot],
            device_id=(flip(dp, order[half][stage]), tensor),
            device_id_type=MESH,
        )

    def slots(stage):
        return range(1 << (dp_bits - 1 - stage))

    for i in range(count):
        for slot in slots(0):
            for half in (0, 1):
                copy(i, half, 0, slot).start()
                own_copy(i, half, slot).start()
    for stage in range(dp_bits):
        for i in range(count):
            for slot in sorted(slots(stage), key=lambda s: -(s & 1)):
                for half in (0, 1):
                    if stage == 0:
                        own_copy(i, half, slot).wait()
                    copy(i, half, stage, slot).wait_recv()
                    add_into(total[i].at[half, slot << stage], landing[i][stage].at[half, slot])
                    if slot & 1:
                        copy(i, half, stage + 1, slot >> 1).start()

    def z_copy(i, half, other, slot):
        return pltpu.make_async_remote_copy(
            src_ref=specs[i].cut(total[i].at[half, 0], other),
            dst_ref=shares[i].at[slot, half],
            send_sem=z_send.at[i, half, other],
            recv_sem=z_recv.at[i, half, slot],
            device_id=(dp, other),
            device_id_type=MESH,
        )

    for i in range(count):
        for half in (0, 1):
            if specs[i].cut is None:
                specs[i].place(outs[i], half)[...] = total[i][half, 0].astype(jnp.float32)
            else:
                for other in range(tensor_size):

                    @pl.when(other != tensor)
                    def _():
                        z_copy(i, half, other, tensor).start()

                    @pl.when(other == tensor)
                    def _():
                        shares[i][other, half] = specs[i].cut(total[i].at[half, 0], other)[...]

    for i in range(count):
        if specs[i].cut is None:
            continue
        for half in (0, 1):
            for other in range(tensor_size):

                @pl.when(other != tensor)
                def _():
                    z_copy(i, half, other, other).wait_recv()

            summed = shares[i][0, half].astype(jnp.float32)
            for other in range(1, tensor_size):
                summed = summed + shares[i][other, half].astype(jnp.float32)
            specs[i].place(outs[i], half)[...] = summed
    for i in range(count):
        for half in (0, 1):
            for stage in range(dp_bits):
                for slot in slots(stage):
                    copy(i, half, stage, slot).wait_send()
            if specs[i].cut is not None:
                for other in range(tensor_size):

                    @pl.when(other != tensor)
                    def _():
                        z_copy(i, half, other, tensor).wait_send()


def scatter(specs, arrays, dp_size, tensor_size, collective_id):
    count = len(specs)
    dp_bits = dp_size.bit_length() - 1
    scratch = []
    for spec, array in zip(specs, arrays):
        scratch.append(pltpu.VMEM((2, dp_size // 2) + spec.part_shape, array.dtype))
    for spec, array in zip(specs, arrays):
        for stage in range(dp_bits):
            scratch.append(pltpu.VMEM((2, dp_size >> (stage + 1)) + spec.part_shape, array.dtype))
    for spec, array in zip(specs, arrays):
        if spec.cut is not None:
            scratch.append(pltpu.VMEM((tensor_size, 2) + spec.cut_shape, array.dtype))
    return pl.pallas_call(
        functools.partial(scatter_kernel, specs, dp_size, tensor_size),
        out_shape=[jax.ShapeDtypeStruct(spec.shape, jnp.float32) for spec in specs],
        in_specs=[ANY] * count,
        out_specs=[VMEM] * count,
        scratch_shapes=scratch
        + [
            pltpu.SemaphoreType.DMA((count, 2, dp_size // 2)),
            pltpu.SemaphoreType.DMA((count, 2, dp_bits, dp_size // 2)),
            pltpu.SemaphoreType.DMA((count, 2, dp_bits, dp_size // 2)),
            pltpu.SemaphoreType.DMA((count, 2, tensor_size)),
            pltpu.SemaphoreType.DMA((count, 2, tensor_size)),
        ],
        compiler_params=pltpu.CompilerParams(
            collective_id=collective_id, has_side_effects=True, vmem_limit_bytes=VMEM_LIMIT
        ),
    )(*arrays)


def lanes_of(shape):
    return lax.broadcasted_iota(jnp.int32, shape, len(shape) - 1)


def swap_halves(values):
    width = values.shape[-1]
    first = lanes_of(values.shape) % HEAD_DIM < HEAD_DIM // 2
    return jnp.where(
        first,
        pltpu.roll(values, width - HEAD_DIM // 2, 1),
        pltpu.roll(values, HEAD_DIM // 2, 1),
    )


def left_head(block, odd):
    moved = jnp.where(odd, pltpu.roll(block, HEAD_DIM, 1), block)
    return jnp.where(lanes_of(block.shape) < HEAD_DIM, moved, jnp.zeros_like(moved))


def allowed(keys, rows, start):
    key_at = lax.broadcasted_iota(jnp.int32, (keys, rows), 0)
    query_at = lax.broadcasted_iota(jnp.int32, (keys, rows), 1) + start
    return key_at <= query_at


def attend_kernel(
    group_pairs, q_ref, cos_ref, sin_ref, k_ref, v_ref, o_ref, q_out, lse_ref, k_left, v_turned
):
    pair = pl.program_id(0)
    group = pair // group_pairs
    rows = q_ref.shape[0]
    start = lax.axis_index("tensor") * rows

    @pl.when(pair % group_pairs == 0)
    def _():
        odd = group % 2 == 1
        k_left[...] = left_head(k_ref[...].astype(jnp.float32), odd).astype(jnp.bfloat16)
        v_turned[...] = left_head(v_ref[...].astype(jnp.float32), odd).T[:HEAD_DIM].astype(
            jnp.bfloat16
        )

    raw = q_ref[...]
    turned = (raw * cos_ref[...] + swap_halves(raw) * sin_ref[...]).astype(jnp.bfloat16)
    turned = turned.astype(jnp.float32) * HEAD_DIM ** (-0.5)
    q_out[...] = turned.astype(jnp.bfloat16)
    open_at = allowed(k_left.shape[0], rows, start)
    contexts = []
    for head in (0, 1):
        queries = (turned if head == 0 else pltpu.roll(turned, HEAD_DIM, 1)).astype(jnp.bfloat16)
        scores = product_right(k_left[...], queries)
        scores = jnp.where(open_at, scores, -1e30)
        top = jnp.max(scores, axis=0, keepdims=True)
        exponent = jnp.exp(scores - top)
        summed = jnp.sum(exponent, axis=0, keepdims=True)
        context = product(v_turned[...], exponent.astype(jnp.bfloat16))
        contexts.append(context * (1.0 / summed))
        lse_ref[0, head, :] = (top + jnp.log(summed))[0]
    o_ref[...] = jnp.concatenate(contexts, axis=0).T.astype(jnp.bfloat16)


def attend(q_pre, cosines, sines, keys_values, head_count, group_heads):
    rows, width = q_pre.shape
    length, both = keys_values.shape
    pairs, group_pairs = head_count // 2, group_heads // 2
    kv_blocks = both // 256
    wide = pl.BlockSpec((rows, 128), lambda p: (0, p))
    table = pl.BlockSpec((rows, 128), lambda p: (0, 0))
    return pl.pallas_call(
        functools.partial(attend_kernel, group_pairs),
        grid=(pairs,),
        out_shape=[
            jax.ShapeDtypeStruct((rows, width), jnp.bfloat16),
            jax.ShapeDtypeStruct((rows, width), jnp.bfloat16),
            jax.ShapeDtypeStruct((pairs, 2, rows), jnp.float32),
        ],
        in_specs=[
            wide,
            table,
            table,
            pl.BlockSpec((length, 128), lambda p: (0, p // group_pairs // 2)),
            pl.BlockSpec((length, 128), lambda p: (0, kv_blocks + p // group_pairs // 2)),
        ],
        out_specs=[wide, wide, pl.BlockSpec((1, 2, rows), lambda p: (p, 0, 0))],
        scratch_shapes=[
            pltpu.VMEM((length, 128), jnp.bfloat16),
            pltpu.VMEM((HEAD_DIM, length), jnp.bfloat16),
        ],
        compiler_params=pltpu.CompilerParams(vmem_limit_bytes=VMEM_LIMIT),
        cost_estimate=pl.CostEstimate(
            flops=4 * rows * length * width, bytes_accessed=8 * rows * width, transcendentals=0
        ),
    )(q_pre, cosines, sines, keys_values, keys_values)


def attend_back_kernel(
    group_pairs,
    q_ref,
    do_ref,
    lse_ref,
    cos_ref,
    sin_ref,
    k_ref,
    v_ref,
    dq_ref,
    dk_ref,
    dv_ref,
    k_left,
    v_left,
    k_turned,
    dk_sum,
    dv_sum,
):
    pair = pl.program_id(0)
    group = pair // group_pairs
    odd = group % 2 == 1
    rows = q_ref.shape[0]
    start = lax.axis_index("tensor") * rows

    @pl.when(pair % group_pairs == 0)
    def _():
        left = left_head(k_ref[...].astype(jnp.float32), odd)
        k_left[...] = left.astype(jnp.bfloat16)
        k_turned[...] = left.T[:HEAD_DIM].astype(jnp.bfloat16)
        v_left[...] = left_head(v_ref[...].astype(jnp.float32), odd).astype(jnp.bfloat16)
        dk_sum[...] = jnp.zeros_like(dk_sum)
        dv_sum[...] = jnp.zeros_like(dv_sum)

    open_at = allowed(k_left.shape[0], rows, start)
    grads = []
    for head in (0, 1):
        queries, grad_out = q_ref[...], do_ref[...]
        if head == 1:
            queries = pltpu.roll(queries.astype(jnp.float32), HEAD_DIM, 1).astype(jnp.bfloat16)
            grad_out = pltpu.roll(grad_out.astype(jnp.float32), HEAD_DIM, 1).astype(jnp.bfloat16)
        scores = product_right(k_left[...], queries)
        scores = jnp.where(open_at, scores, -1e30)
        softmaxed = jnp.exp(scores - lse_ref[0, head, :][None, :])
        grad_soft = product_right(v_left[...], grad_out)
        mixed = softmaxed * grad_soft
        mixed_sum = jnp.sum(mixed, axis=0, keepdims=True)
        grad_scores = (mixed - softmaxed * mixed_sum).astype(jnp.bfloat16)
        dv_sum[...] += product(softmaxed.astype(jnp.bfloat16), grad_out)
        dk_sum[...] += product(grad_scores, queries)
        grads.append(product(k_turned[...], grad_scores))
    grad_q = jnp.concatenate(grads, axis=0).T * HEAD_DIM ** (-0.5)
    dq_ref[...] = (grad_q * cos_ref[...] - swap_halves(grad_q) * sin_ref[...]).astype(jnp.bfloat16)

    @pl.when(pair % group_pairs == group_pairs - 1)
    def _():
        for total, out in ((dk_sum, dk_ref), (dv_sum, dv_ref)):
            value = total[...]
            left = lanes_of(value.shape) < HEAD_DIM

            @pl.when(jnp.logical_not(odd))
            def _():
                out[...] = jnp.where(left, value, 0.0).astype(out.dtype)

            @pl.when(odd)
            def _():
                out[...] = jnp.where(
                    left, out[...].astype(jnp.float32), pltpu.roll(value, HEAD_DIM, 1)
                ).astype(out.dtype)


def attend_back(queries, grad_context, lse, cosines, sines, keys_values, head_count, group_heads):
    rows, width = queries.shape
    length, both = keys_values.shape
    pairs, group_pairs = head_count // 2, group_heads // 2
    kv_blocks = both // 256
    wide = pl.BlockSpec((rows, 128), lambda p: (0, p))
    table = pl.BlockSpec((rows, 128), lambda p: (0, 0))
    kv_out = pl.BlockSpec((length, 128), lambda p: (0, p // group_pairs // 2))
    return pl.pallas_call(
        functools.partial(attend_back_kernel, group_pairs),
        grid=(pairs,),
        out_shape=[
            jax.ShapeDtypeStruct((rows, width), jnp.bfloat16),
            jax.ShapeDtypeStruct((length, both // 2), jnp.bfloat16),
            jax.ShapeDtypeStruct((length, both // 2), jnp.bfloat16),
        ],
        in_specs=[
            wide,
            wide,
            pl.BlockSpec((1, 2, rows), lambda p: (p, 0, 0)),
            table,
            table,
            pl.BlockSpec((length, 128), lambda p: (0, p // group_pairs // 2)),
            pl.BlockSpec((length, 128), lambda p: (0, kv_blocks + p // group_pairs // 2)),
        ],
        out_specs=[wide, kv_out, kv_out],
        scratch_shapes=[
            pltpu.VMEM((length, 128), jnp.bfloat16),
            pltpu.VMEM((length, 128), jnp.bfloat16),
            pltpu.VMEM((HEAD_DIM, length), jnp.bfloat16),
            pltpu.VMEM((length, 128), jnp.float32),
            pltpu.VMEM((length, 128), jnp.float32),
        ],
        compiler_params=pltpu.CompilerParams(vmem_limit_bytes=VMEM_LIMIT),
        cost_estimate=pl.CostEstimate(
            flops=10 * rows * length * width, bytes_accessed=8 * rows * width, transcendentals=0
        ),
    )(queries, grad_context, lse, cosines, sines, keys_values, keys_values)


def rope_tables(rows, tensor):
    halved = HEAD_DIM // 2
    freqs = theta_base ** (-2.0 * jnp.arange(halved, dtype=jnp.float32) / HEAD_DIM)
    places = (tensor * rows + jnp.arange(rows)).astype(jnp.float32)
    angles = places[:, None] * freqs[None, :]
    cosines, sines = jnp.cos(angles), jnp.sin(angles)
    return (
        jnp.concatenate([cosines, cosines] * 2, axis=1),
        jnp.concatenate([-sines, sines] * 2, axis=1),
    )


def turn_heads(values, cosines, sines):
    rows, width = values.shape
    parts = values.reshape(rows, width // HEAD_DIM, 2, HEAD_DIM // 2)
    swapped = parts[:, :, ::-1, :].reshape(rows, width)
    repeat = width // 128
    return values * jnp.tile(cosines, (1, repeat)) + swapped * jnp.tile(sines, (1, repeat))


def start_row(dp, size):
    return pl.multiple_of(dp * size, size)


def on_device(
    dp_size,
    tensor_size,
    tokens,
    attn_gain,
    w_query,
    w_key,
    w_value,
    w_out,
    mlp_gain,
    w_gate,
    w_up,
    w_down,
    cotangent,
):
    tensor_index = lax.axis_index("tensor")
    rows, width = tokens.shape
    heads = w_query.shape[1] * tensor_size // HEAD_DIM
    kv_width = w_key.shape[1]
    kv_heads = kv_width // HEAD_DIM
    group_heads = heads // kv_heads
    q_rows, q_cols = w_query.shape
    kv_rows = w_key.shape[0]
    o_rows, o_cols = w_out.shape
    gain_part = attn_gain.shape[0]
    call = functools.partial(gather, dp_size=dp_size, tensor_size=tensor_size)

    key_value = jnp.concatenate([w_key, w_value], axis=1)
    gains = jnp.zeros((16, 128), jnp.bfloat16)
    gains = gains.at[0, :gain_part].set(attn_gain).at[1, :gain_part].set(mlp_gain)
    gate_full, up_full, down_full = (
        lax.all_gather(w_gate, "dp", axis=0, tiled=True),
        lax.all_gather(w_up, "dp", axis=0, tiled=True),
        lax.all_gather(w_down, "dp", axis=1, tiled=True),
    )
    cot_all = lax.all_gather(cotangent, "tensor", axis=0, tiled=True)
    query_spec = Gather(
        (width, heads * HEAD_DIM),
        lambda ref, dp, t: ref.at[
            pl.ds(start_row(dp, q_rows), q_rows), pl.ds(start_row(t, q_cols), q_cols)
        ],
        lambda ref, dp, half: ref.at[
            pl.ds(pl.multiple_of(dp * q_rows + half * (q_rows // 2), q_rows // 2), q_rows // 2), :
        ],
    )
    kv_all_rows = kv_rows * tensor_size
    kv_spec = Gather(
        (width, 2 * kv_width),
        lambda ref, dp, t: ref.at[pl.ds(start_row(dp * tensor_size + t, kv_rows), kv_rows), :],
        lambda ref, dp, half: ref.at[
            pl.ds(
                pl.multiple_of(dp * kv_all_rows + half * (kv_all_rows // 2), kv_all_rows // 2),
                kv_all_rows // 2,
            ),
            :,
        ],
    )
    gain_spec = Gather(
        (dp_size * tensor_size * 16, 128),
        lambda ref, dp, t: ref.at[pl.ds(start_row(dp * tensor_size + t, 16), 16), :],
        lambda ref, dp, half: ref.at[
            pl.ds(
                pl.multiple_of((2 * dp + half) * tensor_size * 8, tensor_size * 8),
                tensor_size * 8,
            ),
            :,
        ],
    )
    out_spec = Gather(
        (heads * HEAD_DIM, width),
        lambda ref, dp, t: ref.at[
            pl.ds(start_row(t, o_rows), o_rows), pl.ds(start_row(dp, o_cols), o_cols)
        ],
        lambda ref, dp, half: ref.at[
            pl.ds(half * (heads * HEAD_DIM // 2), heads * HEAD_DIM // 2),
            pl.ds(start_row(dp, o_cols), o_cols),
        ],
    )
    row_spec = lambda shape: Gather(
        (tensor_size * shape[0], shape[1]),
        lambda ref, dp, t: ref.at[pl.ds(start_row(t, shape[0]), shape[0]), :],
    )
    query_full, key_value_full, gains_full = call(
        [query_spec, kv_spec, gain_spec], [w_query, key_value, gains], collective_id=1
    )
    gains_full = gains_full.reshape(-1, 16, 128)[:, :2, :gain_part].astype(jnp.float32)
    gain_first = gains_full[:, 0].reshape(width)
    gain_second = gains_full[:, 1].reshape(width)
    cosines, sines = rope_tables(rows, tensor_index)

    residual = tokens.astype(jnp.float32)
    scale_first = lax.rsqrt(jnp.mean(residual * residual, axis=-1, keepdims=True) + epsilon)
    unit_first = residual * scale_first
    normed_first = (unit_first * gain_first).astype(jnp.bfloat16)
    kv_pre = product(normed_first, key_value_full)
    kv_own = jnp.concatenate(
        [turn_heads(kv_pre[:, :kv_width], cosines, sines), kv_pre[:, kv_width:]], axis=1
    ).astype(jnp.bfloat16)
    query_pre = product(normed_first, query_full)
    kv_all, out_full = call([row_spec(kv_own.shape), out_spec], [kv_own, w_out], collective_id=2)
    context, queries, log_sums = attend(
        query_pre, cosines, sines, kv_all, heads, group_heads
    )
    middle = residual + product(context, out_full)
    scale_second = lax.rsqrt(jnp.mean(middle * middle, axis=-1, keepdims=True) + epsilon)
    unit_second = middle * scale_second
    normed_own = (unit_second * gain_second).astype(jnp.bfloat16)
    (normed_second,) = call([row_spec(normed_own.shape)], [normed_own], collective_id=3)

    gate_pre = product(normed_second, gate_full)
    upward = product(normed_second, up_full)
    sigmoid_gate = jax.nn.sigmoid(gate_pre)
    silu_gate = gate_pre * sigmoid_gate
    hidden = (silu_gate * upward).astype(jnp.bfloat16)
    mlp_rows = lax.psum_scatter(
        product(hidden, down_full).astype(jnp.bfloat16), "tensor", scatter_dimension=0, tiled=True
    ).astype(jnp.float32)
    output = (middle + mlp_rows).astype(jnp.bfloat16)
    grad_hidden = product_right(cot_all, down_full)
    grad_gate_pre = (
        grad_hidden * upward * sigmoid_gate * (1.0 + gate_pre * (1.0 - sigmoid_gate))
    ).astype(jnp.bfloat16)
    grad_upward = (grad_hidden * silu_gate).astype(jnp.bfloat16)
    back_part = (
        product_right(grad_gate_pre, gate_full) + product_right(grad_upward, up_full)
    ).astype(jnp.bfloat16)
    back_blocks = exchange(back_part.reshape(tensor_size, rows, width), tensor_size, 4)
    back_second = jnp.sum(back_blocks.astype(jnp.float32), axis=0)
    grad_down_w = product_left(hidden, cot_all).astype(jnp.bfloat16)
    grad_gate_w = product_left(normed_second, grad_gate_pre).astype(jnp.bfloat16)
    grad_up_w = product_left(normed_second, grad_upward).astype(jnp.bfloat16)
    sum_gate, sum_up, sum_down = (
        lax.psum_scatter(grad_gate_w, "dp", scatter_dimension=0, tiled=True).astype(jnp.float32),
        lax.psum_scatter(grad_up_w, "dp", scatter_dimension=0, tiled=True).astype(jnp.float32),
        lax.psum_scatter(grad_down_w, "dp", scatter_dimension=1, tiled=True).astype(jnp.float32),
    )

    grad_gain_second = jnp.sum(back_second * unit_second, axis=0)
    grad_middle = cotangent.astype(jnp.float32) + norm_back(
        back_second, unit_second, scale_second, gain_second
    )
    middle_low = grad_middle.astype(jnp.bfloat16)
    grad_context = product_right(middle_low, out_full).astype(jnp.bfloat16)
    grad_out_w = product_left(context, middle_low).astype(jnp.bfloat16)
    grad_queries, grad_keys, grad_values = attend_back(
        queries, grad_context, log_sums, cosines, sines, kv_all, heads, group_heads
    )
    grad_kv = jnp.concatenate([grad_keys, grad_values], axis=1)
    kv_blocks = exchange(grad_kv.reshape(tensor_size, rows, 2 * kv_width), tensor_size, 5)
    grad_kv_own = jnp.sum(kv_blocks.astype(jnp.float32), axis=0)
    grad_kv_own = jnp.concatenate(
        [turn_heads(grad_kv_own[:, :kv_width], cosines, -sines), grad_kv_own[:, kv_width:]], axis=1
    ).astype(jnp.bfloat16)
    grad_query_w = product_left(normed_first, grad_queries).astype(jnp.bfloat16)
    grad_kv_w = product_left(normed_first, grad_kv_own).astype(jnp.bfloat16)
    back_first = product_right(grad_queries, query_full) + product_right(
        grad_kv_own, key_value_full
    )
    grad_gain_first = jnp.sum(back_first * unit_first, axis=0)
    grad_tokens = grad_middle + norm_back(back_first, unit_first, scale_first, gain_first)

    grad_gains = jnp.zeros((dp_size * tensor_size, 16, 128), jnp.float32)
    grad_gains = grad_gains.at[:, 0, :gain_part].set(grad_gain_first.reshape(-1, gain_part))
    grad_gains = grad_gains.at[:, 8, :gain_part].set(grad_gain_second.reshape(-1, gain_part))
    query_scatter = Scatter(
        (q_rows, q_cols),
        query_spec.half,
        (q_rows // 2, tensor_size * q_cols),
        lambda ref, half: ref.at[pl.ds(half * (q_rows // 2), q_rows // 2), :],
        lambda ref, j: ref.at[:, pl.ds(j * q_cols, q_cols)],
        (q_rows // 2, q_cols),
    )
    kv_scatter = Scatter(
        (kv_rows, 2 * kv_width),
        lambda ref, dp, half: ref.at[
            pl.ds(dp * tensor_size, tensor_size), :, pl.ds(half * kv_width, kv_width)
        ],
        (tensor_size, kv_rows, kv_width),
        lambda ref, half: ref.at[:, pl.ds(half * kv_width, kv_width)],
        lambda ref, j: ref.at[j],
        (kv_rows, kv_width),
    )
    out_scatter = Scatter(
        (o_rows, o_cols),
        lambda ref, dp, half: ref.at[
            :, pl.ds(half * (o_rows // 2), o_rows // 2), pl.ds(start_row(dp, o_cols), o_cols)
        ],
        (tensor_size, o_rows // 2, o_cols),
        lambda ref, half: ref.at[pl.ds(half * (o_rows // 2), o_rows // 2), :],
        lambda ref, j: ref.at[j],
        (o_rows // 2, o_cols),
    )
    gain_scatter = Scatter(
        (16, 128),
        lambda ref, dp, half: ref.at[
            pl.ds(dp * tensor_size, tensor_size), pl.ds(half * 8, 8), :
        ],
        (tensor_size, 8, 128),
        lambda ref, half: ref.at[pl.ds(half * 8, 8), :],
        lambda ref, j: ref.at[j],
        (8, 128),
    )
    sum_out, sum_query, sum_kv, sum_gains = scatter(
        [out_scatter, query_scatter, kv_scatter, gain_scatter],
        [
            grad_out_w.reshape(tensor_size, o_rows, width),
            grad_query_w,
            grad_kv_w.reshape(dp_size * tensor_size, kv_rows, 2 * kv_width),
            grad_gains,
        ],
        dp_size,
        tensor_size,
        6,
    )
    return (
        output,
        grad_tokens,
        sum_gains[0, :gain_part],
        sum_query,
        sum_kv[:, :kv_width],
        sum_kv[:, kv_width:],
        sum_out,
        sum_gains[8, :gain_part],
        sum_gate,
        sum_up,
        sum_down,
    )


def solution(mesh):
    placed = (
        P(("dp", "tensor"), None),
        P(("dp", "tensor")),
        P("dp", "tensor"),
        P(("dp", "tensor"), None),
        P(("dp", "tensor"), None),
        P("tensor", "dp"),
        P(("dp", "tensor")),
        P("dp", "tensor"),
        P("dp", "tensor"),
        P("tensor", "dp"),
        P(("dp", "tensor"), None),
    )
    return jax.shard_map(
        functools.partial(on_device, mesh.shape["dp"], mesh.shape["tensor"]),
        mesh=mesh,
        in_specs=placed,
        out_specs=(
            P(("dp", "tensor"), None),
            P(("dp", "tensor"), None),
            P(("dp", "tensor")),
            P("dp", "tensor"),
            P(("dp", "tensor"), None),
            P(("dp", "tensor"), None),
            P("tensor", "dp"),
            P(("dp", "tensor")),
            P("dp", "tensor"),
            P("dp", "tensor"),
            P("tensor", "dp"),
        ),
        check_vma=False,
    )
```

```python
import functools

import jax
import jax.numpy as jnp
from jax import lax
from jax.experimental import pallas as pl
from jax.experimental.pallas import tpu as pltpu
from jax.sharding import PartitionSpec as P

HEAD_DIM = 64
SEQLEN = 1024
MESH = pl.DeviceIdType.MESH
ANY = pl.BlockSpec(memory_space=pl.ANY)
VMEM = pl.BlockSpec(memory_space=pltpu.VMEM)
VMEM_LIMIT = 56 * 2**20

epsilon = 1e-05
theta_base = 10000.0


def product(left, right):
    return jnp.dot(left, right, preferred_element_type=jnp.float32)


def product_left(left, right):
    return lax.dot_general(
        left, right, (((0,), (0,)), ((), ())), preferred_element_type=jnp.float32
    )


def product_right(left, right):
    return lax.dot_general(
        left, right, (((1,), (1,)), ((), ())), preferred_element_type=jnp.float32
    )


def norm_back(grad_normed, unit_rows, scale_rows, gain):
    scaled_grad = grad_normed * gain
    return scale_rows * (
        scaled_grad - unit_rows * jnp.mean(scaled_grad * unit_rows, axis=-1, keepdims=True)
    )


def flip(index, bit):
    size = 1 << bit
    return index + size * (1 - 2 * lax.rem(lax.div(index, size), 2))


def masked(index, bits, rank):
    for place, bit in enumerate(bits):
        if rank >> place & 1:
            index = flip(index, bit)
    return index


def orders(bit_count, core_last):
    up = list(range(1, bit_count))
    down = up[::-1]
    return [up + [0], down + [0]] if core_last else [[0] + up, [0] + down]


def greet(spots, near, all_tensor, dp_bits):
    dp, tensor, tensor_size = spots
    barrier = pltpu.get_barrier_semaphore()

    def signal(where):
        pl.semaphore_signal(barrier, inc=1, device_id=where, device_id_type=MESH)

    peers = dp_bits
    for bit in range(dp_bits):
        signal((flip(dp, bit), tensor))
    if all_tensor:
        peers += tensor_size - 1
        for other in range(tensor_size):
            pl.when(other != tensor)(functools.partial(signal, (dp, other)))
    elif near:
        below, above = tensor > 0, tensor + 1 < tensor_size
        pl.when(below)(functools.partial(signal, (dp, tensor - 1)))
        pl.when(above)(functools.partial(signal, (dp, tensor + 1)))
        peers = peers + below.astype(jnp.int32) + above.astype(jnp.int32)
    pl.semaphore_wait(barrier, peers)


class Gather:
    def __init__(self, shape, slot, half=None):
        self.shape, self.slot, self.half = shape, slot, half


def gather_kernel(specs, dp_size, tensor_size, *refs):
    count = len(specs)
    sources, outs = refs[:count], refs[count : 2 * count]
    own_sem, z_send, z_recv, h_send, h_recv = refs[2 * count :]
    dp, tensor = lax.axis_index("dp"), lax.axis_index("tensor")
    dp_bits = dp_size.bit_length() - 1
    hyper = [i for i in range(count) if specs[i].half is not None]
    greet((dp, tensor, tensor_size), True, False, dp_bits if hyper else 0)

    def z_copy(i, block, way, source=None):
        slot = specs[i].slot(outs[i], dp, block)
        return pltpu.make_async_remote_copy(
            src_ref=slot if source is None else source,
            dst_ref=slot,
            send_sem=z_send.at[i, way, block],
            recv_sem=z_recv.at[i, block],
            device_id=(dp, tensor + 1 if way == 0 else tensor - 1),
            device_id_type=MESH,
        )

    can = [tensor + 1 < tensor_size, tensor > 0]
    for i in range(count):
        for way in (0, 1):

            @pl.when(can[way])
            def _():
                z_copy(i, tensor, way, sources[i]).start()

    owns = [
        pltpu.make_async_copy(sources[i], specs[i].slot(outs[i], dp, tensor), own_sem.at[i])
        for i in range(count)
    ]
    for own in owns:
        own.start()
    for step in range(1, tensor_size):
        for i in range(count):
            for way, block in ((0, tensor - step), (1, tensor + step)):

                @pl.when((block >= 0) & (block < tensor_size))
                def _():
                    z_copy(i, block, way).wait_recv()

                    @pl.when(can[way])
                    def _():
                        z_copy(i, block, way).start()

    for own in owns:
        own.wait()

    order = orders(dp_bits, True)

    def h_copy(n, half, rank, place):
        spec, out = specs[hyper[n]], outs[hyper[n]]
        bits = order[half]
        part = spec.half(out, masked(dp, bits, rank), half)
        return pltpu.make_async_remote_copy(
            src_ref=part,
            dst_ref=part,
            send_sem=h_send.at[n, half, rank, place],
            recv_sem=h_recv.at[n, half, rank | 1 << place],
            device_id=(flip(dp, bits[place]), tensor),
            device_id_type=MESH,
        )

    if hyper:
        for rank in range(1 << dp_bits):
            top = rank.bit_length()
            for n in range(len(hyper)):
                for half in (0, 1):
                    if rank:
                        wait_part(
                            specs[hyper[n]].half(
                                outs[hyper[n]], masked(dp, order[half], rank), half
                            ),
                            h_recv.at[n, half, rank],
                            h_send.at[n, half, 0, 0],
                            (flip(dp, 0), tensor),
                        )
                    for place in range(top, dp_bits):
                        h_copy(n, half, rank, place).start()
        for rank in range(1 << dp_bits):
            for n in range(len(hyper)):
                for half in (0, 1):
                    for place in range(rank.bit_length(), dp_bits):
                        h_copy(n, half, rank, place).wait_send()
    for i in range(count):
        for block in range(tensor_size):
            for way in (0, 1):
                sent = can[way] & ((block <= tensor) if way == 0 else (block >= tensor))

                @pl.when(sent)
                def _():
                    z_copy(i, block, way).wait_send()


def wait_part(part, recv_sem, send_sem, device):
    pltpu.make_async_remote_copy(
        src_ref=part,
        dst_ref=part,
        send_sem=send_sem,
        recv_sem=recv_sem,
        device_id=device,
        device_id_type=MESH,
    ).wait_recv()


def gather(specs, arrays, dp_size, tensor_size, collective_id):
    count = len(specs)
    hyper = max(1, sum(spec.half is not None for spec in specs))
    dp_bits = dp_size.bit_length() - 1
    return pl.pallas_call(
        functools.partial(gather_kernel, specs, dp_size, tensor_size),
        out_shape=[
            jax.ShapeDtypeStruct(spec.shape, array.dtype) for spec, array in zip(specs, arrays)
        ],
        in_specs=[ANY] * count,
        out_specs=[ANY] * count,
        scratch_shapes=[
            pltpu.SemaphoreType.DMA((count,)),
            pltpu.SemaphoreType.DMA((count, 2, tensor_size)),
            pltpu.SemaphoreType.DMA((count, tensor_size)),
            pltpu.SemaphoreType.DMA((hyper, 2, dp_size, max(dp_bits, 1))),
            pltpu.SemaphoreType.DMA((hyper, 2, dp_size)),
        ],
        compiler_params=pltpu.CompilerParams(
            collective_id=collective_id, has_side_effects=True
        ),
    )(*arrays)


def exchange_kernel(tensor_size, source, out, own_sem, send, recv):
    dp, tensor = lax.axis_index("dp"), lax.axis_index("tensor")
    greet((dp, tensor, tensor_size), False, True, 0)
    own = pltpu.make_async_copy(source.at[tensor], out.at[tensor], own_sem)

    def copy(other, slot):
        return pltpu.make_async_remote_copy(
            src_ref=source.at[other],
            dst_ref=out.at[slot],
            send_sem=send.at[other],
            recv_sem=recv.at[slot],
            device_id=(dp, other),
            device_id_type=MESH,
        )

    for other in range(tensor_size):

        @pl.when(other != tensor)
        def _():
            copy(other, tensor).start()

    own.start()
    own.wait()
    for other in range(tensor_size):

        @pl.when(other != tensor)
        def _():
            copy(other, tensor).wait_send()
            copy(other, other).wait_recv()


def exchange(blocks, tensor_size, collective_id):
    return pl.pallas_call(
        functools.partial(exchange_kernel, tensor_size),
        out_shape=jax.ShapeDtypeStruct(blocks.shape, blocks.dtype),
        in_specs=[ANY],
        out_specs=ANY,
        scratch_shapes=[
            pltpu.SemaphoreType.DMA,
            pltpu.SemaphoreType.DMA((tensor_size,)),
            pltpu.SemaphoreType.DMA((tensor_size,)),
        ],
        compiler_params=pltpu.CompilerParams(
            collective_id=collective_id, has_side_effects=True
        ),
    )(blocks)


class Scatter:
    def __init__(self, shape, part, part_shape, place, cut=None, cut_shape=None):
        self.shape, self.part, self.part_shape, self.place = shape, part, part_shape, place
        self.cut, self.cut_shape = cut, cut_shape


def add_into(total, extra):
    shape = total.shape
    rows = shape[-2]
    slab = min(16, rows)
    if len(shape) == 2:

        def body(step, carry):
            at = pl.ds(pl.multiple_of(step * slab, slab), slab)
            total[at, :] = (
                total[at, :].astype(jnp.float32) + extra[at, :].astype(jnp.float32)
            ).astype(total.dtype)
            return carry

        lax.fori_loop(0, rows // slab, body, 0, unroll=2 if (rows // slab) % 2 == 0 else 1)
    else:
        for lead in range(shape[0]):
            add_into(total.at[lead], extra.at[lead])


def scatter_kernel(specs, dp_size, tensor_size, *refs):
    count = len(specs)
    refs = list(refs)
    sources = [refs.pop(0) for _ in specs]
    outs = [refs.pop(0) for _ in specs]
    dp_bits = dp_size.bit_length() - 1
    total = [refs.pop(0) for _ in specs]
    landing = [[refs.pop(0) for _ in range(dp_bits)] for _ in specs]
    shares = [refs.pop(0) if spec.cut is not None else None for spec in specs]
    own_sem, send, recv, z_send, z_recv = refs
    dp, tensor = lax.axis_index("dp"), lax.axis_index("tensor")
    cuts = any(spec.cut is not None for spec in specs)
    greet((dp, tensor, tensor_size), False, cuts, dp_bits)
    order = orders(dp_bits, False)

    def own_copy(i, half, slot):
        return pltpu.make_async_copy(
            specs[i].part(sources[i], masked(dp, order[half], 2 * slot), half),
            total[i].at[half, slot],
            own_sem.at[i, half, slot],
        )

    def copy(i, half, stage, slot):
        if stage == 0:
            source = specs[i].part(sources[i], masked(dp, order[half], 2 * slot + 1), half)
        else:
            source = total[i].at[half, (2 * slot + 1) << (stage - 1)]
        return pltpu.make_async_remote_copy(
            src_ref=source,
            dst_ref=landing[i][stage].at[half, slot],
            send_sem=send.at[i, half, stage, slot],
            recv_sem=recv.at[i, half, stage, slot],
            device_id=(flip(dp, order[half][stage]), tensor),
            device_id_type=MESH,
        )

    def slots(stage):
        return range(1 << (dp_bits - 1 - stage))

    for i in range(count):
        for slot in slots(0):
            for half in (0, 1):
                copy(i, half, 0, slot).start()
                own_copy(i, half, slot).start()
    for stage in range(dp_bits):
        for i in range(count):
            for slot in sorted(slots(stage), key=lambda s: -(s & 1)):
                for half in (0, 1):
                    if stage == 0:
                        own_copy(i, half, slot).wait()
                    copy(i, half, stage, slot).wait_recv()
                    add_into(total[i].at[half, slot << stage], landing[i][stage].at[half, slot])
                    if slot & 1:
                        copy(i, half, stage + 1, slot >> 1).start()

    def z_copy(i, half, other, slot):
        return pltpu.make_async_remote_copy(
            src_ref=specs[i].cut(total[i].at[half, 0], other),
            dst_ref=shares[i].at[slot, half],
            send_sem=z_send.at[i, half, other],
            recv_sem=z_recv.at[i, half, slot],
            device_id=(dp, other),
            device_id_type=MESH,
        )

    for i in range(count):
        for half in (0, 1):
            if specs[i].cut is None:
                specs[i].place(outs[i], half)[...] = total[i][half, 0].astype(jnp.float32)
            else:
                for other in range(tensor_size):

                    @pl.when(other != tensor)
                    def _():
                        z_copy(i, half, other, tensor).start()

                    @pl.when(other == tensor)
                    def _():
                        shares[i][other, half] = specs[i].cut(total[i].at[half, 0], other)[...]

    for i in range(count):
        if specs[i].cut is None:
            continue
        for half in (0, 1):
            for other in range(tensor_size):

                @pl.when(other != tensor)
                def _():
                    z_copy(i, half, other, other).wait_recv()

            summed = shares[i][0, half].astype(jnp.float32)
            for other in range(1, tensor_size):
                summed = summed + shares[i][other, half].astype(jnp.float32)
            specs[i].place(outs[i], half)[...] = summed
    for i in range(count):
        for half in (0, 1):
            for stage in range(dp_bits):
                for slot in slots(stage):
                    copy(i, half, stage, slot).wait_send()
            if specs[i].cut is not None:
                for other in range(tensor_size):

                    @pl.when(other != tensor)
                    def _():
                        z_copy(i, half, other, tensor).wait_send()


def scatter(specs, arrays, dp_size, tensor_size, collective_id):
    count = len(specs)
    dp_bits = dp_size.bit_length() - 1
    scratch = []
    for spec, array in zip(specs, arrays):
        scratch.append(pltpu.VMEM((2, dp_size // 2) + spec.part_shape, array.dtype))
    for spec, array in zip(specs, arrays):
        for stage in range(dp_bits):
            scratch.append(pltpu.VMEM((2, dp_size >> (stage + 1)) + spec.part_shape, array.dtype))
    for spec, array in zip(specs, arrays):
        if spec.cut is not None:
            scratch.append(pltpu.VMEM((tensor_size, 2) + spec.cut_shape, array.dtype))
    return pl.pallas_call(
        functools.partial(scatter_kernel, specs, dp_size, tensor_size),
        out_shape=[jax.ShapeDtypeStruct(spec.shape, jnp.float32) for spec in specs],
        in_specs=[ANY] * count,
        out_specs=[VMEM] * count,
        scratch_shapes=scratch
        + [
            pltpu.SemaphoreType.DMA((count, 2, dp_size // 2)),
            pltpu.SemaphoreType.DMA((count, 2, dp_bits, dp_size // 2)),
            pltpu.SemaphoreType.DMA((count, 2, dp_bits, dp_size // 2)),
            pltpu.SemaphoreType.DMA((count, 2, tensor_size)),
            pltpu.SemaphoreType.DMA((count, 2, tensor_size)),
        ],
        compiler_params=pltpu.CompilerParams(
            collective_id=collective_id, has_side_effects=True, vmem_limit_bytes=VMEM_LIMIT
        ),
    )(*arrays)


def lanes_of(shape):
    return lax.broadcasted_iota(jnp.int32, shape, len(shape) - 1)


def swap_halves(values):
    width = values.shape[-1]
    first = lanes_of(values.shape) % HEAD_DIM < HEAD_DIM // 2
    return jnp.where(
        first,
        pltpu.roll(values, width - HEAD_DIM // 2, 1),
        pltpu.roll(values, HEAD_DIM // 2, 1),
    )


def left_head(block, odd):
    moved = jnp.where(odd, pltpu.roll(block, HEAD_DIM, 1), block)
    return jnp.where(lanes_of(block.shape) < HEAD_DIM, moved, jnp.zeros_like(moved))


def allowed(keys, rows, start):
    key_at = lax.broadcasted_iota(jnp.int32, (keys, rows), 0)
    query_at = lax.broadcasted_iota(jnp.int32, (keys, rows), 1) + start
    return key_at <= query_at


def attend_kernel(
    group_pairs, q_ref, cos_ref, sin_ref, k_ref, v_ref, o_ref, q_out, lse_ref, k_left, v_turned
):
    pair = pl.program_id(0)
    group = pair // group_pairs
    rows = q_ref.shape[0]
    start = lax.axis_index("tensor") * rows

    @pl.when(pair % group_pairs == 0)
    def _():
        odd = group % 2 == 1
        k_left[...] = left_head(k_ref[...].astype(jnp.float32), odd).astype(jnp.bfloat16)
        v_turned[...] = left_head(v_ref[...].astype(jnp.float32), odd).T[:HEAD_DIM].astype(
            jnp.bfloat16
        )

    raw = q_ref[...]
    turned = (raw * cos_ref[...] + swap_halves(raw) * sin_ref[...]).astype(jnp.bfloat16)
    turned = turned.astype(jnp.float32) * HEAD_DIM ** (-0.5)
    q_out[...] = turned.astype(jnp.bfloat16)
    open_at = allowed(k_left.shape[0], rows, start)
    contexts = []
    for head in (0, 1):
        queries = (turned if head == 0 else pltpu.roll(turned, HEAD_DIM, 1)).astype(jnp.bfloat16)
        scores = product_right(k_left[...], queries)
        scores = jnp.where(open_at, scores, -1e30)
        top = jnp.max(scores, axis=0, keepdims=True)
        exponent = jnp.exp(scores - top)
        summed = jnp.sum(exponent, axis=0, keepdims=True)
        context = product(v_turned[...], exponent.astype(jnp.bfloat16))
        contexts.append(context * (1.0 / summed))
        lse_ref[0, head, :] = (top + jnp.log(summed))[0]
    o_ref[...] = jnp.concatenate(contexts, axis=0).T.astype(jnp.bfloat16)


def attend(q_pre, cosines, sines, keys_values, head_count, group_heads):
    rows, width = q_pre.shape
    length, both = keys_values.shape
    pairs, group_pairs = head_count // 2, group_heads // 2
    kv_blocks = both // 256
    wide = pl.BlockSpec((rows, 128), lambda p: (0, p))
    table = pl.BlockSpec((rows, 128), lambda p: (0, 0))
    return pl.pallas_call(
        functools.partial(attend_kernel, group_pairs),
        grid=(pairs,),
        out_shape=[
            jax.ShapeDtypeStruct((rows, width), jnp.bfloat16),
            jax.ShapeDtypeStruct((rows, width), jnp.bfloat16),
            jax.ShapeDtypeStruct((pairs, 2, rows), jnp.float32),
        ],
        in_specs=[
            wide,
            table,
            table,
            pl.BlockSpec((length, 128), lambda p: (0, p // group_pairs // 2)),
            pl.BlockSpec((length, 128), lambda p: (0, kv_blocks + p // group_pairs // 2)),
        ],
        out_specs=[wide, wide, pl.BlockSpec((1, 2, rows), lambda p: (p, 0, 0))],
        scratch_shapes=[
            pltpu.VMEM((length, 128), jnp.bfloat16),
            pltpu.VMEM((HEAD_DIM, length), jnp.bfloat16),
        ],
        compiler_params=pltpu.CompilerParams(vmem_limit_bytes=VMEM_LIMIT),
        cost_estimate=pl.CostEstimate(
            flops=4 * rows * length * width, bytes_accessed=8 * rows * width, transcendentals=0
        ),
    )(q_pre, cosines, sines, keys_values, keys_values)


def attend_back_kernel(
    group_pairs,
    q_ref,
    do_ref,
    lse_ref,
    cos_ref,
    sin_ref,
    k_ref,
    v_ref,
    dq_ref,
    dk_ref,
    dv_ref,
    k_left,
    v_left,
    k_turned,
    dk_sum,
    dv_sum,
):
    pair = pl.program_id(0)
    group = pair // group_pairs
    odd = group % 2 == 1
    rows = q_ref.shape[0]
    start = lax.axis_index("tensor") * rows

    @pl.when(pair % group_pairs == 0)
    def _():
        left = left_head(k_ref[...].astype(jnp.float32), odd)
        k_left[...] = left.astype(jnp.bfloat16)
        k_turned[...] = left.T[:HEAD_DIM].astype(jnp.bfloat16)
        v_left[...] = left_head(v_ref[...].astype(jnp.float32), odd).astype(jnp.bfloat16)
        dk_sum[...] = jnp.zeros_like(dk_sum)
        dv_sum[...] = jnp.zeros_like(dv_sum)

    open_at = allowed(k_left.shape[0], rows, start)
    grads = []
    for head in (0, 1):
        queries, grad_out = q_ref[...], do_ref[...]
        if head == 1:
            queries = pltpu.roll(queries.astype(jnp.float32), HEAD_DIM, 1).astype(jnp.bfloat16)
            grad_out = pltpu.roll(grad_out.astype(jnp.float32), HEAD_DIM, 1).astype(jnp.bfloat16)
        scores = product_right(k_left[...], queries)
        scores = jnp.where(open_at, scores, -1e30)
        softmaxed = jnp.exp(scores - lse_ref[0, head, :][None, :])
        grad_soft = product_right(v_left[...], grad_out)
        mixed = softmaxed * grad_soft
        mixed_sum = jnp.sum(mixed, axis=0, keepdims=True)
        grad_scores = (mixed - softmaxed * mixed_sum).astype(jnp.bfloat16)
        dv_sum[...] += product(softmaxed.astype(jnp.bfloat16), grad_out)
        dk_sum[...] += product(grad_scores, queries)
        grads.append(product(k_turned[...], grad_scores))
    grad_q = jnp.concatenate(grads, axis=0).T * HEAD_DIM ** (-0.5)
    dq_ref[...] = (grad_q * cos_ref[...] - swap_halves(grad_q) * sin_ref[...]).astype(jnp.bfloat16)

    @pl.when(pair % group_pairs == group_pairs - 1)
    def _():
        for total, out in ((dk_sum, dk_ref), (dv_sum, dv_ref)):
            value = total[...]
            left = lanes_of(value.shape) < HEAD_DIM

            @pl.when(jnp.logical_not(odd))
            def _():
                out[...] = jnp.where(left, value, 0.0).astype(out.dtype)

            @pl.when(odd)
            def _():
                out[...] = jnp.where(
                    left, out[...].astype(jnp.float32), pltpu.roll(value, HEAD_DIM, 1)
                ).astype(out.dtype)


def attend_back(queries, grad_context, lse, cosines, sines, keys_values, head_count, group_heads):
    rows, width = queries.shape
    length, both = keys_values.shape
    pairs, group_pairs = head_count // 2, group_heads // 2
    kv_blocks = both // 256
    wide = pl.BlockSpec((rows, 128), lambda p: (0, p))
    table = pl.BlockSpec((rows, 128), lambda p: (0, 0))
    kv_out = pl.BlockSpec((length, 128), lambda p: (0, p // group_pairs // 2))
    return pl.pallas_call(
        functools.partial(attend_back_kernel, group_pairs),
        grid=(pairs,),
        out_shape=[
            jax.ShapeDtypeStruct((rows, width), jnp.bfloat16),
            jax.ShapeDtypeStruct((length, both // 2), jnp.bfloat16),
            jax.ShapeDtypeStruct((length, both // 2), jnp.bfloat16),
        ],
        in_specs=[
            wide,
            wide,
            pl.BlockSpec((1, 2, rows), lambda p: (p, 0, 0)),
            table,
            table,
            pl.BlockSpec((length, 128), lambda p: (0, p // group_pairs // 2)),
            pl.BlockSpec((length, 128), lambda p: (0, kv_blocks + p // group_pairs // 2)),
        ],
        out_specs=[wide, kv_out, kv_out],
        scratch_shapes=[
            pltpu.VMEM((length, 128), jnp.bfloat16),
            pltpu.VMEM((length, 128), jnp.bfloat16),
            pltpu.VMEM((HEAD_DIM, length), jnp.bfloat16),
            pltpu.VMEM((length, 128), jnp.float32),
            pltpu.VMEM((length, 128), jnp.float32),
        ],
        compiler_params=pltpu.CompilerParams(vmem_limit_bytes=VMEM_LIMIT),
        cost_estimate=pl.CostEstimate(
            flops=10 * rows * length * width, bytes_accessed=8 * rows * width, transcendentals=0
        ),
    )(queries, grad_context, lse, cosines, sines, keys_values, keys_values)


def block_at(place, tensor, tensor_size):
    last = tensor_size - 1
    pairs = jnp.minimum(tensor, last - tensor)
    near = lax.div(place + 1, 2)
    paired = jnp.where(lax.rem(place, 2) == 1, tensor - near, tensor + near)
    far = place - pairs
    lone = jnp.where(tensor > last - tensor, tensor - far, tensor + far)
    return jnp.where(place <= 2 * pairs, paired, lone)


def mlp_kernel(
    tensor_size,
    normed_ref,
    cot_ref,
    gate_ref,
    up_ref,
    down_ref,
    back_ref,
    y_ref,
    d_gate_ref,
    d_up_ref,
    d_down_ref,
    normed,
    cot,
    gate,
    up,
    down,
    hidden,
    d_gate,
    d_up,
    y_stage,
    stage,
    landing,
    load_sem,
    n_send,
    n_recv,
    y_sem,
    b_send,
    b_recv,
    out_sem,
):
    dp, tensor = lax.axis_index("dp"), lax.axis_index("tensor")
    rows, width = normed_ref.shape
    units = gate.shape[1]
    loads = [
        pltpu.make_async_copy(source, target, load_sem.at[i])
        for i, (source, target) in enumerate(
            (
                (normed_ref, normed.at[tensor]),
                (gate_ref, gate),
                (up_ref, up),
                (down_ref, down),
                (cot_ref, cot),
            )
        )
    ]
    for load in loads:
        load.start()
    greet((dp, tensor, tensor_size), False, True, 0)
    has = [tensor + 1 < tensor_size, tensor > 0]

    def n_copy(block, way, source=None):
        return pltpu.make_async_remote_copy(
            src_ref=normed.at[block] if source is None else source,
            dst_ref=normed.at[block],
            send_sem=n_send.at[way, block],
            recv_sem=n_recv.at[block],
            device_id=(dp, tensor + 1 if way == 0 else tensor - 1),
            device_id_type=MESH,
        )

    for way in (0, 1):
        pl.when(has[way])(n_copy(tensor, way, normed_ref).start)
    landing[tensor] = jnp.zeros((rows, width), landing.dtype)

    def pump(distance):
        for way, block in ((0, tensor - distance), (1, tensor + distance)):

            @pl.when((block >= 0) & (block < tensor_size))
            def _():
                n_copy(block, way).wait_recv()
                pl.when(has[way])(n_copy(block, way).start)

    def distance_at(place):
        return jnp.abs(block_at(place, tensor, tensor_size) - tensor)

    inner = (tensor > 0) & (tensor + 1 < tensor_size)

    def b_copy(block, slot):
        return pltpu.make_async_remote_copy(
            src_ref=stage.at[block],
            dst_ref=landing.at[slot],
            send_sem=b_send.at[block],
            recv_sem=b_recv.at[slot],
            device_id=(dp, block),
            device_id_type=MESH,
        )

    def y_copy(block, slot):
        return pltpu.make_async_copy(y_stage.at[slot], y_ref.at[block], y_sem.at[slot])

    for load in loads[:3]:
        load.wait()

    def chunk(place, carry):
        block = block_at(place, tensor, tensor_size)
        fresh = (place >= 1) & (distance_at(place) != distance_at(place - 1))

        @pl.when(fresh & jnp.logical_not((place >= 2) & inner))
        def _():
            pump(distance_at(place))

        rows_in = normed[block]
        gate_pre = product(rows_in, gate[...])
        upward = product(rows_in, up[...])

        @pl.when((place >= 1) & (place + 1 < tensor_size) & inner)
        def _():
            @pl.when(distance_at(place + 1) != distance_at(place))
            def _():
                pump(distance_at(place + 1))

        @pl.when(place == 0)
        def _():
            for load in loads[3:]:
                load.wait()

        sigmoid = 1.0 / (1.0 + jnp.exp(-gate_pre))
        silu = gate_pre * sigmoid
        active = (silu * upward).astype(jnp.bfloat16)
        hidden[block] = active
        slot = lax.rem(place, 2)

        @pl.when(place >= 2)
        def _():
            y_copy(block, slot).wait()

        y_stage[slot] = product(active, down[...]).astype(jnp.bfloat16)
        y_copy(block, slot).start()
        grad_hidden = product_right(cot[block], down[...])
        low_gate = (
            grad_hidden * upward * sigmoid * (1.0 + gate_pre * (1.0 - sigmoid))
        ).astype(jnp.bfloat16)
        low_up = (grad_hidden * silu).astype(jnp.bfloat16)
        d_gate[block] = low_gate
        d_up[block] = low_up
        back = product_right(low_gate, gate[...]) + product_right(low_up, up[...])

        @pl.when(block == tensor)
        def _():
            back_ref[...] = back

        @pl.when(block != tensor)
        def _():
            stage[block] = back.astype(stage.dtype)
            b_copy(block, tensor).start()

        return carry

    lax.fori_loop(0, tensor_size, chunk, 0)
    for slot in range(2):
        y_copy(0, slot).wait()

    all_rows = tensor_size * rows

    def weight_grad(left, right, out, out_hbm, sem):
        extent = left.shape[2]
        tile = 256 if extent % 256 == 0 else 128 if extent % 128 == 0 else extent

        def body(step, carry):
            at = pl.ds(pl.multiple_of(step * tile, tile), tile)
            columns = left[:, :, at].reshape(all_rows, tile)
            out[at, :] = product_left(columns, right[...].reshape(all_rows, -1)).astype(out.dtype)
            return carry

        lax.fori_loop(0, extent // tile, body, 0)
        pltpu.make_async_copy(out, out_hbm, sem).start()

    weight_grad(hidden, cot, down, d_down_ref, out_sem.at[0])
    weight_grad(normed, d_gate, gate, d_gate_ref, out_sem.at[1])
    weight_grad(normed, d_up, up, d_up_ref, out_sem.at[2])

    for other in range(tensor_size):

        @pl.when(other != tensor)
        def _():
            b_copy(other, other).wait_recv()

    slab = 16

    def add_slab(step, carry):
        at = pl.ds(pl.multiple_of(step * slab, slab), slab)
        total = back_ref[at, :]
        for other in range(tensor_size):
            total = total + landing[other, at, :].astype(jnp.float32)
        back_ref[at, :] = total
        return carry

    lax.fori_loop(0, rows // slab, add_slab, 0)
    pltpu.make_async_copy(down, d_down_ref, out_sem.at[0]).wait()
    pltpu.make_async_copy(gate, d_gate_ref, out_sem.at[1]).wait()
    pltpu.make_async_copy(up, d_up_ref, out_sem.at[2]).wait()
    for other in range(tensor_size):

        @pl.when(other != tensor)
        def _():
            b_copy(other, tensor).wait_send()

        for way in (0, 1):
            sent = has[way] & ((other <= tensor) if way == 0 else (other >= tensor))
            pl.when(sent)(n_copy(other, way).wait_send)


def feed_forward(normed, cot_all, gate, up, down, tensor_size, collective_id):
    rows, width = normed.shape
    units = gate.shape[1]
    low = jnp.bfloat16
    tokens = (tensor_size, rows, width)
    inner = (tensor_size, rows, units)
    dma = pltpu.SemaphoreType.DMA
    return pl.pallas_call(
        functools.partial(mlp_kernel, tensor_size),
        out_shape=[
            jax.ShapeDtypeStruct((rows, width), jnp.float32),
            jax.ShapeDtypeStruct(tokens, low),
            jax.ShapeDtypeStruct(gate.shape, low),
            jax.ShapeDtypeStruct(up.shape, low),
            jax.ShapeDtypeStruct(down.shape, low),
        ],
        in_specs=[ANY] * 5,
        out_specs=[VMEM] + [ANY] * 4,
        scratch_shapes=[
            pltpu.VMEM(tokens, low),
            pltpu.VMEM(tokens, low),
            pltpu.VMEM(gate.shape, low),
            pltpu.VMEM(up.shape, low),
            pltpu.VMEM(down.shape, low),
            pltpu.VMEM(inner, low),
            pltpu.VMEM(inner, low),
            pltpu.VMEM(inner, low),
            pltpu.VMEM((2, rows, width), low),
            pltpu.VMEM(tokens, low),
            pltpu.VMEM(tokens, low),
            dma((5,)),
            dma((2, tensor_size)),
            dma((tensor_size,)),
            dma((2,)),
            dma((tensor_size,)),
            dma((tensor_size,)),
            dma((3,)),
        ],
        compiler_params=pltpu.CompilerParams(
            collective_id=collective_id, has_side_effects=True, vmem_limit_bytes=60 * 2**20
        ),
        cost_estimate=pl.CostEstimate(
            flops=18 * tensor_size * rows * width * units,
            bytes_accessed=8 * width * units,
            transcendentals=0,
        ),
    )(normed, cot_all.reshape(tokens), gate, up, down)


def rope_tables(rows, tensor):
    halved = HEAD_DIM // 2
    freqs = theta_base ** (-2.0 * jnp.arange(halved, dtype=jnp.float32) / HEAD_DIM)
    places = (tensor * rows + jnp.arange(rows)).astype(jnp.float32)
    angles = places[:, None] * freqs[None, :]
    cosines, sines = jnp.cos(angles), jnp.sin(angles)
    return (
        jnp.concatenate([cosines, cosines] * 2, axis=1),
        jnp.concatenate([-sines, sines] * 2, axis=1),
    )


def turn_heads(values, cosines, sines):
    rows, width = values.shape
    parts = values.reshape(rows, width // HEAD_DIM, 2, HEAD_DIM // 2)
    swapped = parts[:, :, ::-1, :].reshape(rows, width)
    repeat = width // 128
    return values * jnp.tile(cosines, (1, repeat)) + swapped * jnp.tile(sines, (1, repeat))


def start_row(dp, size):
    return pl.multiple_of(dp * size, size)


def on_device(
    dp_size,
    tensor_size,
    tokens,
    attn_gain,
    w_query,
    w_key,
    w_value,
    w_out,
    mlp_gain,
    w_gate,
    w_up,
    w_down,
    cotangent,
):
    tensor_index = lax.axis_index("tensor")
    rows, width = tokens.shape
    heads = w_query.shape[1] * tensor_size // HEAD_DIM
    kv_width = w_key.shape[1]
    kv_heads = kv_width // HEAD_DIM
    group_heads = heads // kv_heads
    q_rows, q_cols = w_query.shape
    kv_rows = w_key.shape[0]
    o_rows, o_cols = w_out.shape
    gain_part = attn_gain.shape[0]
    call = functools.partial(gather, dp_size=dp_size, tensor_size=tensor_size)

    key_value = jnp.concatenate([w_key, w_value], axis=1)
    gains = jnp.zeros((16, 128), jnp.bfloat16)
    gains = gains.at[0, :gain_part].set(attn_gain).at[1, :gain_part].set(mlp_gain)
    gate_full, up_full, down_full = (
        lax.all_gather(w_gate, "dp", axis=0, tiled=True),
        lax.all_gather(w_up, "dp", axis=0, tiled=True),
        lax.all_gather(w_down, "dp", axis=1, tiled=True),
    )
    cot_all = lax.all_gather(cotangent, "tensor", axis=0, tiled=True)
    query_spec = Gather(
        (width, heads * HEAD_DIM),
        lambda ref, dp, t: ref.at[
            pl.ds(start_row(dp, q_rows), q_rows), pl.ds(start_row(t, q_cols), q_cols)
        ],
        lambda ref, dp, half: ref.at[
            pl.ds(pl.multiple_of(dp * q_rows + half * (q_rows // 2), q_rows // 2), q_rows // 2), :
        ],
    )
    kv_all_rows = kv_rows * tensor_size
    kv_spec = Gather(
        (width, 2 * kv_width),
        lambda ref, dp, t: ref.at[pl.ds(start_row(dp * tensor_size + t, kv_rows), kv_rows), :],
        lambda ref, dp, half: ref.at[
            pl.ds(
                pl.multiple_of(dp * kv_all_rows + half * (kv_all_rows // 2), kv_all_rows // 2),
                kv_all_rows // 2,
            ),
            :,
        ],
    )
    gain_spec = Gather(
        (dp_size * tensor_size * 16, 128),
        lambda ref, dp, t: ref.at[pl.ds(start_row(dp * tensor_size + t, 16), 16), :],
        lambda ref, dp, half: ref.at[
            pl.ds(
                pl.multiple_of((2 * dp + half) * tensor_size * 8, tensor_size * 8),
                tensor_size * 8,
            ),
            :,
        ],
    )
    out_spec = Gather(
        (heads * HEAD_DIM, width),
        lambda ref, dp, t: ref.at[
            pl.ds(start_row(t, o_rows), o_rows), pl.ds(start_row(dp, o_cols), o_cols)
        ],
        lambda ref, dp, half: ref.at[
            pl.ds(half * (heads * HEAD_DIM // 2), heads * HEAD_DIM // 2),
            pl.ds(start_row(dp, o_cols), o_cols),
        ],
    )
    row_spec = lambda shape: Gather(
        (tensor_size * shape[0], shape[1]),
        lambda ref, dp, t: ref.at[pl.ds(start_row(t, shape[0]), shape[0]), :],
    )
    query_full, key_value_full, gains_full = call(
        [query_spec, kv_spec, gain_spec], [w_query, key_value, gains], collective_id=1
    )
    gains_full = gains_full.reshape(-1, 16, 128)[:, :2, :gain_part].astype(jnp.float32)
    gain_first = gains_full[:, 0].reshape(width)
    gain_second = gains_full[:, 1].reshape(width)
    cosines, sines = rope_tables(rows, tensor_index)

    residual = tokens.astype(jnp.float32)
    scale_first = lax.rsqrt(jnp.mean(residual * residual, axis=-1, keepdims=True) + epsilon)
    unit_first = residual * scale_first
    normed_first = (unit_first * gain_first).astype(jnp.bfloat16)
    kv_pre = product(normed_first, key_value_full)
    kv_own = jnp.concatenate(
        [turn_heads(kv_pre[:, :kv_width], cosines, sines), kv_pre[:, kv_width:]], axis=1
    ).astype(jnp.bfloat16)
    query_pre = product(normed_first, query_full)
    kv_all, out_full = call([row_spec(kv_own.shape), out_spec], [kv_own, w_out], collective_id=2)
    context, queries, log_sums = attend(
        query_pre, cosines, sines, kv_all, heads, group_heads
    )
    middle = residual + product(context, out_full)
    scale_second = lax.rsqrt(jnp.mean(middle * middle, axis=-1, keepdims=True) + epsilon)
    unit_second = middle * scale_second
    normed_own = (unit_second * gain_second).astype(jnp.bfloat16)
    back_second, mlp_part, grad_gate_w, grad_up_w, grad_down_w = feed_forward(
        normed_own, cot_all, gate_full, up_full, down_full, tensor_size, 3
    )
    mlp_rows = lax.psum_scatter(
        mlp_part.reshape(tensor_size * rows, width), "tensor", scatter_dimension=0, tiled=True
    ).astype(jnp.float32)
    output = (middle + mlp_rows).astype(jnp.bfloat16)
    sum_gate, sum_up, sum_down = (
        lax.psum_scatter(grad_gate_w, "dp", scatter_dimension=0, tiled=True).astype(jnp.float32),
        lax.psum_scatter(grad_up_w, "dp", scatter_dimension=0, tiled=True).astype(jnp.float32),
        lax.psum_scatter(grad_down_w, "dp", scatter_dimension=1, tiled=True).astype(jnp.float32),
    )

    grad_gain_second = jnp.sum(back_second * unit_second, axis=0)
    grad_middle = cotangent.astype(jnp.float32) + norm_back(
        back_second, unit_second, scale_second, gain_second
    )
    middle_low = grad_middle.astype(jnp.bfloat16)
    grad_context = product_right(middle_low, out_full).astype(jnp.bfloat16)
    grad_out_w = product_left(context, middle_low).astype(jnp.bfloat16)
    grad_queries, grad_keys, grad_values = attend_back(
        queries, grad_context, log_sums, cosines, sines, kv_all, heads, group_heads
    )
    grad_kv = jnp.concatenate([grad_keys, grad_values], axis=1)
    kv_blocks = exchange(grad_kv.reshape(tensor_size, rows, 2 * kv_width), tensor_size, 5)
    grad_kv_own = jnp.sum(kv_blocks.astype(jnp.float32), axis=0)
    grad_kv_own = jnp.concatenate(
        [turn_heads(grad_kv_own[:, :kv_width], cosines, -sines), grad_kv_own[:, kv_width:]], axis=1
    ).astype(jnp.bfloat16)
    grad_query_w = product_left(normed_first, grad_queries).astype(jnp.bfloat16)
    grad_kv_w = product_left(normed_first, grad_kv_own).astype(jnp.bfloat16)
    back_first = product_right(grad_queries, query_full) + product_right(
        grad_kv_own, key_value_full
    )
    grad_gain_first = jnp.sum(back_first * unit_first, axis=0)
    grad_tokens = grad_middle + norm_back(back_first, unit_first, scale_first, gain_first)

    grad_gains = jnp.zeros((dp_size * tensor_size, 16, 128), jnp.float32)
    grad_gains = grad_gains.at[:, 0, :gain_part].set(grad_gain_first.reshape(-1, gain_part))
    grad_gains = grad_gains.at[:, 8, :gain_part].set(grad_gain_second.reshape(-1, gain_part))
    query_scatter = Scatter(
        (q_rows, q_cols),
        query_spec.half,
        (q_rows // 2, tensor_size * q_cols),
        lambda ref, half: ref.at[pl.ds(half * (q_rows // 2), q_rows // 2), :],
        lambda ref, j: ref.at[:, pl.ds(j * q_cols, q_cols)],
        (q_rows // 2, q_cols),
    )
    kv_scatter = Scatter(
        (kv_rows, 2 * kv_width),
        lambda ref, dp, half: ref.at[
            pl.ds(dp * tensor_size, tensor_size), :, pl.ds(half * kv_width, kv_width)
        ],
        (tensor_size, kv_rows, kv_width),
        lambda ref, half: ref.at[:, pl.ds(half * kv_width, kv_width)],
        lambda ref, j: ref.at[j],
        (kv_rows, kv_width),
    )
    out_scatter = Scatter(
        (o_rows, o_cols),
        lambda ref, dp, half: ref.at[
            :, pl.ds(half * (o_rows // 2), o_rows // 2), pl.ds(start_row(dp, o_cols), o_cols)
        ],
        (tensor_size, o_rows // 2, o_cols),
        lambda ref, half: ref.at[pl.ds(half * (o_rows // 2), o_rows // 2), :],
        lambda ref, j: ref.at[j],
        (o_rows // 2, o_cols),
    )
    gain_scatter = Scatter(
        (16, 128),
        lambda ref, dp, half: ref.at[
            pl.ds(dp * tensor_size, tensor_size), pl.ds(half * 8, 8), :
        ],
        (tensor_size, 8, 128),
        lambda ref, half: ref.at[pl.ds(half * 8, 8), :],
        lambda ref, j: ref.at[j],
        (8, 128),
    )
    sum_out, sum_query, sum_kv, sum_gains = scatter(
        [out_scatter, query_scatter, kv_scatter, gain_scatter],
        [
            grad_out_w.reshape(tensor_size, o_rows, width),
            grad_query_w,
            grad_kv_w.reshape(dp_size * tensor_size, kv_rows, 2 * kv_width),
            grad_gains,
        ],
        dp_size,
        tensor_size,
        6,
    )
    return (
        output,
        grad_tokens,
        sum_gains[0, :gain_part],
        sum_query,
        sum_kv[:, :kv_width],
        sum_kv[:, kv_width:],
        sum_out,
        sum_gains[8, :gain_part],
        sum_gate,
        sum_up,
        sum_down,
    )


def solution(mesh):
    placed = (
        P(("dp", "tensor"), None),
        P(("dp", "tensor")),
        P("dp", "tensor"),
        P(("dp", "tensor"), None),
        P(("dp", "tensor"), None),
        P("tensor", "dp"),
        P(("dp", "tensor")),
        P("dp", "tensor"),
        P("dp", "tensor"),
        P("tensor", "dp"),
        P(("dp", "tensor"), None),
    )
    return jax.shard_map(
        functools.partial(on_device, mesh.shape["dp"], mesh.shape["tensor"]),
        mesh=mesh,
        in_specs=placed,
        out_specs=(
            P(("dp", "tensor"), None),
            P(("dp", "tensor"), None),
            P(("dp", "tensor")),
            P("dp", "tensor"),
            P(("dp", "tensor"), None),
            P(("dp", "tensor"), None),
            P("tensor", "dp"),
            P(("dp", "tensor")),
            P("dp", "tensor"),
            P("dp", "tensor"),
            P("tensor", "dp"),
        ),
        check_vma=False,
    )
```

```python
import functools

import jax
import jax.numpy as jnp
from jax import lax
from jax.experimental import pallas as pl
from jax.experimental.pallas import tpu as pltpu
from jax.sharding import PartitionSpec as P

HEAD_DIM = 64
SEQLEN = 1024
MESH = pl.DeviceIdType.MESH
ANY = pl.BlockSpec(memory_space=pl.ANY)
VMEM = pl.BlockSpec(memory_space=pltpu.VMEM)
VMEM_LIMIT = 56 * 2**20

epsilon = 1e-05
theta_base = 10000.0


def product(left, right):
    return jnp.dot(left, right, preferred_element_type=jnp.float32)


def product_left(left, right):
    return lax.dot_general(
        left, right, (((0,), (0,)), ((), ())), preferred_element_type=jnp.float32
    )


def product_right(left, right):
    return lax.dot_general(
        left, right, (((1,), (1,)), ((), ())), preferred_element_type=jnp.float32
    )


def norm_back(grad_normed, unit_rows, scale_rows, gain):
    scaled_grad = grad_normed * gain
    return scale_rows * (
        scaled_grad - unit_rows * jnp.mean(scaled_grad * unit_rows, axis=-1, keepdims=True)
    )


def flip(index, bit):
    size = 1 << bit
    return index + size * (1 - 2 * lax.rem(lax.div(index, size), 2))


def masked(index, bits, rank):
    for place, bit in enumerate(bits):
        if rank >> place & 1:
            index = flip(index, bit)
    return index


def orders(bit_count, core_last):
    up = list(range(1, bit_count))
    down = up[::-1]
    return [up + [0], down + [0]] if core_last else [[0] + up, [0] + down]


def greet(spots, near, all_tensor, dp_bits):
    dp, tensor, tensor_size = spots
    barrier = pltpu.get_barrier_semaphore()

    def signal(where):
        pl.semaphore_signal(barrier, inc=1, device_id=where, device_id_type=MESH)

    peers = dp_bits
    for bit in range(dp_bits):
        signal((flip(dp, bit), tensor))
    if all_tensor:
        peers += tensor_size - 1
        for other in range(tensor_size):
            pl.when(other != tensor)(functools.partial(signal, (dp, other)))
    elif near:
        below, above = tensor > 0, tensor + 1 < tensor_size
        pl.when(below)(functools.partial(signal, (dp, tensor - 1)))
        pl.when(above)(functools.partial(signal, (dp, tensor + 1)))
        peers = peers + below.astype(jnp.int32) + above.astype(jnp.int32)
    pl.semaphore_wait(barrier, peers)


class Gather:
    def __init__(self, shape, slot, half=None, line=True):
        self.shape, self.slot, self.half, self.line = shape, slot, half, line


class GatherRun:
    def __init__(self, specs, dp_size, tensor_size, sources, outs, held, sems):
        self.specs, self.sources, self.outs, self.held = specs, sources, outs, held
        self.own_sem, self.z_send, self.z_recv, self.h_send, self.h_recv = sems
        self.dp, self.tensor = lax.axis_index("dp"), lax.axis_index("tensor")
        self.tensor_size, self.dp_bits = tensor_size, dp_size.bit_length() - 1
        self.order = orders(self.dp_bits, True)
        self.hyper = [i for i, spec in enumerate(specs) if spec.half is not None]
        self.lines = [i for i, spec in enumerate(specs) if spec.line]
        self.early = [n for n, i in enumerate(self.hyper) if not specs[i].line]
        self.late = [n for n, i in enumerate(self.hyper) if specs[i].line]
        self.can = [self.tensor + 1 < tensor_size, self.tensor > 0]

    def greet(self):
        greet(
            (self.dp, self.tensor, self.tensor_size),
            bool(self.lines),
            False,
            self.dp_bits if self.hyper else 0,
        )

    def z_copy(self, i, block, way, source=None):
        slot = self.specs[i].slot(self.outs[i], self.dp, block)
        return pltpu.make_async_remote_copy(
            src_ref=slot if source is None else source,
            dst_ref=slot,
            send_sem=self.z_send.at[i, way, block],
            recv_sem=self.z_recv.at[i, block],
            device_id=(self.dp, self.tensor + 1 if way == 0 else self.tensor - 1),
            device_id_type=MESH,
        )

    def own(self, i):
        slot = self.specs[i].slot(self.outs[i], self.dp, self.tensor)
        return pltpu.make_async_copy(self.held[i], slot, self.own_sem.at[i])

    def begin_line(self, i):
        for way in (0, 1):
            pl.when(self.can[way])(self.z_copy(i, self.tensor, way, self.sources[i]).start)

    def begin(self, slow=()):
        loads = [
            pltpu.make_async_copy(source, held, self.own_sem.at[i])
            for i, (source, held) in enumerate(zip(self.sources, self.held))
        ]
        for load in loads:
            load.start()
        for i in self.lines:
            if i not in slow:
                self.begin_line(i)
        for i, load in enumerate(loads):
            load.wait()
            self.own(i).start()
        for n in self.early:
            self.own(self.hyper[n]).wait()
            self.hop(n, 0)

    def line(self, i, step):
        for way, block in ((0, self.tensor - step), (1, self.tensor + step)):

            @pl.when((block >= 0) & (block < self.tensor_size))
            def _():
                self.z_copy(i, block, way).wait_recv()
                pl.when(self.can[way])(self.z_copy(i, block, way).start)

    def part(self, n, half, rank):
        i = self.hyper[n]
        return self.specs[i].half(self.outs[i], masked(self.dp, self.order[half], rank), half)

    def h_copy(self, n, half, rank, place):
        return pltpu.make_async_remote_copy(
            src_ref=self.part(n, half, rank),
            dst_ref=self.part(n, half, rank),
            send_sem=self.h_send.at[n, half, rank, place],
            recv_sem=self.h_recv.at[n, half, rank | 1 << place],
            device_id=(flip(self.dp, self.order[half][place]), self.tensor),
            device_id_type=MESH,
        )

    def hop(self, n, rank):
        for half in (0, 1):
            if rank:
                wait_part(
                    self.part(n, half, rank),
                    self.h_recv.at[n, half, rank],
                    self.h_send.at[n, half, 0, 0],
                    (flip(self.dp, 0), self.tensor),
                )
            for place in range(rank.bit_length(), self.dp_bits):
                self.h_copy(n, half, rank, place).start()

    def end_line(self, i):
        self.own(i).wait()

    def close(self):
        for rank in range(1 << self.dp_bits):
            for n in range(len(self.hyper)):
                for half in (0, 1):
                    for place in range(rank.bit_length(), self.dp_bits):
                        self.h_copy(n, half, rank, place).wait_send()
        for i in self.lines:
            for block in range(self.tensor_size):
                for way in (0, 1):
                    sent = self.can[way] & (
                        (block <= self.tensor) if way == 0 else (block >= self.tensor)
                    )
                    pl.when(sent)(self.z_copy(i, block, way).wait_send)


def gather_kernel(specs, slow, dp_size, tensor_size, *refs):
    count = len(specs)
    run = GatherRun(
        specs,
        dp_size,
        tensor_size,
        refs[:count],
        refs[count : 2 * count],
        refs[2 * count : 3 * count],
        refs[3 * count :],
    )
    run.greet()
    run.begin(slow)
    first = [i for i in run.lines if i not in slow]
    for step in range(1, tensor_size):
        for i in first:
            run.line(i, step)
    for i in first:
        run.end_line(i)
    for n in run.late:
        run.hop(n, 0)
    for i in slow:
        run.begin_line(i)
    ranks = 1 << run.dp_bits
    for rank in range(1, max(ranks, tensor_size)):
        if rank < ranks:
            for n in range(len(run.hyper)):
                run.hop(n, rank)
        if rank < tensor_size:
            for i in slow:
                run.line(i, rank)
    for i in slow:
        run.end_line(i)
    run.close()


def gather_scratch(specs, arrays, dp_size, tensor_size):
    count = len(specs)
    hyper = max(1, sum(spec.half is not None for spec in specs))
    dp_bits = dp_size.bit_length() - 1
    return [pltpu.VMEM(array.shape, array.dtype) for array in arrays], [
        pltpu.SemaphoreType.DMA((count,)),
        pltpu.SemaphoreType.DMA((count, 2, tensor_size)),
        pltpu.SemaphoreType.DMA((count, tensor_size)),
        pltpu.SemaphoreType.DMA((hyper, 2, dp_size, max(dp_bits, 1))),
        pltpu.SemaphoreType.DMA((hyper, 2, dp_size)),
    ]


def wait_part(part, recv_sem, send_sem, device):
    pltpu.make_async_remote_copy(
        src_ref=part,
        dst_ref=part,
        send_sem=send_sem,
        recv_sem=recv_sem,
        device_id=device,
        device_id_type=MESH,
    ).wait_recv()


def gather_shapes(specs, arrays):
    return [jax.ShapeDtypeStruct(spec.shape, array.dtype) for spec, array in zip(specs, arrays)]


def gather(specs, arrays, dp_size, tensor_size, collective_id, slow=()):
    count = len(specs)
    held, sems = gather_scratch(specs, arrays, dp_size, tensor_size)
    return pl.pallas_call(
        functools.partial(gather_kernel, specs, slow, dp_size, tensor_size),
        out_shape=gather_shapes(specs, arrays),
        in_specs=[ANY] * count,
        out_specs=[ANY] * count,
        scratch_shapes=held + sems,
        compiler_params=pltpu.CompilerParams(
            collective_id=collective_id, has_side_effects=True, vmem_limit_bytes=VMEM_LIMIT
        ),
    )(*arrays)


class Scatter:
    def __init__(self, kind, shape, part, part_shape, place, cut=None, cut_shape=None):
        self.kind, self.shape, self.part, self.part_shape = kind, shape, part, part_shape
        self.place, self.cut = place, cut
        self.cut_shape = part_shape if kind == "own" else cut_shape


def add_into(total, extra):
    shape = total.shape
    rows = shape[-2]
    slab = min(16, rows)
    if len(shape) == 2:

        def body(step, carry):
            at = pl.ds(pl.multiple_of(step * slab, slab), slab)
            total[at, :] = (
                total[at, :].astype(jnp.float32) + extra[at, :].astype(jnp.float32)
            ).astype(total.dtype)
            return carry

        lax.fori_loop(0, rows // slab, body, 0, unroll=2 if (rows // slab) % 2 == 0 else 1)
    else:
        for lead in range(shape[0]):
            add_into(total.at[lead], extra.at[lead])


class ScatterRun:
    def __init__(self, specs, dp_size, tensor_size, sources, outs, scratch):
        scratch = list(scratch)
        self.specs, self.sources, self.outs = specs, sources, outs
        self.tensor_size, self.dp_bits = tensor_size, dp_size.bit_length() - 1
        self.total = [scratch.pop(0) for _ in specs]
        self.landing = [[scratch.pop(0) for _ in range(self.dp_bits)] for _ in specs]
        self.shares = [scratch.pop(0) if spec.kind != "dp" else None for spec in specs]
        self.own_sem, self.send, self.recv, self.z_send, self.z_recv = scratch
        self.dp, self.tensor = lax.axis_index("dp"), lax.axis_index("tensor")
        self.order = orders(self.dp_bits, False)
        self.units = scatter_units(specs, tensor_size)

    def greet(self):
        cuts = any(spec.kind != "dp" for spec in self.specs)
        greet((self.dp, self.tensor, self.tensor_size), False, cuts, self.dp_bits)

    def slots(self, stage):
        return range(1 << (self.dp_bits - 1 - stage))

    def part(self, unit, half, rank):
        i, owner = self.units[unit]
        place = masked(self.dp, self.order[half], rank)
        return self.specs[i].part(self.sources[i], place, half, owner or 0)

    def sum_at(self, unit, half, slot):
        i, owner = self.units[unit]
        return self.total[i].at[owner or 0, half, slot]

    def own_copy(self, unit, half, slot):
        return pltpu.make_async_copy(
            self.part(unit, half, 2 * slot),
            self.sum_at(unit, half, slot),
            self.own_sem.at[unit, half, slot],
        )

    def landed(self, unit, half, stage, slot):
        i, owner = self.units[unit]
        return self.landing[i][stage].at[owner or 0, half, slot]

    def copy(self, unit, half, stage, slot):
        if stage == 0:
            source = self.part(unit, half, 2 * slot + 1)
        else:
            source = self.sum_at(unit, half, (2 * slot + 1) << (stage - 1))
        return pltpu.make_async_remote_copy(
            src_ref=source,
            dst_ref=self.landed(unit, half, stage, slot),
            send_sem=self.send.at[unit, half, stage, slot],
            recv_sem=self.recv.at[unit, half, stage, slot],
            device_id=(flip(self.dp, self.order[half][stage]), self.tensor),
            device_id_type=MESH,
        )

    def begin(self):
        for unit in range(len(self.units)):
            for slot in self.slots(0):
                for half in (0, 1):
                    self.copy(unit, half, 0, slot).start()
                    self.own_copy(unit, half, slot).start()

    def z_copy(self, unit, half, other, slot):
        i, owner = self.units[unit]
        spec, total = self.specs[i], self.sum_at(unit, half, 0)
        return pltpu.make_async_remote_copy(
            src_ref=total if spec.kind == "own" else spec.cut(total, other),
            dst_ref=self.shares[i].at[slot, half],
            send_sem=self.z_send.at[i, half, other],
            recv_sem=self.z_recv.at[i, half, slot],
            device_id=(self.dp, other),
            device_id_type=MESH,
        )

    def others(self, unit):
        owner = self.units[unit][1]
        return range(self.tensor_size) if owner is None else [owner]

    def step(self, unit, stage):
        i, owner = self.units[unit]
        spec = self.specs[i]
        if stage < self.dp_bits:
            for slot in sorted(self.slots(stage), key=lambda s: -(s & 1)):
                for half in (0, 1):
                    if stage == 0:
                        self.own_copy(unit, half, slot).wait()
                    self.copy(unit, half, stage, slot).wait_recv()
                    add_into(
                        self.sum_at(unit, half, slot << stage),
                        self.landed(unit, half, stage, slot),
                    )
                    if slot & 1:
                        self.copy(unit, half, stage + 1, slot >> 1).start()
            return
        for half in (0, 1):
            total = self.sum_at(unit, half, 0)
            if spec.kind == "dp":
                spec.place(self.outs[i], half)[...] = total[...].astype(jnp.float32)
                continue
            for other in self.others(unit):

                @pl.when(other != self.tensor)
                def _():
                    self.z_copy(unit, half, other, self.tensor).start()

                @pl.when(other == self.tensor)
                def _():
                    mine = total if spec.kind == "own" else spec.cut(total, other)
                    self.shares[i][other, half] = mine[...]

    def steps(self):
        count = len(self.units)
        return [
            (unit, turn - unit)
            for turn in range(count + self.dp_bits)
            for unit in range(count)
            if 0 <= turn - unit <= self.dp_bits
        ]

    def close(self):
        for i, spec in enumerate(self.specs):
            if spec.kind == "dp":
                continue
            unit = [u for u, (at, owner) in enumerate(self.units) if at == i][0]
            for half in (0, 1):
                for other in range(self.tensor_size):

                    @pl.when(other != self.tensor)
                    def _():
                        self.z_copy(unit, half, other, other).wait_recv()

                summed = self.shares[i][0, half].astype(jnp.float32)
                for other in range(1, self.tensor_size):
                    summed = summed + self.shares[i][other, half].astype(jnp.float32)
                spec.place(self.outs[i], half)[...] = summed
        for unit, (i, owner) in enumerate(self.units):
            for half in (0, 1):
                for stage in range(self.dp_bits):
                    for slot in self.slots(stage):
                        self.copy(unit, half, stage, slot).wait_send()
                if self.specs[i].kind != "dp":
                    for other in self.others(unit):

                        @pl.when(other != self.tensor)
                        def _():
                            self.z_copy(unit, half, other, self.tensor).wait_send()


def scatter_units(specs, tensor_size):
    units = []
    for i, spec in enumerate(specs):
        units += [(i, j) for j in range(tensor_size)] if spec.kind == "own" else [(i, None)]
    return units


def scatter_kernel(specs, dp_size, tensor_size, *refs):
    count = len(specs)
    run = ScatterRun(
        specs, dp_size, tensor_size, refs[:count], refs[count : 2 * count], refs[2 * count :]
    )
    run.greet()
    run.begin()
    for unit, stage in run.steps():
        run.step(unit, stage)
    run.close()


def scatter_scratch(specs, arrays, dp_size, tensor_size):
    dp_bits = dp_size.bit_length() - 1
    scratch = []
    units = len(scatter_units(specs, tensor_size))
    pieces = [tensor_size if spec.kind == "own" else 1 for spec in specs]
    for spec, array, count in zip(specs, arrays, pieces):
        scratch.append(pltpu.VMEM((count, 2, dp_size // 2) + spec.part_shape, array.dtype))
    for spec, array, count in zip(specs, arrays, pieces):
        for stage in range(dp_bits):
            scratch.append(
                pltpu.VMEM((count, 2, dp_size >> (stage + 1)) + spec.part_shape, array.dtype)
            )
    for spec, array in zip(specs, arrays):
        if spec.kind != "dp":
            scratch.append(pltpu.VMEM((tensor_size, 2) + spec.cut_shape, array.dtype))
    dma = pltpu.SemaphoreType.DMA
    return scratch + [
        dma((units, 2, dp_size // 2)),
        dma((units, 2, dp_bits, dp_size // 2)),
        dma((units, 2, dp_bits, dp_size // 2)),
        dma((len(specs), 2, tensor_size)),
        dma((len(specs), 2, tensor_size)),
    ]


def scatter_shapes(specs):
    return [jax.ShapeDtypeStruct(spec.shape, jnp.float32) for spec in specs]


def scatter(specs, arrays, dp_size, tensor_size, collective_id):
    count = len(specs)
    return pl.pallas_call(
        functools.partial(scatter_kernel, specs, dp_size, tensor_size),
        out_shape=scatter_shapes(specs),
        in_specs=[ANY] * count,
        out_specs=[VMEM] * count,
        scratch_shapes=scatter_scratch(specs, arrays, dp_size, tensor_size),
        compiler_params=pltpu.CompilerParams(
            collective_id=collective_id, has_side_effects=True, vmem_limit_bytes=VMEM_LIMIT
        ),
    )(*arrays)


class ExchangeRun:
    def __init__(self, tensor_size, source, out, own_sem, send, recv):
        self.tensor_size, self.source, self.out = tensor_size, source, out
        self.own_sem, self.send, self.recv = own_sem, send, recv
        self.dp, self.tensor = lax.axis_index("dp"), lax.axis_index("tensor")

    def copy(self, other, slot):
        return pltpu.make_async_remote_copy(
            src_ref=self.source.at[other],
            dst_ref=self.out.at[slot],
            send_sem=self.send.at[other],
            recv_sem=self.recv.at[slot],
            device_id=(self.dp, other),
            device_id_type=MESH,
        )

    def own(self):
        return pltpu.make_async_copy(
            self.source.at[self.tensor], self.out.at[self.tensor], self.own_sem
        )

    def begin(self):
        for other in range(self.tensor_size):
            pl.when(other != self.tensor)(self.copy(other, self.tensor).start)
        self.own().start()

    def close(self):
        self.own().wait()
        for other in range(self.tensor_size):

            @pl.when(other != self.tensor)
            def _():
                self.copy(other, self.tensor).wait_send()
                self.copy(other, other).wait_recv()


def exchange_kernel(specs, dp_size, tensor_size, *refs):
    count = len(specs)
    run = ScatterRun(
        specs,
        dp_size,
        tensor_size,
        refs[1 : count + 1],
        refs[count + 2 : 2 * count + 2],
        refs[2 * count + 6 :],
    )
    blocks, summed = refs[0], refs[count + 1]
    landing = refs[2 * count + 2]
    exchange_run = ExchangeRun(tensor_size, blocks, landing, *refs[2 * count + 3 : 2 * count + 6])
    greet((run.dp, run.tensor, tensor_size), False, True, run.dp_bits)
    exchange_run.begin()
    run.begin()
    for unit, stage in run.steps():
        run.step(unit, stage)
    exchange_run.close()
    total = landing[0].astype(jnp.float32)
    for other in range(1, tensor_size):
        total = total + landing[other].astype(jnp.float32)
    summed[...] = total
    run.close()


def exchange(blocks, specs, arrays, sizes, collective_id):
    dp_size, tensor_size = sizes
    count = len(specs)
    dma = pltpu.SemaphoreType.DMA
    return pl.pallas_call(
        functools.partial(exchange_kernel, specs, dp_size, tensor_size),
        out_shape=[jax.ShapeDtypeStruct(blocks.shape[1:], jnp.float32)] + scatter_shapes(specs),
        in_specs=[ANY] * (count + 1),
        out_specs=[VMEM] * (count + 1),
        scratch_shapes=[
            pltpu.VMEM(blocks.shape, blocks.dtype),
            dma,
            dma((tensor_size,)),
            dma((tensor_size,)),
        ]
        + scatter_scratch(specs, arrays, dp_size, tensor_size),
        compiler_params=pltpu.CompilerParams(
            collective_id=collective_id, has_side_effects=True, vmem_limit_bytes=VMEM_LIMIT
        ),
    )(blocks, *arrays)


def lanes_of(shape):
    return lax.broadcasted_iota(jnp.int32, shape, len(shape) - 1)


def swap_halves(values):
    width = values.shape[-1]
    first = lanes_of(values.shape) % HEAD_DIM < HEAD_DIM // 2
    return jnp.where(
        first,
        pltpu.roll(values, width - HEAD_DIM // 2, 1),
        pltpu.roll(values, HEAD_DIM // 2, 1),
    )


def left_head(block, odd):
    moved = jnp.where(odd, pltpu.roll(block, HEAD_DIM, 1), block)
    return jnp.where(lanes_of(block.shape) < HEAD_DIM, moved, jnp.zeros_like(moved))


def allowed(keys, rows, start):
    key_at = lax.broadcasted_iota(jnp.int32, (keys, rows), 0)
    query_at = lax.broadcasted_iota(jnp.int32, (keys, rows), 1) + start
    return key_at <= query_at


def at_steps(actions, step, steps):
    places = [(min(steps - 1, int(time * steps)), action) for time, action in actions]
    for place in sorted({place for place, _ in places}):

        @pl.when(step == place)
        def _():
            for at, action in places:
                if at == place:
                    action()


def gather_plan(run):
    plan = [(0.0, run.greet), (0.0, run.begin)]
    for rank in range(1, 1 << run.dp_bits):
        if rank >> (run.dp_bits - 1):
            time = 1.0
        else:
            time = 0.45 + 0.35 * (rank.bit_count() - 1) / max(1, run.dp_bits - 2)
        plan += [(time, functools.partial(run.hop, n, rank)) for n in range(len(run.hyper))]
    for step in range(1, run.tensor_size):
        time = 0.95 * step / (run.tensor_size - 1)
        plan += [(time, functools.partial(run.line, i, step)) for i in run.lines]
    plan += [(1.0, functools.partial(run.end_line, i)) for i in run.lines]
    return sorted(plan, key=lambda entry: entry[0]) + [(1.0, run.close)]


def attend_kernel(group_pairs, pairs, specs, dp_size, tensor_size, *refs):
    count = len(specs)
    refs = list(refs)
    q_ref, cos_ref, sin_ref, k_ref, v_ref = (refs.pop(0) for _ in range(5))
    sources = [refs.pop(0) for _ in specs]
    o_ref, q_out, lse_ref = (refs.pop(0) for _ in range(3))
    outs = [refs.pop(0) for _ in specs]
    k_left, v_turned = (refs.pop(0) for _ in range(2))
    run = GatherRun(specs, dp_size, tensor_size, sources, outs, refs[:count], refs[count:])
    pair = pl.program_id(0)
    group = pair // group_pairs
    rows = q_ref.shape[0]
    start = lax.axis_index("tensor") * rows
    plan = gather_plan(run)
    at_steps([entry for entry in plan if entry[0] < 1.0], pair, pairs)

    @pl.when(pair % group_pairs == 0)
    def _():
        odd = group % 2 == 1
        k_left[...] = left_head(k_ref[...].astype(jnp.float32), odd).astype(jnp.bfloat16)
        v_turned[...] = left_head(v_ref[...].astype(jnp.float32), odd).T[:HEAD_DIM].astype(
            jnp.bfloat16
        )

    raw = q_ref[...]
    turned = (raw * cos_ref[...] + swap_halves(raw) * sin_ref[...]).astype(jnp.bfloat16)
    turned = turned.astype(jnp.float32) * HEAD_DIM ** (-0.5)
    q_out[...] = turned.astype(jnp.bfloat16)
    open_at = allowed(k_left.shape[0], rows, start)
    contexts = []
    for head in (0, 1):
        queries = (turned if head == 0 else pltpu.roll(turned, HEAD_DIM, 1)).astype(jnp.bfloat16)
        scores = product_right(k_left[...], queries)
        scores = jnp.where(open_at, scores, -1e30)
        top = jnp.max(scores, axis=0, keepdims=True)
        exponent = jnp.exp(scores - top)
        summed = jnp.sum(exponent, axis=0, keepdims=True)
        context = product(v_turned[...], exponent.astype(jnp.bfloat16))
        contexts.append(context * (1.0 / summed))
        lse_ref[0, head, :] = (top + jnp.log(summed))[0]
    o_ref[...] = jnp.concatenate(contexts, axis=0).T.astype(jnp.bfloat16)
    at_steps([entry for entry in plan if entry[0] >= 1.0], pair, pairs)


def attend(
    q_pre, cosines, sines, keys_values, head_count, group_heads, specs, arrays, sizes, collective_id
):
    rows, width = q_pre.shape
    length, both = keys_values.shape
    pairs, group_pairs = head_count // 2, group_heads // 2
    kv_blocks = both // 256
    wide = pl.BlockSpec((rows, 128), lambda p: (0, p))
    table = pl.BlockSpec((rows, 128), lambda p: (0, 0))
    held, sems = gather_scratch(specs, arrays, *sizes)
    return pl.pallas_call(
        functools.partial(attend_kernel, group_pairs, pairs, specs, *sizes),
        grid=(pairs,),
        out_shape=[
            jax.ShapeDtypeStruct((rows, width), jnp.bfloat16),
            jax.ShapeDtypeStruct((rows, width), jnp.bfloat16),
            jax.ShapeDtypeStruct((pairs, 2, rows), jnp.float32),
        ]
        + gather_shapes(specs, arrays),
        in_specs=[
            wide,
            table,
            table,
            pl.BlockSpec((length, 128), lambda p: (0, p // group_pairs // 2)),
            pl.BlockSpec((length, 128), lambda p: (0, kv_blocks + p // group_pairs // 2)),
        ]
        + [ANY] * len(specs),
        out_specs=[wide, wide, pl.BlockSpec((1, 2, rows), lambda p: (p, 0, 0))]
        + [ANY] * len(specs),
        scratch_shapes=[
            pltpu.VMEM((length, 128), jnp.bfloat16),
            pltpu.VMEM((HEAD_DIM, length), jnp.bfloat16),
        ]
        + held
        + sems,
        compiler_params=pltpu.CompilerParams(
            collective_id=collective_id, has_side_effects=True, vmem_limit_bytes=VMEM_LIMIT
        ),
        cost_estimate=pl.CostEstimate(
            flops=4 * rows * length * width, bytes_accessed=8 * rows * width, transcendentals=0
        ),
    )(q_pre, cosines, sines, keys_values, keys_values, *arrays)


def scatter_plan(run):
    plan = [(0.0, run.greet), (0.0, run.begin)]
    for unit, stage in run.steps():
        time = 0.15 + 0.1 * unit if stage == 0 else 0.55 + 0.35 * unit if stage == 1 else 1.0
        plan.append((min(time, 1.0), functools.partial(run.step, unit, stage)))
    return plan + [(1.0, run.close)]


def attend_back_kernel(group_pairs, pairs, specs, dp_size, tensor_size, *refs):
    refs = list(refs)
    q_ref, do_ref, lse_ref, cos_ref, sin_ref, k_ref, v_ref = (refs.pop(0) for _ in range(7))
    sources = [refs.pop(0) for _ in specs]
    dq_ref, dk_ref, dv_ref = (refs.pop(0) for _ in range(3))
    outs = [refs.pop(0) for _ in specs]
    k_left, v_left, k_turned, dk_sum, dv_sum = (refs.pop(0) for _ in range(5))
    run = ScatterRun(specs, dp_size, tensor_size, sources, outs, refs)
    plan = scatter_plan(run)
    at_steps([entry for entry in plan if entry[0] < 1.0], pl.program_id(0), pairs)
    pair = pl.program_id(0)
    group = pair // group_pairs
    odd = group % 2 == 1
    rows = q_ref.shape[0]
    start = lax.axis_index("tensor") * rows

    @pl.when(pair % group_pairs == 0)
    def _():
        left = left_head(k_ref[...].astype(jnp.float32), odd)
        k_left[...] = left.astype(jnp.bfloat16)
        k_turned[...] = left.T[:HEAD_DIM].astype(jnp.bfloat16)
        v_left[...] = left_head(v_ref[...].astype(jnp.float32), odd).astype(jnp.bfloat16)
        dk_sum[...] = jnp.zeros_like(dk_sum)
        dv_sum[...] = jnp.zeros_like(dv_sum)

    open_at = allowed(k_left.shape[0], rows, start)
    grads = []
    for head in (0, 1):
        queries, grad_out = q_ref[...], do_ref[...]
        if head == 1:
            queries = pltpu.roll(queries.astype(jnp.float32), HEAD_DIM, 1).astype(jnp.bfloat16)
            grad_out = pltpu.roll(grad_out.astype(jnp.float32), HEAD_DIM, 1).astype(jnp.bfloat16)
        scores = product_right(k_left[...], queries)
        scores = jnp.where(open_at, scores, -1e30)
        softmaxed = jnp.exp(scores - lse_ref[0, head, :][None, :])
        grad_soft = product_right(v_left[...], grad_out)
        mixed = softmaxed * grad_soft
        mixed_sum = jnp.sum(mixed, axis=0, keepdims=True)
        grad_scores = (mixed - softmaxed * mixed_sum).astype(jnp.bfloat16)
        dv_sum[...] += product(softmaxed.astype(jnp.bfloat16), grad_out)
        dk_sum[...] += product(grad_scores, queries)
        grads.append(product(k_turned[...], grad_scores))
    grad_q = jnp.concatenate(grads, axis=0).T * HEAD_DIM ** (-0.5)
    dq_ref[...] = (grad_q * cos_ref[...] - swap_halves(grad_q) * sin_ref[...]).astype(jnp.bfloat16)

    @pl.when(pair % group_pairs == group_pairs - 1)
    def _():
        for total, out in ((dk_sum, dk_ref), (dv_sum, dv_ref)):
            value = total[...]
            left = lanes_of(value.shape) < HEAD_DIM

            @pl.when(jnp.logical_not(odd))
            def _():
                out[...] = jnp.where(left, value, 0.0).astype(out.dtype)

            @pl.when(odd)
            def _():
                out[...] = jnp.where(
                    left, out[...].astype(jnp.float32), pltpu.roll(value, HEAD_DIM, 1)
                ).astype(out.dtype)
    at_steps([entry for entry in plan if entry[0] >= 1.0], pair, pairs)


def attend_back(
    queries,
    grad_context,
    lse,
    cosines,
    sines,
    keys_values,
    head_count,
    group_heads,
    specs,
    arrays,
    sizes,
    collective_id,
):
    rows, width = queries.shape
    length, both = keys_values.shape
    pairs, group_pairs = head_count // 2, group_heads // 2
    kv_blocks = both // 256
    wide = pl.BlockSpec((rows, 128), lambda p: (0, p))
    table = pl.BlockSpec((rows, 128), lambda p: (0, 0))
    kv_out = pl.BlockSpec((length, 128), lambda p: (0, p // group_pairs // 2))
    return pl.pallas_call(
        functools.partial(attend_back_kernel, group_pairs, pairs, specs, *sizes),
        grid=(pairs,),
        out_shape=[
            jax.ShapeDtypeStruct((rows, width), jnp.bfloat16),
            jax.ShapeDtypeStruct((length, both // 2), jnp.bfloat16),
            jax.ShapeDtypeStruct((length, both // 2), jnp.bfloat16),
        ]
        + scatter_shapes(specs),
        in_specs=[
            wide,
            wide,
            pl.BlockSpec((1, 2, rows), lambda p: (p, 0, 0)),
            table,
            table,
            pl.BlockSpec((length, 128), lambda p: (0, p // group_pairs // 2)),
            pl.BlockSpec((length, 128), lambda p: (0, kv_blocks + p // group_pairs // 2)),
        ]
        + [ANY] * len(specs),
        out_specs=[wide, kv_out, kv_out] + [VMEM] * len(specs),
        scratch_shapes=[
            pltpu.VMEM((length, 128), jnp.bfloat16),
            pltpu.VMEM((length, 128), jnp.bfloat16),
            pltpu.VMEM((HEAD_DIM, length), jnp.bfloat16),
            pltpu.VMEM((length, 128), jnp.float32),
            pltpu.VMEM((length, 128), jnp.float32),
        ]
        + scatter_scratch(specs, arrays, *sizes),
        compiler_params=pltpu.CompilerParams(
            collective_id=collective_id, has_side_effects=True, vmem_limit_bytes=VMEM_LIMIT
        ),
        cost_estimate=pl.CostEstimate(
            flops=10 * rows * length * width, bytes_accessed=8 * rows * width, transcendentals=0
        ),
    )(queries, grad_context, lse, cosines, sines, keys_values, keys_values, *arrays)


def block_at(place, tensor, tensor_size):
    last = tensor_size - 1
    pairs = jnp.minimum(tensor, last - tensor)
    near = lax.div(place + 1, 2)
    paired = jnp.where(lax.rem(place, 2) == 1, tensor - near, tensor + near)
    far = place - pairs
    lone = jnp.where(tensor > last - tensor, tensor - far, tensor + far)
    return jnp.where(place <= 2 * pairs, paired, lone)


def mlp_kernel(
    tensor_size,
    normed_ref,
    cot_low_ref,
    cot_high_ref,
    gate_ref,
    up_ref,
    down_ref,
    back_ref,
    y_ref,
    d_gate_ref,
    d_up_ref,
    d_down_ref,
    normed,
    cot,
    gate,
    up,
    down,
    hidden,
    d_gate,
    d_up,
    y_stage,
    stage,
    landing,
    load_sem,
    n_send,
    n_recv,
    y_sem,
    b_send,
    b_recv,
    out_sem,
):
    dp, tensor = lax.axis_index("dp"), lax.axis_index("tensor")
    rows, width = normed_ref.shape
    units = gate.shape[1]
    loads = [
        pltpu.make_async_copy(source, target, load_sem.at[i])
        for i, (source, target) in enumerate(
            (
                (normed_ref, normed.at[tensor]),
                (gate_ref, gate),
                (up_ref, up),
                (down_ref, down),
                (cot_low_ref, cot.at[:, : cot_low_ref.shape[1]]),
                (cot_high_ref, cot.at[:, cot_low_ref.shape[1] :]),
            )
        )
    ]
    for load in loads:
        load.start()
    greet((dp, tensor, tensor_size), False, True, 0)
    has = [tensor + 1 < tensor_size, tensor > 0]

    def n_copy(block, way, source=None):
        return pltpu.make_async_remote_copy(
            src_ref=normed.at[block] if source is None else source,
            dst_ref=normed.at[block],
            send_sem=n_send.at[way, block],
            recv_sem=n_recv.at[block],
            device_id=(dp, tensor + 1 if way == 0 else tensor - 1),
            device_id_type=MESH,
        )

    for way in (0, 1):
        pl.when(has[way])(n_copy(tensor, way, normed_ref).start)
    landing[tensor] = jnp.zeros((rows, width), landing.dtype)

    def pump(distance):
        for way, block in ((0, tensor - distance), (1, tensor + distance)):

            @pl.when((block >= 0) & (block < tensor_size))
            def _():
                n_copy(block, way).wait_recv()
                pl.when(has[way])(n_copy(block, way).start)

    def distance_at(place):
        return jnp.abs(block_at(place, tensor, tensor_size) - tensor)

    inner = (tensor > 0) & (tensor + 1 < tensor_size)

    def b_copy(block, slot):
        return pltpu.make_async_remote_copy(
            src_ref=stage.at[block],
            dst_ref=landing.at[slot],
            send_sem=b_send.at[block],
            recv_sem=b_recv.at[slot],
            device_id=(dp, block),
            device_id_type=MESH,
        )

    def y_copy(block, slot):
        return pltpu.make_async_copy(y_stage.at[slot], y_ref.at[block], y_sem.at[slot])

    for load in loads[:3]:
        load.wait()

    def chunk(place, carry):
        block = block_at(place, tensor, tensor_size)
        fresh = (place >= 1) & (distance_at(place) != distance_at(place - 1))

        @pl.when(fresh & jnp.logical_not((place >= 2) & inner))
        def _():
            pump(distance_at(place))

        rows_in = normed[block]
        gate_pre = product(rows_in, gate[...])
        upward = product(rows_in, up[...])

        @pl.when((place >= 1) & (place + 1 < tensor_size) & inner)
        def _():
            @pl.when(distance_at(place + 1) != distance_at(place))
            def _():
                pump(distance_at(place + 1))

        @pl.when(place == 0)
        def _():
            for load in loads[3:]:
                load.wait()

        sigmoid = 1.0 / (1.0 + jnp.exp(-gate_pre))
        silu = gate_pre * sigmoid
        active = (silu * upward).astype(jnp.bfloat16)
        hidden[block] = active
        slot = lax.rem(place, 2)

        @pl.when(place >= 2)
        def _():
            y_copy(block, slot).wait()

        y_stage[slot] = product(active, down[...]).astype(jnp.bfloat16)
        y_copy(block, slot).start()
        grad_hidden = product_right(cot[block], down[...])
        low_gate = (
            grad_hidden * upward * sigmoid * (1.0 + gate_pre * (1.0 - sigmoid))
        ).astype(jnp.bfloat16)
        low_up = (grad_hidden * silu).astype(jnp.bfloat16)
        d_gate[block] = low_gate
        d_up[block] = low_up
        back = product_right(low_gate, gate[...]) + product_right(low_up, up[...])

        @pl.when(block == tensor)
        def _():
            back_ref[...] = back

        @pl.when(block != tensor)
        def _():
            stage[block] = back.astype(stage.dtype)
            b_copy(block, tensor).start()

        return carry

    lax.fori_loop(0, tensor_size, chunk, 0)
    for slot in range(2):
        y_copy(0, slot).wait()

    all_rows = tensor_size * rows

    def weight_grad(left, right, out, out_hbm, sem):
        extent = left.shape[2]
        tile = 256 if extent % 256 == 0 else 128 if extent % 128 == 0 else extent

        def body(step, carry):
            at = pl.ds(pl.multiple_of(step * tile, tile), tile)
            columns = left[:, :, at].reshape(all_rows, tile)
            out[at, :] = product_left(columns, right[...].reshape(all_rows, -1)).astype(out.dtype)
            return carry

        lax.fori_loop(0, extent // tile, body, 0)
        pltpu.make_async_copy(out, out_hbm, sem).start()

    weight_grad(hidden, cot, down, d_down_ref, out_sem.at[0])
    weight_grad(normed, d_gate, gate, d_gate_ref, out_sem.at[1])
    weight_grad(normed, d_up, up, d_up_ref, out_sem.at[2])

    for other in range(tensor_size):

        @pl.when(other != tensor)
        def _():
            b_copy(other, other).wait_recv()

    slab = 16

    def add_slab(step, carry):
        at = pl.ds(pl.multiple_of(step * slab, slab), slab)
        total = back_ref[at, :]
        for other in range(tensor_size):
            total = total + landing[other, at, :].astype(jnp.float32)
        back_ref[at, :] = total
        return carry

    lax.fori_loop(0, rows // slab, add_slab, 0)
    pltpu.make_async_copy(down, d_down_ref, out_sem.at[0]).wait()
    pltpu.make_async_copy(gate, d_gate_ref, out_sem.at[1]).wait()
    pltpu.make_async_copy(up, d_up_ref, out_sem.at[2]).wait()
    for other in range(tensor_size):

        @pl.when(other != tensor)
        def _():
            b_copy(other, tensor).wait_send()

        for way in (0, 1):
            sent = has[way] & ((other <= tensor) if way == 0 else (other >= tensor))
            pl.when(sent)(n_copy(other, way).wait_send)


def feed_forward(normed, cot_low, cot_high, gate, up, down, tensor_size, collective_id):
    rows, width = normed.shape
    units = gate.shape[1]
    low = jnp.bfloat16
    tokens = (tensor_size, rows, width)
    inner = (tensor_size, rows, units)
    dma = pltpu.SemaphoreType.DMA
    return pl.pallas_call(
        functools.partial(mlp_kernel, tensor_size),
        out_shape=[
            jax.ShapeDtypeStruct((rows, width), jnp.float32),
            jax.ShapeDtypeStruct(tokens, low),
            jax.ShapeDtypeStruct(gate.shape, low),
            jax.ShapeDtypeStruct(up.shape, low),
            jax.ShapeDtypeStruct(down.shape, low),
        ],
        in_specs=[ANY] * 6,
        out_specs=[VMEM] + [ANY] * 4,
        scratch_shapes=[
            pltpu.VMEM(tokens, low),
            pltpu.VMEM(tokens, low),
            pltpu.VMEM(gate.shape, low),
            pltpu.VMEM(up.shape, low),
            pltpu.VMEM(down.shape, low),
            pltpu.VMEM(inner, low),
            pltpu.VMEM(inner, low),
            pltpu.VMEM(inner, low),
            pltpu.VMEM((2, rows, width), low),
            pltpu.VMEM(tokens, low),
            pltpu.VMEM(tokens, low),
            dma((6,)),
            dma((2, tensor_size)),
            dma((tensor_size,)),
            dma((2,)),
            dma((tensor_size,)),
            dma((tensor_size,)),
            dma((3,)),
        ],
        compiler_params=pltpu.CompilerParams(
            collective_id=collective_id, has_side_effects=True, vmem_limit_bytes=60 * 2**20
        ),
        cost_estimate=pl.CostEstimate(
            flops=18 * tensor_size * rows * width * units,
            bytes_accessed=8 * width * units,
            transcendentals=0,
        ),
    )(
        normed,
        cot_low.reshape(tensor_size, -1, width),
        cot_high.reshape(tensor_size, -1, width),
        gate,
        up,
        down,
    )


def rope_tables(rows, tensor):
    halved = HEAD_DIM // 2
    freqs = theta_base ** (-2.0 * jnp.arange(halved, dtype=jnp.float32) / HEAD_DIM)
    places = (tensor * rows + jnp.arange(rows)).astype(jnp.float32)
    angles = places[:, None] * freqs[None, :]
    cosines, sines = jnp.cos(angles), jnp.sin(angles)
    return (
        jnp.concatenate([cosines, cosines] * 2, axis=1),
        jnp.concatenate([-sines, sines] * 2, axis=1),
    )


def turn_heads(values, cosines, sines):
    rows, width = values.shape
    parts = values.reshape(rows, width // HEAD_DIM, 2, HEAD_DIM // 2)
    swapped = parts[:, :, ::-1, :].reshape(rows, width)
    repeat = width // 128
    return values * jnp.tile(cosines, (1, repeat)) + swapped * jnp.tile(sines, (1, repeat))


def start_row(dp, size):
    return pl.multiple_of(dp * size, size)


def on_device(
    dp_size,
    tensor_size,
    tokens,
    attn_gain,
    w_query,
    w_key,
    w_value,
    w_out,
    mlp_gain,
    w_gate,
    w_up,
    w_down,
    cotangent,
):
    tensor_index = lax.axis_index("tensor")
    rows, width = tokens.shape
    heads = w_query.shape[1] * tensor_size // HEAD_DIM
    kv_width = w_key.shape[1]
    kv_heads = kv_width // HEAD_DIM
    group_heads = heads // kv_heads
    q_rows, q_cols = w_query.shape
    kv_rows = w_key.shape[0]
    o_rows, o_cols = w_out.shape
    gain_part = attn_gain.shape[0]
    call = functools.partial(gather, dp_size=dp_size, tensor_size=tensor_size)

    key_value = jnp.concatenate([w_key, w_value], axis=1)
    gains = jnp.zeros((16, 128), jnp.bfloat16)
    gains = gains.at[0, :gain_part].set(attn_gain).at[1, :gain_part].set(mlp_gain)
    query_spec = Gather(
        (width, heads * HEAD_DIM),
        lambda ref, dp, t: ref.at[
            pl.ds(start_row(dp, q_rows), q_rows), pl.ds(start_row(t, q_cols), q_cols)
        ],
        lambda ref, dp, half: ref.at[
            pl.ds(pl.multiple_of(dp * q_rows + half * (q_rows // 2), q_rows // 2), q_rows // 2), :
        ],
    )
    kv_all_rows = kv_rows * tensor_size
    kv_spec = Gather(
        (width, 2 * kv_width),
        lambda ref, dp, t: ref.at[pl.ds(start_row(dp * tensor_size + t, kv_rows), kv_rows), :],
        lambda ref, dp, half: ref.at[
            pl.ds(
                pl.multiple_of(dp * kv_all_rows + half * (kv_all_rows // 2), kv_all_rows // 2),
                kv_all_rows // 2,
            ),
            :,
        ],
    )
    gain_spec = Gather(
        (dp_size * tensor_size * 16, 128),
        lambda ref, dp, t: ref.at[pl.ds(start_row(dp * tensor_size + t, 16), 16), :],
        lambda ref, dp, half: ref.at[
            pl.ds(
                pl.multiple_of((2 * dp + half) * tensor_size * 8, tensor_size * 8),
                tensor_size * 8,
            ),
            :,
        ],
    )
    out_spec = Gather(
        (heads * HEAD_DIM, width),
        lambda ref, dp, t: ref.at[
            pl.ds(start_row(t, o_rows), o_rows), pl.ds(start_row(dp, o_cols), o_cols)
        ],
        lambda ref, dp, half: ref.at[
            pl.ds(half * (heads * HEAD_DIM // 2), heads * HEAD_DIM // 2),
            pl.ds(start_row(dp, o_cols), o_cols),
        ],
    )
    row_spec = lambda shape: Gather(
        (tensor_size * shape[0], shape[1]),
        lambda ref, dp, t: ref.at[pl.ds(start_row(t, shape[0]), shape[0]), :],
    )
    up_rows, units = w_gate.shape
    column_spec = Gather(
        (width, units),
        lambda ref, dp, t: ref.at[pl.ds(start_row(dp, up_rows), up_rows), :],
        lambda ref, dp, half: ref.at[
            pl.ds(
                pl.multiple_of(dp * up_rows + half * (up_rows // 2), up_rows // 2), up_rows // 2
            ),
            :,
        ],
        False,
    )
    down_cols = w_down.shape[1]
    down_spec = Gather(
        (units, width),
        lambda ref, dp, t: ref.at[:, pl.ds(start_row(dp, down_cols), down_cols)],
        lambda ref, dp, half: ref.at[
            pl.ds(half * (units // 2), units // 2), pl.ds(start_row(dp, down_cols), down_cols)
        ],
        False,
    )
    low_rows = rows // 4 * 3
    cot_low_spec, cot_high_spec = row_spec((low_rows, width)), row_spec((rows - low_rows, width))
    sizes = (dp_size, tensor_size)
    query_full, key_value_full, gains_full, gate_full, cot_low = call(
        [query_spec, kv_spec, gain_spec, column_spec, cot_low_spec],
        [w_query, key_value, gains, w_gate, cotangent[:low_rows]],
        collective_id=1,
        slow=(4,),
    )
    down_late, query_full = lax.optimization_barrier((w_down, query_full))
    down_full = lax.all_gather(down_late, "dp", axis=1, tiled=True)
    gains_full = gains_full.reshape(-1, 16, 128)[:, :2, :gain_part].astype(jnp.float32)
    gain_first = gains_full[:, 0].reshape(width)
    gain_second = gains_full[:, 1].reshape(width)
    cosines, sines = rope_tables(rows, tensor_index)

    residual = tokens.astype(jnp.float32)
    scale_first = lax.rsqrt(jnp.mean(residual * residual, axis=-1, keepdims=True) + epsilon)
    unit_first = residual * scale_first
    normed_first = (unit_first * gain_first).astype(jnp.bfloat16)
    kv_pre = product(normed_first, key_value_full)
    kv_own = jnp.concatenate(
        [turn_heads(kv_pre[:, :kv_width], cosines, sines), kv_pre[:, kv_width:]], axis=1
    ).astype(jnp.bfloat16)
    query_pre = product(normed_first, query_full)
    kv_all, out_full = call([row_spec(kv_own.shape), out_spec], [kv_own, w_out], collective_id=2)
    context, queries, log_sums, up_full, cot_high = attend(
        query_pre,
        cosines,
        sines,
        kv_all,
        heads,
        group_heads,
        [column_spec, cot_high_spec],
        [w_up, cotangent[low_rows:]],
        sizes,
        8,
    )
    middle = residual + product(context, out_full)
    scale_second = lax.rsqrt(jnp.mean(middle * middle, axis=-1, keepdims=True) + epsilon)
    unit_second = middle * scale_second
    normed_own = (unit_second * gain_second).astype(jnp.bfloat16)
    back_second, mlp_part, grad_gate_w, grad_up_w, grad_down_w = feed_forward(
        normed_own, cot_low, cot_high, gate_full, up_full, down_full, tensor_size, 3
    )
    mlp_rows = lax.psum_scatter(
        mlp_part.reshape(tensor_size * rows, width), "tensor", scatter_dimension=0, tiled=True
    )
    grad_gain_second = jnp.sum(back_second * unit_second, axis=0)
    grad_middle = cotangent.astype(jnp.float32) + norm_back(
        back_second, unit_second, scale_second, gain_second
    )
    middle_low = grad_middle.astype(jnp.bfloat16)
    grad_context = product_right(middle_low, out_full).astype(jnp.bfloat16)
    grad_out_w = product_left(context, middle_low).astype(jnp.bfloat16)
    query_scatter = Scatter(
        "own",
        (q_rows, q_cols),
        lambda ref, dp, half, j: ref.at[
            pl.ds(pl.multiple_of(dp * q_rows + half * (q_rows // 2), q_rows // 2), q_rows // 2),
            pl.ds(j * q_cols, q_cols),
        ],
        (q_rows // 2, q_cols),
        lambda ref, half: ref.at[pl.ds(half * (q_rows // 2), q_rows // 2), :],
    )
    kv_scatter = Scatter(
        "cut",
        (kv_rows, 2 * kv_width),
        lambda ref, dp, half, j: ref.at[
            pl.ds(dp * tensor_size, tensor_size), :, pl.ds(half * kv_width, kv_width)
        ],
        (tensor_size, kv_rows, kv_width),
        lambda ref, half: ref.at[:, pl.ds(half * kv_width, kv_width)],
        lambda ref, j: ref.at[j],
        (kv_rows, kv_width),
    )
    out_scatter = Scatter(
        "own",
        (o_rows, o_cols),
        lambda ref, dp, half, j: ref.at[
            pl.ds(j * o_rows + half * (o_rows // 2), o_rows // 2),
            pl.ds(start_row(dp, o_cols), o_cols),
        ],
        (o_rows // 2, o_cols),
        lambda ref, half: ref.at[pl.ds(half * (o_rows // 2), o_rows // 2), :],
    )
    gain_scatter = Scatter(
        "cut",
        (16, 128),
        lambda ref, dp, half, j: ref.at[
            pl.ds(dp * tensor_size, tensor_size), pl.ds(half * 8, 8), :
        ],
        (tensor_size, 8, 128),
        lambda ref, half: ref.at[pl.ds(half * 8, 8), :],
        lambda ref, j: ref.at[j],
        (8, 128),
    )
    column_scatter = Scatter(
        "dp",
        (up_rows, units),
        lambda ref, dp, half, j: column_spec.half(ref, dp, half),
        (up_rows // 2, units),
        lambda ref, half: ref.at[pl.ds(half * (up_rows // 2), up_rows // 2), :],
    )
    down_scatter = Scatter(
        "dp",
        (units, down_cols),
        lambda ref, dp, half, j: down_spec.half(ref, dp, half),
        (units // 2, down_cols),
        lambda ref, half: ref.at[pl.ds(half * (units // 2), units // 2), :],
    )
    grad_queries, grad_keys, grad_values, sum_gate, sum_up = attend_back(
        queries,
        grad_context,
        log_sums,
        cosines,
        sines,
        kv_all,
        heads,
        group_heads,
        [column_scatter, column_scatter],
        [grad_gate_w, grad_up_w],
        sizes,
        7,
    )
    grad_kv = jnp.concatenate([grad_keys, grad_values], axis=1)
    grad_kv_own, sum_out, sum_down = exchange(
        grad_kv.reshape(tensor_size, rows, 2 * kv_width),
        [out_scatter, down_scatter],
        [grad_out_w, grad_down_w],
        sizes,
        5,
    )
    grad_kv_own = jnp.concatenate(
        [turn_heads(grad_kv_own[:, :kv_width], cosines, -sines), grad_kv_own[:, kv_width:]], axis=1
    ).astype(jnp.bfloat16)
    grad_query_w = product_left(normed_first, grad_queries).astype(jnp.bfloat16)
    grad_kv_w = product_left(normed_first, grad_kv_own).astype(jnp.bfloat16)
    back_first = product_right(grad_queries, query_full) + product_right(
        grad_kv_own, key_value_full
    )
    grad_gain_first = jnp.sum(back_first * unit_first, axis=0)
    grad_tokens = grad_middle + norm_back(back_first, unit_first, scale_first, gain_first)

    grad_gains = jnp.zeros((dp_size * tensor_size, 16, 128), jnp.float32)
    grad_gains = grad_gains.at[:, 0, :gain_part].set(grad_gain_first.reshape(-1, gain_part))
    grad_gains = grad_gains.at[:, 8, :gain_part].set(grad_gain_second.reshape(-1, gain_part))
    sum_query, sum_kv, sum_gains = scatter(
        [query_scatter, kv_scatter, gain_scatter],
        [
            grad_query_w,
            grad_kv_w.reshape(dp_size * tensor_size, kv_rows, 2 * kv_width),
            grad_gains,
        ],
        dp_size,
        tensor_size,
        6,
    )
    middle, mlp_rows, sum_query = lax.optimization_barrier((middle, mlp_rows, sum_query))
    output = (middle + mlp_rows.astype(jnp.float32)).astype(jnp.bfloat16)
    return (
        output,
        grad_tokens,
        sum_gains[0, :gain_part],
        sum_query,
        sum_kv[:, :kv_width],
        sum_kv[:, kv_width:],
        sum_out,
        sum_gains[8, :gain_part],
        sum_gate,
        sum_up,
        sum_down,
    )


def solution(mesh):
    placed = (
        P(("dp", "tensor"), None),
        P(("dp", "tensor")),
        P("dp", "tensor"),
        P(("dp", "tensor"), None),
        P(("dp", "tensor"), None),
        P("tensor", "dp"),
        P(("dp", "tensor")),
        P("dp", "tensor"),
        P("dp", "tensor"),
        P("tensor", "dp"),
        P(("dp", "tensor"), None),
    )
    return jax.shard_map(
        functools.partial(on_device, mesh.shape["dp"], mesh.shape["tensor"]),
        mesh=mesh,
        in_specs=placed,
        out_specs=(
            P(("dp", "tensor"), None),
            P(("dp", "tensor"), None),
            P(("dp", "tensor")),
            P("dp", "tensor"),
            P(("dp", "tensor"), None),
            P(("dp", "tensor"), None),
            P("tensor", "dp"),
            P(("dp", "tensor")),
            P("dp", "tensor"),
            P("dp", "tensor"),
            P("tensor", "dp"),
        ),
        check_vma=False,
    )
```

```python
import functools

import jax
import jax.numpy as jnp
from jax import lax
from jax.experimental import pallas as pl
from jax.experimental.pallas import tpu as pltpu
from jax.sharding import PartitionSpec as P

HEAD_DIM = 64
SEQLEN = 1024
MESH = pl.DeviceIdType.MESH
ANY = pl.BlockSpec(memory_space=pl.ANY)
VMEM = pl.BlockSpec(memory_space=pltpu.VMEM)
VMEM_LIMIT = 56 * 2**20

epsilon = 1e-05
theta_base = 10000.0


def product(left, right):
    return jnp.dot(left, right, preferred_element_type=jnp.float32)


def product_left(left, right):
    return lax.dot_general(
        left, right, (((0,), (0,)), ((), ())), preferred_element_type=jnp.float32
    )


def product_right(left, right):
    return lax.dot_general(
        left, right, (((1,), (1,)), ((), ())), preferred_element_type=jnp.float32
    )


def norm_back(grad_normed, unit_rows, scale_rows, gain):
    scaled_grad = grad_normed * gain
    return scale_rows * (
        scaled_grad - unit_rows * jnp.mean(scaled_grad * unit_rows, axis=-1, keepdims=True)
    )


def flip(index, bit):
    size = 1 << bit
    return index + size * (1 - 2 * lax.rem(lax.div(index, size), 2))


def masked(index, bits, rank):
    for place, bit in enumerate(bits):
        if rank >> place & 1:
            index = flip(index, bit)
    return index


def orders(bit_count, core_last):
    up = list(range(1, bit_count))
    down = up[::-1]
    return [up + [0], down + [0]] if core_last else [[0] + up, [0] + down]


def greet(spots, near, all_tensor, dp_bits):
    dp, tensor, tensor_size = spots
    barrier = pltpu.get_barrier_semaphore()

    def signal(where):
        pl.semaphore_signal(barrier, inc=1, device_id=where, device_id_type=MESH)

    peers = dp_bits
    for bit in range(dp_bits):
        signal((flip(dp, bit), tensor))
    if all_tensor:
        peers += tensor_size - 1
        for other in range(tensor_size):
            pl.when(other != tensor)(functools.partial(signal, (dp, other)))
    elif near:
        below, above = tensor > 0, tensor + 1 < tensor_size
        pl.when(below)(functools.partial(signal, (dp, tensor - 1)))
        pl.when(above)(functools.partial(signal, (dp, tensor + 1)))
        peers = peers + below.astype(jnp.int32) + above.astype(jnp.int32)
    pl.semaphore_wait(barrier, peers)


class Gather:
    def __init__(self, shape, slot, half=None, line=True):
        self.shape, self.slot, self.half, self.line = shape, slot, half, line


class GatherRun:
    def __init__(self, specs, dp_size, tensor_size, sources, outs, held, sems):
        self.specs, self.sources, self.outs, self.held = specs, sources, outs, held
        self.own_sem, self.z_send, self.z_recv, self.h_send, self.h_recv = sems
        self.dp, self.tensor = lax.axis_index("dp"), lax.axis_index("tensor")
        self.tensor_size, self.dp_bits = tensor_size, dp_size.bit_length() - 1
        self.order = orders(self.dp_bits, True)
        self.hyper = [i for i, spec in enumerate(specs) if spec.half is not None]
        self.lines = [i for i, spec in enumerate(specs) if spec.line]
        self.early = [n for n, i in enumerate(self.hyper) if not specs[i].line]
        self.late = [n for n, i in enumerate(self.hyper) if specs[i].line]
        self.can = [self.tensor + 1 < tensor_size, self.tensor > 0]

    def greet(self):
        greet(
            (self.dp, self.tensor, self.tensor_size),
            bool(self.lines),
            False,
            self.dp_bits if self.hyper else 0,
        )

    def z_copy(self, i, block, way, source=None):
        slot = self.specs[i].slot(self.outs[i], self.dp, block)
        return pltpu.make_async_remote_copy(
            src_ref=slot if source is None else source,
            dst_ref=slot,
            send_sem=self.z_send.at[i, way, block],
            recv_sem=self.z_recv.at[i, block],
            device_id=(self.dp, self.tensor + 1 if way == 0 else self.tensor - 1),
            device_id_type=MESH,
        )

    def own(self, i):
        slot = self.specs[i].slot(self.outs[i], self.dp, self.tensor)
        return pltpu.make_async_copy(self.held[i], slot, self.own_sem.at[i])

    def begin_line(self, i):
        for way in (0, 1):
            pl.when(self.can[way])(self.z_copy(i, self.tensor, way, self.sources[i]).start)

    def begin(self, slow=()):
        loads = [
            pltpu.make_async_copy(source, held, self.own_sem.at[i])
            for i, (source, held) in enumerate(zip(self.sources, self.held))
        ]
        for load in loads:
            load.start()
        for i in self.lines:
            if i not in slow:
                self.begin_line(i)
        for i, load in enumerate(loads):
            load.wait()
            self.own(i).start()
        for n in self.early:
            self.own(self.hyper[n]).wait()
            self.hop(n, 0)

    def line(self, i, step):
        for way, block in ((0, self.tensor - step), (1, self.tensor + step)):

            @pl.when((block >= 0) & (block < self.tensor_size))
            def _():
                self.z_copy(i, block, way).wait_recv()
                pl.when(self.can[way])(self.z_copy(i, block, way).start)

    def part(self, n, half, rank):
        i = self.hyper[n]
        return self.specs[i].half(self.outs[i], masked(self.dp, self.order[half], rank), half)

    def h_copy(self, n, half, rank, place):
        return pltpu.make_async_remote_copy(
            src_ref=self.part(n, half, rank),
            dst_ref=self.part(n, half, rank),
            send_sem=self.h_send.at[n, half, rank, place],
            recv_sem=self.h_recv.at[n, half, rank | 1 << place],
            device_id=(flip(self.dp, self.order[half][place]), self.tensor),
            device_id_type=MESH,
        )

    def hop(self, n, rank):
        for half in (0, 1):
            if rank:
                wait_part(
                    self.part(n, half, rank),
                    self.h_recv.at[n, half, rank],
                    self.h_send.at[n, half, 0, 0],
                    (flip(self.dp, 0), self.tensor),
                )
            for place in range(rank.bit_length(), self.dp_bits):
                self.h_copy(n, half, rank, place).start()

    def end_line(self, i):
        self.own(i).wait()

    def close(self):
        for rank in range(1 << self.dp_bits):
            for n in range(len(self.hyper)):
                for half in (0, 1):
                    for place in range(rank.bit_length(), self.dp_bits):
                        self.h_copy(n, half, rank, place).wait_send()
        for i in self.lines:
            for block in range(self.tensor_size):
                for way in (0, 1):
                    sent = self.can[way] & (
                        (block <= self.tensor) if way == 0 else (block >= self.tensor)
                    )
                    pl.when(sent)(self.z_copy(i, block, way).wait_send)


def gather_scratch(specs, arrays, dp_size, tensor_size):
    count = len(specs)
    hyper = max(1, sum(spec.half is not None for spec in specs))
    dp_bits = dp_size.bit_length() - 1
    return [pltpu.VMEM(array.shape, array.dtype) for array in arrays], [
        pltpu.SemaphoreType.DMA((count,)),
        pltpu.SemaphoreType.DMA((count, 2, tensor_size)),
        pltpu.SemaphoreType.DMA((count, tensor_size)),
        pltpu.SemaphoreType.DMA((hyper, 2, dp_size, max(dp_bits, 1))),
        pltpu.SemaphoreType.DMA((hyper, 2, dp_size)),
    ]


def wait_part(part, recv_sem, send_sem, device):
    pltpu.make_async_remote_copy(
        src_ref=part,
        dst_ref=part,
        send_sem=send_sem,
        recv_sem=recv_sem,
        device_id=device,
        device_id_type=MESH,
    ).wait_recv()


def gather_shapes(specs, arrays):
    return [jax.ShapeDtypeStruct(spec.shape, array.dtype) for spec, array in zip(specs, arrays)]


class Scatter:
    def __init__(self, kind, shape, part, part_shape, place, cut=None, cut_shape=None):
        self.kind, self.shape, self.part, self.part_shape = kind, shape, part, part_shape
        self.place, self.cut = place, cut
        self.cut_shape = part_shape if kind == "own" else cut_shape


def add_into(total, extra):
    shape = total.shape
    rows = shape[-2]
    slab = min(16, rows)
    if len(shape) == 2:

        def body(step, carry):
            at = pl.ds(pl.multiple_of(step * slab, slab), slab)
            total[at, :] = (
                total[at, :].astype(jnp.float32) + extra[at, :].astype(jnp.float32)
            ).astype(total.dtype)
            return carry

        lax.fori_loop(0, rows // slab, body, 0, unroll=2 if (rows // slab) % 2 == 0 else 1)
    else:
        for lead in range(shape[0]):
            add_into(total.at[lead], extra.at[lead])


class ScatterRun:
    def __init__(self, specs, dp_size, tensor_size, sources, outs, scratch, in_place=False):
        scratch = list(scratch)
        self.specs, self.sources, self.outs = specs, sources, outs
        self.tensor_size, self.dp_bits = tensor_size, dp_size.bit_length() - 1
        self.in_place = in_place
        self.total = None if in_place else [scratch.pop(0) for _ in specs]
        self.landing = [[scratch.pop(0) for _ in range(self.dp_bits)] for _ in specs]
        self.shares = [scratch.pop(0) if spec.kind != "dp" else None for spec in specs]
        self.own_sem, self.send, self.recv, self.z_send, self.z_recv = scratch
        self.dp, self.tensor = lax.axis_index("dp"), lax.axis_index("tensor")
        self.order = orders(self.dp_bits, False)
        self.units = scatter_units(specs, tensor_size)

    def greet(self):
        cuts = any(spec.kind != "dp" for spec in self.specs)
        greet((self.dp, self.tensor, self.tensor_size), False, cuts, self.dp_bits)

    def slots(self, stage):
        return range(1 << (self.dp_bits - 1 - stage))

    def part(self, unit, half, rank):
        i, owner = self.units[unit]
        place = masked(self.dp, self.order[half], rank)
        return self.specs[i].part(self.sources[i], place, half, owner or 0)

    def sum_at(self, unit, half, slot):
        i, owner = self.units[unit]
        if self.in_place:
            return self.part(unit, half, 2 * slot)
        return self.total[i].at[owner or 0, half, slot]

    def own_copy(self, unit, half, slot):
        return pltpu.make_async_copy(
            self.part(unit, half, 2 * slot),
            self.sum_at(unit, half, slot),
            self.own_sem.at[unit, half, slot],
        )

    def landed(self, unit, half, stage, slot):
        i, owner = self.units[unit]
        return self.landing[i][stage].at[owner or 0, half, slot]

    def copy(self, unit, half, stage, slot):
        if stage == 0:
            source = self.part(unit, half, 2 * slot + 1)
        else:
            source = self.sum_at(unit, half, (2 * slot + 1) << (stage - 1))
        return pltpu.make_async_remote_copy(
            src_ref=source,
            dst_ref=self.landed(unit, half, stage, slot),
            send_sem=self.send.at[unit, half, stage, slot],
            recv_sem=self.recv.at[unit, half, stage, slot],
            device_id=(flip(self.dp, self.order[half][stage]), self.tensor),
            device_id_type=MESH,
        )

    def begin_unit(self, unit):
        for slot in self.slots(0):
            for half in (0, 1):
                self.copy(unit, half, 0, slot).start()
                if not self.in_place:
                    self.own_copy(unit, half, slot).start()

    def begin(self):
        for unit in range(len(self.units)):
            self.begin_unit(unit)

    def z_copy(self, unit, half, other, slot):
        i, owner = self.units[unit]
        spec, total = self.specs[i], self.sum_at(unit, half, 0)
        return pltpu.make_async_remote_copy(
            src_ref=total if spec.kind == "own" else spec.cut(total, other),
            dst_ref=self.shares[i].at[slot, half],
            send_sem=self.z_send.at[i, half, other],
            recv_sem=self.z_recv.at[i, half, slot],
            device_id=(self.dp, other),
            device_id_type=MESH,
        )

    def others(self, unit):
        owner = self.units[unit][1]
        return range(self.tensor_size) if owner is None else [owner]

    def step(self, unit, stage):
        i, owner = self.units[unit]
        spec = self.specs[i]
        if stage < self.dp_bits:
            for slot in sorted(self.slots(stage), key=lambda s: -(s & 1)):
                for half in (0, 1):
                    if stage == 0 and not self.in_place:
                        self.own_copy(unit, half, slot).wait()
                    self.copy(unit, half, stage, slot).wait_recv()
                    add_into(
                        self.sum_at(unit, half, slot << stage),
                        self.landed(unit, half, stage, slot),
                    )
                    if slot & 1:
                        self.copy(unit, half, stage + 1, slot >> 1).start()
            return
        for half in (0, 1):
            total = self.sum_at(unit, half, 0)
            if spec.kind == "dp":
                spec.place(self.outs[i], half)[...] = total[...].astype(jnp.float32)
                continue
            for other in self.others(unit):

                @pl.when(other != self.tensor)
                def _():
                    self.z_copy(unit, half, other, self.tensor).start()

                @pl.when(other == self.tensor)
                def _():
                    mine = total if spec.kind == "own" else spec.cut(total, other)
                    self.shares[i][other, half] = mine[...]

    def steps(self):
        count = len(self.units)
        return [
            (unit, turn - unit)
            for turn in range(count + self.dp_bits)
            for unit in range(count)
            if 0 <= turn - unit <= self.dp_bits
        ]

    def close(self):
        for i, spec in enumerate(self.specs):
            if spec.kind == "dp":
                continue
            unit = [u for u, (at, owner) in enumerate(self.units) if at == i][0]
            for half in (0, 1):
                for other in range(self.tensor_size):

                    @pl.when(other != self.tensor)
                    def _():
                        self.z_copy(unit, half, other, other).wait_recv()

                summed = self.shares[i][0, half].astype(jnp.float32)
                for other in range(1, self.tensor_size):
                    summed = summed + self.shares[i][other, half].astype(jnp.float32)
                spec.place(self.outs[i], half)[...] = summed
        for unit, (i, owner) in enumerate(self.units):
            for half in (0, 1):
                for stage in range(self.dp_bits):
                    for slot in self.slots(stage):
                        self.copy(unit, half, stage, slot).wait_send()
                if self.specs[i].kind != "dp":
                    for other in self.others(unit):

                        @pl.when(other != self.tensor)
                        def _():
                            self.z_copy(unit, half, other, self.tensor).wait_send()


def scatter_units(specs, tensor_size):
    units = []
    for i, spec in enumerate(specs):
        units += [(i, j) for j in range(tensor_size)] if spec.kind == "own" else [(i, None)]
    return units


def scatter_kernel(specs, dp_size, tensor_size, *refs):
    count = len(specs)
    run = ScatterRun(
        specs, dp_size, tensor_size, refs[:count], refs[count : 2 * count], refs[2 * count :]
    )
    run.greet()
    run.begin()
    for unit, stage in run.steps():
        run.step(unit, stage)
    run.close()


def scatter_scratch(specs, arrays, dp_size, tensor_size, in_place=False):
    dp_bits = dp_size.bit_length() - 1
    scratch = []
    units = len(scatter_units(specs, tensor_size))
    pieces = [tensor_size if spec.kind == "own" else 1 for spec in specs]
    for spec, array, count in zip(specs, arrays, pieces):
        if not in_place:
            scratch.append(pltpu.VMEM((count, 2, dp_size // 2) + spec.part_shape, array.dtype))
    for spec, array, count in zip(specs, arrays, pieces):
        for stage in range(dp_bits):
            scratch.append(
                pltpu.VMEM((count, 2, dp_size >> (stage + 1)) + spec.part_shape, array.dtype)
            )
    for spec, array in zip(specs, arrays):
        if spec.kind != "dp":
            scratch.append(pltpu.VMEM((tensor_size, 2) + spec.cut_shape, array.dtype))
    dma = pltpu.SemaphoreType.DMA
    return scratch + [
        dma((units, 2, dp_size // 2)),
        dma((units, 2, dp_bits, dp_size // 2)),
        dma((units, 2, dp_bits, dp_size // 2)),
        dma((len(specs), 2, tensor_size)),
        dma((len(specs), 2, tensor_size)),
    ]


def scatter_shapes(specs):
    return [jax.ShapeDtypeStruct(spec.shape, jnp.float32) for spec in specs]


def scatter(specs, arrays, dp_size, tensor_size, collective_id):
    count = len(specs)
    return pl.pallas_call(
        functools.partial(scatter_kernel, specs, dp_size, tensor_size),
        out_shape=scatter_shapes(specs),
        in_specs=[ANY] * count,
        out_specs=[VMEM] * count,
        scratch_shapes=scatter_scratch(specs, arrays, dp_size, tensor_size),
        compiler_params=pltpu.CompilerParams(
            collective_id=collective_id, has_side_effects=True, vmem_limit_bytes=VMEM_LIMIT
        ),
    )(*arrays)


class ExchangeRun:
    def __init__(self, tensor_size, source, out, own_sem, send, recv):
        self.tensor_size, self.source, self.out = tensor_size, source, out
        self.own_sem, self.send, self.recv = own_sem, send, recv
        self.dp, self.tensor = lax.axis_index("dp"), lax.axis_index("tensor")

    def copy(self, other, slot):
        return pltpu.make_async_remote_copy(
            src_ref=self.source.at[other],
            dst_ref=self.out.at[slot],
            send_sem=self.send.at[other],
            recv_sem=self.recv.at[slot],
            device_id=(self.dp, other),
            device_id_type=MESH,
        )

    def own(self):
        return pltpu.make_async_copy(
            self.source.at[self.tensor], self.out.at[self.tensor], self.own_sem
        )

    def begin(self):
        for other in range(self.tensor_size):
            pl.when(other != self.tensor)(self.copy(other, self.tensor).start)
        self.own().start()

    def close(self):
        self.own().wait()
        for other in range(self.tensor_size):

            @pl.when(other != self.tensor)
            def _():
                self.copy(other, self.tensor).wait_send()
                self.copy(other, other).wait_recv()


def lanes_of(shape):
    return lax.broadcasted_iota(jnp.int32, shape, len(shape) - 1)


def swap_halves(values):
    width = values.shape[-1]
    first = lanes_of(values.shape) % HEAD_DIM < HEAD_DIM // 2
    return jnp.where(
        first,
        pltpu.roll(values, width - HEAD_DIM // 2, 1),
        pltpu.roll(values, HEAD_DIM // 2, 1),
    )


def left_head(block, odd):
    moved = jnp.where(odd, pltpu.roll(block, HEAD_DIM, 1), block)
    return jnp.where(lanes_of(block.shape) < HEAD_DIM, moved, jnp.zeros_like(moved))


def allowed(keys, rows, start):
    key_at = lax.broadcasted_iota(jnp.int32, (keys, rows), 0)
    query_at = lax.broadcasted_iota(jnp.int32, (keys, rows), 1) + start
    return key_at <= query_at


def at_steps(actions, step, steps):
    places = [(min(steps - 1, int(time * steps)), action) for time, action in actions]
    for place in sorted({place for place, _ in places}):

        @pl.when(step == place)
        def _():
            for at, action in places:
                if at == place:
                    action()


def attend_pair(pair, group_pairs, q_pre, cos_ref, sin_ref, kv_all, k_left, v_turned, outs):
    context, queries_out, lse_ref = outs
    rows = q_pre.shape[0]
    kv_width = kv_all.shape[1] // 2
    group = lax.div(pair, group_pairs)
    start = lax.axis_index("tensor") * rows
    at = pl.ds(pl.multiple_of(pair * 128, 128), 128)

    @pl.when(lax.rem(pair, group_pairs) == 0)
    def _():
        odd = lax.rem(group, 2) == 1
        lane = pl.multiple_of(lax.div(group, 2) * 128, 128)
        keys = kv_all[:, pl.ds(lane, 128)].astype(jnp.float32)
        values = kv_all[:, pl.ds(kv_width + lane, 128)].astype(jnp.float32)
        k_left[...] = left_head(keys, odd).astype(jnp.bfloat16)
        v_turned[...] = left_head(values, odd).T[:HEAD_DIM].astype(jnp.bfloat16)

    raw = q_pre[:, at]
    turned = (raw * cos_ref[...] + swap_halves(raw) * sin_ref[...]).astype(jnp.bfloat16)
    turned = turned.astype(jnp.float32) * HEAD_DIM ** (-0.5)
    queries_out[:, at] = turned.astype(jnp.bfloat16)
    open_at = allowed(k_left.shape[0], rows, start)
    contexts = []
    for head in (0, 1):
        queries = (turned if head == 0 else pltpu.roll(turned, HEAD_DIM, 1)).astype(jnp.bfloat16)
        scores = product_right(k_left[...], queries)
        scores = jnp.where(open_at, scores, -1e30)
        top = jnp.max(scores, axis=0, keepdims=True)
        exponent = jnp.exp(scores - top)
        summed = jnp.sum(exponent, axis=0, keepdims=True)
        part = product(v_turned[...], exponent.astype(jnp.bfloat16))
        contexts.append(part * (1.0 / summed))
        lse_ref[pair, pl.ds(head, 1), :] = top + jnp.log(summed)
    context[:, at] = jnp.concatenate(contexts, axis=0).T.astype(jnp.bfloat16)


def front_kernel(specs, kv_spec, group_pairs, dp_size, tensor_size, *refs):
    refs = list(refs)

    def take(count):
        return [refs.pop(0) for _ in range(count)]

    count = len(specs)
    tokens, cos_ref, sin_ref = take(3)
    sources = take(count)
    context, queries, lse_ref, normed, normed_two, middle, gain_rows, kv_all = take(8)
    outs = take(count)
    held = take(count)
    weights, kv_weights, gain_blocks, q_pre, k_left, v_turned = take(6)
    sems = take(5)
    kv_sems = take(5)
    (load_sem,) = take(1)
    key_value, gains, query, out, gate, up, down, cot = range(count)
    run = GatherRun(specs, dp_size, tensor_size, sources, outs, held, sems)
    rows, width = tokens.shape
    own_rows = pl.ds(pl.multiple_of(run.tensor * rows, rows), rows)
    kv_run = GatherRun(
        [kv_spec], dp_size, tensor_size, [kv_all.at[own_rows, :]], [kv_all], [None], kv_sems
    )
    kv_width = kv_all.shape[1] // 2
    near = [1 << bit for bit in range(run.dp_bits - 1)]
    far = [r for r in range(1, 1 << (run.dp_bits - 1)) if r not in near]
    far.sort(key=lambda rank: rank.bit_count())
    core = list(range(1 << (run.dp_bits - 1), 1 << run.dp_bits))

    def hops(ranks, *units):
        for unit in units:
            for rank in ranks:
                run.hop(unit, rank)

    run.greet()
    loads = [
        pltpu.make_async_copy(source, target, run.own_sem.at[i])
        for i, (source, target) in enumerate(zip(sources, held))
    ]
    for load in loads:
        load.start()
    first = (key_value, gains, query)
    for i in first:
        run.begin_line(i)
    for i, load in enumerate(loads):
        load.wait()
        run.own(i).start()
    run.end_line(gate)
    hops([0], gate)
    for step in range(1, tensor_size):
        for i in first:
            run.line(i, step)
        if step == tensor_size // 2:
            hops(near, gate)
    for i in first:
        run.end_line(i)
    hops([0], *first)
    run.begin_line(out)
    hops(far, gate)
    for step in range(1, tensor_size):
        run.line(out, step)
    run.begin_line(cot)
    hops(near, key_value, gains)
    hops(far, key_value, gains)
    hops(near, query)
    for i in (out, up, down):
        run.end_line(i)
    hops([0], out)
    hops(core, key_value, gains)

    kv_load = pltpu.make_async_copy(outs[key_value], kv_weights, load_sem.at[0])
    kv_load.start()
    gain_load = pltpu.make_async_copy(outs[gains], gain_blocks, load_sem.at[1])
    gain_load.start()
    gain_load.wait()
    blocks = gain_blocks.shape[0] // 16
    lanes = width // 128
    per = blocks // lanes
    for lane in range(lanes):
        row = jnp.zeros((16, 128), jnp.float32)
        for other in range(per):
            at = (lane * per + other) * 16
            row = row + gain_blocks[at : at + 16, :].astype(jnp.float32)
        gain_rows[:, lane * 128 : (lane + 1) * 128] = row[:8]
    slab = 16

    def norm_first(step, carry):
        at = pl.ds(pl.multiple_of(step * slab, slab), slab)
        raw = tokens[at, :].astype(jnp.float32)
        scale = lax.rsqrt(jnp.mean(raw * raw, axis=-1, keepdims=True) + epsilon)
        normed[at, :] = (raw * scale * gain_rows[0:1, :]).astype(normed.dtype)
        return carry

    lax.fori_loop(0, rows // slab, norm_first, 0)
    kv_load.wait()
    own_kv = product(normed[...], kv_weights[...])
    repeat = kv_width // cos_ref.shape[1]
    own_keys = own_kv[:, :kv_width]
    own_keys = own_keys * jnp.concatenate([cos_ref[...]] * repeat, axis=1) + swap_halves(
        own_keys
    ) * jnp.concatenate([sin_ref[...]] * repeat, axis=1)
    kv_all[own_rows, :] = jnp.concatenate([own_keys, own_kv[:, kv_width:]], axis=1).astype(
        kv_all.dtype
    )
    run.line(cot, 1)
    kv_run.begin_line(0)
    hops(far, query)
    hops(core, query)
    hops([0], up)
    query_load = pltpu.make_async_copy(outs[query], weights, load_sem.at[0])
    query_load.start()
    query_load.wait()
    tiles = max(4, tensor_size)
    tile = width // tiles
    for j in range(tiles):
        columns = slice(j * tile, (j + 1) * tile)
        q_pre[:, columns] = product(normed[...], weights[:, columns])
        if 1 <= j < tensor_size:
            kv_run.line(0, j)
    assert tiles >= tensor_size
    pairs = lse_ref.shape[0]
    plan = [
        (0.1, lambda: hops(near, out)),
        (0.3, lambda: hops(far, out)),
        (0.3, lambda: hops([0], down)),
        (0.55, lambda: hops(near, up)),
        (0.8, lambda: hops(far, up)),
    ]
    for step in range(2, tensor_size):
        time = 0.05 + 0.6 * (step - 2) / max(1, tensor_size - 3)
        plan.append((time, functools.partial(run.line, cot, step)))
    plan.sort(key=lambda entry: entry[0])

    def pair_step(pair, carry):
        at_steps(plan, pair, pairs)
        attend_pair(
            pair,
            group_pairs,
            q_pre,
            cos_ref,
            sin_ref,
            kv_all,
            k_left,
            v_turned,
            (context, queries, lse_ref),
        )
        return carry

    lax.fori_loop(0, pairs, pair_step, 0)
    hops(core, out)
    out_load = pltpu.make_async_copy(outs[out], weights, load_sem.at[0])
    out_load.start()
    hops(near, down)
    out_load.wait()
    for j in range(4):
        columns = slice(j * (width // 4), (j + 1) * (width // 4))
        middle[:, columns] = tokens[:, columns].astype(jnp.float32) + product(
            context[...], weights[:, columns]
        )

    def norm_second(step, carry):
        at = pl.ds(pl.multiple_of(step * slab, slab), slab)
        raw = middle[at, :]
        scale = lax.rsqrt(jnp.mean(raw * raw, axis=-1, keepdims=True) + epsilon)
        normed_two[at, :] = (raw * scale * gain_rows[1:2, :]).astype(normed_two.dtype)
        return carry

    lax.fori_loop(0, rows // slab, norm_second, 0)
    hops(far, down)
    hops(core, gate, up, down)
    run.end_line(cot)
    run.close()
    kv_run.close()


def front(tokens, cosines, sines, arrays, specs, kv_spec, heads, group_heads, sizes, collective_id):
    dp_size, tensor_size = sizes
    rows, width = tokens.shape
    length = rows * tensor_size
    low, full = jnp.bfloat16, jnp.float32
    held, sems = gather_scratch(specs, arrays, *sizes)
    _, kv_sems = gather_scratch([kv_spec], [], *sizes)
    kv_both = specs[0].shape[1]
    pairs = heads // 2
    tokens_low = jax.ShapeDtypeStruct((rows, width), low)
    return pl.pallas_call(
        functools.partial(front_kernel, specs, kv_spec, group_heads // 2, *sizes),
        out_shape=[
            tokens_low,
            tokens_low,
            jax.ShapeDtypeStruct((pairs, 2, rows), full),
            tokens_low,
            tokens_low,
            jax.ShapeDtypeStruct((rows, width), full),
            jax.ShapeDtypeStruct((8, width), full),
            jax.ShapeDtypeStruct((length, kv_both), low),
        ]
        + gather_shapes(specs, arrays),
        in_specs=[VMEM] * 3 + [ANY] * len(specs),
        out_specs=[VMEM] * 8 + [ANY] * len(specs),
        scratch_shapes=held
        + [
            pltpu.VMEM((width, width), low),
            pltpu.VMEM((width, kv_both), low),
            pltpu.VMEM(specs[1].shape, low),
            pltpu.VMEM((rows, width), full),
            pltpu.VMEM((length, 128), low),
            pltpu.VMEM((HEAD_DIM, length), low),
        ]
        + sems
        + kv_sems
        + [pltpu.SemaphoreType.DMA((2,))],
        compiler_params=pltpu.CompilerParams(
            collective_id=collective_id, has_side_effects=True, vmem_limit_bytes=VMEM_LIMIT
        ),
    )(tokens, cosines, sines, *arrays)


def scatter_plan(run):
    plan = [(0.0, run.greet), (0.0, run.begin)]
    for unit, stage in run.steps():
        time = 0.15 + 0.1 * unit if stage == 0 else 0.55 + 0.35 * unit if stage == 1 else 1.0
        plan.append((min(time, 1.0), functools.partial(run.step, unit, stage)))
    return plan + [(1.0, run.close)]


def attend_back_kernel(group_pairs, pairs, specs, dp_size, tensor_size, *refs):
    refs = list(refs)
    q_ref, do_ref, lse_ref, cos_ref, sin_ref, k_ref, v_ref = (refs.pop(0) for _ in range(7))
    sources = [refs.pop(0) for _ in specs]
    dq_ref, dk_ref, dv_ref = (refs.pop(0) for _ in range(3))
    outs = [refs.pop(0) for _ in specs]
    k_left, v_left, k_turned, dk_sum, dv_sum = (refs.pop(0) for _ in range(5))
    run = ScatterRun(specs, dp_size, tensor_size, sources, outs, refs)
    plan = scatter_plan(run)
    at_steps([entry for entry in plan if entry[0] < 1.0], pl.program_id(0), pairs)
    pair = pl.program_id(0)
    group = pair // group_pairs
    odd = group % 2 == 1
    rows = q_ref.shape[0]
    start = lax.axis_index("tensor") * rows

    @pl.when(pair % group_pairs == 0)
    def _():
        left = left_head(k_ref[...].astype(jnp.float32), odd)
        k_left[...] = left.astype(jnp.bfloat16)
        k_turned[...] = left.T[:HEAD_DIM].astype(jnp.bfloat16)
        v_left[...] = left_head(v_ref[...].astype(jnp.float32), odd).astype(jnp.bfloat16)
        dk_sum[...] = jnp.zeros_like(dk_sum)
        dv_sum[...] = jnp.zeros_like(dv_sum)

    open_at = allowed(k_left.shape[0], rows, start)
    grads = []
    for head in (0, 1):
        queries, grad_out = q_ref[...], do_ref[...]
        if head == 1:
            queries = pltpu.roll(queries.astype(jnp.float32), HEAD_DIM, 1).astype(jnp.bfloat16)
            grad_out = pltpu.roll(grad_out.astype(jnp.float32), HEAD_DIM, 1).astype(jnp.bfloat16)
        scores = product_right(k_left[...], queries)
        scores = jnp.where(open_at, scores, -1e30)
        softmaxed = jnp.exp(scores - lse_ref[0, head, :][None, :])
        grad_soft = product_right(v_left[...], grad_out)
        mixed = softmaxed * grad_soft
        mixed_sum = jnp.sum(mixed, axis=0, keepdims=True)
        grad_scores = (mixed - softmaxed * mixed_sum).astype(jnp.bfloat16)
        dv_sum[...] += product(softmaxed.astype(jnp.bfloat16), grad_out)
        dk_sum[...] += product(grad_scores, queries)
        grads.append(product(k_turned[...], grad_scores))
    grad_q = jnp.concatenate(grads, axis=0).T * HEAD_DIM ** (-0.5)
    dq_ref[...] = (grad_q * cos_ref[...] - swap_halves(grad_q) * sin_ref[...]).astype(jnp.bfloat16)

    @pl.when(pair % group_pairs == group_pairs - 1)
    def _():
        for total, out in ((dk_sum, dk_ref), (dv_sum, dv_ref)):
            value = total[...]
            left = lanes_of(value.shape) < HEAD_DIM

            @pl.when(jnp.logical_not(odd))
            def _():
                out[...] = jnp.where(left, value, 0.0).astype(out.dtype)

            @pl.when(odd)
            def _():
                out[...] = jnp.where(
                    left, out[...].astype(jnp.float32), pltpu.roll(value, HEAD_DIM, 1)
                ).astype(out.dtype)
    at_steps([entry for entry in plan if entry[0] >= 1.0], pair, pairs)


def attend_back(
    queries,
    grad_context,
    lse,
    cosines,
    sines,
    keys_values,
    head_count,
    group_heads,
    specs,
    arrays,
    sizes,
    collective_id,
):
    rows, width = queries.shape
    length, both = keys_values.shape
    pairs, group_pairs = head_count // 2, group_heads // 2
    kv_blocks = both // 256
    wide = pl.BlockSpec((rows, 128), lambda p: (0, p))
    table = pl.BlockSpec((rows, 128), lambda p: (0, 0))
    kv_out = pl.BlockSpec((length, 128), lambda p: (0, p // group_pairs // 2))
    return pl.pallas_call(
        functools.partial(attend_back_kernel, group_pairs, pairs, specs, *sizes),
        grid=(pairs,),
        out_shape=[
            jax.ShapeDtypeStruct((rows, width), jnp.bfloat16),
            jax.ShapeDtypeStruct((length, both // 2), jnp.bfloat16),
            jax.ShapeDtypeStruct((length, both // 2), jnp.bfloat16),
        ]
        + scatter_shapes(specs),
        in_specs=[
            wide,
            wide,
            pl.BlockSpec((1, 2, rows), lambda p: (p, 0, 0)),
            table,
            table,
            pl.BlockSpec((length, 128), lambda p: (0, p // group_pairs // 2)),
            pl.BlockSpec((length, 128), lambda p: (0, kv_blocks + p // group_pairs // 2)),
        ]
        + [ANY] * len(specs),
        out_specs=[wide, kv_out, kv_out] + [VMEM] * len(specs),
        scratch_shapes=[
            pltpu.VMEM((length, 128), jnp.bfloat16),
            pltpu.VMEM((length, 128), jnp.bfloat16),
            pltpu.VMEM((HEAD_DIM, length), jnp.bfloat16),
            pltpu.VMEM((length, 128), jnp.float32),
            pltpu.VMEM((length, 128), jnp.float32),
        ]
        + scatter_scratch(specs, arrays, *sizes),
        compiler_params=pltpu.CompilerParams(
            collective_id=collective_id, has_side_effects=True, vmem_limit_bytes=VMEM_LIMIT
        ),
        cost_estimate=pl.CostEstimate(
            flops=10 * rows * length * width, bytes_accessed=8 * rows * width, transcendentals=0
        ),
    )(queries, grad_context, lse, cosines, sines, keys_values, keys_values, *arrays)


def block_at(place, tensor, tensor_size):
    above = tensor_size - 1 - tensor
    up = jnp.where(place <= above, tensor + place, tensor - (place - above))
    down = jnp.where(place <= tensor, tensor - place, place)
    return jnp.where(tensor <= above, up, down)


def mlp_kernel(
    specs,
    dp_size,
    tensor_size,
    normed_ref,
    cot_ref,
    gate_ref,
    up_ref,
    down_ref,
    back_ref,
    y_ref,
    d_gate_ref,
    d_up_ref,
    down_sum,
    normed,
    cot,
    gate,
    up,
    down,
    hidden,
    d_gate,
    d_up,
    y_stage,
    stage,
    landing,
    load_sem,
    n_send,
    n_recv,
    y_sem,
    b_send,
    b_recv,
    out_sem,
    *scatter_refs,
):
    run = ScatterRun(
        specs, dp_size, tensor_size, [down], [down_sum], scatter_refs, in_place=True
    )
    dp, tensor = lax.axis_index("dp"), lax.axis_index("tensor")
    rows, width = normed_ref.shape
    units = gate.shape[1]
    loads = [
        pltpu.make_async_copy(source, target, load_sem.at[i])
        for i, (source, target) in enumerate(
            (
                (normed_ref, normed.at[tensor]),
                (gate_ref, gate),
                (up_ref, up),
                (down_ref, down),
                (cot_ref, cot),
            )
        )
    ]
    for load in loads:
        load.start()
    greet((dp, tensor, tensor_size), False, True, run.dp_bits)
    has = [tensor + 1 < tensor_size, tensor > 0]

    def n_copy(block, way, source=None):
        return pltpu.make_async_remote_copy(
            src_ref=normed.at[block] if source is None else source,
            dst_ref=normed.at[block],
            send_sem=n_send.at[way, block],
            recv_sem=n_recv.at[block],
            device_id=(dp, tensor + 1 if way == 0 else tensor - 1),
            device_id_type=MESH,
        )

    for way in (0, 1):
        pl.when(has[way])(n_copy(tensor, way, normed_ref).start)
    landing[tensor] = jnp.zeros((rows, width), landing.dtype)

    def pump(distance):
        for way, block in ((0, tensor - distance), (1, tensor + distance)):

            @pl.when((block >= 0) & (block < tensor_size))
            def _():
                n_copy(block, way).wait_recv()
                pl.when(has[way])(n_copy(block, way).start)

    farthest = jnp.maximum(tensor, tensor_size - 1 - tensor)

    def b_copy(block, slot):
        return pltpu.make_async_remote_copy(
            src_ref=stage.at[block],
            dst_ref=landing.at[slot],
            send_sem=b_send.at[block],
            recv_sem=b_recv.at[slot],
            device_id=(dp, block),
            device_id_type=MESH,
        )

    def y_copy(block, slot):
        return pltpu.make_async_copy(y_stage.at[slot], y_ref.at[block], y_sem.at[slot])

    for load in loads[:3]:
        load.wait()

    def chunk(place, carry):
        block = block_at(place, tensor, tensor_size)

        @pl.when((place >= 1) & (place <= farthest))
        def _():
            pump(place)

        rows_in = normed[block]
        gate_pre = product(rows_in, gate[...])
        upward = product(rows_in, up[...])

        @pl.when(place == 0)
        def _():
            for load in loads[3:]:
                load.wait()

        sigmoid = 1.0 / (1.0 + jnp.exp(-gate_pre))
        silu = gate_pre * sigmoid
        active = (silu * upward).astype(jnp.bfloat16)
        hidden[block] = active
        slot = lax.rem(place, 2)

        @pl.when(place >= 2)
        def _():
            y_copy(block, slot).wait()

        y_stage[slot] = product(active, down[...]).astype(jnp.bfloat16)
        y_copy(block, slot).start()
        grad_hidden = product_right(cot[block], down[...])
        low_gate = (
            grad_hidden * upward * sigmoid * (1.0 + gate_pre * (1.0 - sigmoid))
        ).astype(jnp.bfloat16)
        low_up = (grad_hidden * silu).astype(jnp.bfloat16)
        d_gate[block] = low_gate
        d_up[block] = low_up
        back = product_right(low_gate, gate[...]) + product_right(low_up, up[...])

        @pl.when(block == tensor)
        def _():
            back_ref[...] = back

        @pl.when(block != tensor)
        def _():
            stage[block] = back.astype(stage.dtype)
            b_copy(block, tensor).start()

        return carry

    lax.fori_loop(0, tensor_size, chunk, 0)
    for slot in range(2):
        y_copy(0, slot).wait()

    all_rows = tensor_size * rows

    def weight_grad(left, right, out):
        extent = left.shape[2]
        tile = 256 if extent % 256 == 0 else 128 if extent % 128 == 0 else extent

        def body(step, carry):
            at = pl.ds(pl.multiple_of(step * tile, tile), tile)
            columns = left[:, :, at].reshape(all_rows, tile)
            out[at, :] = product_left(columns, right[...].reshape(all_rows, -1)).astype(out.dtype)
            return carry

        lax.fori_loop(0, extent // tile, body, 0)

    weight_grad(hidden, cot, down)
    run.begin_unit(0)
    weight_grad(normed, d_gate, gate)
    pltpu.make_async_copy(gate, d_gate_ref, out_sem.at[0]).start()
    run.step(0, 0)
    weight_grad(normed, d_up, up)
    pltpu.make_async_copy(up, d_up_ref, out_sem.at[1]).start()
    run.step(0, 1)

    for other in range(tensor_size):

        @pl.when(other != tensor)
        def _():
            b_copy(other, other).wait_recv()

    slab = 16

    def add_slab(step, carry):
        at = pl.ds(pl.multiple_of(step * slab, slab), slab)
        total = back_ref[at, :]
        for other in range(tensor_size):
            total = total + landing[other, at, :].astype(jnp.float32)
        back_ref[at, :] = total
        return carry

    lax.fori_loop(0, rows // slab, add_slab, 0)
    for later in range(2, run.dp_bits + 1):
        run.step(0, later)
    run.close()
    pltpu.make_async_copy(gate, d_gate_ref, out_sem.at[0]).wait()
    pltpu.make_async_copy(up, d_up_ref, out_sem.at[1]).wait()
    for other in range(tensor_size):

        @pl.when(other != tensor)
        def _():
            b_copy(other, tensor).wait_send()

        for way in (0, 1):
            sent = has[way] & ((other <= tensor) if way == 0 else (other >= tensor))
            pl.when(sent)(n_copy(other, way).wait_send)


def feed_forward(normed, cot_all, gate, up, down, specs, sizes, collective_id):
    dp_size, tensor_size = sizes
    rows, width = normed.shape
    units = gate.shape[1]
    low = jnp.bfloat16
    tokens = (tensor_size, rows, width)
    inner = (tensor_size, rows, units)
    dma = pltpu.SemaphoreType.DMA
    return pl.pallas_call(
        functools.partial(mlp_kernel, specs, dp_size, tensor_size),
        out_shape=[
            jax.ShapeDtypeStruct((rows, width), jnp.float32),
            jax.ShapeDtypeStruct(tokens, low),
            jax.ShapeDtypeStruct(gate.shape, low),
            jax.ShapeDtypeStruct(up.shape, low),
        ]
        + scatter_shapes(specs),
        in_specs=[ANY] * 5,
        out_specs=[VMEM] + [ANY] * 3 + [VMEM],
        scratch_shapes=[
            pltpu.VMEM(tokens, low),
            pltpu.VMEM(tokens, low),
            pltpu.VMEM(gate.shape, low),
            pltpu.VMEM(up.shape, low),
            pltpu.VMEM(down.shape, low),
            pltpu.VMEM(inner, low),
            pltpu.VMEM(inner, low),
            pltpu.VMEM(inner, low),
            pltpu.VMEM((2, rows, width), low),
            pltpu.VMEM(tokens, low),
            pltpu.VMEM(tokens, low),
            dma((5,)),
            dma((2, tensor_size)),
            dma((tensor_size,)),
            dma((2,)),
            dma((tensor_size,)),
            dma((tensor_size,)),
            dma((2,)),
        ]
        + scatter_scratch(specs, [down], dp_size, tensor_size, in_place=True),
        compiler_params=pltpu.CompilerParams(
            collective_id=collective_id, has_side_effects=True, vmem_limit_bytes=63 * 2**20
        ),
        cost_estimate=pl.CostEstimate(
            flops=18 * tensor_size * rows * width * units,
            bytes_accessed=8 * width * units,
            transcendentals=0,
        ),
    )(
        normed,
        cot_all.reshape(tokens),
        gate,
        up,
        down,
    )


def tail_kernel(specs, dp_size, tensor_size, *refs):
    refs = list(refs)

    def take(count):
        return [refs.pop(0) for _ in range(count)]

    sources = take(7)
    blocks, wq_ref, cos_ref, sin_ref, gain_ref, second_ref = take(6)
    tokens_out, out_sum, query_sum, kv_sum, gain_sum = take(5)
    held = take(7)
    context, middle_low, normed, dq, wkv, tokens, middle = held
    o_grad, q_grad, kv_grad, gain_grad, wq_tile, kv_landing, kv_low, column_sum = take(8)
    load_sem, tile_sem, ex_own, ex_send, ex_recv = take(5)
    run = ScatterRun(
        specs,
        dp_size,
        tensor_size,
        [o_grad, q_grad, kv_grad, gain_grad],
        [out_sum, query_sum, kv_sum, gain_sum],
        refs,
        in_place=True,
    )
    rows, width = tokens.shape
    q_cols = q_grad.shape[2]
    o_rows = o_grad.shape[1]
    kv_width = kv_low.shape[1] // 2
    loads = [
        pltpu.make_async_copy(source, target, load_sem.at[i])
        for i, (source, target) in enumerate(zip(sources, held))
    ]
    for load in loads:
        load.start()

    def tile_copy(j):
        return pltpu.make_async_copy(
            wq_ref.at[:, pl.ds(j * q_cols, q_cols)], wq_tile.at[j % 2], tile_sem.at[j % 2]
        )

    tile_copy(0).start()
    exchange_run = ExchangeRun(tensor_size, blocks, kv_landing, ex_own, ex_send, ex_recv)
    greet((run.dp, run.tensor, tensor_size), False, True, run.dp_bits)
    exchange_run.begin()

    def out_piece(j):
        tile = min(256, o_rows)
        for row in range(0, o_rows, tile):
            o_grad[j, row : row + tile, :] = product_left(
                context[:, j * o_rows + row : j * o_rows + row + tile], middle_low[...]
            ).astype(o_grad.dtype)
        run.begin_unit(j)

    def query_piece(j):
        grads = dq[:, j * q_cols : (j + 1) * q_cols]
        tile = 512
        for row in range(0, width, tile):
            q_grad[j, row : row + tile, :] = product_left(
                normed[:, row : row + tile], grads
            ).astype(q_grad.dtype)
        run.begin_unit(tensor_size + j)

    def back_piece(j):
        if j + 1 < tensor_size:
            tile_copy(j + 1).start()
        tile_copy(j).wait()
        part = product_right(dq[:, j * q_cols : (j + 1) * q_cols], wq_tile[j % 2])
        if j == 0:
            tokens_out[...] = part
        else:
            tokens_out[...] += part

    def kv_piece():
        exchange_run.close()
        total = kv_landing[0].astype(jnp.float32)
        for other in range(1, tensor_size):
            total = total + kv_landing[other].astype(jnp.float32)
        grad_keys = total[:, :kv_width]
        repeat = kv_width // cos_ref.shape[1]
        cosines = jnp.concatenate([cos_ref[...]] * repeat, axis=1)
        sines = jnp.concatenate([sin_ref[...]] * repeat, axis=1)
        kv_low[:, :kv_width] = (grad_keys * cosines - swap_halves(grad_keys) * sines).astype(
            kv_low.dtype
        )
        kv_low[:, kv_width:] = total[:, kv_width:].astype(kv_low.dtype)
        for row in range(0, width, 512):
            kv_grad[row : row + 512, :] = product_left(
                normed[:, row : row + 512], kv_low[...]
            ).astype(kv_grad.dtype)
        run.begin_unit(2 * tensor_size)
        tokens_out[...] += product_right(kv_low[...], wkv[...])

    slab = 16

    def finish(step, carry):
        at = pl.ds(pl.multiple_of(step * slab, slab), slab)
        raw = tokens[at, :].astype(jnp.float32)
        scale = lax.rsqrt(jnp.mean(raw * raw, axis=-1, keepdims=True) + epsilon)
        unit = raw * scale
        grad = tokens_out[at, :]
        gained = grad * unit
        column_sum[...] += gained[:8] + gained[8:]
        scaled = grad * gain_ref[...]
        mean = jnp.mean(scaled * unit, axis=-1, keepdims=True)
        tokens_out[at, :] = middle[at, :] + scale * (scaled - unit * mean)
        return carry

    def last_piece():
        column_sum[...] = jnp.zeros_like(column_sum)
        lax.fori_loop(0, rows // slab, finish, 0)
        gain_grad[...] = jnp.zeros_like(gain_grad)
        gain_grad[0:1, :] = jnp.sum(column_sum[...], axis=0, keepdims=True)
        gain_grad[8:9, :] = second_ref[...]
        run.begin_unit(2 * tensor_size + 1)

    loads[0].wait()
    loads[1].wait()
    for j in range(tensor_size):
        out_piece(j)
        if 1 <= j <= 2:
            run.step(j - 1, 0)
    for load in loads[2:]:
        load.wait()
    count = len(run.units)
    work = {j: [functools.partial(query_piece, j)] for j in range(tensor_size)}
    room = max(1, tensor_size - 2)
    for j in range(tensor_size):
        work.setdefault(tensor_size + j * room // tensor_size, []).append(
            functools.partial(back_piece, j)
        )
    work.setdefault(2 * tensor_size - 2, []).append(kv_piece)
    work.setdefault(2 * tensor_size - 1, []).append(last_piece)
    for tick in range(count + 1):
        for piece in work.get(tick, []):
            piece()
        if tick < count:
            run.step(tick, 1)
        if tick + 2 < count:
            run.step(tick + 2, 0)
        if tick:
            for stage in range(2, run.dp_bits + 1):
                run.step(tick - 1, stage)
    run.close()


def tail(
    context,
    middle_low,
    normed,
    dq,
    key_value,
    tokens,
    middle,
    kv_blocks,
    query,
    cosines,
    sines,
    gain,
    second,
    specs,
    sizes,
    collective_id,
):
    dp_size, tensor_size = sizes
    rows, width = tokens.shape
    low, full = jnp.bfloat16, jnp.float32
    o_spec, q_spec = specs[0], specs[1]
    kv_both = key_value.shape[1]
    dma = pltpu.SemaphoreType.DMA
    arrays = [
        jax.ShapeDtypeStruct((tensor_size, o_spec.shape[0], width), low),
        jax.ShapeDtypeStruct((tensor_size, width, q_spec.shape[1]), low),
        jax.ShapeDtypeStruct((width, kv_both), low),
        jax.ShapeDtypeStruct((16, width), full),
    ]
    loaded = [context, middle_low, normed, dq, key_value, tokens, middle]
    return pl.pallas_call(
        functools.partial(tail_kernel, specs, dp_size, tensor_size),
        out_shape=[jax.ShapeDtypeStruct((rows, width), full)] + scatter_shapes(specs),
        in_specs=[ANY] * 9 + [VMEM] * 4,
        out_specs=[VMEM] * (1 + len(specs)),
        scratch_shapes=[pltpu.VMEM(array.shape, array.dtype) for array in loaded]
        + [pltpu.VMEM(array.shape, array.dtype) for array in arrays]
        + [
            pltpu.VMEM((2, width, q_spec.shape[1]), low),
            pltpu.VMEM(kv_blocks.shape, low),
            pltpu.VMEM((rows, kv_both), low),
            pltpu.VMEM((8, width), full),
            dma((7,)),
            dma((2,)),
            dma,
            dma((tensor_size,)),
            dma((tensor_size,)),
        ]
        + scatter_scratch(specs, arrays, dp_size, tensor_size, in_place=True),
        compiler_params=pltpu.CompilerParams(
            collective_id=collective_id, has_side_effects=True, vmem_limit_bytes=60 * 2**20
        ),
    )(*loaded, kv_blocks, query, cosines, sines, gain, second)


def rope_tables(rows, tensor):
    halved = HEAD_DIM // 2
    freqs = theta_base ** (-2.0 * jnp.arange(halved, dtype=jnp.float32) / HEAD_DIM)
    places = (tensor * rows + jnp.arange(rows)).astype(jnp.float32)
    angles = places[:, None] * freqs[None, :]
    cosines, sines = jnp.cos(angles), jnp.sin(angles)
    return (
        jnp.concatenate([cosines, cosines] * 2, axis=1),
        jnp.concatenate([-sines, sines] * 2, axis=1),
    )


def start_row(dp, size):
    return pl.multiple_of(dp * size, size)


def on_device(
    dp_size,
    tensor_size,
    tokens,
    attn_gain,
    w_query,
    w_key,
    w_value,
    w_out,
    mlp_gain,
    w_gate,
    w_up,
    w_down,
    cotangent,
):
    tensor_index = lax.axis_index("tensor")
    rows, width = tokens.shape
    heads = w_query.shape[1] * tensor_size // HEAD_DIM
    kv_width = w_key.shape[1]
    kv_heads = kv_width // HEAD_DIM
    group_heads = heads // kv_heads
    q_rows, q_cols = w_query.shape
    kv_rows = w_key.shape[0]
    o_rows, o_cols = w_out.shape
    gain_part = attn_gain.shape[0]

    key_value = jnp.concatenate([w_key, w_value], axis=1)
    per = 128 // gain_part
    spot = lax.rem(lax.axis_index("dp") * tensor_size + tensor_index, per)
    rows_at = lax.broadcasted_iota(jnp.int32, (16, 128), 0)
    here = lax.div(lax.broadcasted_iota(jnp.int32, (16, 128), 1), gain_part) == spot
    gains = jnp.where(rows_at == 0, jnp.tile(attn_gain, per), jnp.tile(mlp_gain, per))
    gains = jnp.where(here & (rows_at < 2), gains, jnp.zeros_like(gains))
    query_spec = Gather(
        (width, heads * HEAD_DIM),
        lambda ref, dp, t: ref.at[
            pl.ds(start_row(dp, q_rows), q_rows), pl.ds(start_row(t, q_cols), q_cols)
        ],
        lambda ref, dp, half: ref.at[
            pl.ds(pl.multiple_of(dp * q_rows + half * (q_rows // 2), q_rows // 2), q_rows // 2), :
        ],
    )
    kv_all_rows = kv_rows * tensor_size
    kv_spec = Gather(
        (width, 2 * kv_width),
        lambda ref, dp, t: ref.at[pl.ds(start_row(dp * tensor_size + t, kv_rows), kv_rows), :],
        lambda ref, dp, half: ref.at[
            pl.ds(
                pl.multiple_of(dp * kv_all_rows + half * (kv_all_rows // 2), kv_all_rows // 2),
                kv_all_rows // 2,
            ),
            :,
        ],
    )
    gain_spec = Gather(
        (dp_size * tensor_size * 16, 128),
        lambda ref, dp, t: ref.at[pl.ds(start_row(dp * tensor_size + t, 16), 16), :],
        lambda ref, dp, half: ref.at[
            pl.ds(
                pl.multiple_of((2 * dp + half) * tensor_size * 8, tensor_size * 8),
                tensor_size * 8,
            ),
            :,
        ],
    )
    out_spec = Gather(
        (heads * HEAD_DIM, width),
        lambda ref, dp, t: ref.at[
            pl.ds(start_row(t, o_rows), o_rows), pl.ds(start_row(dp, o_cols), o_cols)
        ],
        lambda ref, dp, half: ref.at[
            pl.ds(half * (heads * HEAD_DIM // 2), heads * HEAD_DIM // 2),
            pl.ds(start_row(dp, o_cols), o_cols),
        ],
    )
    row_spec = lambda shape: Gather(
        (tensor_size * shape[0], shape[1]),
        lambda ref, dp, t: ref.at[pl.ds(start_row(t, shape[0]), shape[0]), :],
    )
    up_rows, units = w_gate.shape
    column_spec = Gather(
        (width, units),
        lambda ref, dp, t: ref.at[pl.ds(start_row(dp, up_rows), up_rows), :],
        lambda ref, dp, half: ref.at[
            pl.ds(
                pl.multiple_of(dp * up_rows + half * (up_rows // 2), up_rows // 2), up_rows // 2
            ),
            :,
        ],
        False,
    )
    down_cols = w_down.shape[1]
    down_spec = Gather(
        (units, width),
        lambda ref, dp, t: ref.at[:, pl.ds(start_row(dp, down_cols), down_cols)],
        lambda ref, dp, half: ref.at[
            pl.ds(half * (units // 2), units // 2), pl.ds(start_row(dp, down_cols), down_cols)
        ],
        False,
    )
    sizes = (dp_size, tensor_size)
    cosines, sines = rope_tables(rows, tensor_index)
    (
        context,
        queries,
        log_sums,
        normed_first,
        normed_own,
        middle,
        gain_rows,
        kv_all,
        key_value_full,
        _,
        query_full,
        out_full,
        gate_full,
        up_full,
        down_full,
        cot_all,
    ) = front(
        tokens,
        cosines,
        sines,
        [key_value, gains, w_query, w_out, w_gate, w_up, w_down, cotangent],
        [
            kv_spec,
            gain_spec,
            query_spec,
            out_spec,
            column_spec,
            column_spec,
            down_spec,
            row_spec(cotangent.shape),
        ],
        row_spec((rows, 2 * kv_width)),
        heads,
        group_heads,
        sizes,
        1,
    )
    gain_first, gain_second = gain_rows[0], gain_rows[1]
    scale_second = lax.rsqrt(jnp.mean(middle * middle, axis=-1, keepdims=True) + epsilon)
    unit_second = middle * scale_second
    column_scatter = Scatter(
        "dp",
        (up_rows, units),
        lambda ref, dp, half, j: column_spec.half(ref, dp, half),
        (up_rows // 2, units),
        lambda ref, half: ref.at[pl.ds(half * (up_rows // 2), up_rows // 2), :],
    )
    down_scatter = Scatter(
        "dp",
        (units, down_cols),
        lambda ref, dp, half, j: down_spec.half(ref, dp, half),
        (units // 2, down_cols),
        lambda ref, half: ref.at[pl.ds(half * (units // 2), units // 2), :],
    )
    back_second, mlp_part, grad_gate_w, grad_up_w, sum_down = feed_forward(
        normed_own, cot_all, gate_full, up_full, down_full, [down_scatter], sizes, 3
    )
    mlp_rows = lax.psum_scatter(
        mlp_part.reshape(tensor_size * rows, width), "tensor", scatter_dimension=0, tiled=True
    )
    grad_gain_second = jnp.sum(back_second * unit_second, axis=0)
    grad_middle = cotangent.astype(jnp.float32) + norm_back(
        back_second, unit_second, scale_second, gain_second
    )
    middle_low = grad_middle.astype(jnp.bfloat16)
    grad_context = product_right(middle_low, out_full).astype(jnp.bfloat16)
    query_scatter = Scatter(
        "own",
        (q_rows, q_cols),
        lambda ref, dp, half, j: ref.at[
            j,
            pl.ds(pl.multiple_of(dp * q_rows + half * (q_rows // 2), q_rows // 2), q_rows // 2),
            :,
        ],
        (q_rows // 2, q_cols),
        lambda ref, half: ref.at[pl.ds(half * (q_rows // 2), q_rows // 2), :],
    )
    kv_scatter = Scatter(
        "cut",
        (kv_rows, 2 * kv_width),
        lambda ref, dp, half, j: ref.at[
            pl.ds(start_row(dp, kv_all_rows), kv_all_rows), pl.ds(half * kv_width, kv_width)
        ],
        (kv_all_rows, kv_width),
        lambda ref, half: ref.at[:, pl.ds(half * kv_width, kv_width)],
        lambda ref, j: ref.at[pl.ds(j * kv_rows, kv_rows), :],
        (kv_rows, kv_width),
    )
    out_scatter = Scatter(
        "own",
        (o_rows, o_cols),
        lambda ref, dp, half, j: ref.at[
            j,
            pl.ds(half * (o_rows // 2), o_rows // 2),
            pl.ds(start_row(dp, o_cols), o_cols),
        ],
        (o_rows // 2, o_cols),
        lambda ref, half: ref.at[pl.ds(half * (o_rows // 2), o_rows // 2), :],
    )
    gain_cols = tensor_size * gain_part
    gain_scatter = Scatter(
        "cut",
        (16, gain_cols),
        lambda ref, dp, half, j: ref.at[
            pl.ds(half * 8, 8), pl.ds(start_row(dp, gain_cols), gain_cols)
        ],
        (8, gain_cols),
        lambda ref, half: ref.at[pl.ds(half * 8, 8), :],
        lambda ref, j: ref,
        (8, gain_cols),
    )
    grad_queries, grad_keys, grad_values, sum_gate, sum_up = attend_back(
        queries,
        grad_context,
        log_sums,
        cosines,
        sines,
        kv_all,
        heads,
        group_heads,
        [column_scatter, column_scatter],
        [grad_gate_w, grad_up_w],
        sizes,
        7,
    )
    grad_kv = jnp.concatenate([grad_keys, grad_values], axis=1)
    grad_tokens, sum_out, sum_query, sum_kv, sum_gains = tail(
        context,
        middle_low,
        normed_first,
        grad_queries,
        key_value_full,
        tokens,
        grad_middle,
        grad_kv.reshape(tensor_size, rows, 2 * kv_width),
        query_full,
        cosines,
        sines,
        gain_first.reshape(1, width),
        grad_gain_second.reshape(1, width),
        [out_scatter, query_scatter, kv_scatter, gain_scatter],
        sizes,
        5,
    )
    sum_gains = lax.dynamic_slice_in_dim(sum_gains, tensor_index * gain_part, gain_part, 1)
    middle, mlp_rows, sum_query = lax.optimization_barrier((middle, mlp_rows, sum_query))
    output = (middle + mlp_rows.astype(jnp.float32)).astype(jnp.bfloat16)
    return (
        output,
        grad_tokens,
        sum_gains[0],
        sum_query,
        sum_kv[:, :kv_width],
        sum_kv[:, kv_width:],
        sum_out,
        sum_gains[8],
        sum_gate,
        sum_up,
        sum_down,
    )


def solution(mesh):
    placed = (
        P(("dp", "tensor"), None),
        P(("dp", "tensor")),
        P("dp", "tensor"),
        P(("dp", "tensor"), None),
        P(("dp", "tensor"), None),
        P("tensor", "dp"),
        P(("dp", "tensor")),
        P("dp", "tensor"),
        P("dp", "tensor"),
        P("tensor", "dp"),
        P(("dp", "tensor"), None),
    )
    return jax.shard_map(
        functools.partial(on_device, mesh.shape["dp"], mesh.shape["tensor"]),
        mesh=mesh,
        in_specs=placed,
        out_specs=(
            P(("dp", "tensor"), None),
            P(("dp", "tensor"), None),
            P(("dp", "tensor")),
            P("dp", "tensor"),
            P(("dp", "tensor"), None),
            P(("dp", "tensor"), None),
            P("tensor", "dp"),
            P(("dp", "tensor")),
            P("dp", "tensor"),
            P("dp", "tensor"),
            P("tensor", "dp"),
        ),
        check_vma=False,
    )
```

```python
import functools

import jax
import jax.numpy as jnp
from jax import lax
from jax.experimental import pallas as pl
from jax.experimental.pallas import tpu as pltpu
from jax.sharding import PartitionSpec as P

HEAD_DIM = 64
SEQLEN = 1024
MESH = pl.DeviceIdType.MESH
ANY = pl.BlockSpec(memory_space=pl.ANY)
VMEM = pl.BlockSpec(memory_space=pltpu.VMEM)
VMEM_LIMIT = 56 * 2**20

epsilon = 1e-05
theta_base = 10000.0


def product(left, right):
    return jnp.dot(left, right, preferred_element_type=jnp.float32)


def product_left(left, right):
    return lax.dot_general(
        left, right, (((0,), (0,)), ((), ())), preferred_element_type=jnp.float32
    )


def product_right(left, right):
    return lax.dot_general(
        left, right, (((1,), (1,)), ((), ())), preferred_element_type=jnp.float32
    )


def flip(index, bit):
    size = 1 << bit
    return index + size * (1 - 2 * lax.rem(lax.div(index, size), 2))


def masked(index, bits, rank):
    for place, bit in enumerate(bits):
        if rank >> place & 1:
            index = flip(index, bit)
    return index


def orders(bit_count, core_last):
    up = list(range(1, bit_count))
    down = up[::-1]
    return [up + [0], down + [0]] if core_last else [[0] + up, [0] + down]


def greet(spots, near, all_tensor, dp_bits):
    dp, tensor, tensor_size = spots
    barrier = pltpu.get_barrier_semaphore()

    def signal(where):
        pl.semaphore_signal(barrier, inc=1, device_id=where, device_id_type=MESH)

    peers = dp_bits
    for bit in range(dp_bits):
        signal((flip(dp, bit), tensor))
    if all_tensor:
        peers += tensor_size - 1
        for other in range(tensor_size):
            pl.when(other != tensor)(functools.partial(signal, (dp, other)))
    elif near:
        below, above = tensor > 0, tensor + 1 < tensor_size
        pl.when(below)(functools.partial(signal, (dp, tensor - 1)))
        pl.when(above)(functools.partial(signal, (dp, tensor + 1)))
        peers = peers + below.astype(jnp.int32) + above.astype(jnp.int32)
    pl.semaphore_wait(barrier, peers)


class Gather:
    def __init__(self, shape, slot, half=None, line=True, pieces=1):
        self.shape, self.slot, self.half, self.line = shape, slot, half, line
        self.pieces = pieces


class GatherRun:
    def __init__(self, specs, dp_size, tensor_size, sources, outs, held, sems):
        self.specs, self.sources, self.outs, self.held = specs, sources, outs, held
        self.own_sem, self.z_send, self.z_recv, self.h_send, self.h_recv = sems
        self.dp, self.tensor = lax.axis_index("dp"), lax.axis_index("tensor")
        self.tensor_size, self.dp_bits = tensor_size, dp_size.bit_length() - 1
        self.order = orders(self.dp_bits, True)
        self.hyper = [i for i, spec in enumerate(specs) if spec.half is not None]
        self.lines = [i for i, spec in enumerate(specs) if spec.line]
        self.base, total = {}, 0
        for i in self.hyper:
            self.base[i] = total
            total += specs[i].pieces
        self.can = [self.tensor + 1 < tensor_size, self.tensor > 0]

    def greet(self):
        greet(
            (self.dp, self.tensor, self.tensor_size),
            bool(self.lines),
            False,
            self.dp_bits if self.hyper else 0,
        )

    def z_copy(self, i, block, way, source=None):
        slot = self.specs[i].slot(self.outs[i], self.dp, block)
        return pltpu.make_async_remote_copy(
            src_ref=slot if source is None else source,
            dst_ref=slot,
            send_sem=self.z_send.at[i, way, block],
            recv_sem=self.z_recv.at[i, block],
            device_id=(self.dp, self.tensor + 1 if way == 0 else self.tensor - 1),
            device_id_type=MESH,
        )

    def own(self, i):
        slot = self.specs[i].slot(self.outs[i], self.dp, self.tensor)
        return pltpu.make_async_copy(self.held[i], slot, self.own_sem.at[i])

    def begin_line(self, i):
        for way in (0, 1):
            pl.when(self.can[way])(self.z_copy(i, self.tensor, way, self.sources[i]).start)

    def line(self, i, step):
        for way, block in ((0, self.tensor - step), (1, self.tensor + step)):

            @pl.when((block >= 0) & (block < self.tensor_size))
            def _():
                self.z_copy(i, block, way).wait_recv()
                pl.when(self.can[way])(self.z_copy(i, block, way).start)

    def part(self, i, half, rank, piece):
        place = masked(self.dp, self.order[half], rank)
        return self.specs[i].half(self.outs[i], place, half, piece)

    def h_copy(self, i, half, rank, place, piece):
        n = self.base[i] + piece
        return pltpu.make_async_remote_copy(
            src_ref=self.part(i, half, rank, piece),
            dst_ref=self.part(i, half, rank, piece),
            send_sem=self.h_send.at[n, half, rank, place],
            recv_sem=self.h_recv.at[n, half, rank | 1 << place],
            device_id=(flip(self.dp, self.order[half][place]), self.tensor),
            device_id_type=MESH,
        )

    def hop(self, i, rank, piece=0):
        n = self.base[i] + piece
        for half in (0, 1):
            if rank:
                wait_part(
                    self.part(i, half, rank, piece),
                    self.h_recv.at[n, half, rank],
                    self.h_send.at[n, half, 0, 0],
                    (flip(self.dp, 0), self.tensor),
                )
            for place in range(rank.bit_length(), self.dp_bits):
                self.h_copy(i, half, rank, place, piece).start()

    def hop_from(self, i, rank, step):
        if step == 0:
            self.hop(i, rank, self.tensor)
            return
        for block in (self.tensor - step, self.tensor + step):

            @pl.when((block >= 0) & (block < self.tensor_size))
            def _():
                self.hop(i, rank, block)

    def end_line(self, i):
        self.own(i).wait()

    def close(self):
        for rank in range(1 << self.dp_bits):
            for i in self.hyper:
                for piece in range(self.specs[i].pieces):
                    for half in (0, 1):
                        for place in range(rank.bit_length(), self.dp_bits):
                            self.h_copy(i, half, rank, place, piece).wait_send()
        for i in self.lines:
            for block in range(self.tensor_size):
                for way in (0, 1):
                    sent = self.can[way] & (
                        (block <= self.tensor) if way == 0 else (block >= self.tensor)
                    )
                    pl.when(sent)(self.z_copy(i, block, way).wait_send)


def gather_scratch(specs, arrays, dp_size, tensor_size):
    count = len(specs)
    hyper = max(1, sum(spec.pieces for spec in specs if spec.half is not None))
    dp_bits = dp_size.bit_length() - 1
    return [pltpu.VMEM(array.shape, array.dtype) for array in arrays], [
        pltpu.SemaphoreType.DMA((count,)),
        pltpu.SemaphoreType.DMA((count, 2, tensor_size)),
        pltpu.SemaphoreType.DMA((count, tensor_size)),
        pltpu.SemaphoreType.DMA((hyper, 2, dp_size, max(dp_bits, 1))),
        pltpu.SemaphoreType.DMA((hyper, 2, dp_size)),
    ]


def wait_part(part, recv_sem, send_sem, device):
    pltpu.make_async_remote_copy(
        src_ref=part,
        dst_ref=part,
        send_sem=send_sem,
        recv_sem=recv_sem,
        device_id=device,
        device_id_type=MESH,
    ).wait_recv()


def gather_shapes(specs, arrays):
    return [jax.ShapeDtypeStruct(spec.shape, array.dtype) for spec, array in zip(specs, arrays)]


class Scatter:
    def __init__(self, kind, shape, part, part_shape, place, cut=None, cut_shape=None):
        self.kind, self.shape, self.part, self.part_shape = kind, shape, part, part_shape
        self.place, self.cut = place, cut
        self.cut_shape = part_shape if kind == "own" else cut_shape


def add_into(total, extra):
    shape = total.shape
    rows = shape[-2]
    slab = min(16, rows)
    if len(shape) == 2:

        def body(step, carry):
            at = pl.ds(pl.multiple_of(step * slab, slab), slab)
            total[at, :] = total[at, :] + extra[at, :]
            return carry

        lax.fori_loop(0, rows // slab, body, 0, unroll=4 if (rows // slab) % 4 == 0 else 1)
    else:
        for lead in range(shape[0]):
            add_into(total.at[lead], extra.at[lead])


class ScatterRun:
    def __init__(self, specs, dp_size, tensor_size, sources, outs, scratch, in_place=False):
        scratch = list(scratch)
        self.specs, self.sources, self.outs = specs, sources, outs
        self.tensor_size, self.dp_bits = tensor_size, dp_size.bit_length() - 1
        self.in_place = in_place
        self.total = None if in_place else [scratch.pop(0) for _ in specs]
        self.landing = [[scratch.pop(0) for _ in range(self.dp_bits)] for _ in specs]
        self.shares = [scratch.pop(0) if spec.kind != "dp" else None for spec in specs]
        self.own_sem, self.send, self.recv, self.z_send, self.z_recv = scratch
        self.dp, self.tensor = lax.axis_index("dp"), lax.axis_index("tensor")
        self.order = orders(self.dp_bits, False)
        self.units = scatter_units(specs, tensor_size)

    def greet(self):
        cuts = any(spec.kind != "dp" for spec in self.specs)
        greet((self.dp, self.tensor, self.tensor_size), False, cuts, self.dp_bits)

    def slots(self, stage):
        return range(1 << (self.dp_bits - 1 - stage))

    def part(self, unit, half, rank):
        i, owner = self.units[unit]
        place = masked(self.dp, self.order[half], rank)
        return self.specs[i].part(self.sources[i], place, half, owner or 0)

    def sum_at(self, unit, half, slot):
        i, owner = self.units[unit]
        if self.in_place:
            return self.part(unit, half, 2 * slot)
        return self.total[i].at[owner or 0, half, slot]

    def own_copy(self, unit, half, slot):
        return pltpu.make_async_copy(
            self.part(unit, half, 2 * slot),
            self.sum_at(unit, half, slot),
            self.own_sem.at[unit, half, slot],
        )

    def landed(self, unit, half, stage, slot):
        i, owner = self.units[unit]
        return self.landing[i][stage].at[owner or 0, half, slot]

    def copy(self, unit, half, stage, slot):
        if stage == 0:
            source = self.part(unit, half, 2 * slot + 1)
        else:
            source = self.sum_at(unit, half, (2 * slot + 1) << (stage - 1))
        return pltpu.make_async_remote_copy(
            src_ref=source,
            dst_ref=self.landed(unit, half, stage, slot),
            send_sem=self.send.at[unit, half, stage, slot],
            recv_sem=self.recv.at[unit, half, stage, slot],
            device_id=(flip(self.dp, self.order[half][stage]), self.tensor),
            device_id_type=MESH,
        )

    def begin_unit(self, unit):
        for slot in self.slots(0):
            for half in (0, 1):
                self.copy(unit, half, 0, slot).start()
                if not self.in_place:
                    self.own_copy(unit, half, slot).start()

    def begin(self):
        for unit in range(len(self.units)):
            self.begin_unit(unit)

    def z_copy(self, unit, half, other, slot):
        i, owner = self.units[unit]
        spec, total = self.specs[i], self.sum_at(unit, half, 0)
        return pltpu.make_async_remote_copy(
            src_ref=total if spec.kind == "own" else spec.cut(total, other),
            dst_ref=self.shares[i].at[slot, half],
            send_sem=self.z_send.at[i, half, other],
            recv_sem=self.z_recv.at[i, half, slot],
            device_id=(self.dp, other),
            device_id_type=MESH,
        )

    def others(self, unit):
        owner = self.units[unit][1]
        return range(self.tensor_size) if owner is None else [owner]

    def step(self, unit, stage):
        i, owner = self.units[unit]
        spec = self.specs[i]
        if stage < self.dp_bits:
            for slot in sorted(self.slots(stage), key=lambda s: -(s & 1)):
                for half in (0, 1):
                    if stage == 0 and not self.in_place:
                        self.own_copy(unit, half, slot).wait()
                    self.copy(unit, half, stage, slot).wait_recv()
                    add_into(
                        self.sum_at(unit, half, slot << stage),
                        self.landed(unit, half, stage, slot),
                    )
                    if slot & 1:
                        self.copy(unit, half, stage + 1, slot >> 1).start()
            return
        for half in (0, 1):
            total = self.sum_at(unit, half, 0)
            if spec.kind == "dp":
                spec.place(self.outs[i], half)[...] = total[...].astype(jnp.float32)
                continue
            for other in self.others(unit):

                @pl.when(other != self.tensor)
                def _():
                    self.z_copy(unit, half, other, self.tensor).start()

                @pl.when(other == self.tensor)
                def _():
                    mine = total if spec.kind == "own" else spec.cut(total, other)
                    self.shares[i][other, half] = mine[...]

    def steps(self):
        count = len(self.units)
        return [
            (unit, turn - unit)
            for turn in range(count + self.dp_bits)
            for unit in range(count)
            if 0 <= turn - unit <= self.dp_bits
        ]

    def close(self):
        for i, spec in enumerate(self.specs):
            if spec.kind == "dp":
                continue
            unit = [u for u, (at, owner) in enumerate(self.units) if at == i][0]
            for half in (0, 1):
                for other in range(self.tensor_size):

                    @pl.when(other != self.tensor)
                    def _():
                        self.z_copy(unit, half, other, other).wait_recv()

                summed = self.shares[i][0, half].astype(jnp.float32)
                for other in range(1, self.tensor_size):
                    summed = summed + self.shares[i][other, half].astype(jnp.float32)
                spec.place(self.outs[i], half)[...] = summed
        for unit, (i, owner) in enumerate(self.units):
            for half in (0, 1):
                for stage in range(self.dp_bits):
                    for slot in self.slots(stage):
                        self.copy(unit, half, stage, slot).wait_send()
                if self.specs[i].kind != "dp":
                    for other in self.others(unit):

                        @pl.when(other != self.tensor)
                        def _():
                            self.z_copy(unit, half, other, self.tensor).wait_send()


def scatter_units(specs, tensor_size):
    units = []
    for i, spec in enumerate(specs):
        units += [(i, j) for j in range(tensor_size)] if spec.kind == "own" else [(i, None)]
    return units


def scatter_scratch(specs, arrays, dp_size, tensor_size, in_place=False):
    dp_bits = dp_size.bit_length() - 1
    scratch = []
    units = len(scatter_units(specs, tensor_size))
    pieces = [tensor_size if spec.kind == "own" else 1 for spec in specs]
    for spec, array, count in zip(specs, arrays, pieces):
        if not in_place:
            scratch.append(pltpu.VMEM((count, 2, dp_size // 2) + spec.part_shape, array.dtype))
    for spec, array, count in zip(specs, arrays, pieces):
        for stage in range(dp_bits):
            scratch.append(
                pltpu.VMEM((count, 2, dp_size >> (stage + 1)) + spec.part_shape, array.dtype)
            )
    for spec, array in zip(specs, arrays):
        if spec.kind != "dp":
            scratch.append(pltpu.VMEM((tensor_size, 2) + spec.cut_shape, array.dtype))
    dma = pltpu.SemaphoreType.DMA
    return scratch + [
        dma((units, 2, dp_size // 2)),
        dma((units, 2, dp_bits, dp_size // 2)),
        dma((units, 2, dp_bits, dp_size // 2)),
        dma((len(specs), 2, tensor_size)),
        dma((len(specs), 2, tensor_size)),
    ]


def scatter_shapes(specs):
    return [jax.ShapeDtypeStruct(spec.shape, jnp.float32) for spec in specs]


class ExchangeRun:
    def __init__(self, tensor_size, source, out, own_sem, send, recv):
        self.tensor_size, self.source, self.out = tensor_size, source, out
        self.own_sem, self.send, self.recv = own_sem, send, recv
        self.dp, self.tensor = lax.axis_index("dp"), lax.axis_index("tensor")

    def copy(self, other, slot):
        return pltpu.make_async_remote_copy(
            src_ref=self.source.at[other],
            dst_ref=self.out.at[slot],
            send_sem=self.send.at[other],
            recv_sem=self.recv.at[slot],
            device_id=(self.dp, other),
            device_id_type=MESH,
        )

    def own(self):
        return pltpu.make_async_copy(
            self.source.at[self.tensor], self.out.at[self.tensor], self.own_sem
        )

    def begin(self):
        for other in range(self.tensor_size):
            pl.when(other != self.tensor)(self.copy(other, self.tensor).start)
        self.own().start()

    def close(self):
        self.own().wait()
        for other in range(self.tensor_size):

            @pl.when(other != self.tensor)
            def _():
                self.copy(other, self.tensor).wait_send()
                self.copy(other, other).wait_recv()


def lanes_of(shape):
    return lax.broadcasted_iota(jnp.int32, shape, len(shape) - 1)


def swap_halves(values):
    width = values.shape[-1]
    first = lanes_of(values.shape) % HEAD_DIM < HEAD_DIM // 2
    return jnp.where(
        first,
        pltpu.roll(values, width - HEAD_DIM // 2, 1),
        pltpu.roll(values, HEAD_DIM // 2, 1),
    )


def left_head(block, odd):
    moved = jnp.where(odd, pltpu.roll(block, HEAD_DIM, 1), block)
    return jnp.where(lanes_of(block.shape) < HEAD_DIM, moved, jnp.zeros_like(moved))


def allowed(keys, rows, start):
    key_at = lax.broadcasted_iota(jnp.int32, (keys, rows), 0)
    query_at = lax.broadcasted_iota(jnp.int32, (keys, rows), 1) + start
    return key_at <= query_at


def at_steps(actions, step, steps):
    places = [(min(steps - 1, int(time * steps)), action) for time, action in actions]
    for place in sorted({place for place, _ in places}):

        @pl.when(step == place)
        def _():
            for at, action in places:
                if at == place:
                    action()


def attend_pair(pair, group_pairs, q_pre, cos_ref, sin_ref, kv_all, k_left, v_turned, outs):
    context, queries_out, lse_ref = outs
    rows = q_pre.shape[0]
    kv_width = kv_all.shape[1] // 2
    group = lax.div(pair, group_pairs)
    start = lax.axis_index("tensor") * rows
    at = pl.ds(pl.multiple_of(pair * 128, 128), 128)

    @pl.when(lax.rem(pair, group_pairs) == 0)
    def _():
        odd = lax.rem(group, 2) == 1
        lane = pl.multiple_of(lax.div(group, 2) * 128, 128)
        keys = kv_all[:, pl.ds(lane, 128)].astype(jnp.float32)
        values = kv_all[:, pl.ds(kv_width + lane, 128)].astype(jnp.float32)
        k_left[...] = left_head(keys, odd).astype(jnp.bfloat16)
        v_turned[...] = left_head(values, odd).T[:HEAD_DIM].astype(jnp.bfloat16)

    raw = q_pre[:, at]
    turned = (raw * cos_ref[...] + swap_halves(raw) * sin_ref[...]).astype(jnp.bfloat16)
    turned = turned.astype(jnp.float32) * HEAD_DIM ** (-0.5)
    queries_out[:, at] = turned.astype(jnp.bfloat16)
    open_at = allowed(k_left.shape[0], rows, start)
    contexts = []
    for head in (0, 1):
        queries = (turned if head == 0 else pltpu.roll(turned, HEAD_DIM, 1)).astype(jnp.bfloat16)
        scores = product_right(k_left[...], queries)
        scores = jnp.where(open_at, scores, -1e30)
        top = jnp.max(scores, axis=0, keepdims=True)
        exponent = jnp.exp(scores - top)
        summed = jnp.sum(exponent, axis=0, keepdims=True)
        part = product(v_turned[...], exponent.astype(jnp.bfloat16))
        contexts.append(part * (1.0 / summed))
        lse_ref[pair, pl.ds(head, 1), :] = top + jnp.log(summed)
    context[:, at] = jnp.concatenate(contexts, axis=0).T.astype(jnp.bfloat16)


def front_kernel(specs, kv_spec, n_spec, group_pairs, dp_size, tensor_size, *refs):
    refs = list(refs)

    def take(count):
        return [refs.pop(0) for _ in range(count)]

    count = len(specs)
    tokens, cos_ref, sin_ref = take(3)
    sources = take(count)
    context, queries, lse_ref, normed, middle, gain_rows, kv_all, normed_all = take(8)
    outs = take(count)
    held = take(count)
    weights, kv_weights, gain_blocks, q_pre, k_left, v_turned, normed_two = take(7)
    sems = take(5)
    kv_sems = take(5)
    n_sems = take(5)
    (load_sem,) = take(1)
    key_value, gains, query, out, gate, up, cot = range(count)
    run = GatherRun(specs, dp_size, tensor_size, sources, outs, held, sems)
    rows, width = tokens.shape
    own_rows = pl.ds(pl.multiple_of(run.tensor * rows, rows), rows)
    kv_run = GatherRun(
        [kv_spec], dp_size, tensor_size, [kv_all.at[own_rows, :]], [kv_all], [None], kv_sems
    )
    kv_width = kv_all.shape[1] // 2
    near = [1 << bit for bit in range(run.dp_bits - 1)]
    far = [r for r in range(1, 1 << (run.dp_bits - 1)) if r not in near]
    far.sort(key=lambda rank: rank.bit_count())
    core = list(range(1 << (run.dp_bits - 1), 1 << run.dp_bits))

    n_run = GatherRun(
        [n_spec], dp_size, tensor_size, [normed_two], [normed_all], [normed_two], n_sems
    )

    def hops(ranks, *units):
        for unit in units:
            for rank in ranks:
                run.hop(unit, rank)

    def query_hops(ranks, *steps):
        for step in steps:
            for rank in ranks:
                run.hop_from(query, rank, step)

    run.greet()
    loads = [
        pltpu.make_async_copy(source, target, run.own_sem.at[i])
        for i, (source, target) in enumerate(zip(sources, held))
    ]
    for load in loads:
        load.start()
    small = (key_value, gains)
    for i in (*small, query):
        run.begin_line(i)
    for i in (query, key_value, gains, out, gate, up, cot):
        loads[i].wait()
        run.own(i).start()
        if i == query:
            run.end_line(query)
            query_hops([0], 0)
    for step in range(1, tensor_size):
        for i in small:
            run.line(i, step)
    for i in small:
        run.end_line(i)
    hops([0], *small)
    steps = range(1, tensor_size)
    for step in steps:
        run.line(query, step)
        query_hops([0], step)
        if step == max(1, tensor_size - 2):
            hops(near, *small)
    run.begin_line(out)
    run.begin_line(cot)
    hops(far, *small)
    hops(core, *small)
    run.line(out, 1)

    kv_load = pltpu.make_async_copy(outs[key_value], kv_weights, load_sem.at[0])
    kv_load.start()
    gain_load = pltpu.make_async_copy(outs[gains], gain_blocks, load_sem.at[1])
    gain_load.start()
    gain_load.wait()
    blocks = gain_blocks.shape[0] // 16
    lanes = width // 128
    per = blocks // lanes
    for lane in range(lanes):
        row = jnp.zeros((16, 128), jnp.float32)
        for other in range(per):
            at = (lane * per + other) * 16
            row = row + gain_blocks[at : at + 16, :].astype(jnp.float32)
        gain_rows[:, lane * 128 : (lane + 1) * 128] = row[:8]
    slab = 16

    def norm_first(step, carry):
        at = pl.ds(pl.multiple_of(step * slab, slab), slab)
        raw = tokens[at, :].astype(jnp.float32)
        scale = lax.rsqrt(jnp.mean(raw * raw, axis=-1, keepdims=True) + epsilon)
        normed[at, :] = (raw * scale * gain_rows[0:1, :]).astype(normed.dtype)
        return carry

    lax.fori_loop(0, rows // slab, norm_first, 0)
    kv_load.wait()
    own_kv = product(normed[...], kv_weights[...])
    repeat = kv_width // cos_ref.shape[1]
    own_keys = own_kv[:, :kv_width]
    own_keys = own_keys * jnp.concatenate([cos_ref[...]] * repeat, axis=1) + swap_halves(
        own_keys
    ) * jnp.concatenate([sin_ref[...]] * repeat, axis=1)
    kv_all[own_rows, :] = jnp.concatenate([own_keys, own_kv[:, kv_width:]], axis=1).astype(
        kv_all.dtype
    )
    kv_run.begin_line(0)
    query_hops(near, 0, *steps)
    kv_run.line(0, 1)
    query_hops(far, 0, *steps)
    for step in steps[1:-1]:
        run.line(out, step)
        kv_run.line(0, step)
    query_hops(core, 0, *steps)
    query_load = pltpu.make_async_copy(outs[query], weights, load_sem.at[0])
    query_load.start()
    for step in steps[-1:]:
        run.line(out, step)
    for i in (out, gate, up):
        run.end_line(i)
    hops([0], out)
    query_load.wait()
    tiles = 4
    tile = width // tiles
    for j in range(tiles):
        columns = slice(j * tile, (j + 1) * tile)
        q_pre[:, columns] = product(normed[...], weights[:, columns])
        if j == 1:
            for step in steps[-1:]:
                kv_run.line(0, step)
    pairs = lse_ref.shape[0]
    plan = [
        (0.3, lambda: hops(near, out)),
        (0.31, lambda: hops([0], gate)),
        (0.75, lambda: hops(far, out)),
        (0.88, lambda: hops(near, gate)),
        (0.89, lambda: hops([0], up)),
    ]
    early = max(1, tensor_size - 2)
    for step in steps[:early]:
        plan.append((0.2 + 0.75 * (step - 1) / early, functools.partial(run.line, cot, step)))
    plan.sort(key=lambda entry: entry[0])

    def pair_step(pair, carry):
        at_steps(plan, pair, pairs)
        attend_pair(
            pair,
            group_pairs,
            q_pre,
            cos_ref,
            sin_ref,
            kv_all,
            k_left,
            v_turned,
            (context, queries, lse_ref),
        )
        return carry

    lax.fori_loop(0, pairs, pair_step, 0)
    hops(core, out)
    out_load = pltpu.make_async_copy(outs[out], weights, load_sem.at[0])
    out_load.start()
    out_load.wait()
    for j in range(4):
        columns = slice(j * (width // 4), (j + 1) * (width // 4))
        middle[:, columns] = tokens[:, columns].astype(jnp.float32) + product(
            context[...], weights[:, columns]
        )

    def norm_second(step, carry):
        at = pl.ds(pl.multiple_of(step * slab, slab), slab)
        raw = middle[at, :]
        scale = lax.rsqrt(jnp.mean(raw * raw, axis=-1, keepdims=True) + epsilon)
        normed_two[at, :] = (raw * scale * gain_rows[1:2, :]).astype(normed_two.dtype)
        return carry

    lax.fori_loop(0, rows // slab, norm_second, 0)
    n_run.begin_line(0)
    n_run.own(0).start()
    hops(far, gate)
    for step in steps[early:]:
        run.line(cot, step)
    hops(near, up)
    hops(core, gate)
    hops(far, up)
    hops(core, up)
    for way, block in ((0, run.tensor - 1), (1, run.tensor + 1)):
        arrives = (block >= 0) & (block < tensor_size)
        pl.when(arrives)(n_run.z_copy(0, block, way).wait_recv)
        pl.when(run.can[way])(n_run.z_copy(0, run.tensor, way, normed_two).wait_send)
    n_run.end_line(0)
    run.end_line(cot)
    run.close()
    kv_run.close()


def front(
    tokens, cosines, sines, arrays, specs, kv_spec, n_spec, heads, group_heads, sizes, collective_id
):
    dp_size, tensor_size = sizes
    rows, width = tokens.shape
    length = rows * tensor_size
    low, full = jnp.bfloat16, jnp.float32
    held, sems = gather_scratch(specs, arrays, *sizes)
    _, line_sems = gather_scratch([kv_spec], [], *sizes)
    kv_both = specs[0].shape[1]
    pairs = heads // 2
    tokens_low = jax.ShapeDtypeStruct((rows, width), low)
    return pl.pallas_call(
        functools.partial(front_kernel, specs, kv_spec, n_spec, group_heads // 2, *sizes),
        out_shape=[
            tokens_low,
            tokens_low,
            jax.ShapeDtypeStruct((pairs, 2, rows), full),
            tokens_low,
            jax.ShapeDtypeStruct((rows, width), full),
            jax.ShapeDtypeStruct((8, width), full),
            jax.ShapeDtypeStruct((length, kv_both), low),
            jax.ShapeDtypeStruct((length, width), low),
        ]
        + gather_shapes(specs, arrays),
        in_specs=[VMEM] * 3 + [ANY] * len(specs),
        out_specs=[VMEM] * 7 + [ANY] * (1 + len(specs)),
        scratch_shapes=held
        + [
            pltpu.VMEM((width, width), low),
            pltpu.VMEM((width, kv_both), low),
            pltpu.VMEM(specs[1].shape, low),
            pltpu.VMEM((rows, width), full),
            pltpu.VMEM((length, 128), low),
            pltpu.VMEM((HEAD_DIM, length), low),
            pltpu.VMEM((rows, width), low),
        ]
        + sems
        + line_sems
        + line_sems
        + [pltpu.SemaphoreType.DMA((2,))],
        compiler_params=pltpu.CompilerParams(
            collective_id=collective_id, has_side_effects=True, vmem_limit_bytes=VMEM_LIMIT
        ),
    )(tokens, cosines, sines, *arrays)


def scatter_plan(run):
    plan = [(0.0, run.greet), (0.0, run.begin)]
    times = [(0.12, 0.08), (0.55, 0.3), (0.88, 0.12), (0.95, 0.05)]
    for unit, stage in run.steps():
        first, behind = times[min(stage, len(times) - 1)]
        plan.append((min(first + behind * unit, 1.0), functools.partial(run.step, unit, stage)))
    plan.sort(key=lambda entry: entry[0])
    return plan + [(1.0, run.close)]


def attend_back_kernel(group_pairs, pairs, specs, dp_size, tensor_size, *refs):
    refs = list(refs)
    q_ref, out_ref, lse_ref, cos_ref, sin_ref, k_ref, v_ref = (refs.pop(0) for _ in range(7))
    back_ref, middle_ref, cot_ref, gain_ref = (refs.pop(0) for _ in range(4))
    sources = [refs.pop(0) for _ in specs]
    dq_ref, dk_ref, dv_ref, grad_middle, middle_low, gain_sum = (refs.pop(0) for _ in range(6))
    outs = [refs.pop(0) for _ in specs]
    k_left, v_left, k_turned, dk_sum, dv_sum, column_sum = (refs.pop(0) for _ in range(6))
    run = ScatterRun(specs, dp_size, tensor_size, sources, outs, refs)
    plan = scatter_plan(run)
    at_steps([entry for entry in plan if entry[0] < 1.0], pl.program_id(0), pairs)
    pair = pl.program_id(0)
    group = pair // group_pairs
    odd = group % 2 == 1
    rows = q_ref.shape[0]
    start = lax.axis_index("tensor") * rows

    @pl.when(pair == 0)
    def _():
        slab = 16
        column_sum[...] = jnp.zeros_like(column_sum)

        def norm_slab(step, carry):
            at = pl.ds(pl.multiple_of(step * slab, slab), slab)
            raw = middle_ref[at, :]
            scale = lax.rsqrt(jnp.mean(raw * raw, axis=-1, keepdims=True) + epsilon)
            unit = raw * scale
            grad = back_ref[at, :]
            gained = grad * unit
            column_sum[...] += gained[:8] + gained[8:]
            scaled = grad * gain_ref[...]
            mean = jnp.mean(scaled * unit, axis=-1, keepdims=True)
            total = cot_ref[at, :].astype(jnp.float32) + scale * (scaled - unit * mean)
            grad_middle[at, :] = total
            middle_low[at, :] = total.astype(middle_low.dtype)
            return carry

        lax.fori_loop(0, rows // slab, norm_slab, 0)
        gain_sum[...] = jnp.sum(column_sum[...], axis=0, keepdims=True)

    grad_context = product_right(middle_low[...], out_ref[...])

    @pl.when(pair % group_pairs == 0)
    def _():
        left = left_head(k_ref[...].astype(jnp.float32), odd)
        k_left[...] = left.astype(jnp.bfloat16)
        k_turned[...] = left.T[:HEAD_DIM].astype(jnp.bfloat16)
        v_left[...] = left_head(v_ref[...].astype(jnp.float32), odd).astype(jnp.bfloat16)
        dk_sum[...] = jnp.zeros_like(dk_sum)
        dv_sum[...] = jnp.zeros_like(dv_sum)

    open_at = allowed(k_left.shape[0], rows, start)
    grads = []
    for head in (0, 1):
        queries, grad_out = q_ref[...], grad_context.astype(jnp.bfloat16)
        if head == 1:
            queries = pltpu.roll(queries.astype(jnp.float32), HEAD_DIM, 1).astype(jnp.bfloat16)
            grad_out = pltpu.roll(grad_context, HEAD_DIM, 1).astype(jnp.bfloat16)
        scores = product_right(k_left[...], queries)
        scores = jnp.where(open_at, scores, -1e30)
        softmaxed = jnp.exp(scores - lse_ref[0, head, :][None, :])
        grad_soft = product_right(v_left[...], grad_out)
        mixed = softmaxed * grad_soft
        mixed_sum = jnp.sum(mixed, axis=0, keepdims=True)
        grad_scores = (mixed - softmaxed * mixed_sum).astype(jnp.bfloat16)
        dv_sum[...] += product(softmaxed.astype(jnp.bfloat16), grad_out)
        dk_sum[...] += product(grad_scores, queries)
        grads.append(product(k_turned[...], grad_scores))
    grad_q = jnp.concatenate(grads, axis=0).T * HEAD_DIM ** (-0.5)
    dq_ref[...] = (grad_q * cos_ref[...] - swap_halves(grad_q) * sin_ref[...]).astype(jnp.bfloat16)

    @pl.when(pair % group_pairs == group_pairs - 1)
    def _():
        for total, out in ((dk_sum, dk_ref), (dv_sum, dv_ref)):
            value = total[...]
            left = lanes_of(value.shape) < HEAD_DIM

            @pl.when(jnp.logical_not(odd))
            def _():
                out[...] = jnp.where(left, value, 0.0).astype(out.dtype)

            @pl.when(odd)
            def _():
                out[...] = jnp.where(
                    left, out[...].astype(jnp.float32), pltpu.roll(value, HEAD_DIM, 1)
                ).astype(out.dtype)
    at_steps([entry for entry in plan if entry[0] >= 1.0], pair, pairs)


def attend_back(
    queries,
    out_full,
    lse,
    cosines,
    sines,
    keys_values,
    back,
    middle,
    cotangent,
    gain,
    head_count,
    group_heads,
    specs,
    arrays,
    sizes,
    collective_id,
):
    rows, width = queries.shape
    length, both = keys_values.shape
    pairs, group_pairs = head_count // 2, group_heads // 2
    kv_blocks = both // 256
    low, full = jnp.bfloat16, jnp.float32
    wide = pl.BlockSpec((rows, 128), lambda p: (0, p))
    table = pl.BlockSpec((rows, 128), lambda p: (0, 0))
    kv_out = pl.BlockSpec((length, 128), lambda p: (0, p // group_pairs // 2))
    return pl.pallas_call(
        functools.partial(attend_back_kernel, group_pairs, pairs, specs, *sizes),
        grid=(pairs,),
        out_shape=[
            jax.ShapeDtypeStruct((rows, width), low),
            jax.ShapeDtypeStruct((length, both // 2), low),
            jax.ShapeDtypeStruct((length, both // 2), low),
            jax.ShapeDtypeStruct((rows, width), full),
            jax.ShapeDtypeStruct((rows, width), low),
            jax.ShapeDtypeStruct((1, width), full),
        ]
        + scatter_shapes(specs),
        in_specs=[
            wide,
            pl.BlockSpec((128, width), lambda p: (p, 0)),
            pl.BlockSpec((1, 2, rows), lambda p: (p, 0, 0)),
            table,
            table,
            pl.BlockSpec((length, 128), lambda p: (0, p // group_pairs // 2)),
            pl.BlockSpec((length, 128), lambda p: (0, kv_blocks + p // group_pairs // 2)),
        ]
        + [VMEM] * 4
        + [ANY] * len(specs),
        out_specs=[wide, kv_out, kv_out] + [VMEM] * (3 + len(specs)),
        scratch_shapes=[
            pltpu.VMEM((length, 128), low),
            pltpu.VMEM((length, 128), low),
            pltpu.VMEM((HEAD_DIM, length), low),
            pltpu.VMEM((length, 128), full),
            pltpu.VMEM((length, 128), full),
            pltpu.VMEM((8, width), full),
        ]
        + scatter_scratch(specs, arrays, *sizes),
        compiler_params=pltpu.CompilerParams(
            collective_id=collective_id, has_side_effects=True, vmem_limit_bytes=VMEM_LIMIT
        ),
        cost_estimate=pl.CostEstimate(
            flops=10 * rows * length * width, bytes_accessed=8 * rows * width, transcendentals=0
        ),
    )(
        queries,
        out_full,
        lse,
        cosines,
        sines,
        keys_values,
        keys_values,
        back,
        middle,
        cotangent,
        gain,
        *arrays,
    )


def block_at(place, tensor, tensor_size):
    above = tensor_size - 1 - tensor
    up = jnp.where(place < above, tensor + 1 + place, tensor - 1 - (place - above))
    down = jnp.where(place < tensor, tensor - 1 - place, 1 + place)
    other = jnp.where(tensor <= above, up, down)
    return jnp.where(place == tensor_size - 1, tensor, other)


def mlp_kernel(
    gather_specs,
    specs,
    dp_size,
    tensor_size,
    normed_ref,
    cot_ref,
    gate_ref,
    up_ref,
    down_ref,
    back_ref,
    y_ref,
    d_gate_ref,
    d_up_ref,
    down_sum,
    normed,
    cot,
    gate,
    up,
    down,
    hidden,
    d_gate,
    d_up,
    y_stage,
    stage,
    landing,
    load_sem,
    n_send,
    n_recv,
    y_sem,
    b_send,
    b_recv,
    out_sem,
    *more_refs,
):
    run = ScatterRun(
        specs, dp_size, tensor_size, [down], [down_sum], more_refs[5:], in_place=True
    )
    down_run = GatherRun(
        gather_specs, dp_size, tensor_size, [down_ref], [down], [down_ref], more_refs[:5]
    )
    dp, tensor = lax.axis_index("dp"), lax.axis_index("tensor")
    _, rows, width = normed_ref.shape
    units = gate.shape[1]
    loads = [
        pltpu.make_async_copy(source, target, load_sem.at[i])
        for i, (source, target) in enumerate(((gate_ref, gate), (up_ref, up), (cot_ref, cot)))
    ]
    has = [tensor + 1 < tensor_size, tensor > 0]

    def near_load(step):
        block = tensor + step
        return pltpu.make_async_copy(
            normed_ref.at[block], normed.at[block], load_sem.at[4 + step]
        )

    def near_loads(act):
        act(near_load(0))
        for way, step in ((0, 1), (1, -1)):

            @pl.when(has[way])
            def _():
                act(near_load(step))

    near_loads(lambda load: load.start())
    down_run.own(0).start()
    for load in loads:
        load.start()
    greet((dp, tensor, tensor_size), False, True, run.dp_bits)

    def n_copy(block, way, source=None):
        return pltpu.make_async_remote_copy(
            src_ref=normed.at[block] if source is None else source,
            dst_ref=normed.at[block],
            send_sem=n_send.at[way, block],
            recv_sem=n_recv.at[block],
            device_id=(dp, tensor + 1 if way == 0 else tensor - 1),
            device_id_type=MESH,
        )

    for way, step in ((0, -1), (1, 1)):
        both = has[0] & has[1]
        pl.when(both)(n_copy(tensor + step, way, normed_ref.at[tensor + step]).start)
    down_run.end_line(0)
    down_run.hop(0, 0)
    landing[tensor] = jnp.zeros((rows, width), landing.dtype)

    def pump(distance):
        for way, block in ((0, tensor - distance), (1, tensor + distance)):

            @pl.when((block >= 0) & (block < tensor_size))
            def _():
                n_copy(block, way).wait_recv()
                pl.when(has[way])(n_copy(block, way).start)

    farthest = jnp.maximum(tensor, tensor_size - 1 - tensor)
    core_rank = 1 << (run.dp_bits - 1)
    down_ranks = [
        sorted(range(1, core_rank), key=lambda rank: rank.bit_count()),
        range(core_rank, 2 * core_rank),
    ]

    def b_copy(block, slot):
        return pltpu.make_async_remote_copy(
            src_ref=stage.at[block],
            dst_ref=landing.at[slot],
            send_sem=b_send.at[block],
            recv_sem=b_recv.at[slot],
            device_id=(dp, block),
            device_id_type=MESH,
        )

    def y_copy(block, slot):
        return pltpu.make_async_copy(y_stage.at[slot], y_ref.at[block], y_sem.at[slot])

    for load in loads:
        load.wait()
    near_loads(lambda load: load.wait())

    def chunk(place, carry):
        block = block_at(place, tensor, tensor_size)
        rows_in = normed[block]
        gate_pre = product(rows_in, gate[...])
        upward = product(rows_in, up[...])

        @pl.when(place == 0)
        def _():
            for rank in down_ranks[0]:
                down_run.hop(0, rank)

        @pl.when(place + 2 <= farthest)
        def _():
            pump(place + 2)

        @pl.when(place == 0)
        def _():
            for rank in down_ranks[1]:
                down_run.hop(0, rank)

        sigmoid = 1.0 / (1.0 + jnp.exp(-gate_pre))
        silu = gate_pre * sigmoid
        active = (silu * upward).astype(jnp.bfloat16)
        hidden[block] = active
        slot = lax.rem(place, 2)

        @pl.when(place >= 2)
        def _():
            y_copy(block, slot).wait()

        y_stage[slot] = product(active, down[...]).astype(jnp.bfloat16)
        y_copy(block, slot).start()
        grad_hidden = product_right(cot[block], down[...])
        low_gate = (
            grad_hidden * upward * sigmoid * (1.0 + gate_pre * (1.0 - sigmoid))
        ).astype(jnp.bfloat16)
        low_up = (grad_hidden * silu).astype(jnp.bfloat16)
        d_gate[block] = low_gate
        d_up[block] = low_up
        back = product_right(low_gate, gate[...]) + product_right(low_up, up[...])

        @pl.when(block == tensor)
        def _():
            back_ref[...] = back

        @pl.when(block != tensor)
        def _():
            stage[block] = back.astype(stage.dtype)
            b_copy(block, tensor).start()

        return carry

    lax.fori_loop(0, tensor_size, chunk, 0)
    for slot in range(2):
        y_copy(0, slot).wait()

    all_rows = tensor_size * rows

    def weight_grad(left, right, out):
        extent = left.shape[2]
        tile = 256 if extent % 256 == 0 else 128 if extent % 128 == 0 else extent

        def body(step, carry):
            at = pl.ds(pl.multiple_of(step * tile, tile), tile)
            columns = left[:, :, at].reshape(all_rows, tile)
            out[at, :] = product_left(columns, right[...].reshape(all_rows, -1)).astype(out.dtype)
            return carry

        lax.fori_loop(0, extent // tile, body, 0)

    down_run.close()
    weight_grad(hidden, cot, down)
    run.begin_unit(0)
    weight_grad(normed, d_gate, gate)
    pltpu.make_async_copy(gate, d_gate_ref, out_sem.at[0]).start()
    run.step(0, 0)
    weight_grad(normed, d_up, up)
    pltpu.make_async_copy(up, d_up_ref, out_sem.at[1]).start()
    run.step(0, 1)

    for other in range(tensor_size):

        @pl.when(other != tensor)
        def _():
            b_copy(other, other).wait_recv()

    slab = 16

    def add_slab(step, carry):
        at = pl.ds(pl.multiple_of(step * slab, slab), slab)
        total = back_ref[at, :]
        for other in range(tensor_size):
            total = total + landing[other, at, :].astype(jnp.float32)
        back_ref[at, :] = total
        return carry

    lax.fori_loop(0, rows // slab, add_slab, 0)
    for later in range(2, run.dp_bits + 1):
        run.step(0, later)
    run.close()
    pltpu.make_async_copy(gate, d_gate_ref, out_sem.at[0]).wait()
    pltpu.make_async_copy(up, d_up_ref, out_sem.at[1]).wait()
    for other in range(tensor_size):

        @pl.when(other != tensor)
        def _():
            b_copy(other, tensor).wait_send()

        for way in (0, 1):
            sent = has[way] & ((other < tensor) if way == 0 else (other > tensor))
            pl.when(sent)(n_copy(other, way).wait_send)


def feed_forward(
    normed, cot_all, gate, up, down, gather_specs, specs, sizes, collective_id
):
    dp_size, tensor_size = sizes
    rows, width = normed.shape[0] // tensor_size, normed.shape[1]
    units = gate.shape[1]
    low = jnp.bfloat16
    tokens = (tensor_size, rows, width)
    inner = (tensor_size, rows, units)
    dma = pltpu.SemaphoreType.DMA
    return pl.pallas_call(
        functools.partial(mlp_kernel, gather_specs, specs, dp_size, tensor_size),
        out_shape=[
            jax.ShapeDtypeStruct((rows, width), jnp.float32),
            jax.ShapeDtypeStruct(tokens, low),
            jax.ShapeDtypeStruct(gate.shape, low),
            jax.ShapeDtypeStruct(up.shape, low),
        ]
        + scatter_shapes(specs),
        in_specs=[ANY] * 5,
        out_specs=[VMEM] + [ANY] * 3 + [VMEM],
        scratch_shapes=[
            pltpu.VMEM(tokens, low),
            pltpu.VMEM(tokens, low),
            pltpu.VMEM(gate.shape, low),
            pltpu.VMEM(up.shape, low),
            pltpu.VMEM(gather_specs[0].shape, low),
            pltpu.VMEM(inner, low),
            pltpu.VMEM(inner, low),
            pltpu.VMEM(inner, low),
            pltpu.VMEM((2, rows, width), low),
            pltpu.VMEM(tokens, low),
            pltpu.VMEM(tokens, low),
            dma((6,)),
            dma((2, tensor_size)),
            dma((tensor_size,)),
            dma((2,)),
            dma((tensor_size,)),
            dma((tensor_size,)),
            dma((2,)),
        ]
        + gather_scratch(gather_specs, [], dp_size, tensor_size)[1]
        + scatter_scratch(specs, [down], dp_size, tensor_size, in_place=True),
        compiler_params=pltpu.CompilerParams(
            collective_id=collective_id, has_side_effects=True, vmem_limit_bytes=63 * 2**20
        ),
        cost_estimate=pl.CostEstimate(
            flops=18 * tensor_size * rows * width * units,
            bytes_accessed=8 * width * units,
            transcendentals=0,
        ),
    )(
        normed.reshape(tokens),
        cot_all.reshape(tokens),
        gate,
        up,
        down,
    )


def tail_kernel(specs, dp_size, tensor_size, *refs):
    refs = list(refs)

    def take(count):
        return [refs.pop(0) for _ in range(count)]

    sources = take(7)
    k_blocks, v_blocks, wq_ref, cos_ref, sin_ref, gain_ref, second_ref = take(7)
    tokens_out, out_sum, query_sum, kv_sum, gain_sum = take(5)
    held = take(7)
    context, middle_low, normed, dq, wkv, tokens, middle = held
    o_grad, q_grad, kv_grad, gain_grad, wq_tile, k_landing, v_landing, kv_low, column_sum = take(9)
    load_sem, tile_sem = take(2)
    k_sems, v_sems = take(3), take(3)
    run = ScatterRun(
        specs,
        dp_size,
        tensor_size,
        [o_grad, q_grad, kv_grad, gain_grad],
        [out_sum, query_sum, kv_sum, gain_sum],
        refs,
        in_place=True,
    )
    rows, width = tokens.shape
    q_cols = q_grad.shape[2]
    o_rows = o_grad.shape[1]
    kv_width = kv_low.shape[1] // 2
    loads = [
        pltpu.make_async_copy(source, target, load_sem.at[i])
        for i, (source, target) in enumerate(zip(sources, held))
    ]
    for load in loads:
        load.start()

    def tile_copy(j):
        return pltpu.make_async_copy(
            wq_ref.at[:, pl.ds(j * q_cols, q_cols)], wq_tile.at[j % 2], tile_sem.at[j % 2]
        )

    tile_copy(0).start()
    exchanges = [
        ExchangeRun(tensor_size, k_blocks, k_landing, *k_sems),
        ExchangeRun(tensor_size, v_blocks, v_landing, *v_sems),
    ]
    greet((run.dp, run.tensor, tensor_size), False, True, run.dp_bits)
    for exchange in exchanges:
        exchange.begin()

    def out_piece(j):
        tile = min(256, o_rows)
        for row in range(0, o_rows, tile):
            o_grad[j, row : row + tile, :] = product_left(
                context[:, j * o_rows + row : j * o_rows + row + tile], middle_low[...]
            ).astype(o_grad.dtype)
        run.begin_unit(j)

    def query_piece(j):
        grads = dq[:, j * q_cols : (j + 1) * q_cols]
        tile = 512
        for row in range(0, width, tile):
            q_grad[j, row : row + tile, :] = product_left(
                normed[:, row : row + tile], grads
            ).astype(q_grad.dtype)
        run.begin_unit(tensor_size + j)

    def back_piece(j):
        if j + 1 < tensor_size:
            tile_copy(j + 1).start()
        tile_copy(j).wait()
        part = product_right(dq[:, j * q_cols : (j + 1) * q_cols], wq_tile[j % 2])
        if j == 0:
            tokens_out[...] = part
        else:
            tokens_out[...] += part

    def kv_piece():
        for exchange in exchanges:
            exchange.close()
        grad_keys = k_landing[0].astype(jnp.float32)
        grad_values = v_landing[0].astype(jnp.float32)
        for other in range(1, tensor_size):
            grad_keys = grad_keys + k_landing[other].astype(jnp.float32)
            grad_values = grad_values + v_landing[other].astype(jnp.float32)
        repeat = kv_width // cos_ref.shape[1]
        cosines = jnp.concatenate([cos_ref[...]] * repeat, axis=1)
        sines = jnp.concatenate([sin_ref[...]] * repeat, axis=1)
        kv_low[:, :kv_width] = (grad_keys * cosines - swap_halves(grad_keys) * sines).astype(
            kv_low.dtype
        )
        kv_low[:, kv_width:] = grad_values.astype(kv_low.dtype)
        for row in range(0, width, 512):
            kv_grad[row : row + 512, :] = product_left(
                normed[:, row : row + 512], kv_low[...]
            ).astype(kv_grad.dtype)
        run.begin_unit(2 * tensor_size)
        tokens_out[...] += product_right(kv_low[...], wkv[...])

    slab = 16

    def finish(step, carry):
        at = pl.ds(pl.multiple_of(step * slab, slab), slab)
        raw = tokens[at, :].astype(jnp.float32)
        scale = lax.rsqrt(jnp.mean(raw * raw, axis=-1, keepdims=True) + epsilon)
        unit = raw * scale
        grad = tokens_out[at, :]
        gained = grad * unit
        column_sum[...] += gained[:8] + gained[8:]
        scaled = grad * gain_ref[...]
        mean = jnp.mean(scaled * unit, axis=-1, keepdims=True)
        tokens_out[at, :] = middle[at, :] + scale * (scaled - unit * mean)
        return carry

    def last_piece():
        column_sum[...] = jnp.zeros_like(column_sum)
        lax.fori_loop(0, rows // slab, finish, 0)
        gain_grad[...] = jnp.zeros_like(gain_grad)
        gain_grad[0:1, :] = jnp.sum(column_sum[...], axis=0, keepdims=True)
        gain_grad[8:9, :] = second_ref[...]
        run.begin_unit(2 * tensor_size + 1)

    loads[0].wait()
    loads[1].wait()
    for j in range(tensor_size):
        out_piece(j)
        if 1 <= j <= 2:
            run.step(j - 1, 0)
    for load in loads[2:]:
        load.wait()
    count = len(run.units)
    work = {j: [functools.partial(query_piece, j)] for j in range(tensor_size)}
    room = max(1, tensor_size - 2)
    for j in range(tensor_size):
        work.setdefault(tensor_size + j * room // tensor_size, []).append(
            functools.partial(back_piece, j)
        )
    work.setdefault(2 * tensor_size - 2, []).append(kv_piece)
    work.setdefault(2 * tensor_size - 1, []).append(last_piece)
    for tick in range(count + 1):
        for piece in work.get(tick, []):
            piece()
        if tick < count:
            run.step(tick, 1)
        if tick + 2 < count:
            run.step(tick + 2, 0)
        if tick:
            for stage in range(2, run.dp_bits + 1):
                run.step(tick - 1, stage)
    run.close()


def tail(
    context,
    middle_low,
    normed,
    dq,
    key_value,
    tokens,
    middle,
    k_blocks,
    v_blocks,
    query,
    cosines,
    sines,
    gain,
    second,
    specs,
    sizes,
    collective_id,
):
    dp_size, tensor_size = sizes
    rows, width = tokens.shape
    low, full = jnp.bfloat16, jnp.float32
    o_spec, q_spec = specs[0], specs[1]
    kv_both = key_value.shape[1]
    dma = pltpu.SemaphoreType.DMA
    arrays = [
        jax.ShapeDtypeStruct((tensor_size, o_spec.shape[0], width), low),
        jax.ShapeDtypeStruct((tensor_size, width, q_spec.shape[1]), low),
        jax.ShapeDtypeStruct((width, kv_both), low),
        jax.ShapeDtypeStruct((16, width), full),
    ]
    loaded = [context, middle_low, normed, dq, key_value, tokens, middle]
    return pl.pallas_call(
        functools.partial(tail_kernel, specs, dp_size, tensor_size),
        out_shape=[jax.ShapeDtypeStruct((rows, width), full)] + scatter_shapes(specs),
        in_specs=[ANY] * 10 + [VMEM] * 4,
        out_specs=[VMEM] * (1 + len(specs)),
        scratch_shapes=[pltpu.VMEM(array.shape, array.dtype) for array in loaded]
        + [pltpu.VMEM(array.shape, array.dtype) for array in arrays]
        + [
            pltpu.VMEM((2, width, q_spec.shape[1]), low),
            pltpu.VMEM(k_blocks.shape, low),
            pltpu.VMEM(v_blocks.shape, low),
            pltpu.VMEM((rows, kv_both), low),
            pltpu.VMEM((8, width), full),
            dma((7,)),
            dma((2,)),
        ]
        + [dma, dma((tensor_size,)), dma((tensor_size,))] * 2
        + scatter_scratch(specs, arrays, dp_size, tensor_size, in_place=True),
        compiler_params=pltpu.CompilerParams(
            collective_id=collective_id, has_side_effects=True, vmem_limit_bytes=60 * 2**20
        ),
    )(*loaded, k_blocks, v_blocks, query, cosines, sines, gain, second)


def rope_tables(rows, tensor):
    halved = HEAD_DIM // 2
    freqs = theta_base ** (-2.0 * jnp.arange(halved, dtype=jnp.float32) / HEAD_DIM)
    places = (tensor * rows + jnp.arange(rows)).astype(jnp.float32)
    angles = places[:, None] * freqs[None, :]
    cosines, sines = jnp.cos(angles), jnp.sin(angles)
    return (
        jnp.concatenate([cosines, cosines] * 2, axis=1),
        jnp.concatenate([-sines, sines] * 2, axis=1),
    )


def start_row(dp, size):
    return pl.multiple_of(dp * size, size)


def on_device(
    dp_size,
    tensor_size,
    tokens,
    attn_gain,
    w_query,
    w_key,
    w_value,
    w_out,
    mlp_gain,
    w_gate,
    w_up,
    w_down,
    cotangent,
):
    tensor_index = lax.axis_index("tensor")
    rows, width = tokens.shape
    heads = w_query.shape[1] * tensor_size // HEAD_DIM
    kv_width = w_key.shape[1]
    kv_heads = kv_width // HEAD_DIM
    group_heads = heads // kv_heads
    q_rows, q_cols = w_query.shape
    kv_rows = w_key.shape[0]
    o_rows, o_cols = w_out.shape
    gain_part = attn_gain.shape[0]

    key_value = jnp.concatenate([w_key, w_value], axis=1)
    per = 128 // gain_part
    spot = lax.rem(lax.axis_index("dp") * tensor_size + tensor_index, per)
    rows_at = lax.broadcasted_iota(jnp.int32, (16, 128), 0)
    here = lax.div(lax.broadcasted_iota(jnp.int32, (16, 128), 1), gain_part) == spot
    gains = jnp.where(rows_at == 0, jnp.tile(attn_gain, per), jnp.tile(mlp_gain, per))
    gains = jnp.where(here & (rows_at < 2), gains, jnp.zeros_like(gains))
    query_spec = Gather(
        (width, heads * HEAD_DIM),
        lambda ref, dp, t: ref.at[
            pl.ds(start_row(dp, q_rows), q_rows), pl.ds(start_row(t, q_cols), q_cols)
        ],
        lambda ref, dp, half, j: ref.at[
            pl.ds(pl.multiple_of(dp * q_rows + half * (q_rows // 2), q_rows // 2), q_rows // 2),
            pl.ds(start_row(j, q_cols), q_cols),
        ],
        pieces=tensor_size,
    )
    kv_all_rows = kv_rows * tensor_size
    kv_spec = Gather(
        (width, 2 * kv_width),
        lambda ref, dp, t: ref.at[pl.ds(start_row(dp * tensor_size + t, kv_rows), kv_rows), :],
        lambda ref, dp, half, j: ref.at[
            pl.ds(
                pl.multiple_of(dp * kv_all_rows + half * (kv_all_rows // 2), kv_all_rows // 2),
                kv_all_rows // 2,
            ),
            :,
        ],
    )
    gain_spec = Gather(
        (dp_size * tensor_size * 16, 128),
        lambda ref, dp, t: ref.at[pl.ds(start_row(dp * tensor_size + t, 16), 16), :],
        lambda ref, dp, half, j: ref.at[
            pl.ds(
                pl.multiple_of((2 * dp + half) * tensor_size * 8, tensor_size * 8),
                tensor_size * 8,
            ),
            :,
        ],
    )
    out_spec = Gather(
        (heads * HEAD_DIM, width),
        lambda ref, dp, t: ref.at[
            pl.ds(start_row(t, o_rows), o_rows), pl.ds(start_row(dp, o_cols), o_cols)
        ],
        lambda ref, dp, half, j: ref.at[
            pl.ds(half * (heads * HEAD_DIM // 2), heads * HEAD_DIM // 2),
            pl.ds(start_row(dp, o_cols), o_cols),
        ],
    )
    row_spec = lambda shape: Gather(
        (tensor_size * shape[0], shape[1]),
        lambda ref, dp, t: ref.at[pl.ds(start_row(t, shape[0]), shape[0]), :],
    )
    up_rows, units = w_gate.shape
    column_spec = Gather(
        (width, units),
        lambda ref, dp, t: ref.at[pl.ds(start_row(dp, up_rows), up_rows), :],
        lambda ref, dp, half, j: ref.at[
            pl.ds(
                pl.multiple_of(dp * up_rows + half * (up_rows // 2), up_rows // 2), up_rows // 2
            ),
            :,
        ],
        False,
    )
    down_cols = w_down.shape[1]
    down_spec = Gather(
        (units, width),
        lambda ref, dp, t: ref.at[:, pl.ds(start_row(dp, down_cols), down_cols)],
        lambda ref, dp, half, j: ref.at[
            pl.ds(half * (units // 2), units // 2), pl.ds(start_row(dp, down_cols), down_cols)
        ],
        False,
    )
    sizes = (dp_size, tensor_size)
    cosines, sines = rope_tables(rows, tensor_index)
    (
        context,
        queries,
        log_sums,
        normed_first,
        middle,
        gain_rows,
        kv_all,
        normed_all,
        key_value_full,
        _,
        query_full,
        out_full,
        gate_full,
        up_full,
        cot_all,
    ) = front(
        tokens,
        cosines,
        sines,
        [key_value, gains, w_query, w_out, w_gate, w_up, cotangent],
        [
            kv_spec,
            gain_spec,
            query_spec,
            out_spec,
            column_spec,
            column_spec,
            row_spec(cotangent.shape),
        ],
        row_spec((rows, 2 * kv_width)),
        row_spec((rows, width)),
        heads,
        group_heads,
        sizes,
        1,
    )
    column_scatter = Scatter(
        "dp",
        (up_rows, units),
        column_spec.half,
        (up_rows // 2, units),
        lambda ref, half: ref.at[pl.ds(half * (up_rows // 2), up_rows // 2), :],
    )
    down_scatter = Scatter(
        "dp",
        (units, down_cols),
        down_spec.half,
        (units // 2, down_cols),
        lambda ref, half: ref.at[pl.ds(half * (units // 2), units // 2), :],
    )
    back_second, mlp_part, grad_gate_w, grad_up_w, sum_down = feed_forward(
        normed_all, cot_all, gate_full, up_full, w_down, [down_spec], [down_scatter], sizes, 3
    )
    mlp_rows = lax.psum_scatter(
        mlp_part.reshape(tensor_size * rows, width), "tensor", scatter_dimension=0, tiled=True
    )
    query_scatter = Scatter(
        "own",
        (q_rows, q_cols),
        lambda ref, dp, half, j: ref.at[
            j,
            pl.ds(pl.multiple_of(dp * q_rows + half * (q_rows // 2), q_rows // 2), q_rows // 2),
            :,
        ],
        (q_rows // 2, q_cols),
        lambda ref, half: ref.at[pl.ds(half * (q_rows // 2), q_rows // 2), :],
    )
    kv_scatter = Scatter(
        "cut",
        (kv_rows, 2 * kv_width),
        lambda ref, dp, half, j: ref.at[
            pl.ds(start_row(dp, kv_all_rows), kv_all_rows), pl.ds(half * kv_width, kv_width)
        ],
        (kv_all_rows, kv_width),
        lambda ref, half: ref.at[:, pl.ds(half * kv_width, kv_width)],
        lambda ref, j: ref.at[pl.ds(j * kv_rows, kv_rows), :],
        (kv_rows, kv_width),
    )
    out_scatter = Scatter(
        "own",
        (o_rows, o_cols),
        lambda ref, dp, half, j: ref.at[
            j,
            pl.ds(half * (o_rows // 2), o_rows // 2),
            pl.ds(start_row(dp, o_cols), o_cols),
        ],
        (o_rows // 2, o_cols),
        lambda ref, half: ref.at[pl.ds(half * (o_rows // 2), o_rows // 2), :],
    )
    gain_cols = tensor_size * gain_part
    gain_scatter = Scatter(
        "cut",
        (16, gain_cols),
        lambda ref, dp, half, j: ref.at[
            pl.ds(half * 8, 8), pl.ds(start_row(dp, gain_cols), gain_cols)
        ],
        (8, gain_cols),
        lambda ref, half: ref.at[pl.ds(half * 8, 8), :],
        lambda ref, j: ref,
        (8, gain_cols),
    )
    (
        grad_queries,
        grad_keys,
        grad_values,
        grad_middle,
        middle_low,
        grad_gain_second,
        sum_gate,
        sum_up,
    ) = attend_back(
        queries,
        out_full,
        log_sums,
        cosines,
        sines,
        kv_all,
        back_second,
        middle,
        cotangent,
        gain_rows[1:2],
        heads,
        group_heads,
        [column_scatter, column_scatter],
        [grad_gate_w, grad_up_w],
        sizes,
        7,
    )
    grad_tokens, sum_out, sum_query, sum_kv, sum_gains = tail(
        context,
        middle_low,
        normed_first,
        grad_queries,
        key_value_full,
        tokens,
        grad_middle,
        grad_keys.reshape(tensor_size, rows, kv_width),
        grad_values.reshape(tensor_size, rows, kv_width),
        query_full,
        cosines,
        sines,
        gain_rows[0:1],
        grad_gain_second,
        [out_scatter, query_scatter, kv_scatter, gain_scatter],
        sizes,
        5,
    )
    sum_gains = lax.dynamic_slice_in_dim(sum_gains, tensor_index * gain_part, gain_part, 1)
    middle, mlp_rows, sum_query = lax.optimization_barrier((middle, mlp_rows, sum_query))
    output = (middle + mlp_rows.astype(jnp.float32)).astype(jnp.bfloat16)
    return (
        output,
        grad_tokens,
        sum_gains[0],
        sum_query,
        sum_kv[:, :kv_width],
        sum_kv[:, kv_width:],
        sum_out,
        sum_gains[8],
        sum_gate,
        sum_up,
        sum_down,
    )


def solution(mesh):
    placed = (
        P(("dp", "tensor"), None),
        P(("dp", "tensor")),
        P("dp", "tensor"),
        P(("dp", "tensor"), None),
        P(("dp", "tensor"), None),
        P("tensor", "dp"),
        P(("dp", "tensor")),
        P("dp", "tensor"),
        P("dp", "tensor"),
        P("tensor", "dp"),
        P(("dp", "tensor"), None),
    )
    return jax.shard_map(
        functools.partial(on_device, mesh.shape["dp"], mesh.shape["tensor"]),
        mesh=mesh,
        in_specs=placed,
        out_specs=(
            P(("dp", "tensor"), None),
            P(("dp", "tensor"), None),
            P(("dp", "tensor")),
            P("dp", "tensor"),
            P(("dp", "tensor"), None),
            P(("dp", "tensor"), None),
            P("tensor", "dp"),
            P(("dp", "tensor")),
            P("dp", "tensor"),
            P("dp", "tensor"),
            P("tensor", "dp"),
        ),
        check_vma=False,
    )
```

```python
import functools

import jax
import jax.numpy as jnp
from jax import lax
from jax.experimental import pallas as pl
from jax.experimental.pallas import tpu as pltpu
from jax.sharding import PartitionSpec as P

HEAD_DIM = 64
SEQLEN = 1024
MESH = pl.DeviceIdType.MESH
ANY = pl.BlockSpec(memory_space=pl.ANY)
VMEM = pl.BlockSpec(memory_space=pltpu.VMEM)
VMEM_LIMIT = 56 * 2**20

epsilon = 1e-05
theta_base = 10000.0


def product(left, right):
    return jnp.dot(left, right, preferred_element_type=jnp.float32)


def product_left(left, right):
    return lax.dot_general(
        left, right, (((0,), (0,)), ((), ())), preferred_element_type=jnp.float32
    )


def product_right(left, right):
    return lax.dot_general(
        left, right, (((1,), (1,)), ((), ())), preferred_element_type=jnp.float32
    )


def flip(index, bit):
    size = 1 << bit
    return index + size * (1 - 2 * lax.rem(lax.div(index, size), 2))


def masked(index, bits, rank):
    for place, bit in enumerate(bits):
        if rank >> place & 1:
            index = flip(index, bit)
    return index


def orders(bit_count, core_last):
    up = list(range(1, bit_count))
    down = up[::-1]
    return [up + [0], down + [0]] if core_last else [[0] + up, [0] + down]


def greet(spots, near, all_tensor, dp_bits):
    dp, tensor, tensor_size = spots
    barrier = pltpu.get_barrier_semaphore()

    def signal(where):
        pl.semaphore_signal(barrier, inc=1, device_id=where, device_id_type=MESH)

    peers = dp_bits
    for bit in range(dp_bits):
        signal((flip(dp, bit), tensor))
    if all_tensor:
        peers += tensor_size - 1
        for other in range(tensor_size):
            pl.when(other != tensor)(functools.partial(signal, (dp, other)))
    elif near:
        below, above = tensor > 0, tensor + 1 < tensor_size
        pl.when(below)(functools.partial(signal, (dp, tensor - 1)))
        pl.when(above)(functools.partial(signal, (dp, tensor + 1)))
        peers = peers + below.astype(jnp.int32) + above.astype(jnp.int32)
    pl.semaphore_wait(barrier, peers)


class Gather:
    def __init__(self, shape, slot, half=None, line=True, pieces=1):
        self.shape, self.slot, self.half, self.line = shape, slot, half, line
        self.pieces = pieces


class GatherRun:
    def __init__(self, specs, dp_size, tensor_size, sources, outs, held, sems):
        self.specs, self.sources, self.outs, self.held = specs, sources, outs, held
        self.own_sem, self.z_send, self.z_recv, self.h_send, self.h_recv = sems
        self.dp, self.tensor = lax.axis_index("dp"), lax.axis_index("tensor")
        self.tensor_size, self.dp_bits = tensor_size, dp_size.bit_length() - 1
        self.order = orders(self.dp_bits, True)
        self.hyper = [i for i, spec in enumerate(specs) if spec.half is not None]
        self.lines = [i for i, spec in enumerate(specs) if spec.line]
        self.base, total = {}, 0
        for i in self.hyper:
            self.base[i] = total
            total += specs[i].pieces
        self.can = [self.tensor + 1 < tensor_size, self.tensor > 0]

    def greet(self):
        greet(
            (self.dp, self.tensor, self.tensor_size),
            bool(self.lines),
            False,
            self.dp_bits if self.hyper else 0,
        )

    def z_copy(self, i, block, way, source=None):
        slot = self.specs[i].slot(self.outs[i], self.dp, block)
        return pltpu.make_async_remote_copy(
            src_ref=slot if source is None else source,
            dst_ref=slot,
            send_sem=self.z_send.at[i, way, block],
            recv_sem=self.z_recv.at[i, block],
            device_id=(self.dp, self.tensor + 1 if way == 0 else self.tensor - 1),
            device_id_type=MESH,
        )

    def own(self, i):
        slot = self.specs[i].slot(self.outs[i], self.dp, self.tensor)
        return pltpu.make_async_copy(self.held[i], slot, self.own_sem.at[i])

    def begin_line(self, i):
        for way in (0, 1):
            pl.when(self.can[way])(self.z_copy(i, self.tensor, way, self.sources[i]).start)

    def line(self, i, step):
        for way, block in ((0, self.tensor - step), (1, self.tensor + step)):

            @pl.when((block >= 0) & (block < self.tensor_size))
            def _():
                self.z_copy(i, block, way).wait_recv()
                pl.when(self.can[way])(self.z_copy(i, block, way).start)

    def part(self, i, half, rank, piece):
        place = masked(self.dp, self.order[half], rank)
        return self.specs[i].half(self.outs[i], place, half, piece)

    def h_copy(self, i, half, rank, place, piece):
        n = self.base[i] + piece
        return pltpu.make_async_remote_copy(
            src_ref=self.part(i, half, rank, piece),
            dst_ref=self.part(i, half, rank, piece),
            send_sem=self.h_send.at[n, half, rank, place],
            recv_sem=self.h_recv.at[n, half, rank | 1 << place],
            device_id=(flip(self.dp, self.order[half][place]), self.tensor),
            device_id_type=MESH,
        )

    def hop(self, i, rank, piece=0):
        n = self.base[i] + piece
        for half in (0, 1):
            if rank:
                wait_part(
                    self.part(i, half, rank, piece),
                    self.h_recv.at[n, half, rank],
                    self.h_send.at[n, half, 0, 0],
                    (flip(self.dp, 0), self.tensor),
                )
            for place in range(rank.bit_length(), self.dp_bits):
                self.h_copy(i, half, rank, place, piece).start()

    def hop_from(self, i, rank, step):
        if step == 0:
            self.hop(i, rank, self.tensor)
            return
        for block in (self.tensor - step, self.tensor + step):

            @pl.when((block >= 0) & (block < self.tensor_size))
            def _():
                self.hop(i, rank, block)

    def end_line(self, i):
        self.own(i).wait()

    def close(self):
        for rank in range(1 << self.dp_bits):
            for i in self.hyper:
                for piece in range(self.specs[i].pieces):
                    for half in (0, 1):
                        for place in range(rank.bit_length(), self.dp_bits):
                            self.h_copy(i, half, rank, place, piece).wait_send()
        for i in self.lines:
            for block in range(self.tensor_size):
                for way in (0, 1):
                    sent = self.can[way] & (
                        (block <= self.tensor) if way == 0 else (block >= self.tensor)
                    )
                    pl.when(sent)(self.z_copy(i, block, way).wait_send)


def gather_scratch(specs, arrays, dp_size, tensor_size):
    count = len(specs)
    hyper = max(1, sum(spec.pieces for spec in specs if spec.half is not None))
    dp_bits = dp_size.bit_length() - 1
    return [pltpu.VMEM(array.shape, array.dtype) for array in arrays], [
        pltpu.SemaphoreType.DMA((count,)),
        pltpu.SemaphoreType.DMA((count, 2, tensor_size)),
        pltpu.SemaphoreType.DMA((count, tensor_size)),
        pltpu.SemaphoreType.DMA((hyper, 2, dp_size, max(dp_bits, 1))),
        pltpu.SemaphoreType.DMA((hyper, 2, dp_size)),
    ]


def wait_part(part, recv_sem, send_sem, device):
    pltpu.make_async_remote_copy(
        src_ref=part,
        dst_ref=part,
        send_sem=send_sem,
        recv_sem=recv_sem,
        device_id=device,
        device_id_type=MESH,
    ).wait_recv()


def gather_shapes(specs, arrays):
    return [jax.ShapeDtypeStruct(spec.shape, array.dtype) for spec, array in zip(specs, arrays)]


class Scatter:
    def __init__(self, kind, shape, part, part_shape, place, cut=None, cut_shape=None):
        self.kind, self.shape, self.part, self.part_shape = kind, shape, part, part_shape
        self.place, self.cut = place, cut
        self.cut_shape = part_shape if kind == "own" else cut_shape


def add_into(total, extra):
    shape = total.shape
    rows = shape[-2]
    slab = min(16, rows)
    if len(shape) == 2:

        def body(step, carry):
            at = pl.ds(pl.multiple_of(step * slab, slab), slab)
            total[at, :] = total[at, :] + extra[at, :]
            return carry

        lax.fori_loop(0, rows // slab, body, 0, unroll=4 if (rows // slab) % 4 == 0 else 1)
    else:
        for lead in range(shape[0]):
            add_into(total.at[lead], extra.at[lead])


class ScatterRun:
    def __init__(self, specs, dp_size, tensor_size, sources, outs, scratch, in_place=False):
        scratch = list(scratch)
        self.specs, self.sources, self.outs = specs, sources, outs
        self.tensor_size, self.dp_bits = tensor_size, dp_size.bit_length() - 1
        self.in_place = in_place
        self.total = None if in_place else [scratch.pop(0) for _ in specs]
        self.landing = [[scratch.pop(0) for _ in range(self.dp_bits)] for _ in specs]
        self.shares = [scratch.pop(0) if spec.kind != "dp" else None for spec in specs]
        self.own_sem, self.send, self.recv, self.z_send, self.z_recv = scratch
        self.dp, self.tensor = lax.axis_index("dp"), lax.axis_index("tensor")
        self.order = orders(self.dp_bits, False)
        self.units = scatter_units(specs, tensor_size)

    def greet(self):
        cuts = any(spec.kind != "dp" for spec in self.specs)
        greet((self.dp, self.tensor, self.tensor_size), False, cuts, self.dp_bits)

    def slots(self, stage):
        return range(1 << (self.dp_bits - 1 - stage))

    def part(self, unit, half, rank):
        i, owner = self.units[unit]
        place = masked(self.dp, self.order[half], rank)
        return self.specs[i].part(self.sources[i], place, half, owner or 0)

    def sum_at(self, unit, half, slot):
        i, owner = self.units[unit]
        if self.in_place:
            return self.part(unit, half, 2 * slot)
        return self.total[i].at[owner or 0, half, slot]

    def own_copy(self, unit, half, slot):
        return pltpu.make_async_copy(
            self.part(unit, half, 2 * slot),
            self.sum_at(unit, half, slot),
            self.own_sem.at[unit, half, slot],
        )

    def landed(self, unit, half, stage, slot):
        i, owner = self.units[unit]
        return self.landing[i][stage].at[owner or 0, half, slot]

    def copy(self, unit, half, stage, slot):
        if stage == 0:
            source = self.part(unit, half, 2 * slot + 1)
        else:
            source = self.sum_at(unit, half, (2 * slot + 1) << (stage - 1))
        return pltpu.make_async_remote_copy(
            src_ref=source,
            dst_ref=self.landed(unit, half, stage, slot),
            send_sem=self.send.at[unit, half, stage, slot],
            recv_sem=self.recv.at[unit, half, stage, slot],
            device_id=(flip(self.dp, self.order[half][stage]), self.tensor),
            device_id_type=MESH,
        )

    def begin_unit(self, unit):
        for slot in self.slots(0):
            for half in (0, 1):
                self.copy(unit, half, 0, slot).start()
                if not self.in_place:
                    self.own_copy(unit, half, slot).start()

    def begin(self):
        for unit in range(len(self.units)):
            self.begin_unit(unit)

    def z_copy(self, unit, half, other, slot):
        i, owner = self.units[unit]
        spec, total = self.specs[i], self.sum_at(unit, half, 0)
        return pltpu.make_async_remote_copy(
            src_ref=total if spec.kind == "own" else spec.cut(total, other),
            dst_ref=self.shares[i].at[slot, half],
            send_sem=self.z_send.at[i, half, other],
            recv_sem=self.z_recv.at[i, half, slot],
            device_id=(self.dp, other),
            device_id_type=MESH,
        )

    def others(self, unit):
        owner = self.units[unit][1]
        return range(self.tensor_size) if owner is None else [owner]

    def step(self, unit, stage):
        i, owner = self.units[unit]
        spec = self.specs[i]
        if stage < self.dp_bits:
            for slot in sorted(self.slots(stage), key=lambda s: -(s & 1)):
                for half in (0, 1):
                    if stage == 0 and not self.in_place:
                        self.own_copy(unit, half, slot).wait()
                    self.copy(unit, half, stage, slot).wait_recv()
                    add_into(
                        self.sum_at(unit, half, slot << stage),
                        self.landed(unit, half, stage, slot),
                    )
                    if slot & 1:
                        self.copy(unit, half, stage + 1, slot >> 1).start()
            return
        for half in (0, 1):
            total = self.sum_at(unit, half, 0)
            if spec.kind == "dp":
                spec.place(self.outs[i], half)[...] = total[...].astype(jnp.float32)
                continue
            for other in self.others(unit):

                @pl.when(other != self.tensor)
                def _():
                    self.z_copy(unit, half, other, self.tensor).start()

                @pl.when(other == self.tensor)
                def _():
                    mine = total if spec.kind == "own" else spec.cut(total, other)
                    self.shares[i][other, half] = mine[...]

    def steps(self):
        count = len(self.units)
        return [
            (unit, turn - unit)
            for turn in range(count + self.dp_bits)
            for unit in range(count)
            if 0 <= turn - unit <= self.dp_bits
        ]

    def close(self):
        for i, spec in enumerate(self.specs):
            if spec.kind == "dp":
                continue
            unit = [u for u, (at, owner) in enumerate(self.units) if at == i][0]
            for half in (0, 1):
                for other in range(self.tensor_size):

                    @pl.when(other != self.tensor)
                    def _():
                        self.z_copy(unit, half, other, other).wait_recv()

                summed = self.shares[i][0, half].astype(jnp.float32)
                for other in range(1, self.tensor_size):
                    summed = summed + self.shares[i][other, half].astype(jnp.float32)
                spec.place(self.outs[i], half)[...] = summed
        for unit, (i, owner) in enumerate(self.units):
            for half in (0, 1):
                for stage in range(self.dp_bits):
                    for slot in self.slots(stage):
                        self.copy(unit, half, stage, slot).wait_send()
                if self.specs[i].kind != "dp":
                    for other in self.others(unit):

                        @pl.when(other != self.tensor)
                        def _():
                            self.z_copy(unit, half, other, self.tensor).wait_send()


def scatter_units(specs, tensor_size):
    units = []
    for i, spec in enumerate(specs):
        units += [(i, j) for j in range(tensor_size)] if spec.kind == "own" else [(i, None)]
    return units


def scatter_scratch(specs, arrays, dp_size, tensor_size, in_place=False):
    dp_bits = dp_size.bit_length() - 1
    scratch = []
    units = len(scatter_units(specs, tensor_size))
    pieces = [tensor_size if spec.kind == "own" else 1 for spec in specs]
    for spec, array, count in zip(specs, arrays, pieces):
        if not in_place:
            scratch.append(pltpu.VMEM((count, 2, dp_size // 2) + spec.part_shape, array.dtype))
    for spec, array, count in zip(specs, arrays, pieces):
        for stage in range(dp_bits):
            scratch.append(
                pltpu.VMEM((count, 2, dp_size >> (stage + 1)) + spec.part_shape, array.dtype)
            )
    for spec, array in zip(specs, arrays):
        if spec.kind != "dp":
            scratch.append(pltpu.VMEM((tensor_size, 2) + spec.cut_shape, array.dtype))
    dma = pltpu.SemaphoreType.DMA
    return scratch + [
        dma((units, 2, dp_size // 2)),
        dma((units, 2, dp_bits, dp_size // 2)),
        dma((units, 2, dp_bits, dp_size // 2)),
        dma((len(specs), 2, tensor_size)),
        dma((len(specs), 2, tensor_size)),
    ]


def scatter_shapes(specs):
    return [jax.ShapeDtypeStruct(spec.shape, jnp.float32) for spec in specs]


class ExchangeRun:
    def __init__(self, tensor_size, source, out, own_sem, send, recv):
        self.tensor_size, self.source, self.out = tensor_size, source, out
        self.own_sem, self.send, self.recv = own_sem, send, recv
        self.dp, self.tensor = lax.axis_index("dp"), lax.axis_index("tensor")

    def copy(self, other, slot):
        return pltpu.make_async_remote_copy(
            src_ref=self.source.at[other],
            dst_ref=self.out.at[slot],
            send_sem=self.send.at[other],
            recv_sem=self.recv.at[slot],
            device_id=(self.dp, other),
            device_id_type=MESH,
        )

    def own(self):
        return pltpu.make_async_copy(
            self.source.at[self.tensor], self.out.at[self.tensor], self.own_sem
        )

    def begin(self):
        for other in range(self.tensor_size):
            pl.when(other != self.tensor)(self.copy(other, self.tensor).start)
        self.own().start()

    def close(self):
        self.own().wait()
        for other in range(self.tensor_size):

            @pl.when(other != self.tensor)
            def _():
                self.copy(other, self.tensor).wait_send()
                self.copy(other, other).wait_recv()


def lanes_of(shape):
    return lax.broadcasted_iota(jnp.int32, shape, len(shape) - 1)


def swap_halves(values):
    width = values.shape[-1]
    first = lanes_of(values.shape) % HEAD_DIM < HEAD_DIM // 2
    return jnp.where(
        first,
        pltpu.roll(values, width - HEAD_DIM // 2, 1),
        pltpu.roll(values, HEAD_DIM // 2, 1),
    )


def left_head(block, odd):
    moved = jnp.where(odd, pltpu.roll(block, HEAD_DIM, 1), block)
    return jnp.where(lanes_of(block.shape) < HEAD_DIM, moved, jnp.zeros_like(moved))


def allowed(keys, rows, start):
    key_at = lax.broadcasted_iota(jnp.int32, (keys, rows), 0)
    query_at = lax.broadcasted_iota(jnp.int32, (keys, rows), 1) + start
    return key_at <= query_at


def at_steps(actions, step, steps):
    places = [(min(steps - 1, int(time * steps)), action) for time, action in actions]
    for place in sorted({place for place, _ in places}):

        @pl.when(step == place)
        def _():
            for at, action in places:
                if at == place:
                    action()


def attend_pair(pair, group_pairs, q_pre, cos_ref, sin_ref, kv_all, k_left, v_turned, outs):
    context, queries_out, lse_ref = outs
    rows = q_pre.shape[0]
    kv_width = kv_all.shape[1] // 2
    group = lax.div(pair, group_pairs)
    start = lax.axis_index("tensor") * rows
    at = pl.ds(pl.multiple_of(pair * 128, 128), 128)

    @pl.when(lax.rem(pair, group_pairs) == 0)
    def _():
        odd = lax.rem(group, 2) == 1
        lane = pl.multiple_of(lax.div(group, 2) * 128, 128)
        keys = kv_all[:, pl.ds(lane, 128)].astype(jnp.float32)
        values = kv_all[:, pl.ds(kv_width + lane, 128)].astype(jnp.float32)
        k_left[...] = left_head(keys, odd).astype(jnp.bfloat16)
        v_turned[...] = left_head(values, odd).T[:HEAD_DIM].astype(jnp.bfloat16)

    raw = q_pre[:, at]
    turned = (raw * cos_ref[...] + swap_halves(raw) * sin_ref[...]).astype(jnp.bfloat16)
    turned = turned.astype(jnp.float32) * HEAD_DIM ** (-0.5)
    queries_out[:, at] = turned.astype(jnp.bfloat16)
    open_at = allowed(k_left.shape[0], rows, start)
    contexts = []
    for head in (0, 1):
        queries = (turned if head == 0 else pltpu.roll(turned, HEAD_DIM, 1)).astype(jnp.bfloat16)
        scores = product_right(k_left[...], queries)
        scores = jnp.where(open_at, scores, -1e30)
        top = jnp.max(scores, axis=0, keepdims=True)
        exponent = jnp.exp(scores - top)
        summed = jnp.sum(exponent, axis=0, keepdims=True)
        part = product(v_turned[...], exponent.astype(jnp.bfloat16))
        contexts.append(part * (1.0 / summed))
        lse_ref[pair, pl.ds(head, 1), :] = top + jnp.log(summed)
    context[:, at] = jnp.concatenate(contexts, axis=0).T.astype(jnp.bfloat16)


def front_kernel(specs, kv_spec, n_spec, group_pairs, dp_size, tensor_size, *refs):
    refs = list(refs)

    def take(count):
        return [refs.pop(0) for _ in range(count)]

    count = len(specs)
    tokens, cos_ref, sin_ref = take(3)
    sources = take(count)
    context, queries, lse_ref, normed, middle, gain_rows, kv_all, normed_all = take(8)
    outs = take(count)
    held = take(count)
    weights, kv_weights, gain_blocks, q_pre, k_left, v_turned, normed_two = take(7)
    sems = take(5)
    kv_sems = take(5)
    n_sems = take(5)
    (load_sem,) = take(1)
    key_value, gains, query, out, gate, up, cot = range(count)
    run = GatherRun(specs, dp_size, tensor_size, sources, outs, held, sems)
    rows, width = tokens.shape
    own_rows = pl.ds(pl.multiple_of(run.tensor * rows, rows), rows)
    kv_run = GatherRun(
        [kv_spec], dp_size, tensor_size, [kv_all.at[own_rows, :]], [kv_all], [None], kv_sems
    )
    kv_width = kv_all.shape[1] // 2
    near = [1 << bit for bit in range(run.dp_bits - 1)]
    far = [r for r in range(1, 1 << (run.dp_bits - 1)) if r not in near]
    far.sort(key=lambda rank: rank.bit_count())
    core = list(range(1 << (run.dp_bits - 1), 1 << run.dp_bits))

    n_run = GatherRun(
        [n_spec], dp_size, tensor_size, [normed_two], [normed_all], [normed_two], n_sems
    )

    def hops(ranks, *units):
        for unit in units:
            for rank in ranks:
                run.hop(unit, rank)

    def query_hops(ranks, *steps):
        for step in steps:
            for rank in ranks:
                run.hop_from(query, rank, step)

    run.greet()
    loads = [
        pltpu.make_async_copy(source, target, run.own_sem.at[i])
        for i, (source, target) in enumerate(zip(sources, held))
    ]
    for load in loads:
        load.start()
    small = (key_value, gains)
    for i in (*small, query):
        run.begin_line(i)
    for i in (query, key_value, gains, out, gate, up, cot):
        loads[i].wait()
        run.own(i).start()
        if i == query:
            run.end_line(query)
            query_hops([0], 0)
    for step in range(1, tensor_size):
        for i in small:
            run.line(i, step)
    for i in small:
        run.end_line(i)
    hops([0], *small)
    steps = range(1, tensor_size)
    for step in steps:
        run.line(query, step)
        query_hops([0], step)
        if step == max(1, tensor_size - 2):
            hops(near, *small)
    run.begin_line(out)
    run.begin_line(cot)
    hops(far, *small)
    hops(core, *small)
    run.line(out, 1)

    kv_load = pltpu.make_async_copy(outs[key_value], kv_weights, load_sem.at[0])
    kv_load.start()
    gain_load = pltpu.make_async_copy(outs[gains], gain_blocks, load_sem.at[1])
    gain_load.start()
    gain_load.wait()
    blocks = gain_blocks.shape[0] // 16
    lanes = width // 128
    per = blocks // lanes
    for lane in range(lanes):
        row = jnp.zeros((16, 128), jnp.float32)
        for other in range(per):
            at = (lane * per + other) * 16
            row = row + gain_blocks[at : at + 16, :].astype(jnp.float32)
        gain_rows[:, lane * 128 : (lane + 1) * 128] = row[:8]
    slab = 16

    def norm_first(step, carry):
        at = pl.ds(pl.multiple_of(step * slab, slab), slab)
        raw = tokens[at, :].astype(jnp.float32)
        scale = lax.rsqrt(jnp.mean(raw * raw, axis=-1, keepdims=True) + epsilon)
        normed[at, :] = (raw * scale * gain_rows[0:1, :]).astype(normed.dtype)
        return carry

    lax.fori_loop(0, rows // slab, norm_first, 0)
    kv_load.wait()
    own_kv = product(normed[...], kv_weights[...])
    repeat = kv_width // cos_ref.shape[1]
    own_keys = own_kv[:, :kv_width]
    own_keys = own_keys * jnp.concatenate([cos_ref[...]] * repeat, axis=1) + swap_halves(
        own_keys
    ) * jnp.concatenate([sin_ref[...]] * repeat, axis=1)
    kv_all[own_rows, :] = jnp.concatenate([own_keys, own_kv[:, kv_width:]], axis=1).astype(
        kv_all.dtype
    )
    kv_run.begin_line(0)
    query_hops(near, 0, *steps)
    kv_run.line(0, 1)
    query_hops(far, 0, *steps)
    for step in steps[1:-1]:
        run.line(out, step)
        kv_run.line(0, step)
    query_hops(core, 0, *steps)
    query_load = pltpu.make_async_copy(outs[query], weights, load_sem.at[0])
    query_load.start()
    for step in steps[-1:]:
        run.line(out, step)
    for i in (out, gate, up):
        run.end_line(i)
    hops([0], out)
    query_load.wait()
    tiles = 4
    tile = width // tiles
    for j in range(tiles):
        columns = slice(j * tile, (j + 1) * tile)
        q_pre[:, columns] = product(normed[...], weights[:, columns])
        if j == 1:
            for step in steps[-1:]:
                kv_run.line(0, step)
            run.line(cot, 1)
    pairs = lse_ref.shape[0]
    plan = [
        (0.3, lambda: hops(near, out)),
        (0.31, lambda: hops([0], gate)),
        (0.75, lambda: hops(far, out)),
        (0.89, lambda: hops([0], up)),
    ]
    early = max(1, tensor_size - 2)
    for step in steps[1:early]:
        time = 0.52 + 0.4 * (step - 2) / early
        plan.append((time, functools.partial(run.line, cot, step)))
    plan.sort(key=lambda entry: entry[0])

    def pair_step(pair, carry):
        at_steps(plan, pair, pairs)
        attend_pair(
            pair,
            group_pairs,
            q_pre,
            cos_ref,
            sin_ref,
            kv_all,
            k_left,
            v_turned,
            (context, queries, lse_ref),
        )
        return carry

    lax.fori_loop(0, pairs, pair_step, 0)
    hops(core, out)
    hops(near, gate)
    out_load = pltpu.make_async_copy(outs[out], weights, load_sem.at[0])
    out_load.start()
    out_load.wait()
    for j in range(4):
        columns = slice(j * (width // 4), (j + 1) * (width // 4))
        middle[:, columns] = tokens[:, columns].astype(jnp.float32) + product(
            context[...], weights[:, columns]
        )

    def norm_second(step, carry):
        at = pl.ds(pl.multiple_of(step * slab, slab), slab)
        raw = middle[at, :]
        scale = lax.rsqrt(jnp.mean(raw * raw, axis=-1, keepdims=True) + epsilon)
        normed_two[at, :] = (raw * scale * gain_rows[1:2, :]).astype(normed_two.dtype)
        return carry

    lax.fori_loop(0, rows // slab, norm_second, 0)
    n_run.begin_line(0)
    n_run.own(0).start()
    hops(far, gate)
    for step in steps[early:]:
        run.line(cot, step)
    hops(near, up)
    hops(core, gate)
    hops(far, up)
    hops(core, up)
    for way, block in ((0, run.tensor - 1), (1, run.tensor + 1)):
        arrives = (block >= 0) & (block < tensor_size)
        pl.when(arrives)(n_run.z_copy(0, block, way).wait_recv)
        pl.when(run.can[way])(n_run.z_copy(0, run.tensor, way, normed_two).wait_send)
    n_run.end_line(0)
    run.end_line(cot)
    run.close()
    kv_run.close()


def front(
    tokens, cosines, sines, arrays, specs, kv_spec, n_spec, heads, group_heads, sizes, collective_id
):
    dp_size, tensor_size = sizes
    rows, width = tokens.shape
    length = rows * tensor_size
    low, full = jnp.bfloat16, jnp.float32
    held, sems = gather_scratch(specs, arrays, *sizes)
    _, line_sems = gather_scratch([kv_spec], [], *sizes)
    kv_both = specs[0].shape[1]
    pairs = heads // 2
    tokens_low = jax.ShapeDtypeStruct((rows, width), low)
    return pl.pallas_call(
        functools.partial(front_kernel, specs, kv_spec, n_spec, group_heads // 2, *sizes),
        out_shape=[
            tokens_low,
            tokens_low,
            jax.ShapeDtypeStruct((pairs, 2, rows), full),
            tokens_low,
            jax.ShapeDtypeStruct((rows, width), full),
            jax.ShapeDtypeStruct((8, width), full),
            jax.ShapeDtypeStruct((length, kv_both), low),
            jax.ShapeDtypeStruct((length, width), low),
        ]
        + gather_shapes(specs, arrays),
        in_specs=[VMEM] * 3 + [ANY] * len(specs),
        out_specs=[VMEM] * 7 + [ANY] * (1 + len(specs)),
        scratch_shapes=held
        + [
            pltpu.VMEM((width, width), low),
            pltpu.VMEM((width, kv_both), low),
            pltpu.VMEM(specs[1].shape, low),
            pltpu.VMEM((rows, width), full),
            pltpu.VMEM((length, 128), low),
            pltpu.VMEM((HEAD_DIM, length), low),
            pltpu.VMEM((rows, width), low),
        ]
        + sems
        + line_sems
        + line_sems
        + [pltpu.SemaphoreType.DMA((2,))],
        compiler_params=pltpu.CompilerParams(
            collective_id=collective_id, has_side_effects=True, vmem_limit_bytes=VMEM_LIMIT
        ),
    )(tokens, cosines, sines, *arrays)


def scatter_plan(run):
    plan = [(0.0, run.greet), (0.0, run.begin)]
    times = [(0.12, 0.08), (0.55, 0.3), (0.88, 0.12), (0.95, 0.05)]
    for unit, stage in run.steps():
        first, behind = times[min(stage, len(times) - 1)]
        plan.append((min(first + behind * unit, 1.0), functools.partial(run.step, unit, stage)))
    plan.sort(key=lambda entry: entry[0])
    return plan + [(1.0, run.close)]


def attend_back_kernel(group_pairs, pairs, specs, dp_size, tensor_size, *refs):
    refs = list(refs)
    q_ref, context_ref, out_ref = (refs.pop(0) for _ in range(3))
    lse_ref, cos_ref, sin_ref, k_ref, v_ref = (refs.pop(0) for _ in range(5))
    back_ref, middle_ref, cot_ref, gain_ref = (refs.pop(0) for _ in range(4))
    sources = [refs.pop(0) for _ in specs]
    dq_ref, dk_ref, dv_ref, grad_middle, middle_low, gain_sum = (refs.pop(0) for _ in range(6))
    outs = [refs.pop(0) for _ in specs]
    k_left, v_left, k_turned, dk_sum, dv_sum, column_sum = (refs.pop(0) for _ in range(6))
    run = ScatterRun(specs, dp_size, tensor_size, sources, outs, refs)
    plan = scatter_plan(run)
    at_steps([entry for entry in plan if entry[0] < 1.0], pl.program_id(0), pairs)
    pair = pl.program_id(0)
    group = pair // group_pairs
    odd = group % 2 == 1
    rows = q_ref.shape[0]
    start = lax.axis_index("tensor") * rows

    @pl.when(pair == 0)
    def _():
        slab = 16
        column_sum[...] = jnp.zeros_like(column_sum)

        def norm_slab(step, carry):
            at = pl.ds(pl.multiple_of(step * slab, slab), slab)
            raw = middle_ref[at, :]
            scale = lax.rsqrt(jnp.mean(raw * raw, axis=-1, keepdims=True) + epsilon)
            unit = raw * scale
            grad = back_ref[at, :]
            gained = grad * unit
            column_sum[...] += gained[:8] + gained[8:]
            scaled = grad * gain_ref[...]
            mean = jnp.mean(scaled * unit, axis=-1, keepdims=True)
            total = cot_ref[at, :].astype(jnp.float32) + scale * (scaled - unit * mean)
            grad_middle[at, :] = total
            middle_low[at, :] = total.astype(middle_low.dtype)
            return carry

        lax.fori_loop(0, rows // slab, norm_slab, 0)
        gain_sum[...] = jnp.sum(column_sum[...], axis=0, keepdims=True)

    grad_context = product_right(middle_low[...], out_ref[...])
    grad_low = grad_context.astype(jnp.bfloat16)
    heads_at = lax.broadcasted_iota(jnp.int32, (8, 128), 0)
    own_lanes = lax.div(lanes_of((8, 128)), HEAD_DIM) == heads_at
    mixed_sums = lax.dot_general(
        jnp.where(own_lanes, 1.0, 0.0),
        grad_low.astype(jnp.float32) * context_ref[...].astype(jnp.float32),
        (((1,), (1,)), ((), ())),
        precision=lax.Precision.HIGHEST,
        preferred_element_type=jnp.float32,
    )

    @pl.when(pair % group_pairs == 0)
    def _():
        left = left_head(k_ref[...].astype(jnp.float32), odd)
        k_left[...] = left.astype(jnp.bfloat16)
        k_turned[...] = left.T[:HEAD_DIM].astype(jnp.bfloat16)
        v_left[...] = left_head(v_ref[...].astype(jnp.float32), odd).astype(jnp.bfloat16)
        dk_sum[...] = jnp.zeros_like(dk_sum)
        dv_sum[...] = jnp.zeros_like(dv_sum)

    open_at = allowed(k_left.shape[0], rows, start)
    grads = []
    for head in (0, 1):
        queries, grad_out = q_ref[...], grad_low
        if head == 1:
            queries = pltpu.roll(queries.astype(jnp.float32), HEAD_DIM, 1).astype(jnp.bfloat16)
            grad_out = pltpu.roll(grad_context, HEAD_DIM, 1).astype(jnp.bfloat16)
        scores = product_right(k_left[...], queries)
        scores = jnp.where(open_at, scores, -1e30)
        softmaxed = jnp.exp(scores - lse_ref[0, head, :][None, :])
        grad_soft = product_right(v_left[...], grad_out)
        mixed_sum = mixed_sums[head : head + 1, :]
        grad_scores = (softmaxed * (grad_soft - mixed_sum)).astype(jnp.bfloat16)
        dv_sum[...] += product(softmaxed.astype(jnp.bfloat16), grad_out)
        dk_sum[...] += product(grad_scores, queries)
        grads.append(product(k_turned[...], grad_scores))
    grad_q = jnp.concatenate(grads, axis=0).T * HEAD_DIM ** (-0.5)
    dq_ref[...] = (grad_q * cos_ref[...] - swap_halves(grad_q) * sin_ref[...]).astype(jnp.bfloat16)

    @pl.when(pair % group_pairs == group_pairs - 1)
    def _():
        for total, out in ((dk_sum, dk_ref), (dv_sum, dv_ref)):
            value = total[...]
            left = lanes_of(value.shape) < HEAD_DIM

            @pl.when(jnp.logical_not(odd))
            def _():
                out[...] = jnp.where(left, value, 0.0).astype(out.dtype)

            @pl.when(odd)
            def _():
                out[...] = jnp.where(
                    left, out[...].astype(jnp.float32), pltpu.roll(value, HEAD_DIM, 1)
                ).astype(out.dtype)
    at_steps([entry for entry in plan if entry[0] >= 1.0], pair, pairs)


def attend_back(
    queries,
    context,
    out_full,
    lse,
    cosines,
    sines,
    keys_values,
    back,
    middle,
    cotangent,
    gain,
    head_count,
    group_heads,
    specs,
    arrays,
    sizes,
    collective_id,
):
    rows, width = queries.shape
    length, both = keys_values.shape
    pairs, group_pairs = head_count // 2, group_heads // 2
    kv_blocks = both // 256
    low, full = jnp.bfloat16, jnp.float32
    wide = pl.BlockSpec((rows, 128), lambda p: (0, p))
    table = pl.BlockSpec((rows, 128), lambda p: (0, 0))
    kv_out = pl.BlockSpec((length, 128), lambda p: (0, p // group_pairs // 2))
    return pl.pallas_call(
        functools.partial(attend_back_kernel, group_pairs, pairs, specs, *sizes),
        grid=(pairs,),
        out_shape=[
            jax.ShapeDtypeStruct((rows, width), low),
            jax.ShapeDtypeStruct((length, both // 2), low),
            jax.ShapeDtypeStruct((length, both // 2), low),
            jax.ShapeDtypeStruct((rows, width), full),
            jax.ShapeDtypeStruct((rows, width), low),
            jax.ShapeDtypeStruct((1, width), full),
        ]
        + scatter_shapes(specs),
        in_specs=[
            wide,
            wide,
            pl.BlockSpec((128, width), lambda p: (p, 0)),
            pl.BlockSpec((1, 2, rows), lambda p: (p, 0, 0)),
            table,
            table,
            pl.BlockSpec((length, 128), lambda p: (0, p // group_pairs // 2)),
            pl.BlockSpec((length, 128), lambda p: (0, kv_blocks + p // group_pairs // 2)),
        ]
        + [VMEM] * 4
        + [ANY] * len(specs),
        out_specs=[wide, kv_out, kv_out] + [VMEM] * (3 + len(specs)),
        scratch_shapes=[
            pltpu.VMEM((length, 128), low),
            pltpu.VMEM((length, 128), low),
            pltpu.VMEM((HEAD_DIM, length), low),
            pltpu.VMEM((length, 128), full),
            pltpu.VMEM((length, 128), full),
            pltpu.VMEM((8, width), full),
        ]
        + scatter_scratch(specs, arrays, *sizes),
        compiler_params=pltpu.CompilerParams(
            collective_id=collective_id, has_side_effects=True, vmem_limit_bytes=VMEM_LIMIT
        ),
        cost_estimate=pl.CostEstimate(
            flops=10 * rows * length * width, bytes_accessed=8 * rows * width, transcendentals=0
        ),
    )(
        queries,
        context,
        out_full,
        lse,
        cosines,
        sines,
        keys_values,
        keys_values,
        back,
        middle,
        cotangent,
        gain,
        *arrays,
    )


def block_at(place, tensor, tensor_size):
    above = tensor_size - 1 - tensor
    up = jnp.where(place < above, tensor + 1 + place, tensor - 1 - (place - above))
    down = jnp.where(place < tensor, tensor - 1 - place, 1 + place)
    other = jnp.where(tensor <= above, up, down)
    return jnp.where(place == tensor_size - 1, tensor, other)


def mlp_kernel(
    gather_specs,
    specs,
    dp_size,
    tensor_size,
    normed_ref,
    cot_ref,
    gate_ref,
    up_ref,
    down_ref,
    back_ref,
    y_ref,
    d_gate_ref,
    d_up_ref,
    down_sum,
    normed,
    cot,
    gate,
    up,
    down,
    hidden,
    d_gate,
    d_up,
    y_stage,
    stage,
    landing,
    load_sem,
    n_send,
    n_recv,
    y_sem,
    b_send,
    b_recv,
    out_sem,
    *more_refs,
):
    run = ScatterRun(
        specs, dp_size, tensor_size, [down], [down_sum], more_refs[5:], in_place=True
    )
    down_run = GatherRun(
        gather_specs, dp_size, tensor_size, [down_ref], [down], [down_ref], more_refs[:5]
    )
    dp, tensor = lax.axis_index("dp"), lax.axis_index("tensor")
    _, rows, width = normed_ref.shape
    units = gate.shape[1]
    loads = [
        pltpu.make_async_copy(source, target, load_sem.at[i])
        for i, (source, target) in enumerate(((gate_ref, gate), (up_ref, up), (cot_ref, cot)))
    ]
    has = [tensor + 1 < tensor_size, tensor > 0]

    def near_load(step):
        block = tensor + step
        return pltpu.make_async_copy(
            normed_ref.at[block], normed.at[block], load_sem.at[4 + step]
        )

    def near_loads(act):
        act(near_load(0))
        for way, step in ((0, 1), (1, -1)):

            @pl.when(has[way])
            def _():
                act(near_load(step))

    near_loads(lambda load: load.start())
    down_run.own(0).start()
    for load in loads:
        load.start()
    greet((dp, tensor, tensor_size), False, True, run.dp_bits)

    def n_copy(block, way, source=None):
        return pltpu.make_async_remote_copy(
            src_ref=normed.at[block] if source is None else source,
            dst_ref=normed.at[block],
            send_sem=n_send.at[way, block],
            recv_sem=n_recv.at[block],
            device_id=(dp, tensor + 1 if way == 0 else tensor - 1),
            device_id_type=MESH,
        )

    for way, step in ((0, -1), (1, 1)):
        both = has[0] & has[1]
        pl.when(both)(n_copy(tensor + step, way, normed_ref.at[tensor + step]).start)
    down_run.end_line(0)
    down_run.hop(0, 0)
    landing[tensor] = jnp.zeros((rows, width), landing.dtype)

    def pump(distance):
        for way, block in ((0, tensor - distance), (1, tensor + distance)):

            @pl.when((block >= 0) & (block < tensor_size))
            def _():
                n_copy(block, way).wait_recv()
                pl.when(has[way])(n_copy(block, way).start)

    farthest = jnp.maximum(tensor, tensor_size - 1 - tensor)
    core_rank = 1 << (run.dp_bits - 1)
    down_ranks = [
        sorted(range(1, core_rank), key=lambda rank: rank.bit_count()),
        range(core_rank, 2 * core_rank),
    ]

    def b_copy(block, slot):
        return pltpu.make_async_remote_copy(
            src_ref=stage.at[block],
            dst_ref=landing.at[slot],
            send_sem=b_send.at[block],
            recv_sem=b_recv.at[slot],
            device_id=(dp, block),
            device_id_type=MESH,
        )

    def y_copy(block, slot):
        return pltpu.make_async_copy(y_stage.at[slot], y_ref.at[block], y_sem.at[slot])

    for load in loads:
        load.wait()
    near_loads(lambda load: load.wait())

    def chunk(place, carry):
        block = block_at(place, tensor, tensor_size)
        rows_in = normed[block]
        gate_pre = product(rows_in, gate[...])
        upward = product(rows_in, up[...])

        @pl.when(place == 0)
        def _():
            for rank in down_ranks[0]:
                down_run.hop(0, rank)

        @pl.when(place + 2 <= farthest)
        def _():
            pump(place + 2)

        @pl.when(place == 0)
        def _():
            for rank in down_ranks[1]:
                down_run.hop(0, rank)

        sigmoid = 1.0 / (1.0 + jnp.exp(-gate_pre))
        silu = gate_pre * sigmoid
        active = (silu * upward).astype(jnp.bfloat16)
        hidden[block] = active
        grad_hidden = product_right(cot[block], down[...])
        low_gate = (
            grad_hidden * upward * sigmoid * (1.0 + gate_pre * (1.0 - sigmoid))
        ).astype(jnp.bfloat16)
        low_up = (grad_hidden * silu).astype(jnp.bfloat16)
        d_gate[block] = low_gate
        d_up[block] = low_up
        back = product_right(low_gate, gate[...]) + product_right(low_up, up[...])

        @pl.when(block == tensor)
        def _():
            back_ref[...] = back

        @pl.when(block != tensor)
        def _():
            stage[block] = back.astype(stage.dtype)
            b_copy(block, tensor).start()

        slot = lax.rem(place, 2)

        @pl.when(place >= 2)
        def _():
            y_copy(block, slot).wait()

        y_stage[slot] = product(active, down[...]).astype(jnp.bfloat16)
        y_copy(block, slot).start()

        return carry

    lax.fori_loop(0, tensor_size, chunk, 0)
    for slot in range(2):
        y_copy(0, slot).wait()

    all_rows = tensor_size * rows

    def weight_grad(left, right, out):
        extent = left.shape[2]
        tile = 256 if extent % 256 == 0 else 128 if extent % 128 == 0 else extent

        def body(step, carry):
            at = pl.ds(pl.multiple_of(step * tile, tile), tile)
            columns = left[:, :, at].reshape(all_rows, tile)
            out[at, :] = product_left(columns, right[...].reshape(all_rows, -1)).astype(out.dtype)
            return carry

        lax.fori_loop(0, extent // tile, body, 0)

    down_run.close()
    weight_grad(hidden, cot, down)
    run.begin_unit(0)
    weight_grad(normed, d_gate, gate)
    pltpu.make_async_copy(gate, d_gate_ref, out_sem.at[0]).start()
    run.step(0, 0)
    weight_grad(normed, d_up, up)
    pltpu.make_async_copy(up, d_up_ref, out_sem.at[1]).start()
    run.step(0, 1)

    for other in range(tensor_size):

        @pl.when(other != tensor)
        def _():
            b_copy(other, other).wait_recv()

    slab = 16

    def add_slab(step, carry):
        at = pl.ds(pl.multiple_of(step * slab, slab), slab)
        total = back_ref[at, :]
        for other in range(tensor_size):
            total = total + landing[other, at, :].astype(jnp.float32)
        back_ref[at, :] = total
        return carry

    lax.fori_loop(0, rows // slab, add_slab, 0)
    for later in range(2, run.dp_bits + 1):
        run.step(0, later)
    run.close()
    pltpu.make_async_copy(gate, d_gate_ref, out_sem.at[0]).wait()
    pltpu.make_async_copy(up, d_up_ref, out_sem.at[1]).wait()
    for other in range(tensor_size):

        @pl.when(other != tensor)
        def _():
            b_copy(other, tensor).wait_send()

        for way in (0, 1):
            sent = has[way] & ((other < tensor) if way == 0 else (other > tensor))
            pl.when(sent)(n_copy(other, way).wait_send)


def feed_forward(
    normed, cot_all, gate, up, down, gather_specs, specs, sizes, collective_id
):
    dp_size, tensor_size = sizes
    rows, width = normed.shape[0] // tensor_size, normed.shape[1]
    units = gate.shape[1]
    low = jnp.bfloat16
    tokens = (tensor_size, rows, width)
    inner = (tensor_size, rows, units)
    dma = pltpu.SemaphoreType.DMA
    return pl.pallas_call(
        functools.partial(mlp_kernel, gather_specs, specs, dp_size, tensor_size),
        out_shape=[
            jax.ShapeDtypeStruct((rows, width), jnp.float32),
            jax.ShapeDtypeStruct(tokens, low),
            jax.ShapeDtypeStruct(gate.shape, low),
            jax.ShapeDtypeStruct(up.shape, low),
        ]
        + scatter_shapes(specs),
        in_specs=[ANY] * 5,
        out_specs=[VMEM] + [ANY] * 3 + [VMEM],
        scratch_shapes=[
            pltpu.VMEM(tokens, low),
            pltpu.VMEM(tokens, low),
            pltpu.VMEM(gate.shape, low),
            pltpu.VMEM(up.shape, low),
            pltpu.VMEM(gather_specs[0].shape, low),
            pltpu.VMEM(inner, low),
            pltpu.VMEM(inner, low),
            pltpu.VMEM(inner, low),
            pltpu.VMEM((2, rows, width), low),
            pltpu.VMEM(tokens, low),
            pltpu.VMEM(tokens, low),
            dma((6,)),
            dma((2, tensor_size)),
            dma((tensor_size,)),
            dma((2,)),
            dma((tensor_size,)),
            dma((tensor_size,)),
            dma((2,)),
        ]
        + gather_scratch(gather_specs, [], dp_size, tensor_size)[1]
        + scatter_scratch(specs, [down], dp_size, tensor_size, in_place=True),
        compiler_params=pltpu.CompilerParams(
            collective_id=collective_id, has_side_effects=True, vmem_limit_bytes=63 * 2**20
        ),
        cost_estimate=pl.CostEstimate(
            flops=18 * tensor_size * rows * width * units,
            bytes_accessed=8 * width * units,
            transcendentals=0,
        ),
    )(
        normed.reshape(tokens),
        cot_all.reshape(tokens),
        gate,
        up,
        down,
    )


def tail_kernel(specs, dp_size, tensor_size, *refs):
    refs = list(refs)

    def take(count):
        return [refs.pop(0) for _ in range(count)]

    sources = take(7)
    k_blocks, v_blocks, wq_ref, cos_ref, sin_ref, gain_ref, second_ref = take(7)
    tokens_out, out_sum, query_sum, kv_sum, gain_sum = take(5)
    held = take(7)
    context, middle_low, normed, dq, wkv, tokens, middle = held
    o_grad, q_grad, kv_grad, gain_grad, wq_tile, k_landing, v_landing, kv_low, column_sum = take(9)
    load_sem, tile_sem = take(2)
    k_sems, v_sems = take(3), take(3)
    run = ScatterRun(
        specs,
        dp_size,
        tensor_size,
        [o_grad, q_grad, kv_grad, gain_grad],
        [out_sum, query_sum, kv_sum, gain_sum],
        refs,
        in_place=True,
    )
    rows, width = tokens.shape
    q_cols = q_grad.shape[2]
    o_rows = o_grad.shape[1]
    kv_width = kv_low.shape[1] // 2
    loads = [
        pltpu.make_async_copy(source, target, load_sem.at[i])
        for i, (source, target) in enumerate(zip(sources, held))
    ]
    for load in loads:
        load.start()

    def tile_copy(j):
        return pltpu.make_async_copy(
            wq_ref.at[:, pl.ds(j * q_cols, q_cols)], wq_tile.at[j % 2], tile_sem.at[j % 2]
        )

    tile_copy(0).start()
    exchanges = [
        ExchangeRun(tensor_size, k_blocks, k_landing, *k_sems),
        ExchangeRun(tensor_size, v_blocks, v_landing, *v_sems),
    ]
    greet((run.dp, run.tensor, tensor_size), False, True, run.dp_bits)
    for exchange in exchanges:
        exchange.begin()

    def out_piece(j):
        tile = min(256, o_rows)
        for row in range(0, o_rows, tile):
            o_grad[j, row : row + tile, :] = product_left(
                context[:, j * o_rows + row : j * o_rows + row + tile], middle_low[...]
            ).astype(o_grad.dtype)
        run.begin_unit(j)

    def query_piece(j):
        grads = dq[:, j * q_cols : (j + 1) * q_cols]
        tile = 512
        for row in range(0, width, tile):
            q_grad[j, row : row + tile, :] = product_left(
                normed[:, row : row + tile], grads
            ).astype(q_grad.dtype)
        run.begin_unit(tensor_size + j)

    def back_piece(j):
        if j + 1 < tensor_size:
            tile_copy(j + 1).start()
        tile_copy(j).wait()
        part = product_right(dq[:, j * q_cols : (j + 1) * q_cols], wq_tile[j % 2])
        if j == 0:
            tokens_out[...] = part
        else:
            tokens_out[...] += part

    def kv_piece():
        for exchange in exchanges:
            exchange.close()
        grad_keys = k_landing[0].astype(jnp.float32)
        grad_values = v_landing[0].astype(jnp.float32)
        for other in range(1, tensor_size):
            grad_keys = grad_keys + k_landing[other].astype(jnp.float32)
            grad_values = grad_values + v_landing[other].astype(jnp.float32)
        repeat = kv_width // cos_ref.shape[1]
        cosines = jnp.concatenate([cos_ref[...]] * repeat, axis=1)
        sines = jnp.concatenate([sin_ref[...]] * repeat, axis=1)
        kv_low[:, :kv_width] = (grad_keys * cosines - swap_halves(grad_keys) * sines).astype(
            kv_low.dtype
        )
        kv_low[:, kv_width:] = grad_values.astype(kv_low.dtype)
        for row in range(0, width, 512):
            kv_grad[row : row + 512, :] = product_left(
                normed[:, row : row + 512], kv_low[...]
            ).astype(kv_grad.dtype)
        run.begin_unit(2 * tensor_size)
        tokens_out[...] += product_right(kv_low[...], wkv[...])

    slab = 16

    def finish(step, carry):
        at = pl.ds(pl.multiple_of(step * slab, slab), slab)
        raw = tokens[at, :].astype(jnp.float32)
        scale = lax.rsqrt(jnp.mean(raw * raw, axis=-1, keepdims=True) + epsilon)
        unit = raw * scale
        grad = tokens_out[at, :]
        gained = grad * unit
        column_sum[...] += gained[:8] + gained[8:]
        scaled = grad * gain_ref[...]
        mean = jnp.mean(scaled * unit, axis=-1, keepdims=True)
        tokens_out[at, :] = middle[at, :] + scale * (scaled - unit * mean)
        return carry

    def last_piece():
        column_sum[...] = jnp.zeros_like(column_sum)
        lax.fori_loop(0, rows // slab, finish, 0)
        gain_grad[...] = jnp.zeros_like(gain_grad)
        gain_grad[0:1, :] = jnp.sum(column_sum[...], axis=0, keepdims=True)
        gain_grad[8:9, :] = second_ref[...]
        run.begin_unit(2 * tensor_size + 1)

    loads[0].wait()
    loads[1].wait()
    for j in range(tensor_size):
        out_piece(j)
        if 1 <= j <= 2:
            run.step(j - 1, 0)
    for load in loads[2:]:
        load.wait()
    count = len(run.units)
    work = {j: [functools.partial(query_piece, j)] for j in range(tensor_size)}
    room = max(1, tensor_size - 2)
    for j in range(tensor_size):
        work.setdefault(tensor_size + j * room // tensor_size, []).append(
            functools.partial(back_piece, j)
        )
    work.setdefault(2 * tensor_size - 2, []).append(kv_piece)
    work.setdefault(2 * tensor_size - 1, []).append(last_piece)
    for tick in range(count + 1):
        for piece in work.get(tick, []):
            piece()
        if tick < count:
            run.step(tick, 1)
        if tick + 2 < count:
            run.step(tick + 2, 0)
        if tick:
            for stage in range(2, run.dp_bits + 1):
                run.step(tick - 1, stage)
    run.close()


def tail(
    context,
    middle_low,
    normed,
    dq,
    key_value,
    tokens,
    middle,
    k_blocks,
    v_blocks,
    query,
    cosines,
    sines,
    gain,
    second,
    specs,
    sizes,
    collective_id,
):
    dp_size, tensor_size = sizes
    rows, width = tokens.shape
    low, full = jnp.bfloat16, jnp.float32
    o_spec, q_spec = specs[0], specs[1]
    kv_both = key_value.shape[1]
    dma = pltpu.SemaphoreType.DMA
    arrays = [
        jax.ShapeDtypeStruct((tensor_size, o_spec.shape[0], width), low),
        jax.ShapeDtypeStruct((tensor_size, width, q_spec.shape[1]), low),
        jax.ShapeDtypeStruct((width, kv_both), low),
        jax.ShapeDtypeStruct((16, width), full),
    ]
    loaded = [context, middle_low, normed, dq, key_value, tokens, middle]
    return pl.pallas_call(
        functools.partial(tail_kernel, specs, dp_size, tensor_size),
        out_shape=[jax.ShapeDtypeStruct((rows, width), full)] + scatter_shapes(specs),
        in_specs=[ANY] * 10 + [VMEM] * 4,
        out_specs=[VMEM] * (1 + len(specs)),
        scratch_shapes=[pltpu.VMEM(array.shape, array.dtype) for array in loaded]
        + [pltpu.VMEM(array.shape, array.dtype) for array in arrays]
        + [
            pltpu.VMEM((2, width, q_spec.shape[1]), low),
            pltpu.VMEM(k_blocks.shape, low),
            pltpu.VMEM(v_blocks.shape, low),
            pltpu.VMEM((rows, kv_both), low),
            pltpu.VMEM((8, width), full),
            dma((7,)),
            dma((2,)),
        ]
        + [dma, dma((tensor_size,)), dma((tensor_size,))] * 2
        + scatter_scratch(specs, arrays, dp_size, tensor_size, in_place=True),
        compiler_params=pltpu.CompilerParams(
            collective_id=collective_id, has_side_effects=True, vmem_limit_bytes=60 * 2**20
        ),
    )(*loaded, k_blocks, v_blocks, query, cosines, sines, gain, second)


def rope_tables(rows, tensor):
    halved = HEAD_DIM // 2
    lane = lax.rem(jnp.arange(128), HEAD_DIM)
    turn = lax.rem(lane, halved).astype(jnp.float32)
    freqs = theta_base ** (-2.0 * turn / HEAD_DIM)
    places = (tensor * rows + jnp.arange(rows)).astype(jnp.float32)
    angles = places[:, None] * freqs[None, :]
    return jnp.cos(angles), jnp.where(lane < halved, -1.0, 1.0)[None, :] * jnp.sin(angles)


def start_row(dp, size):
    return pl.multiple_of(dp * size, size)


def on_device(
    dp_size,
    tensor_size,
    tokens,
    attn_gain,
    w_query,
    w_key,
    w_value,
    w_out,
    mlp_gain,
    w_gate,
    w_up,
    w_down,
    cotangent,
):
    tensor_index = lax.axis_index("tensor")
    rows, width = tokens.shape
    heads = w_query.shape[1] * tensor_size // HEAD_DIM
    kv_width = w_key.shape[1]
    kv_heads = kv_width // HEAD_DIM
    group_heads = heads // kv_heads
    q_rows, q_cols = w_query.shape
    kv_rows = w_key.shape[0]
    o_rows, o_cols = w_out.shape
    gain_part = attn_gain.shape[0]

    key_value = jnp.concatenate([w_key, w_value], axis=1)
    per = 128 // gain_part
    spot = lax.rem(lax.axis_index("dp") * tensor_size + tensor_index, per)
    rows_at = lax.broadcasted_iota(jnp.int32, (16, 128), 0)
    here = lax.div(lax.broadcasted_iota(jnp.int32, (16, 128), 1), gain_part) == spot
    gains = jnp.where(rows_at == 0, jnp.tile(attn_gain, per), jnp.tile(mlp_gain, per))
    gains = jnp.where(here & (rows_at < 2), gains, jnp.zeros_like(gains))
    query_spec = Gather(
        (width, heads * HEAD_DIM),
        lambda ref, dp, t: ref.at[
            pl.ds(start_row(dp, q_rows), q_rows), pl.ds(start_row(t, q_cols), q_cols)
        ],
        lambda ref, dp, half, j: ref.at[
            pl.ds(pl.multiple_of(dp * q_rows + half * (q_rows // 2), q_rows // 2), q_rows // 2),
            pl.ds(start_row(j, q_cols), q_cols),
        ],
        pieces=tensor_size,
    )
    kv_all_rows = kv_rows * tensor_size
    kv_spec = Gather(
        (width, 2 * kv_width),
        lambda ref, dp, t: ref.at[pl.ds(start_row(dp * tensor_size + t, kv_rows), kv_rows), :],
        lambda ref, dp, half, j: ref.at[
            pl.ds(
                pl.multiple_of(dp * kv_all_rows + half * (kv_all_rows // 2), kv_all_rows // 2),
                kv_all_rows // 2,
            ),
            :,
        ],
    )
    gain_spec = Gather(
        (dp_size * tensor_size * 16, 128),
        lambda ref, dp, t: ref.at[pl.ds(start_row(dp * tensor_size + t, 16), 16), :],
        lambda ref, dp, half, j: ref.at[
            pl.ds(
                pl.multiple_of((2 * dp + half) * tensor_size * 8, tensor_size * 8),
                tensor_size * 8,
            ),
            :,
        ],
    )
    out_spec = Gather(
        (heads * HEAD_DIM, width),
        lambda ref, dp, t: ref.at[
            pl.ds(start_row(t, o_rows), o_rows), pl.ds(start_row(dp, o_cols), o_cols)
        ],
        lambda ref, dp, half, j: ref.at[
            pl.ds(half * (heads * HEAD_DIM // 2), heads * HEAD_DIM // 2),
            pl.ds(start_row(dp, o_cols), o_cols),
        ],
    )
    row_spec = lambda shape: Gather(
        (tensor_size * shape[0], shape[1]),
        lambda ref, dp, t: ref.at[pl.ds(start_row(t, shape[0]), shape[0]), :],
    )
    up_rows, units = w_gate.shape
    column_spec = Gather(
        (width, units),
        lambda ref, dp, t: ref.at[pl.ds(start_row(dp, up_rows), up_rows), :],
        lambda ref, dp, half, j: ref.at[
            pl.ds(
                pl.multiple_of(dp * up_rows + half * (up_rows // 2), up_rows // 2), up_rows // 2
            ),
            :,
        ],
        False,
    )
    down_cols = w_down.shape[1]
    down_spec = Gather(
        (units, width),
        lambda ref, dp, t: ref.at[:, pl.ds(start_row(dp, down_cols), down_cols)],
        lambda ref, dp, half, j: ref.at[
            pl.ds(half * (units // 2), units // 2), pl.ds(start_row(dp, down_cols), down_cols)
        ],
        False,
    )
    sizes = (dp_size, tensor_size)
    cosines, sines = rope_tables(rows, tensor_index)
    (
        context,
        queries,
        log_sums,
        normed_first,
        middle,
        gain_rows,
        kv_all,
        normed_all,
        key_value_full,
        _,
        query_full,
        out_full,
        gate_full,
        up_full,
        cot_all,
    ) = front(
        tokens,
        cosines,
        sines,
        [key_value, gains, w_query, w_out, w_gate, w_up, cotangent],
        [
            kv_spec,
            gain_spec,
            query_spec,
            out_spec,
            column_spec,
            column_spec,
            row_spec(cotangent.shape),
        ],
        row_spec((rows, 2 * kv_width)),
        row_spec((rows, width)),
        heads,
        group_heads,
        sizes,
        1,
    )
    column_scatter = Scatter(
        "dp",
        (up_rows, units),
        column_spec.half,
        (up_rows // 2, units),
        lambda ref, half: ref.at[pl.ds(half * (up_rows // 2), up_rows // 2), :],
    )
    down_scatter = Scatter(
        "dp",
        (units, down_cols),
        down_spec.half,
        (units // 2, down_cols),
        lambda ref, half: ref.at[pl.ds(half * (units // 2), units // 2), :],
    )
    back_second, mlp_part, grad_gate_w, grad_up_w, sum_down = feed_forward(
        normed_all, cot_all, gate_full, up_full, w_down, [down_spec], [down_scatter], sizes, 3
    )
    mlp_rows = lax.psum_scatter(
        mlp_part.reshape(tensor_size * rows, width), "tensor", scatter_dimension=0, tiled=True
    )
    query_scatter = Scatter(
        "own",
        (q_rows, q_cols),
        lambda ref, dp, half, j: ref.at[
            j,
            pl.ds(pl.multiple_of(dp * q_rows + half * (q_rows // 2), q_rows // 2), q_rows // 2),
            :,
        ],
        (q_rows // 2, q_cols),
        lambda ref, half: ref.at[pl.ds(half * (q_rows // 2), q_rows // 2), :],
    )
    kv_scatter = Scatter(
        "cut",
        (kv_rows, 2 * kv_width),
        lambda ref, dp, half, j: ref.at[
            pl.ds(start_row(dp, kv_all_rows), kv_all_rows), pl.ds(half * kv_width, kv_width)
        ],
        (kv_all_rows, kv_width),
        lambda ref, half: ref.at[:, pl.ds(half * kv_width, kv_width)],
        lambda ref, j: ref.at[pl.ds(j * kv_rows, kv_rows), :],
        (kv_rows, kv_width),
    )
    out_scatter = Scatter(
        "own",
        (o_rows, o_cols),
        lambda ref, dp, half, j: ref.at[
            j,
            pl.ds(half * (o_rows // 2), o_rows // 2),
            pl.ds(start_row(dp, o_cols), o_cols),
        ],
        (o_rows // 2, o_cols),
        lambda ref, half: ref.at[pl.ds(half * (o_rows // 2), o_rows // 2), :],
    )
    gain_cols = tensor_size * gain_part
    gain_scatter = Scatter(
        "cut",
        (16, gain_cols),
        lambda ref, dp, half, j: ref.at[
            pl.ds(half * 8, 8), pl.ds(start_row(dp, gain_cols), gain_cols)
        ],
        (8, gain_cols),
        lambda ref, half: ref.at[pl.ds(half * 8, 8), :],
        lambda ref, j: ref,
        (8, gain_cols),
    )
    (
        grad_queries,
        grad_keys,
        grad_values,
        grad_middle,
        middle_low,
        grad_gain_second,
        sum_gate,
        sum_up,
    ) = attend_back(
        queries,
        context,
        out_full,
        log_sums,
        cosines,
        sines,
        kv_all,
        back_second,
        middle,
        cotangent,
        gain_rows[1:2],
        heads,
        group_heads,
        [column_scatter, column_scatter],
        [grad_gate_w, grad_up_w],
        sizes,
        7,
    )
    grad_tokens, sum_out, sum_query, sum_kv, sum_gains = tail(
        context,
        middle_low,
        normed_first,
        grad_queries,
        key_value_full,
        tokens,
        grad_middle,
        grad_keys.reshape(tensor_size, rows, kv_width),
        grad_values.reshape(tensor_size, rows, kv_width),
        query_full,
        cosines,
        sines,
        gain_rows[0:1],
        grad_gain_second,
        [out_scatter, query_scatter, kv_scatter, gain_scatter],
        sizes,
        5,
    )
    sum_gains = lax.dynamic_slice_in_dim(sum_gains, tensor_index * gain_part, gain_part, 1)
    middle, mlp_rows, sum_query = lax.optimization_barrier((middle, mlp_rows, sum_query))
    output = (middle + mlp_rows.astype(jnp.float32)).astype(jnp.bfloat16)
    return (
        output,
        grad_tokens,
        sum_gains[0],
        sum_query,
        sum_kv[:, :kv_width],
        sum_kv[:, kv_width:],
        sum_out,
        sum_gains[8],
        sum_gate,
        sum_up,
        sum_down,
    )


def solution(mesh):
    placed = (
        P(("dp", "tensor"), None),
        P(("dp", "tensor")),
        P("dp", "tensor"),
        P(("dp", "tensor"), None),
        P(("dp", "tensor"), None),
        P("tensor", "dp"),
        P(("dp", "tensor")),
        P("dp", "tensor"),
        P("dp", "tensor"),
        P("tensor", "dp"),
        P(("dp", "tensor"), None),
    )
    return jax.shard_map(
        functools.partial(on_device, mesh.shape["dp"], mesh.shape["tensor"]),
        mesh=mesh,
        in_specs=placed,
        out_specs=(
            P(("dp", "tensor"), None),
            P(("dp", "tensor"), None),
            P(("dp", "tensor")),
            P("dp", "tensor"),
            P(("dp", "tensor"), None),
            P(("dp", "tensor"), None),
            P("tensor", "dp"),
            P(("dp", "tensor")),
            P("dp", "tensor"),
            P("dp", "tensor"),
            P("tensor", "dp"),
        ),
        check_vma=False,
    )
```

```python
import functools

import jax
import jax.numpy as jnp
from jax import lax
from jax.experimental import pallas as pl
from jax.experimental.pallas import tpu as pltpu
from jax.sharding import PartitionSpec as P

HEAD_DIM = 64
SEQLEN = 1024
MESH = pl.DeviceIdType.MESH
ANY = pl.BlockSpec(memory_space=pl.ANY)
VMEM = pl.BlockSpec(memory_space=pltpu.VMEM)
VMEM_LIMIT = 56 * 2**20

epsilon = 1e-05
theta_base = 10000.0


def product(left, right):
    return jnp.dot(left, right, preferred_element_type=jnp.float32)


def product_left(left, right):
    return lax.dot_general(
        left, right, (((0,), (0,)), ((), ())), preferred_element_type=jnp.float32
    )


def product_right(left, right):
    return lax.dot_general(
        left, right, (((1,), (1,)), ((), ())), preferred_element_type=jnp.float32
    )


def flip(index, bit):
    size = 1 << bit
    return index + size * (1 - 2 * lax.rem(lax.div(index, size), 2))


def masked(index, bits, rank):
    for place, bit in enumerate(bits):
        if rank >> place & 1:
            index = flip(index, bit)
    return index


def orders(bit_count, core_last):
    up = list(range(1, bit_count))
    down = up[::-1]
    return [up + [0], down + [0]] if core_last else [[0] + up, [0] + down]


def greet(spots, near, all_tensor, dp_bits):
    dp, tensor, tensor_size = spots
    barrier = pltpu.get_barrier_semaphore()

    def signal(where):
        pl.semaphore_signal(barrier, inc=1, device_id=where, device_id_type=MESH)

    peers = dp_bits
    for bit in range(dp_bits):
        signal((flip(dp, bit), tensor))
    if all_tensor:
        peers += tensor_size - 1
        for other in range(tensor_size):
            pl.when(other != tensor)(functools.partial(signal, (dp, other)))
    elif near:
        below, above = tensor > 0, tensor + 1 < tensor_size
        pl.when(below)(functools.partial(signal, (dp, tensor - 1)))
        pl.when(above)(functools.partial(signal, (dp, tensor + 1)))
        peers = peers + below.astype(jnp.int32) + above.astype(jnp.int32)
    pl.semaphore_wait(barrier, peers)


class Gather:
    def __init__(self, shape, slot, half=None, line=True, pieces=1):
        self.shape, self.slot, self.half, self.line = shape, slot, half, line
        self.pieces = pieces


class GatherRun:
    def __init__(self, specs, dp_size, tensor_size, sources, outs, held, sems):
        self.specs, self.sources, self.outs, self.held = specs, sources, outs, held
        self.own_sem, self.z_send, self.z_recv, self.h_send, self.h_recv = sems
        self.dp, self.tensor = lax.axis_index("dp"), lax.axis_index("tensor")
        self.tensor_size, self.dp_bits = tensor_size, dp_size.bit_length() - 1
        self.order = orders(self.dp_bits, True)
        self.hyper = [i for i, spec in enumerate(specs) if spec.half is not None]
        self.lines = [i for i, spec in enumerate(specs) if spec.line]
        self.base, total = {}, 0
        for i in self.hyper:
            self.base[i] = total
            total += specs[i].pieces
        self.can = [self.tensor + 1 < tensor_size, self.tensor > 0]

    def greet(self):
        greet(
            (self.dp, self.tensor, self.tensor_size),
            bool(self.lines),
            False,
            self.dp_bits if self.hyper else 0,
        )

    def z_copy(self, i, block, way, source=None):
        slot = self.specs[i].slot(self.outs[i], self.dp, block)
        return pltpu.make_async_remote_copy(
            src_ref=slot if source is None else source,
            dst_ref=slot,
            send_sem=self.z_send.at[i, way, block],
            recv_sem=self.z_recv.at[i, block],
            device_id=(self.dp, self.tensor + 1 if way == 0 else self.tensor - 1),
            device_id_type=MESH,
        )

    def own(self, i):
        slot = self.specs[i].slot(self.outs[i], self.dp, self.tensor)
        return pltpu.make_async_copy(self.held[i], slot, self.own_sem.at[i])

    def begin_line(self, i):
        for way in (0, 1):
            pl.when(self.can[way])(self.z_copy(i, self.tensor, way, self.sources[i]).start)

    def line(self, i, step):
        for way, block in ((0, self.tensor - step), (1, self.tensor + step)):

            @pl.when((block >= 0) & (block < self.tensor_size))
            def _():
                self.z_copy(i, block, way).wait_recv()
                pl.when(self.can[way])(self.z_copy(i, block, way).start)

    def part(self, i, half, rank, piece):
        place = masked(self.dp, self.order[half], rank)
        return self.specs[i].half(self.outs[i], place, half, piece)

    def h_copy(self, i, half, rank, place, piece):
        n = self.base[i] + piece
        return pltpu.make_async_remote_copy(
            src_ref=self.part(i, half, rank, piece),
            dst_ref=self.part(i, half, rank, piece),
            send_sem=self.h_send.at[n, half, rank, place],
            recv_sem=self.h_recv.at[n, half, rank | 1 << place],
            device_id=(flip(self.dp, self.order[half][place]), self.tensor),
            device_id_type=MESH,
        )

    def hop(self, i, rank, piece=0):
        n = self.base[i] + piece
        for half in (0, 1):
            if rank:
                wait_part(
                    self.part(i, half, rank, piece),
                    self.h_recv.at[n, half, rank],
                    self.h_send.at[n, half, 0, 0],
                    (flip(self.dp, 0), self.tensor),
                )
            for place in range(rank.bit_length(), self.dp_bits):
                self.h_copy(i, half, rank, place, piece).start()

    def hop_from(self, i, rank, step):
        if step == 0:
            self.hop(i, rank, self.tensor)
            return
        for block in (self.tensor - step, self.tensor + step):

            @pl.when((block >= 0) & (block < self.tensor_size))
            def _():
                self.hop(i, rank, block)

    def end_line(self, i):
        self.own(i).wait()

    def close(self):
        for rank in range(1 << self.dp_bits):
            for i in self.hyper:
                for piece in range(self.specs[i].pieces):
                    for half in (0, 1):
                        for place in range(rank.bit_length(), self.dp_bits):
                            self.h_copy(i, half, rank, place, piece).wait_send()
        for i in self.lines:
            for block in range(self.tensor_size):
                for way in (0, 1):
                    sent = self.can[way] & (
                        (block <= self.tensor) if way == 0 else (block >= self.tensor)
                    )
                    pl.when(sent)(self.z_copy(i, block, way).wait_send)


def gather_scratch(specs, arrays, dp_size, tensor_size):
    count = len(specs)
    hyper = max(1, sum(spec.pieces for spec in specs if spec.half is not None))
    dp_bits = dp_size.bit_length() - 1
    return [pltpu.VMEM(array.shape, array.dtype) for array in arrays], [
        pltpu.SemaphoreType.DMA((count,)),
        pltpu.SemaphoreType.DMA((count, 2, tensor_size)),
        pltpu.SemaphoreType.DMA((count, tensor_size)),
        pltpu.SemaphoreType.DMA((hyper, 2, dp_size, max(dp_bits, 1))),
        pltpu.SemaphoreType.DMA((hyper, 2, dp_size)),
    ]


def wait_part(part, recv_sem, send_sem, device):
    pltpu.make_async_remote_copy(
        src_ref=part,
        dst_ref=part,
        send_sem=send_sem,
        recv_sem=recv_sem,
        device_id=device,
        device_id_type=MESH,
    ).wait_recv()


def gather_shapes(specs, arrays):
    return [jax.ShapeDtypeStruct(spec.shape, array.dtype) for spec, array in zip(specs, arrays)]


class Scatter:
    def __init__(self, kind, shape, part, part_shape, place, cut=None, cut_shape=None):
        self.kind, self.shape, self.part, self.part_shape = kind, shape, part, part_shape
        self.place, self.cut = place, cut
        self.cut_shape = part_shape if kind == "own" else cut_shape


def add_into(total, extra):
    shape = total.shape
    rows = shape[-2]
    slab = min(16, rows)
    if len(shape) == 2:

        def body(step, carry):
            at = pl.ds(pl.multiple_of(step * slab, slab), slab)
            total[at, :] = total[at, :] + extra[at, :]
            return carry

        lax.fori_loop(0, rows // slab, body, 0, unroll=4 if (rows // slab) % 4 == 0 else 1)
    else:
        for lead in range(shape[0]):
            add_into(total.at[lead], extra.at[lead])


class ScatterRun:
    def __init__(self, specs, dp_size, tensor_size, sources, outs, scratch, in_place=False):
        scratch = list(scratch)
        self.specs, self.sources, self.outs = specs, sources, outs
        self.tensor_size, self.dp_bits = tensor_size, dp_size.bit_length() - 1
        self.in_place = in_place
        self.total = None if in_place else [scratch.pop(0) for _ in specs]
        self.landing = [[scratch.pop(0) for _ in range(self.dp_bits)] for _ in specs]
        self.shares = [scratch.pop(0) if spec.kind != "dp" else None for spec in specs]
        self.own_sem, self.send, self.recv, self.z_send, self.z_recv = scratch
        self.dp, self.tensor = lax.axis_index("dp"), lax.axis_index("tensor")
        self.order = orders(self.dp_bits, False)
        self.units = scatter_units(specs, tensor_size)

    def greet(self):
        cuts = any(spec.kind != "dp" for spec in self.specs)
        greet((self.dp, self.tensor, self.tensor_size), False, cuts, self.dp_bits)

    def slots(self, stage):
        return range(1 << (self.dp_bits - 1 - stage))

    def part(self, unit, half, rank):
        i, owner = self.units[unit]
        place = masked(self.dp, self.order[half], rank)
        return self.specs[i].part(self.sources[i], place, half, owner or 0)

    def sum_at(self, unit, half, slot):
        i, owner = self.units[unit]
        if self.in_place:
            return self.part(unit, half, 2 * slot)
        return self.total[i].at[owner or 0, half, slot]

    def own_copy(self, unit, half, slot):
        return pltpu.make_async_copy(
            self.part(unit, half, 2 * slot),
            self.sum_at(unit, half, slot),
            self.own_sem.at[unit, half, slot],
        )

    def landed(self, unit, half, stage, slot):
        i, owner = self.units[unit]
        return self.landing[i][stage].at[owner or 0, half, slot]

    def copy(self, unit, half, stage, slot):
        if stage == 0:
            source = self.part(unit, half, 2 * slot + 1)
        else:
            source = self.sum_at(unit, half, (2 * slot + 1) << (stage - 1))
        return pltpu.make_async_remote_copy(
            src_ref=source,
            dst_ref=self.landed(unit, half, stage, slot),
            send_sem=self.send.at[unit, half, stage, slot],
            recv_sem=self.recv.at[unit, half, stage, slot],
            device_id=(flip(self.dp, self.order[half][stage]), self.tensor),
            device_id_type=MESH,
        )

    def begin_unit(self, unit):
        for slot in self.slots(0):
            for half in (0, 1):
                self.copy(unit, half, 0, slot).start()
                if not self.in_place:
                    self.own_copy(unit, half, slot).start()

    def begin(self):
        for unit in range(len(self.units)):
            self.begin_unit(unit)

    def z_copy(self, unit, half, other, slot):
        i, owner = self.units[unit]
        spec, total = self.specs[i], self.sum_at(unit, half, 0)
        return pltpu.make_async_remote_copy(
            src_ref=total if spec.kind == "own" else spec.cut(total, other),
            dst_ref=self.shares[i].at[slot, half],
            send_sem=self.z_send.at[i, half, other],
            recv_sem=self.z_recv.at[i, half, slot],
            device_id=(self.dp, other),
            device_id_type=MESH,
        )

    def others(self, unit):
        owner = self.units[unit][1]
        return range(self.tensor_size) if owner is None else [owner]

    def step(self, unit, stage):
        i, owner = self.units[unit]
        spec = self.specs[i]
        if stage < self.dp_bits:
            for slot in sorted(self.slots(stage), key=lambda s: -(s & 1)):
                for half in (0, 1):
                    if stage == 0 and not self.in_place:
                        self.own_copy(unit, half, slot).wait()
                    self.copy(unit, half, stage, slot).wait_recv()
                    add_into(
                        self.sum_at(unit, half, slot << stage),
                        self.landed(unit, half, stage, slot),
                    )
                    if slot & 1:
                        self.copy(unit, half, stage + 1, slot >> 1).start()
            return
        for half in (0, 1):
            total = self.sum_at(unit, half, 0)
            if spec.kind == "dp":
                spec.place(self.outs[i], half)[...] = total[...]
                continue
            for other in self.others(unit):

                @pl.when(other != self.tensor)
                def _():
                    self.z_copy(unit, half, other, self.tensor).start()

                @pl.when(other == self.tensor)
                def _():
                    mine = total if spec.kind == "own" else spec.cut(total, other)
                    self.shares[i][other, half] = mine[...]

    def steps(self):
        count = len(self.units)
        return [
            (unit, turn - unit)
            for turn in range(count + self.dp_bits)
            for unit in range(count)
            if 0 <= turn - unit <= self.dp_bits
        ]

    def close(self):
        for i, spec in enumerate(self.specs):
            if spec.kind == "dp":
                continue
            unit = [u for u, (at, owner) in enumerate(self.units) if at == i][0]
            for half in (0, 1):
                for other in range(self.tensor_size):

                    @pl.when(other != self.tensor)
                    def _():
                        self.z_copy(unit, half, other, other).wait_recv()

                summed = self.shares[i][0, half].astype(jnp.float32)
                for other in range(1, self.tensor_size):
                    summed = summed + self.shares[i][other, half].astype(jnp.float32)
                spec.place(self.outs[i], half)[...] = summed
        for unit, (i, owner) in enumerate(self.units):
            for half in (0, 1):
                for stage in range(self.dp_bits):
                    for slot in self.slots(stage):
                        self.copy(unit, half, stage, slot).wait_send()
                if self.specs[i].kind != "dp":
                    for other in self.others(unit):

                        @pl.when(other != self.tensor)
                        def _():
                            self.z_copy(unit, half, other, self.tensor).wait_send()


def scatter_units(specs, tensor_size):
    units = []
    for i, spec in enumerate(specs):
        units += [(i, j) for j in range(tensor_size)] if spec.kind == "own" else [(i, None)]
    return units


def scatter_scratch(specs, arrays, dp_size, tensor_size, in_place=False):
    dp_bits = dp_size.bit_length() - 1
    scratch = []
    units = len(scatter_units(specs, tensor_size))
    pieces = [tensor_size if spec.kind == "own" else 1 for spec in specs]
    for spec, array, count in zip(specs, arrays, pieces):
        if not in_place:
            scratch.append(pltpu.VMEM((count, 2, dp_size // 2) + spec.part_shape, array.dtype))
    for spec, array, count in zip(specs, arrays, pieces):
        for stage in range(dp_bits):
            scratch.append(
                pltpu.VMEM((count, 2, dp_size >> (stage + 1)) + spec.part_shape, array.dtype)
            )
    for spec, array in zip(specs, arrays):
        if spec.kind != "dp":
            scratch.append(pltpu.VMEM((tensor_size, 2) + spec.cut_shape, array.dtype))
    dma = pltpu.SemaphoreType.DMA
    return scratch + [
        dma((units, 2, dp_size // 2)),
        dma((units, 2, dp_bits, dp_size // 2)),
        dma((units, 2, dp_bits, dp_size // 2)),
        dma((len(specs), 2, tensor_size)),
        dma((len(specs), 2, tensor_size)),
    ]


def scatter_shapes(specs):
    return [
        jax.ShapeDtypeStruct(spec.shape, jnp.bfloat16 if spec.kind == "dp" else jnp.float32)
        for spec in specs
    ]


class ExchangeRun:
    def __init__(self, tensor_size, source, out, own_sem, send, recv):
        self.tensor_size, self.source, self.out = tensor_size, source, out
        self.own_sem, self.send, self.recv = own_sem, send, recv
        self.dp, self.tensor = lax.axis_index("dp"), lax.axis_index("tensor")

    def copy(self, other, slot):
        return pltpu.make_async_remote_copy(
            src_ref=self.source.at[other],
            dst_ref=self.out.at[slot],
            send_sem=self.send.at[other],
            recv_sem=self.recv.at[slot],
            device_id=(self.dp, other),
            device_id_type=MESH,
        )

    def own(self):
        return pltpu.make_async_copy(
            self.source.at[self.tensor], self.out.at[self.tensor], self.own_sem
        )

    def begin(self):
        for other in range(self.tensor_size):
            pl.when(other != self.tensor)(self.copy(other, self.tensor).start)
        self.own().start()

    def close(self):
        self.own().wait()
        for other in range(self.tensor_size):

            @pl.when(other != self.tensor)
            def _():
                self.copy(other, self.tensor).wait_send()
                self.copy(other, other).wait_recv()


def lanes_of(shape):
    return lax.broadcasted_iota(jnp.int32, shape, len(shape) - 1)


def swap_halves(values):
    width = values.shape[-1]
    first = lanes_of(values.shape) % HEAD_DIM < HEAD_DIM // 2
    return jnp.where(
        first,
        pltpu.roll(values, width - HEAD_DIM // 2, 1),
        pltpu.roll(values, HEAD_DIM // 2, 1),
    )


def left_head(block, odd):
    moved = jnp.where(odd, pltpu.roll(block, HEAD_DIM, 1), block)
    return jnp.where(lanes_of(block.shape) < HEAD_DIM, moved, jnp.zeros_like(moved))


def allowed(keys, rows, start):
    key_at = lax.broadcasted_iota(jnp.int32, (keys, rows), 0)
    query_at = lax.broadcasted_iota(jnp.int32, (keys, rows), 1) + start
    return key_at <= query_at


def at_steps(actions, step, steps):
    places = [(min(steps - 1, int(time * steps)), action) for time, action in actions]
    for place in sorted({place for place, _ in places}):

        @pl.when(step == place)
        def _():
            for at, action in places:
                if at == place:
                    action()


def attend_pair(pair, group_pairs, q_pre, cos_ref, sin_ref, kv_all, k_left, v_turned, outs):
    context, queries_out, lse_ref = outs
    rows = q_pre.shape[0]
    kv_width = kv_all.shape[1] // 2
    group = lax.div(pair, group_pairs)
    start = lax.axis_index("tensor") * rows
    at = pl.ds(pl.multiple_of(pair * 128, 128), 128)

    @pl.when(lax.rem(pair, group_pairs) == 0)
    def _():
        odd = lax.rem(group, 2) == 1
        lane = pl.multiple_of(lax.div(group, 2) * 128, 128)
        keys = kv_all[:, pl.ds(lane, 128)].astype(jnp.float32)
        values = kv_all[:, pl.ds(kv_width + lane, 128)].astype(jnp.float32)
        k_left[...] = left_head(keys, odd).astype(jnp.bfloat16)
        v_turned[...] = left_head(values, odd).T[:HEAD_DIM].astype(jnp.bfloat16)

    raw = q_pre[:, at]
    turned = (raw * cos_ref[...] + swap_halves(raw) * sin_ref[...]).astype(jnp.bfloat16)
    turned = turned.astype(jnp.float32) * HEAD_DIM ** (-0.5)
    queries_out[:, at] = turned.astype(jnp.bfloat16)
    open_at = allowed(k_left.shape[0], rows, start)
    contexts = []
    for head in (0, 1):
        queries = (turned if head == 0 else pltpu.roll(turned, HEAD_DIM, 1)).astype(jnp.bfloat16)
        scores = product_right(k_left[...], queries)
        scores = jnp.where(open_at, scores, -1e30)
        top = jnp.max(scores, axis=0, keepdims=True)
        exponent = jnp.exp(scores - top)
        summed = jnp.sum(exponent, axis=0, keepdims=True)
        part = product(v_turned[...], exponent.astype(jnp.bfloat16))
        contexts.append(part * (1.0 / summed))
        lse_ref[pair, pl.ds(head, 1), :] = top + jnp.log(summed)
    context[:, at] = jnp.concatenate(contexts, axis=0).T.astype(jnp.bfloat16)


def front_kernel(specs, kv_spec, n_spec, group_pairs, dp_size, tensor_size, *refs):
    refs = list(refs)

    def take(count):
        return [refs.pop(0) for _ in range(count)]

    count = len(specs)
    tokens, cos_ref, sin_ref = take(3)
    sources = take(count)
    context, queries, lse_ref, normed, middle, gain_rows, kv_all, normed_all = take(8)
    outs = take(count)
    held = take(count)
    weights, kv_weights, gain_blocks, q_pre, k_left, v_turned, normed_two = take(7)
    sems = take(5)
    kv_sems = take(5)
    n_sems = take(5)
    (load_sem,) = take(1)
    key_value, gains, query, out, gate, up, cot = range(count)
    run = GatherRun(specs, dp_size, tensor_size, sources, outs, held, sems)
    rows, width = tokens.shape
    own_rows = pl.ds(pl.multiple_of(run.tensor * rows, rows), rows)
    kv_run = GatherRun(
        [kv_spec], dp_size, tensor_size, [kv_all.at[own_rows, :]], [kv_all], [None], kv_sems
    )
    kv_width = kv_all.shape[1] // 2
    near = [1 << bit for bit in range(run.dp_bits - 1)]
    far = [r for r in range(1, 1 << (run.dp_bits - 1)) if r not in near]
    far.sort(key=lambda rank: rank.bit_count())
    core = list(range(1 << (run.dp_bits - 1), 1 << run.dp_bits))

    n_run = GatherRun(
        [n_spec], dp_size, tensor_size, [normed_two], [normed_all], [normed_two], n_sems
    )

    def hops(ranks, *units):
        for unit in units:
            for rank in ranks:
                run.hop(unit, rank)

    def query_hops(ranks, *steps):
        for step in steps:
            for rank in ranks:
                run.hop_from(query, rank, step)

    run.greet()
    loads = [
        pltpu.make_async_copy(source, target, run.own_sem.at[i])
        for i, (source, target) in enumerate(zip(sources, held))
    ]
    for load in loads:
        load.start()
    small = (key_value, gains)
    for i in (*small, query):
        run.begin_line(i)
    for i in (query, key_value, gains, out, gate, up, cot):
        loads[i].wait()
        run.own(i).start()
        if i == query:
            run.end_line(query)
            query_hops([0], 0)
    for step in range(1, tensor_size):
        for i in small:
            run.line(i, step)
    for i in small:
        run.end_line(i)
    hops([0], *small)
    steps = range(1, tensor_size)
    for step in steps:
        run.line(query, step)
        query_hops([0], step)
        if step == max(1, tensor_size - 2):
            hops(near, *small)
    run.begin_line(out)
    run.begin_line(cot)
    hops(far, *small)
    hops(core, *small)
    run.line(out, 1)

    kv_load = pltpu.make_async_copy(outs[key_value], kv_weights, load_sem.at[0])
    kv_load.start()
    gain_load = pltpu.make_async_copy(outs[gains], gain_blocks, load_sem.at[1])
    gain_load.start()
    gain_load.wait()
    blocks = gain_blocks.shape[0] // 16
    lanes = width // 128
    per = blocks // lanes
    for lane in range(lanes):
        row = jnp.zeros((16, 128), jnp.float32)
        for other in range(per):
            at = (lane * per + other) * 16
            row = row + gain_blocks[at : at + 16, :].astype(jnp.float32)
        gain_rows[:, lane * 128 : (lane + 1) * 128] = row[:8]
    slab = 16

    def norm_first(step, carry):
        at = pl.ds(pl.multiple_of(step * slab, slab), slab)
        raw = tokens[at, :].astype(jnp.float32)
        scale = lax.rsqrt(jnp.mean(raw * raw, axis=-1, keepdims=True) + epsilon)
        normed[at, :] = (raw * scale * gain_rows[0:1, :]).astype(normed.dtype)
        return carry

    lax.fori_loop(0, rows // slab, norm_first, 0)
    kv_load.wait()
    own_kv = product(normed[...], kv_weights[...])
    repeat = kv_width // cos_ref.shape[1]
    own_keys = own_kv[:, :kv_width]
    own_keys = own_keys * jnp.concatenate([cos_ref[...]] * repeat, axis=1) + swap_halves(
        own_keys
    ) * jnp.concatenate([sin_ref[...]] * repeat, axis=1)
    kv_all[own_rows, :] = jnp.concatenate([own_keys, own_kv[:, kv_width:]], axis=1).astype(
        kv_all.dtype
    )
    kv_run.begin_line(0)
    query_hops(near, 0, *steps)
    kv_run.line(0, 1)
    query_hops(far, 0, *steps)
    for step in steps[1:-1]:
        run.line(out, step)
        kv_run.line(0, step)
    query_hops(core, 0, *steps)
    query_load = pltpu.make_async_copy(outs[query], weights, load_sem.at[0])
    query_load.start()
    for step in steps[-1:]:
        run.line(out, step)
    for i in (out, gate, up):
        run.end_line(i)
    hops([0], out)
    query_load.wait()
    tiles = 4
    tile = width // tiles
    for j in range(tiles):
        columns = slice(j * tile, (j + 1) * tile)
        q_pre[:, columns] = product(normed[...], weights[:, columns])
        if j == 1:
            for step in steps[-1:]:
                kv_run.line(0, step)
            run.line(cot, 1)
    pairs = lse_ref.shape[0]
    plan = [
        (0.3, lambda: hops(near, out)),
        (0.31, lambda: hops([0], gate)),
        (0.75, lambda: hops(far, out)),
        (0.89, lambda: hops([0], up)),
    ]
    early = max(1, tensor_size - 2)
    for step in steps[1:early]:
        time = 0.52 + 0.4 * (step - 2) / early
        plan.append((time, functools.partial(run.line, cot, step)))
    plan.sort(key=lambda entry: entry[0])

    def pair_step(pair, carry):
        at_steps(plan, pair, pairs)
        attend_pair(
            pair,
            group_pairs,
            q_pre,
            cos_ref,
            sin_ref,
            kv_all,
            k_left,
            v_turned,
            (context, queries, lse_ref),
        )
        return carry

    lax.fori_loop(0, pairs, pair_step, 0)
    hops(core, out)
    hops(near, gate)
    out_load = pltpu.make_async_copy(outs[out], weights, load_sem.at[0])
    out_load.start()
    out_load.wait()
    for j in range(4):
        columns = slice(j * (width // 4), (j + 1) * (width // 4))
        middle[:, columns] = tokens[:, columns].astype(jnp.float32) + product(
            context[...], weights[:, columns]
        )

    def norm_second(step, carry):
        at = pl.ds(pl.multiple_of(step * slab, slab), slab)
        raw = middle[at, :]
        scale = lax.rsqrt(jnp.mean(raw * raw, axis=-1, keepdims=True) + epsilon)
        normed_two[at, :] = (raw * scale * gain_rows[1:2, :]).astype(normed_two.dtype)
        return carry

    lax.fori_loop(0, rows // slab, norm_second, 0)
    n_run.begin_line(0)
    n_run.own(0).start()
    hops(far, gate)
    for step in steps[early:]:
        run.line(cot, step)
    hops(near, up)
    hops(core, gate)
    hops(far, up)
    hops(core, up)
    for way, block in ((0, run.tensor - 1), (1, run.tensor + 1)):
        arrives = (block >= 0) & (block < tensor_size)
        pl.when(arrives)(n_run.z_copy(0, block, way).wait_recv)
        pl.when(run.can[way])(n_run.z_copy(0, run.tensor, way, normed_two).wait_send)
    n_run.end_line(0)
    run.end_line(cot)
    run.close()
    kv_run.close()


def front(
    tokens, cosines, sines, arrays, specs, kv_spec, n_spec, heads, group_heads, sizes, collective_id
):
    dp_size, tensor_size = sizes
    rows, width = tokens.shape
    length = rows * tensor_size
    low, full = jnp.bfloat16, jnp.float32
    held, sems = gather_scratch(specs, arrays, *sizes)
    _, line_sems = gather_scratch([kv_spec], [], *sizes)
    kv_both = specs[0].shape[1]
    pairs = heads // 2
    tokens_low = jax.ShapeDtypeStruct((rows, width), low)
    return pl.pallas_call(
        functools.partial(front_kernel, specs, kv_spec, n_spec, group_heads // 2, *sizes),
        out_shape=[
            tokens_low,
            tokens_low,
            jax.ShapeDtypeStruct((pairs, 2, rows), full),
            tokens_low,
            jax.ShapeDtypeStruct((rows, width), full),
            jax.ShapeDtypeStruct((8, width), full),
            jax.ShapeDtypeStruct((length, kv_both), low),
            jax.ShapeDtypeStruct((length, width), low),
        ]
        + gather_shapes(specs, arrays),
        in_specs=[VMEM] * 3 + [ANY] * len(specs),
        out_specs=[VMEM] * 7 + [ANY] * (1 + len(specs)),
        scratch_shapes=held
        + [
            pltpu.VMEM((width, width), low),
            pltpu.VMEM((width, kv_both), low),
            pltpu.VMEM(specs[1].shape, low),
            pltpu.VMEM((rows, width), full),
            pltpu.VMEM((length, 128), low),
            pltpu.VMEM((HEAD_DIM, length), low),
            pltpu.VMEM((rows, width), low),
        ]
        + sems
        + line_sems
        + line_sems
        + [pltpu.SemaphoreType.DMA((2,))],
        compiler_params=pltpu.CompilerParams(
            collective_id=collective_id, has_side_effects=True, vmem_limit_bytes=VMEM_LIMIT
        ),
    )(tokens, cosines, sines, *arrays)


def scatter_plan(run):
    plan = [(0.0, run.greet), (0.0, run.begin)]
    times = [(0.12, 0.08), (0.55, 0.3), (0.88, 0.12), (0.95, 0.05)]
    for unit, stage in run.steps():
        first, behind = times[min(stage, len(times) - 1)]
        plan.append((min(first + behind * unit, 1.0), functools.partial(run.step, unit, stage)))
    plan.sort(key=lambda entry: entry[0])
    return plan + [(1.0, run.close)]


def attend_back_kernel(group_pairs, pairs, specs, dp_size, tensor_size, *refs):
    refs = list(refs)
    q_ref, context_ref, out_ref = (refs.pop(0) for _ in range(3))
    lse_ref, cos_ref, sin_ref, k_ref, v_ref = (refs.pop(0) for _ in range(5))
    back_ref, middle_ref, cot_ref, gain_ref = (refs.pop(0) for _ in range(4))
    sources = [refs.pop(0) for _ in specs]
    dq_ref, dk_ref, dv_ref, grad_middle, middle_low, gain_sum = (refs.pop(0) for _ in range(6))
    outs = [refs.pop(0) for _ in specs]
    k_left, v_left, k_turned, dk_sum, dv_sum, column_sum = (refs.pop(0) for _ in range(6))
    run = ScatterRun(specs, dp_size, tensor_size, sources, outs, refs)
    plan = scatter_plan(run)
    at_steps([entry for entry in plan if entry[0] < 1.0], pl.program_id(0), pairs)
    pair = pl.program_id(0)
    group = pair // group_pairs
    odd = group % 2 == 1
    rows = q_ref.shape[0]
    start = lax.axis_index("tensor") * rows

    @pl.when(pair == 0)
    def _():
        slab = 16
        column_sum[...] = jnp.zeros_like(column_sum)

        def norm_slab(step, carry):
            at = pl.ds(pl.multiple_of(step * slab, slab), slab)
            raw = middle_ref[at, :]
            scale = lax.rsqrt(jnp.mean(raw * raw, axis=-1, keepdims=True) + epsilon)
            unit = raw * scale
            grad = back_ref[at, :]
            gained = grad * unit
            column_sum[...] += gained[:8] + gained[8:]
            scaled = grad * gain_ref[...]
            mean = jnp.mean(scaled * unit, axis=-1, keepdims=True)
            total = cot_ref[at, :].astype(jnp.float32) + scale * (scaled - unit * mean)
            grad_middle[at, :] = total
            middle_low[at, :] = total.astype(middle_low.dtype)
            return carry

        lax.fori_loop(0, rows // slab, norm_slab, 0)
        gain_sum[...] = jnp.sum(column_sum[...], axis=0, keepdims=True)

    grad_context = product_right(middle_low[...], out_ref[...])
    grad_low = grad_context.astype(jnp.bfloat16)
    heads_at = lax.broadcasted_iota(jnp.int32, (8, 128), 0)
    own_lanes = lax.div(lanes_of((8, 128)), HEAD_DIM) == heads_at
    mixed_sums = lax.dot_general(
        jnp.where(own_lanes, 1.0, 0.0),
        grad_low.astype(jnp.float32) * context_ref[...].astype(jnp.float32),
        (((1,), (1,)), ((), ())),
        precision=lax.Precision.HIGHEST,
        preferred_element_type=jnp.float32,
    )

    @pl.when(pair % group_pairs == 0)
    def _():
        left = left_head(k_ref[...].astype(jnp.float32), odd)
        k_left[...] = left.astype(jnp.bfloat16)
        k_turned[...] = left.T[:HEAD_DIM].astype(jnp.bfloat16)
        v_left[...] = left_head(v_ref[...].astype(jnp.float32), odd).astype(jnp.bfloat16)
        dk_sum[...] = jnp.zeros_like(dk_sum)
        dv_sum[...] = jnp.zeros_like(dv_sum)

    open_at = allowed(k_left.shape[0], rows, start)
    grads = []
    for head in (0, 1):
        queries, grad_out = q_ref[...], grad_low
        if head == 1:
            queries = pltpu.roll(queries.astype(jnp.float32), HEAD_DIM, 1).astype(jnp.bfloat16)
            grad_out = pltpu.roll(grad_context, HEAD_DIM, 1).astype(jnp.bfloat16)
        scores = product_right(k_left[...], queries)
        scores = jnp.where(open_at, scores, -1e30)
        softmaxed = jnp.exp(scores - lse_ref[0, head, :][None, :])
        grad_soft = product_right(v_left[...], grad_out)
        mixed_sum = mixed_sums[head : head + 1, :]
        grad_scores = (softmaxed * (grad_soft - mixed_sum)).astype(jnp.bfloat16)
        dv_sum[...] += product(softmaxed.astype(jnp.bfloat16), grad_out)
        dk_sum[...] += product(grad_scores, queries)
        grads.append(product(k_turned[...], grad_scores))
    grad_q = jnp.concatenate(grads, axis=0).T * HEAD_DIM ** (-0.5)
    dq_ref[...] = (grad_q * cos_ref[...] - swap_halves(grad_q) * sin_ref[...]).astype(jnp.bfloat16)

    @pl.when(pair % group_pairs == group_pairs - 1)
    def _():
        for total, out in ((dk_sum, dk_ref), (dv_sum, dv_ref)):
            value = total[...]
            left = lanes_of(value.shape) < HEAD_DIM

            @pl.when(jnp.logical_not(odd))
            def _():
                out[...] = jnp.where(left, value, 0.0).astype(out.dtype)

            @pl.when(odd)
            def _():
                out[...] = jnp.where(
                    left, out[...].astype(jnp.float32), pltpu.roll(value, HEAD_DIM, 1)
                ).astype(out.dtype)
    at_steps([entry for entry in plan if entry[0] >= 1.0], pair, pairs)


def attend_back(
    queries,
    context,
    out_full,
    lse,
    cosines,
    sines,
    keys_values,
    back,
    middle,
    cotangent,
    gain,
    head_count,
    group_heads,
    specs,
    arrays,
    sizes,
    collective_id,
):
    rows, width = queries.shape
    length, both = keys_values.shape
    pairs, group_pairs = head_count // 2, group_heads // 2
    kv_blocks = both // 256
    low, full = jnp.bfloat16, jnp.float32
    wide = pl.BlockSpec((rows, 128), lambda p: (0, p))
    table = pl.BlockSpec((rows, 128), lambda p: (0, 0))
    kv_out = pl.BlockSpec((length, 128), lambda p: (0, p // group_pairs // 2))
    return pl.pallas_call(
        functools.partial(attend_back_kernel, group_pairs, pairs, specs, *sizes),
        grid=(pairs,),
        out_shape=[
            jax.ShapeDtypeStruct((rows, width), low),
            jax.ShapeDtypeStruct((length, both // 2), low),
            jax.ShapeDtypeStruct((length, both // 2), low),
            jax.ShapeDtypeStruct((rows, width), full),
            jax.ShapeDtypeStruct((rows, width), low),
            jax.ShapeDtypeStruct((1, width), full),
        ]
        + scatter_shapes(specs),
        in_specs=[
            wide,
            wide,
            pl.BlockSpec((128, width), lambda p: (p, 0)),
            pl.BlockSpec((1, 2, rows), lambda p: (p, 0, 0)),
            table,
            table,
            pl.BlockSpec((length, 128), lambda p: (0, p // group_pairs // 2)),
            pl.BlockSpec((length, 128), lambda p: (0, kv_blocks + p // group_pairs // 2)),
        ]
        + [VMEM] * 4
        + [ANY] * len(specs),
        out_specs=[wide, kv_out, kv_out] + [VMEM] * (3 + len(specs)),
        scratch_shapes=[
            pltpu.VMEM((length, 128), low),
            pltpu.VMEM((length, 128), low),
            pltpu.VMEM((HEAD_DIM, length), low),
            pltpu.VMEM((length, 128), full),
            pltpu.VMEM((length, 128), full),
            pltpu.VMEM((8, width), full),
        ]
        + scatter_scratch(specs, arrays, *sizes),
        compiler_params=pltpu.CompilerParams(
            collective_id=collective_id, has_side_effects=True, vmem_limit_bytes=VMEM_LIMIT
        ),
        cost_estimate=pl.CostEstimate(
            flops=10 * rows * length * width, bytes_accessed=8 * rows * width, transcendentals=0
        ),
    )(
        queries,
        context,
        out_full,
        lse,
        cosines,
        sines,
        keys_values,
        keys_values,
        back,
        middle,
        cotangent,
        gain,
        *arrays,
    )


def block_at(place, tensor, tensor_size):
    above = tensor_size - 1 - tensor
    up = jnp.where(place < above, tensor + 1 + place, tensor - 1 - (place - above))
    down = jnp.where(place < tensor, tensor - 1 - place, 1 + place)
    other = jnp.where(tensor <= above, up, down)
    return jnp.where(place == tensor_size - 1, tensor, other)


def mlp_kernel(
    gather_specs,
    specs,
    dp_size,
    tensor_size,
    normed_ref,
    cot_ref,
    gate_ref,
    up_ref,
    down_ref,
    back_ref,
    y_ref,
    d_gate_ref,
    d_up_ref,
    down_sum,
    normed,
    cot,
    gate,
    up,
    down,
    hidden,
    d_gate,
    d_up,
    y_stage,
    stage,
    landing,
    load_sem,
    n_send,
    n_recv,
    y_sem,
    b_send,
    b_recv,
    out_sem,
    *more_refs,
):
    run = ScatterRun(
        specs, dp_size, tensor_size, [down], [down_sum], more_refs[5:], in_place=True
    )
    down_run = GatherRun(
        gather_specs, dp_size, tensor_size, [down_ref], [down], [down_ref], more_refs[:5]
    )
    dp, tensor = lax.axis_index("dp"), lax.axis_index("tensor")
    _, rows, width = normed_ref.shape
    units = gate.shape[1]
    loads = [
        pltpu.make_async_copy(source, target, load_sem.at[i])
        for i, (source, target) in enumerate(((gate_ref, gate), (up_ref, up), (cot_ref, cot)))
    ]
    has = [tensor + 1 < tensor_size, tensor > 0]

    def near_load(step):
        block = tensor + step
        return pltpu.make_async_copy(
            normed_ref.at[block], normed.at[block], load_sem.at[4 + step]
        )

    def near_loads(act):
        act(near_load(0))
        for way, step in ((0, 1), (1, -1)):

            @pl.when(has[way])
            def _():
                act(near_load(step))

    near_loads(lambda load: load.start())
    down_run.own(0).start()
    for load in loads:
        load.start()
    greet((dp, tensor, tensor_size), False, True, run.dp_bits)

    def n_copy(block, way, source=None):
        return pltpu.make_async_remote_copy(
            src_ref=normed.at[block] if source is None else source,
            dst_ref=normed.at[block],
            send_sem=n_send.at[way, block],
            recv_sem=n_recv.at[block],
            device_id=(dp, tensor + 1 if way == 0 else tensor - 1),
            device_id_type=MESH,
        )

    for way, step in ((0, -1), (1, 1)):
        both = has[0] & has[1]
        pl.when(both)(n_copy(tensor + step, way, normed_ref.at[tensor + step]).start)
    down_run.end_line(0)
    down_run.hop(0, 0)
    landing[tensor] = jnp.zeros((rows, width), landing.dtype)

    def pump(distance):
        for way, block in ((0, tensor - distance), (1, tensor + distance)):

            @pl.when((block >= 0) & (block < tensor_size))
            def _():
                n_copy(block, way).wait_recv()
                pl.when(has[way])(n_copy(block, way).start)

    farthest = jnp.maximum(tensor, tensor_size - 1 - tensor)
    core_rank = 1 << (run.dp_bits - 1)
    down_ranks = [
        sorted(range(1, core_rank), key=lambda rank: rank.bit_count()),
        range(core_rank, 2 * core_rank),
    ]

    def b_copy(block, slot):
        return pltpu.make_async_remote_copy(
            src_ref=stage.at[block],
            dst_ref=landing.at[slot],
            send_sem=b_send.at[block],
            recv_sem=b_recv.at[slot],
            device_id=(dp, block),
            device_id_type=MESH,
        )

    def y_copy(block, slot):
        return pltpu.make_async_copy(y_stage.at[slot], y_ref.at[block], y_sem.at[slot])

    for load in loads:
        load.wait()
    near_loads(lambda load: load.wait())

    def chunk(place, carry):
        block = block_at(place, tensor, tensor_size)
        rows_in = normed[block]
        gate_pre = product(rows_in, gate[...])
        upward = product(rows_in, up[...])

        @pl.when(place == 0)
        def _():
            for rank in down_ranks[0]:
                down_run.hop(0, rank)

        @pl.when(place + 2 <= farthest)
        def _():
            pump(place + 2)

        @pl.when(place == 0)
        def _():
            for rank in down_ranks[1]:
                down_run.hop(0, rank)

        sigmoid = 1.0 / (1.0 + jnp.exp(-gate_pre))
        silu = gate_pre * sigmoid
        active = (silu * upward).astype(jnp.bfloat16)
        hidden[block] = active
        grad_hidden = product_right(cot[block], down[...])
        low_gate = (
            grad_hidden * upward * sigmoid * (1.0 + gate_pre * (1.0 - sigmoid))
        ).astype(jnp.bfloat16)
        low_up = (grad_hidden * silu).astype(jnp.bfloat16)
        d_gate[block] = low_gate
        d_up[block] = low_up
        back = product_right(low_gate, gate[...]) + product_right(low_up, up[...])

        @pl.when(block == tensor)
        def _():
            back_ref[...] = back

        @pl.when(block != tensor)
        def _():
            stage[block] = back.astype(stage.dtype)
            b_copy(block, tensor).start()

        slot = lax.rem(place, 2)

        @pl.when(place >= 2)
        def _():
            y_copy(block, slot).wait()

        y_stage[slot] = product(active, down[...]).astype(jnp.bfloat16)
        y_copy(block, slot).start()

        return carry

    lax.fori_loop(0, tensor_size, chunk, 0)
    for slot in range(2):
        y_copy(0, slot).wait()

    all_rows = tensor_size * rows

    def weight_grad(left, right, out):
        extent = left.shape[2]
        tile = 256 if extent % 256 == 0 else 128 if extent % 128 == 0 else extent

        def body(step, carry):
            at = pl.ds(pl.multiple_of(step * tile, tile), tile)
            columns = left[:, :, at].reshape(all_rows, tile)
            out[at, :] = product_left(columns, right[...].reshape(all_rows, -1)).astype(out.dtype)
            return carry

        lax.fori_loop(0, extent // tile, body, 0)

    down_run.close()
    weight_grad(hidden, cot, down)
    run.begin_unit(0)
    weight_grad(normed, d_gate, gate)
    pltpu.make_async_copy(gate, d_gate_ref, out_sem.at[0]).start()
    run.step(0, 0)
    weight_grad(normed, d_up, up)
    pltpu.make_async_copy(up, d_up_ref, out_sem.at[1]).start()
    run.step(0, 1)

    for other in range(tensor_size):

        @pl.when(other != tensor)
        def _():
            b_copy(other, other).wait_recv()

    slab = 16

    def add_slab(step, carry):
        at = pl.ds(pl.multiple_of(step * slab, slab), slab)
        total = back_ref[at, :]
        for other in range(tensor_size):
            total = total + landing[other, at, :].astype(jnp.float32)
        back_ref[at, :] = total
        return carry

    lax.fori_loop(0, rows // slab, add_slab, 0)
    for later in range(2, run.dp_bits + 1):
        run.step(0, later)
    run.close()
    pltpu.make_async_copy(gate, d_gate_ref, out_sem.at[0]).wait()
    pltpu.make_async_copy(up, d_up_ref, out_sem.at[1]).wait()
    for other in range(tensor_size):

        @pl.when(other != tensor)
        def _():
            b_copy(other, tensor).wait_send()

        for way in (0, 1):
            sent = has[way] & ((other < tensor) if way == 0 else (other > tensor))
            pl.when(sent)(n_copy(other, way).wait_send)


def feed_forward(
    normed, cot_all, gate, up, down, gather_specs, specs, sizes, collective_id
):
    dp_size, tensor_size = sizes
    rows, width = normed.shape[0] // tensor_size, normed.shape[1]
    units = gate.shape[1]
    low = jnp.bfloat16
    tokens = (tensor_size, rows, width)
    inner = (tensor_size, rows, units)
    dma = pltpu.SemaphoreType.DMA
    return pl.pallas_call(
        functools.partial(mlp_kernel, gather_specs, specs, dp_size, tensor_size),
        out_shape=[
            jax.ShapeDtypeStruct((rows, width), jnp.float32),
            jax.ShapeDtypeStruct(tokens, low),
            jax.ShapeDtypeStruct(gate.shape, low),
            jax.ShapeDtypeStruct(up.shape, low),
        ]
        + scatter_shapes(specs),
        in_specs=[ANY] * 5,
        out_specs=[VMEM] + [ANY] * 3 + [VMEM],
        scratch_shapes=[
            pltpu.VMEM(tokens, low),
            pltpu.VMEM(tokens, low),
            pltpu.VMEM(gate.shape, low),
            pltpu.VMEM(up.shape, low),
            pltpu.VMEM(gather_specs[0].shape, low),
            pltpu.VMEM(inner, low),
            pltpu.VMEM(inner, low),
            pltpu.VMEM(inner, low),
            pltpu.VMEM((2, rows, width), low),
            pltpu.VMEM(tokens, low),
            pltpu.VMEM(tokens, low),
            dma((6,)),
            dma((2, tensor_size)),
            dma((tensor_size,)),
            dma((2,)),
            dma((tensor_size,)),
            dma((tensor_size,)),
            dma((2,)),
        ]
        + gather_scratch(gather_specs, [], dp_size, tensor_size)[1]
        + scatter_scratch(specs, [down], dp_size, tensor_size, in_place=True),
        compiler_params=pltpu.CompilerParams(
            collective_id=collective_id, has_side_effects=True, vmem_limit_bytes=63 * 2**20
        ),
        cost_estimate=pl.CostEstimate(
            flops=18 * tensor_size * rows * width * units,
            bytes_accessed=8 * width * units,
            transcendentals=0,
        ),
    )(
        normed.reshape(tokens),
        cot_all.reshape(tokens),
        gate,
        up,
        down,
    )


def tail_kernel(specs, dp_size, tensor_size, *refs):
    refs = list(refs)

    def take(count):
        return [refs.pop(0) for _ in range(count)]

    sources = take(7)
    k_blocks, v_blocks, wq_ref, cos_ref, sin_ref, gain_ref, second_ref = take(7)
    tokens_out, out_sum, query_sum, kv_sum, gain_sum = take(5)
    held = take(7)
    context, middle_low, normed, dq, wkv, tokens, middle = held
    o_grad, q_grad, kv_grad, gain_grad, wq_tile, k_landing, v_landing, kv_low, column_sum = take(9)
    load_sem, tile_sem = take(2)
    k_sems, v_sems = take(3), take(3)
    run = ScatterRun(
        specs,
        dp_size,
        tensor_size,
        [o_grad, q_grad, kv_grad, gain_grad],
        [out_sum, query_sum, kv_sum, gain_sum],
        refs,
        in_place=True,
    )
    rows, width = tokens.shape
    q_cols = q_grad.shape[2]
    o_rows = o_grad.shape[1]
    kv_width = kv_low.shape[1] // 2
    loads = [
        pltpu.make_async_copy(source, target, load_sem.at[i])
        for i, (source, target) in enumerate(zip(sources, held))
    ]
    for load in loads:
        load.start()

    def tile_copy(j):
        return pltpu.make_async_copy(
            wq_ref.at[:, pl.ds(j * q_cols, q_cols)], wq_tile.at[j % 2], tile_sem.at[j % 2]
        )

    tile_copy(0).start()
    exchanges = [
        ExchangeRun(tensor_size, k_blocks, k_landing, *k_sems),
        ExchangeRun(tensor_size, v_blocks, v_landing, *v_sems),
    ]
    greet((run.dp, run.tensor, tensor_size), False, True, run.dp_bits)
    for exchange in exchanges:
        exchange.begin()

    def out_piece(j):
        tile = min(256, o_rows)
        for row in range(0, o_rows, tile):
            o_grad[j, row : row + tile, :] = product_left(
                context[:, j * o_rows + row : j * o_rows + row + tile], middle_low[...]
            ).astype(o_grad.dtype)
        run.begin_unit(j)

    def query_piece(j):
        grads = dq[:, j * q_cols : (j + 1) * q_cols]
        tile = 512
        for row in range(0, width, tile):
            q_grad[j, row : row + tile, :] = product_left(
                normed[:, row : row + tile], grads
            ).astype(q_grad.dtype)
        run.begin_unit(tensor_size + j)

    def back_piece(j):
        if j + 1 < tensor_size:
            tile_copy(j + 1).start()
        tile_copy(j).wait()
        part = product_right(dq[:, j * q_cols : (j + 1) * q_cols], wq_tile[j % 2])
        if j == 0:
            tokens_out[...] = part
        else:
            tokens_out[...] += part

    def kv_piece():
        for exchange in exchanges:
            exchange.close()
        grad_keys = k_landing[0].astype(jnp.float32)
        grad_values = v_landing[0].astype(jnp.float32)
        for other in range(1, tensor_size):
            grad_keys = grad_keys + k_landing[other].astype(jnp.float32)
            grad_values = grad_values + v_landing[other].astype(jnp.float32)
        repeat = kv_width // cos_ref.shape[1]
        cosines = jnp.concatenate([cos_ref[...]] * repeat, axis=1)
        sines = jnp.concatenate([sin_ref[...]] * repeat, axis=1)
        kv_low[:, :kv_width] = (grad_keys * cosines - swap_halves(grad_keys) * sines).astype(
            kv_low.dtype
        )
        kv_low[:, kv_width:] = grad_values.astype(kv_low.dtype)
        for row in range(0, width, 512):
            kv_grad[row : row + 512, :] = product_left(
                normed[:, row : row + 512], kv_low[...]
            ).astype(kv_grad.dtype)
        run.begin_unit(2 * tensor_size)
        tokens_out[...] += product_right(kv_low[...], wkv[...])

    slab = 16

    def finish(step, carry):
        at = pl.ds(pl.multiple_of(step * slab, slab), slab)
        raw = tokens[at, :].astype(jnp.float32)
        scale = lax.rsqrt(jnp.mean(raw * raw, axis=-1, keepdims=True) + epsilon)
        unit = raw * scale
        grad = tokens_out[at, :]
        gained = grad * unit
        column_sum[...] += gained[:8] + gained[8:]
        scaled = grad * gain_ref[...]
        mean = jnp.mean(scaled * unit, axis=-1, keepdims=True)
        tokens_out[at, :] = middle[at, :] + scale * (scaled - unit * mean)
        return carry

    def last_piece():
        column_sum[...] = jnp.zeros_like(column_sum)
        lax.fori_loop(0, rows // slab, finish, 0)
        gain_grad[...] = jnp.zeros_like(gain_grad)
        gain_grad[0:1, :] = jnp.sum(column_sum[...], axis=0, keepdims=True)
        gain_grad[8:9, :] = second_ref[...]
        run.begin_unit(2 * tensor_size + 1)

    loads[0].wait()
    loads[1].wait()
    for j in range(tensor_size):
        out_piece(j)
        if 1 <= j <= 2:
            run.step(j - 1, 0)
    for load in loads[2:]:
        load.wait()
    count = len(run.units)
    work = {j: [functools.partial(query_piece, j)] for j in range(tensor_size)}
    room = max(1, tensor_size - 2)
    for j in range(tensor_size):
        work.setdefault(tensor_size + j * room // tensor_size, []).append(
            functools.partial(back_piece, j)
        )
    work.setdefault(2 * tensor_size - 2, []).append(kv_piece)
    work.setdefault(2 * tensor_size - 1, []).append(last_piece)
    for tick in range(count + 1):
        for piece in work.get(tick, []):
            piece()
        if tick < count:
            run.step(tick, 1)
        if tick + 2 < count:
            run.step(tick + 2, 0)
        if tick:
            for stage in range(2, run.dp_bits + 1):
                run.step(tick - 1, stage)
    run.close()


def tail(
    context,
    middle_low,
    normed,
    dq,
    key_value,
    tokens,
    middle,
    k_blocks,
    v_blocks,
    query,
    cosines,
    sines,
    gain,
    second,
    specs,
    sizes,
    collective_id,
):
    dp_size, tensor_size = sizes
    rows, width = tokens.shape
    low, full = jnp.bfloat16, jnp.float32
    o_spec, q_spec = specs[0], specs[1]
    kv_both = key_value.shape[1]
    dma = pltpu.SemaphoreType.DMA
    arrays = [
        jax.ShapeDtypeStruct((tensor_size, o_spec.shape[0], width), low),
        jax.ShapeDtypeStruct((tensor_size, width, q_spec.shape[1]), low),
        jax.ShapeDtypeStruct((width, kv_both), low),
        jax.ShapeDtypeStruct((16, width), full),
    ]
    loaded = [context, middle_low, normed, dq, key_value, tokens, middle]
    return pl.pallas_call(
        functools.partial(tail_kernel, specs, dp_size, tensor_size),
        out_shape=[jax.ShapeDtypeStruct((rows, width), full)] + scatter_shapes(specs),
        in_specs=[ANY] * 10 + [VMEM] * 4,
        out_specs=[VMEM] * (1 + len(specs)),
        scratch_shapes=[pltpu.VMEM(array.shape, array.dtype) for array in loaded]
        + [pltpu.VMEM(array.shape, array.dtype) for array in arrays]
        + [
            pltpu.VMEM((2, width, q_spec.shape[1]), low),
            pltpu.VMEM(k_blocks.shape, low),
            pltpu.VMEM(v_blocks.shape, low),
            pltpu.VMEM((rows, kv_both), low),
            pltpu.VMEM((8, width), full),
            dma((7,)),
            dma((2,)),
        ]
        + [dma, dma((tensor_size,)), dma((tensor_size,))] * 2
        + scatter_scratch(specs, arrays, dp_size, tensor_size, in_place=True),
        compiler_params=pltpu.CompilerParams(
            collective_id=collective_id, has_side_effects=True, vmem_limit_bytes=60 * 2**20
        ),
    )(*loaded, k_blocks, v_blocks, query, cosines, sines, gain, second)


def rope_tables(rows, tensor):
    halved = HEAD_DIM // 2
    lane = lax.rem(jnp.arange(128), HEAD_DIM)
    turn = lax.rem(lane, halved).astype(jnp.float32)
    freqs = theta_base ** (-2.0 * turn / HEAD_DIM)
    places = (tensor * rows + jnp.arange(rows)).astype(jnp.float32)
    angles = places[:, None] * freqs[None, :]
    return jnp.cos(angles), jnp.where(lane < halved, -1.0, 1.0)[None, :] * jnp.sin(angles)


def start_row(dp, size):
    return pl.multiple_of(dp * size, size)


def on_device(
    dp_size,
    tensor_size,
    tokens,
    attn_gain,
    w_query,
    w_key,
    w_value,
    w_out,
    mlp_gain,
    w_gate,
    w_up,
    w_down,
    cotangent,
):
    tensor_index = lax.axis_index("tensor")
    rows, width = tokens.shape
    heads = w_query.shape[1] * tensor_size // HEAD_DIM
    kv_width = w_key.shape[1]
    kv_heads = kv_width // HEAD_DIM
    group_heads = heads // kv_heads
    q_rows, q_cols = w_query.shape
    kv_rows = w_key.shape[0]
    o_rows, o_cols = w_out.shape
    gain_part = attn_gain.shape[0]

    key_value = jnp.concatenate([w_key, w_value], axis=1)
    per = 128 // gain_part
    spot = lax.rem(lax.axis_index("dp") * tensor_size + tensor_index, per)
    rows_at = lax.broadcasted_iota(jnp.int32, (16, 128), 0)
    here = lax.div(lax.broadcasted_iota(jnp.int32, (16, 128), 1), gain_part) == spot
    wide = [
        jnp.broadcast_to(gain.reshape(1, 1, -1), (16, per, gain_part)).reshape(16, 128)
        for gain in (attn_gain, mlp_gain)
    ]
    gains = jnp.where(rows_at == 0, *wide)
    gains = jnp.where(here & (rows_at < 2), gains, jnp.zeros_like(gains))
    query_spec = Gather(
        (width, heads * HEAD_DIM),
        lambda ref, dp, t: ref.at[
            pl.ds(start_row(dp, q_rows), q_rows), pl.ds(start_row(t, q_cols), q_cols)
        ],
        lambda ref, dp, half, j: ref.at[
            pl.ds(pl.multiple_of(dp * q_rows + half * (q_rows // 2), q_rows // 2), q_rows // 2),
            pl.ds(start_row(j, q_cols), q_cols),
        ],
        pieces=tensor_size,
    )
    kv_all_rows = kv_rows * tensor_size
    kv_spec = Gather(
        (width, 2 * kv_width),
        lambda ref, dp, t: ref.at[pl.ds(start_row(dp * tensor_size + t, kv_rows), kv_rows), :],
        lambda ref, dp, half, j: ref.at[
            pl.ds(
                pl.multiple_of(dp * kv_all_rows + half * (kv_all_rows // 2), kv_all_rows // 2),
                kv_all_rows // 2,
            ),
            :,
        ],
    )
    gain_spec = Gather(
        (dp_size * tensor_size * 16, 128),
        lambda ref, dp, t: ref.at[pl.ds(start_row(dp * tensor_size + t, 16), 16), :],
        lambda ref, dp, half, j: ref.at[
            pl.ds(
                pl.multiple_of((2 * dp + half) * tensor_size * 8, tensor_size * 8),
                tensor_size * 8,
            ),
            :,
        ],
    )
    out_spec = Gather(
        (heads * HEAD_DIM, width),
        lambda ref, dp, t: ref.at[
            pl.ds(start_row(t, o_rows), o_rows), pl.ds(start_row(dp, o_cols), o_cols)
        ],
        lambda ref, dp, half, j: ref.at[
            pl.ds(half * (heads * HEAD_DIM // 2), heads * HEAD_DIM // 2),
            pl.ds(start_row(dp, o_cols), o_cols),
        ],
    )
    row_spec = lambda shape: Gather(
        (tensor_size * shape[0], shape[1]),
        lambda ref, dp, t: ref.at[pl.ds(start_row(t, shape[0]), shape[0]), :],
    )
    up_rows, units = w_gate.shape
    column_spec = Gather(
        (width, units),
        lambda ref, dp, t: ref.at[pl.ds(start_row(dp, up_rows), up_rows), :],
        lambda ref, dp, half, j: ref.at[
            pl.ds(
                pl.multiple_of(dp * up_rows + half * (up_rows // 2), up_rows // 2), up_rows // 2
            ),
            :,
        ],
        False,
    )
    down_cols = w_down.shape[1]
    down_spec = Gather(
        (units, width),
        lambda ref, dp, t: ref.at[:, pl.ds(start_row(dp, down_cols), down_cols)],
        lambda ref, dp, half, j: ref.at[
            pl.ds(half * (units // 2), units // 2), pl.ds(start_row(dp, down_cols), down_cols)
        ],
        False,
    )
    sizes = (dp_size, tensor_size)
    cosines, sines = rope_tables(rows, tensor_index)
    (
        context,
        queries,
        log_sums,
        normed_first,
        middle,
        gain_rows,
        kv_all,
        normed_all,
        key_value_full,
        _,
        query_full,
        out_full,
        gate_full,
        up_full,
        cot_all,
    ) = front(
        tokens,
        cosines,
        sines,
        [key_value, gains, w_query, w_out, w_gate, w_up, cotangent],
        [
            kv_spec,
            gain_spec,
            query_spec,
            out_spec,
            column_spec,
            column_spec,
            row_spec(cotangent.shape),
        ],
        row_spec((rows, 2 * kv_width)),
        row_spec((rows, width)),
        heads,
        group_heads,
        sizes,
        1,
    )
    column_scatter = Scatter(
        "dp",
        (up_rows, units),
        column_spec.half,
        (up_rows // 2, units),
        lambda ref, half: ref.at[pl.ds(half * (up_rows // 2), up_rows // 2), :],
    )
    down_scatter = Scatter(
        "dp",
        (units, down_cols),
        down_spec.half,
        (units // 2, down_cols),
        lambda ref, half: ref.at[pl.ds(half * (units // 2), units // 2), :],
    )
    back_second, mlp_part, grad_gate_w, grad_up_w, sum_down = feed_forward(
        normed_all, cot_all, gate_full, up_full, w_down, [down_spec], [down_scatter], sizes, 3
    )
    mlp_rows = lax.psum_scatter(
        mlp_part.reshape(tensor_size * rows, width), "tensor", scatter_dimension=0, tiled=True
    )
    query_scatter = Scatter(
        "own",
        (q_rows, q_cols),
        lambda ref, dp, half, j: ref.at[
            j,
            pl.ds(pl.multiple_of(dp * q_rows + half * (q_rows // 2), q_rows // 2), q_rows // 2),
            :,
        ],
        (q_rows // 2, q_cols),
        lambda ref, half: ref.at[pl.ds(half * (q_rows // 2), q_rows // 2), :],
    )
    kv_scatter = Scatter(
        "cut",
        (kv_rows, 2 * kv_width),
        lambda ref, dp, half, j: ref.at[
            pl.ds(start_row(dp, kv_all_rows), kv_all_rows), pl.ds(half * kv_width, kv_width)
        ],
        (kv_all_rows, kv_width),
        lambda ref, half: ref.at[:, pl.ds(half * kv_width, kv_width)],
        lambda ref, j: ref.at[pl.ds(j * kv_rows, kv_rows), :],
        (kv_rows, kv_width),
    )
    out_scatter = Scatter(
        "own",
        (o_rows, o_cols),
        lambda ref, dp, half, j: ref.at[
            j,
            pl.ds(half * (o_rows // 2), o_rows // 2),
            pl.ds(start_row(dp, o_cols), o_cols),
        ],
        (o_rows // 2, o_cols),
        lambda ref, half: ref.at[pl.ds(half * (o_rows // 2), o_rows // 2), :],
    )
    gain_cols = tensor_size * gain_part
    gain_scatter = Scatter(
        "cut",
        (16, gain_cols),
        lambda ref, dp, half, j: ref.at[
            pl.ds(half * 8, 8), pl.ds(start_row(dp, gain_cols), gain_cols)
        ],
        (8, gain_cols),
        lambda ref, half: ref.at[pl.ds(half * 8, 8), :],
        lambda ref, j: ref,
        (8, gain_cols),
    )
    (
        grad_queries,
        grad_keys,
        grad_values,
        grad_middle,
        middle_low,
        grad_gain_second,
        sum_gate,
        sum_up,
    ) = attend_back(
        queries,
        context,
        out_full,
        log_sums,
        cosines,
        sines,
        kv_all,
        back_second,
        middle,
        cotangent,
        gain_rows[1:2],
        heads,
        group_heads,
        [column_scatter, column_scatter],
        [grad_gate_w, grad_up_w],
        sizes,
        7,
    )
    grad_tokens, sum_out, sum_query, sum_kv, sum_gains = tail(
        context,
        middle_low,
        normed_first,
        grad_queries,
        key_value_full,
        tokens,
        grad_middle,
        grad_keys.reshape(tensor_size, rows, kv_width),
        grad_values.reshape(tensor_size, rows, kv_width),
        query_full,
        cosines,
        sines,
        gain_rows[0:1],
        grad_gain_second,
        [out_scatter, query_scatter, kv_scatter, gain_scatter],
        sizes,
        5,
    )
    sum_gains = lax.dynamic_slice_in_dim(sum_gains, tensor_index * gain_part, gain_part, 1)
    middle, mlp_rows, sum_query = lax.optimization_barrier((middle, mlp_rows, sum_query))
    output = (middle + mlp_rows.astype(jnp.float32)).astype(jnp.bfloat16)
    return (
        output,
        grad_tokens,
        sum_gains[0],
        sum_query,
        sum_kv[:, :kv_width],
        sum_kv[:, kv_width:],
        sum_out,
        sum_gains[8],
        sum_gate.astype(jnp.float32),
        sum_up.astype(jnp.float32),
        sum_down.astype(jnp.float32),
    )


def solution(mesh):
    placed = (
        P(("dp", "tensor"), None),
        P(("dp", "tensor")),
        P("dp", "tensor"),
        P(("dp", "tensor"), None),
        P(("dp", "tensor"), None),
        P("tensor", "dp"),
        P(("dp", "tensor")),
        P("dp", "tensor"),
        P("dp", "tensor"),
        P("tensor", "dp"),
        P(("dp", "tensor"), None),
    )
    return jax.shard_map(
        functools.partial(on_device, mesh.shape["dp"], mesh.shape["tensor"]),
        mesh=mesh,
        in_specs=placed,
        out_specs=(
            P(("dp", "tensor"), None),
            P(("dp", "tensor"), None),
            P(("dp", "tensor")),
            P("dp", "tensor"),
            P(("dp", "tensor"), None),
            P(("dp", "tensor"), None),
            P("tensor", "dp"),
            P(("dp", "tensor")),
            P("dp", "tensor"),
            P("dp", "tensor"),
            P("tensor", "dp"),
        ),
        check_vma=False,
    )
```
